32 devices in a mesh: lat: 4 (over y, x), lon: 8 (over z, core).
Axes of the slice: x: 2, y: 2, z: 4, core: 2. Of those that a mesh axis runs over, the one named last changes fastest.
Arguments:
- inputs: bfloat16 [64, 1024, 64], P('lat', 'lon'), may hold values from -6 to 6
- pre_first: bfloat16 [64, 1024, 128], P('lat', 'lon'), may hold values from -6 to 6
- grad_out: bfloat16 [32, 512, 128], P('lat', 'lon'), may hold values from -6 to 6
- w_first: bfloat16 [3, 3, 64, 128], replicated, may hold values from -0.25 to 0.25
- w_second: bfloat16 [3, 3, 128, 128], replicated, may hold values from -0.1875 to 0.1875
Outputs:
- grad_inputs: bfloat16 [64, 1024, 64], P('lat', 'lon')
- grad_w_first: float32 [3, 3, 64, 128], replicated
- grad_w_second: float32 [3, 3, 128, 128], replicated
The draws below stay inside these ranges and needn't reach their ends.
All inputs are finite; a program needn't handle non-finite values.
Results may differ from the reference program's by a relative error of at most 0.0049.
Values may be sent and summed in bfloat16 or wider, within the bound.
No kernel may reach another device: no remote copies, remote signals or barrier semaphores. Data moves between devices by JAX's collectives and lax.ppermute only.
A program may use at most 64 MiB of HBM per device.

```python
import jax
import jax.numpy as jnp
from jax import lax

C0 = 64
C1 = 128
NLAT = 64
NLON = 1024


def levels(own_key, shape, shards, smallest, high):
    factor_of, own = 1.0, jax.random.fold_in(own_key, 6)
    for dim, shards_of in shards:
        steps = jnp.exp(jax.random.uniform(jax.random.fold_in(own, dim), (shards_of,), jnp.float32, smallest / len(shards), high / len(shards)))
        factor_of = factor_of * jnp.repeat(steps, shape[dim] // shards_of).reshape([-1 if axis == dim else 1 for axis in range(len(shape))])
    return factor_of


def scatter_about(own_key, extent, scale, limit, shards=(), kind=jnp.bfloat16):
    drawn = jax.random.normal(own_key, extent, jnp.float32) * scale
    if len(shards) > 0:
        drawn = levels(own_key, extent, shards, -0.22, 0.18) * drawn
    return jnp.clip(drawn, min=-limit, max=limit).astype(kind)


def setup_inputs(seed: int = 0) -> dict:
    key_list = jax.random.split(jax.random.key(seed), 6)
    inputs = scatter_about(key_list[0], (NLAT, NLON, C0), 1.0, 6.0, ((0, 4), (1, 8)))
    pre_first = scatter_about(key_list[1], (NLAT, NLON, C1), 1.0, 6.0, ((0, 4), (1, 8)))
    grad_out = scatter_about(key_list[2], (NLAT // 2, NLON // 2, C1), 1.0, 6.0, ((0, 4), (1, 8)))
    w_first = scatter_about(key_list[3], (3, 3, C0, C1), (9 * C0) ** -0.5, 0.25)
    w_second = scatter_about(key_list[4], (3, 3, C1, C1), (9 * C1) ** -0.5, 0.1875)
    return dict(inputs=inputs, pre_first=pre_first, grad_out=grad_out, w_first=w_first, w_second=w_second)


inv_root = 0.7071067811865476
density = 0.3989422804014327

def pad_fold(field):
    width = field.shape[1]
    cycle = jnp.concatenate([field[:, -1:], field, field[:, :1]], 1)
    turned = jnp.roll(field[0], -(width // 2), axis=0)
    top = jnp.concatenate([turned[-1:], turned, turned[:1]], 0)
    bottom = jnp.zeros_like(top)
    return jnp.concatenate([top[None], cycle, bottom[None]], 0)

def adjoint(grid, shape):
    _, pull = jax.vjp(pad_fold, jnp.zeros(shape, jnp.float32))
    return pull(grid)[0]

def taps_product(padded, grads):
    rows, cols = (grads.shape[0], grads.shape[1])
    flat = grads.reshape(rows * cols, grads.shape[2])
    result = []
    for a in range(3):
        line = []
        for b in range(3):
            piece = padded[a:a + rows, b:b + cols].reshape(rows * cols, padded.shape[2])
            line.append(jnp.dot(piece.T, flat, preferred_element_type=jnp.float32))
        result.append(jnp.stack(line, 0))
    return jnp.stack(result, 0)

def spread(grads, weight):
    rows, cols, cout = grads.shape
    cin = weight.shape[2]
    every = jnp.transpose(weight, (3, 0, 1, 2)).reshape(cout, 9 * cin)
    terms = jnp.dot(grads.reshape(rows * cols, cout), every, preferred_element_type=jnp.float32)
    terms = terms.reshape(rows, cols, 3, 3, cin)
    grid = jnp.zeros((rows + 2, cols + 2, cin), jnp.float32)
    for a in range(3):
        for b in range(3):
            grid = grid.at[a:a + rows, b:b + cols].add(terms[:, :, a, b])
    return grid

def reference(inputs, pre_first, grad_out, w_first, w_second):
    value = pre_first.astype(jnp.float32)
    cdf = 0.5 * (1.0 + lax.erf(value * inv_root))
    activated = (value * cdf).astype(jnp.bfloat16)
    slope = cdf + value * jnp.exp(-0.5 * value * value) * density
    grad_pool = jnp.repeat(jnp.repeat(grad_out, 2, 0), 2, 1) * jnp.asarray(0.25, grad_out.dtype)
    grad_w_second = taps_product(pad_fold(activated), grad_pool)
    grad_act = adjoint(spread(grad_pool, w_second), activated.shape)
    grad_pre = (grad_act * slope).astype(jnp.bfloat16)
    grad_w_first = taps_product(pad_fold(inputs), grad_pre)
    grad_inputs = adjoint(spread(grad_pre, w_first), inputs.shape).astype(jnp.bfloat16)
    return (grad_inputs, grad_w_first, grad_w_second)
```

```python
import functools

import jax
import jax.numpy as jnp
from jax import lax
from jax.experimental import pallas as pl
from jax.experimental.pallas import tpu as pltpu
from jax.sharding import PartitionSpec as P

inv_root = 0.7071067811865476
density = 0.3989422804014327

F32 = jnp.float32
BF16 = jnp.bfloat16
EDGE = 16
AREA = ("lat", "lon")


def cdf_of(value):
    return 0.5 * (1.0 + lax.erf(value * inv_root))


def slope_of(value, cdf):
    return 0.25 * (cdf + value * jnp.exp(-0.5 * value * value) * density)


def dot(left, right):
    return jnp.dot(left, right, preferred_element_type=F32)


def dot_nt(left, right):
    return lax.dot_general(left, right, (((1,), (1,)), ((), ())), preferred_element_type=F32)


def local_kernel(pre, fields, w_first, w_second, slope, act_t, fields_t, taps_first, taps_second,
                 line, thin, act_s, fields_s):
    rows, cols, c1 = pre.shape
    c0 = fields.shape[2]
    half = cols // 2

    def one_row(r, carry):
        line[...] = pre[r].astype(F32)
        thin[...] = fields[r].astype(F32)
        for pc in range(2):
            value = line[pl.ds(pc, half, stride=2), :]
            cdf = cdf_of(value)
            act_s[r % 2, r // 2, :, pc * c1:(pc + 1) * c1] = (value * cdf).astype(BF16)
            slope[r, :, pc * c1:(pc + 1) * c1] = slope_of(value, cdf)
            fields_s[pc, r] = thin[pl.ds(pc, half, stride=2), :].astype(BF16)
        return carry

    lax.fori_loop(0, rows, one_row, 0)
    for pr in range(2):
        act_t[pr] = act_s[pr].reshape(rows // 2 * half, 2 * c1).T
        fields_t[pr * c0:(pr + 1) * c0, :] = fields_s[pr].reshape(rows * half, c0).T
    taps_second[...] = jnp.zeros_like(taps_second)
    taps_first[...] = jnp.zeros_like(taps_first)
    for a in range(3):
        for pc, blocks in ((0, (2, 1, None, 0)), (1, (None, 2, 0, 1))):
            for k, b in enumerate(blocks):
                if b is not None:
                    taps_second[a, pc * c1:(pc + 1) * c1, k * c1:(k + 1) * c1] = w_second[a, b]
        for pc, blocks in ((0, (2, 1, 0, None)), (1, (None, 2, 1, 0))):
            for k, b in enumerate(blocks):
                if b is not None:
                    low = (2 * a + pc) * c0
                    taps_first[low:low + c0, k * c1:(k + 1) * c1] = w_first[a, b]


def middle_kernel(flags, grad_out, top, bottom, left, right, slope, act_t, fields_t, taps,
                  spread, own, other,
                  grid, wide, prods, ends, line, side, sides, sums, corner, keep):
    first, last, core = flags[0], flags[1], flags[2]
    rows, half, c2 = slope.shape
    c1 = c2 // 2
    pooled = rows // 2
    c0 = fields_t.shape[0] // 2
    cells = pooled * half

    grid[:, half:, :] = jnp.zeros((pooled + 2, EDGE, c1), F32)
    grid[1:pooled + 1, :half, :] = grad_out[...].astype(F32)
    grid[0, :half, :] = top[2 * half:, :].astype(F32)
    grid[pooled + 1, :half, :] = bottom[2 * half:, :].astype(F32)
    side[0] = left[...].astype(F32)
    side[1] = right[...].astype(F32)
    for i in range(pooled + 2):
        grid[i, half:half + 1, :] = side[1, rows + 2 + i:rows + 3 + i, :]
        grid[i, half + EDGE - 1:half + EDGE, :] = side[0, rows + 2 + i:rows + 3 + i, :]
    for i in range(pooled + 2):
        here = grid[i]
        wide[i, :, :c1] = pltpu.roll(here, 1, 0).astype(BF16)
        wide[i, :, c1:2 * c1] = here.astype(BF16)
        wide[i, :, 2 * c1:3 * c1] = pltpu.roll(here, half + EDGE - 1, 0).astype(BF16)
        wide[i, :, 3 * c1:] = here.astype(BF16)

    flat = wide[1:pooled + 1].reshape(pooled * (half + EDGE), 4 * c1)
    for a in range(3):
        prods[a] = dot_nt(flat, taps[a]).reshape(pooled, half + EDGE, c2)
    fold = jnp.where(first == 1, taps[0], taps[2])
    ends[0] = dot_nt(wide[0], fold)
    ends[1] = dot_nt(wide[0], taps[1])
    ends[2] = dot_nt(wide[pooled + 1], taps[0])
    ends[3] = dot_nt(wide[pooled + 1], taps[1])

    for s in range(2):
        sides[s] = slope_of(side[s], cdf_of(side[s]))

    def place(r, total, incline):
        inner = total[:half] * incline
        rim = total[half:]
        after = rim[:1, :c1] * sides[1, pl.ds(r, 1), :]
        before = rim[EDGE - 1:, c1:] * sides[0, pl.ds(r, 1), :]
        even, odd = inner[:, :c1], inner[:, c1:]
        at = lax.broadcasted_iota(jnp.int32, (half, c1), 0)
        spread[r, :, :c1] = jnp.where(at == 0, before, pltpu.roll(odd, 1, 0)).astype(BF16)
        spread[r, :, c1:2 * c1] = even.astype(BF16)
        spread[r, :, 2 * c1:3 * c1] = odd.astype(BF16)
        spread[r, :, 3 * c1:] = jnp.where(at == half - 1, after, pltpu.roll(even, half - 1, 0)).astype(BF16)

    def halo_slope(message):
        line[...] = message[:2 * half, :].astype(F32)
        both = [line[pl.ds(pc, half, stride=2), :] for pc in range(2)]
        return jnp.concatenate([slope_of(v, cdf_of(v)) for v in both], axis=1)

    place(0, ends[0] + ends[1] + prods[0, 0], halo_slope(top))
    place(1, ends[0] + prods[1, 0] + prods[0, 0], slope[0])

    def pair(i, carry):
        middle = prods[2, i] + prods[1, i]
        place(2 * i + 2, middle + prods[0, i + 1], slope[2 * i + 1])
        place(2 * i + 3, prods[2, i] + prods[1, i + 1] + prods[0, i + 1], slope[2 * i + 2])
        return carry

    lax.fori_loop(0, pooled - 1, pair, 0)
    final = prods[2, pooled - 1]
    place(rows, final + prods[1, pooled - 1] + ends[2], slope[rows - 1])
    outside = jnp.where(last == 1, 0.0, 1.0)
    place(rows + 1, (final + ends[3] + ends[2]) * outside, halo_slope(bottom))

    is_first = jnp.where(first == 1, 1.0, 0.0).astype(BF16)
    not_first = jnp.where(first == 1, 0.0, 1.0).astype(BF16)
    above = wide[0, :half, :3 * c1]
    wide[0, :half, :3 * c1] = above * not_first
    for n, (pr, start) in enumerate(((0, 0), (0, 1), (1, 1), (1, 2))):
        around = wide[start:start + pooled, :half, :3 * c1].reshape(cells, 3 * c1)
        sums[n] = dot(act_t[pr], around)
    corner[...] = dot(act_t[0, :, :half], above * is_first)

    unit = c0
    per_tap = c1 // unit
    count = 9 * per_tap + 9
    split = (count + 1) // 2

    def put(k, value):
        keep[k // split, (k % split) * unit:(k % split + 1) * unit, :] = value

    pieces = {0: ((0, 1), (1, 3)), 1: ((0, 1), (1, 2)), 2: ((0, 0), (1, 2))}
    for a in range(3):
        for b in range(3):
            total = None
            for pr, n in pieces[a]:
                for pc in range(2):
                    k = (pc + 1 - b) // 2 + 1
                    term = sums[n, pc * c1:(pc + 1) * c1, k * c1:(k + 1) * c1]
                    total = term if total is None else total + term
            if a == 0:
                for pc in range(2):
                    k = (pc + 1 - b) // 2 + 1
                    total = total + corner[pc * c1:(pc + 1) * c1, k * c1:(k + 1) * c1]
            total = total * 0.25
            for part in range(per_tap):
                put((3 * a + b) * per_tap + part, total[part * unit:(part + 1) * unit])

    head = spread[0]
    spread[0] = head * not_first
    folded = dot(fields_t[:, :half], head * is_first)
    for a in range(3):
        around = spread[2 - a:2 - a + rows].reshape(rows * half, 4 * c1)
        got = dot(fields_t[...], around)
        if a == 0:
            got = got + folded
        for b in range(3):
            even = got[:c0, (2 - b) * c1:(3 - b) * c1]
            odd = got[c0:, (3 - b) * c1:(4 - b) * c1]
            put(9 * per_tap + 3 * a + b, even + odd)
    spread[0] = head
    for k in range(count, 2 * split):
        put(k, jnp.zeros((unit, c1), F32))
    if own.shape[0] > split * unit:
        rest = jnp.zeros((own.shape[0] - split * unit, c1), F32)
        own[split * unit:] = rest
        other[split * unit:] = rest
    own[:split * unit] = keep[core]
    other[:split * unit] = keep[1 - core]


def last_kernel(flags, spread, taps, out, prods, line):
    rows, cols, c0 = out.shape
    half = cols // 2
    c2 = 2 * c0
    prods[...] = dot_nt(spread[1:rows + 1].reshape(rows * half, spread.shape[2]), taps[...]).reshape(
        rows, half, 3 * c2)
    fold = jnp.where(flags[0] == 1, taps[:c2], taps[2 * c2:])
    above = dot_nt(spread[0], fold)
    below = dot_nt(spread[rows + 1], taps[:c2])

    def emit(r, total):
        line[pl.ds(0, half, stride=2), :] = total[:, :c0]
        line[pl.ds(1, half, stride=2), :] = total[:, c0:]
        out[r] = line[...].astype(BF16)

    emit(0, prods[1, :, :c2] + prods[0, :, c2:2 * c2] + above)

    def inner(r, carry):
        emit(r, prods[r + 1, :, :c2] + prods[r, :, c2:2 * c2] + prods[r - 1, :, 2 * c2:])
        return carry

    lax.fori_loop(1, rows - 1, inner, 0)
    emit(rows - 1, below + prods[rows - 1, :, c2:2 * c2] + prods[rows - 2, :, 2 * c2:])


def vmem(count):
    return [pl.BlockSpec(memory_space=pltpu.VMEM)] * count


def params():
    return pltpu.CompilerParams(vmem_limit_bytes=48 * 1024 * 1024)


def shape(dims, kind):
    return jax.ShapeDtypeStruct(dims, kind)


def body(inputs, pre_first, grad_out, w_first, w_second):
    rows, cols, c1 = pre_first.shape
    c0 = inputs.shape[2]
    half, pooled = cols // 2, rows // 2
    lats, lons = lax.axis_size("lat"), lax.axis_size("lon")
    band, place = lax.axis_index("lat"), lax.axis_index("lon")
    core = lax.rem(place, 2)
    flags = jnp.stack([band == 0, band == lats - 1, core]).astype(jnp.int32)

    head = jnp.concatenate([pre_first[0], grad_out[0]], 0)
    tail = jnp.concatenate([pre_first[-1], grad_out[-1]], 0)
    down = lax.ppermute(tail, "lat", [(i, i + 1) for i in range(lats - 1)])
    up = lax.ppermute(head, "lat", [(i + 1, i) for i in range(lats - 1)])
    over = lax.ppermute(head, AREA, [(i, (i + lons // 2) % lons) for i in range(lons)])
    top = jnp.where(band == 0, over, down)
    bottom = up

    slope, act_t, fields_t, taps_first, taps_second = pl.pallas_call(
        local_kernel,
        out_shape=(
            shape((rows, half, 2 * c1), F32),
            shape((2, 2 * c1, pooled * half), BF16),
            shape((2 * c0, rows * half), BF16),
            shape((6 * c0, 4 * c1), BF16),
            shape((3, 2 * c1, 4 * c1), BF16),
        ),
        in_specs=vmem(4),
        out_specs=tuple(vmem(5)),
        scratch_shapes=[
            pltpu.VMEM((cols, c1), F32),
            pltpu.VMEM((cols, c0), F32),
            pltpu.VMEM((2, pooled, half, 2 * c1), BF16),
            pltpu.VMEM((2, rows, half, c0), BF16),
        ],
        compiler_params=params(),
        cost_estimate=pl.CostEstimate(flops=60 * rows * cols * c1, bytes_accessed=6 << 20,
                                      transcendentals=2 * rows * cols * c1),
    )(pre_first, inputs, w_first, w_second)

    def column(at):
        p, g = at * (cols - 1), at * (half - 1)
        parts = [top[p:p + 1], pre_first[:, p], bottom[p:p + 1],
                 top[cols + g:cols + g + 1], grad_out[:, g], bottom[cols + g:cols + g + 1]]
        pad = -(rows + pooled + 4) % 16
        return jnp.concatenate(parts + [jnp.zeros((pad, c1), BF16)], 0)

    left = lax.ppermute(column(1), "lon", [(i, (i + 1) % lons) for i in range(lons)])
    right = lax.ppermute(column(0), "lon", [(i, (i - 1) % lons) for i in range(lons)])

    chips = lats * lons // 2
    unit = 8 * chips
    split = (9 * (c1 // c0) + 10) // 2 * c0
    held = -(-split // unit) * unit
    span = half + EDGE
    spread, own, other = pl.pallas_call(
        middle_kernel,
        out_shape=(
            shape((rows + 2, half, 4 * c1), BF16),
            shape((held, c1), F32),
            shape((held, c1), F32),
        ),
        in_specs=[pl.BlockSpec(memory_space=pltpu.SMEM)] + vmem(9),
        out_specs=tuple(vmem(3)),
        scratch_shapes=[
            pltpu.VMEM((pooled + 2, span, c1), F32),
            pltpu.VMEM((pooled + 2, span, 4 * c1), BF16),
            pltpu.VMEM((3, pooled, span, 2 * c1), F32),
            pltpu.VMEM((4, span, 2 * c1), F32),
            pltpu.VMEM((cols, c1), F32),
            pltpu.VMEM((2, left.shape[0], c1), F32),
            pltpu.VMEM((2, left.shape[0], c1), F32),
            pltpu.VMEM((4, 2 * c1, 3 * c1), F32),
            pltpu.VMEM((2 * c1, 3 * c1), F32),
            pltpu.VMEM((2, split, c1), F32),
        ],
        compiler_params=params(),
        cost_estimate=pl.CostEstimate(flops=2 * rows * cols * c1 * 9 * (2 * c1 + c0), bytes_accessed=8 << 20,
                                      transcendentals=0),
    )(flags, grad_out, top, bottom, left, right, slope, act_t, fields_t, taps_second)

    swap = [(i, i ^ 1) for i in range(lons)]
    mine = own + lax.ppermute(other, "lon", swap)
    groups = [[2 * i + k for i in range(chips)] for k in range(2)]
    parts = lax.all_to_all(mine.reshape(chips, held // chips, c1), AREA, 0, 0,
                           axis_index_groups=groups, tiled=True)
    total = jnp.sum(parts, 0)
    every = lax.all_to_all(jnp.broadcast_to(total[None], parts.shape), AREA, 0, 0,
                           axis_index_groups=groups, tiled=True)
    mine = every.reshape(held, c1)[:split]
    theirs = lax.ppermute(mine, "lon", swap)

    grad_inputs = pl.pallas_call(
        last_kernel,
        out_shape=shape((rows, cols, c0), BF16),
        in_specs=[pl.BlockSpec(memory_space=pltpu.SMEM)] + vmem(2),
        out_specs=vmem(1)[0],
        scratch_shapes=[
            pltpu.VMEM((rows, half, 6 * c0), F32),
            pltpu.VMEM((cols, c0), F32),
        ],
        compiler_params=params(),
        cost_estimate=pl.CostEstimate(flops=2 * rows * cols * c1 * 9 * c0, bytes_accessed=3 << 20, transcendentals=0),
    )(flags, spread, taps_first)

    low = jnp.where(core == 0, mine, theirs)
    high = jnp.where(core == 0, theirs, mine)
    both = jnp.concatenate([low, high], 0)
    size = 9 * c1
    grad_w_second = both[:size].reshape(3, 3, c1, c1)
    grad_w_first = both[size:size + 9 * c0].reshape(3, 3, c0, c1)
    return (grad_inputs, grad_w_first, grad_w_second)


def solution(mesh):
    in_specs = (P("lat", "lon", None), P("lat", "lon", None), P("lat", "lon", None), P(), P())
    out_specs = (P("lat", "lon", None), P(), P())
    return jax.shard_map(body, mesh=mesh, in_specs=in_specs, out_specs=out_specs, check_vma=False)
```

```python
import jax
import jax.numpy as jnp
from jax import lax
from jax.experimental import pallas as pl
from jax.experimental.pallas import tpu as pltpu
from jax.sharding import PartitionSpec as P

inv_root = 0.7071067811865476
density = 0.3989422804014327

F32 = jnp.float32
BF16 = jnp.bfloat16
EDGE = 16
AREA = ("lat", "lon")


def cdf_of(value):
    return 0.5 * (1.0 + lax.erf(value * inv_root))


def slope_of(value, cdf):
    return 0.25 * (cdf + value * jnp.exp(-0.5 * value * value) * density)


def dot(left, right):
    return jnp.dot(left, right, preferred_element_type=F32)


def dot_nt(left, right):
    return lax.dot_general(left, right, (((1,), (1,)), ((), ())), preferred_element_type=F32)


def pack_kernel(pre, grad_out, head, tail, first_col, last_col, hold):
    rows, cols, c1 = pre.shape
    pooled, half = grad_out.shape[:2]
    head[:cols] = pre[0]
    head[cols:] = grad_out[0]
    tail[:cols] = pre[rows - 1]
    tail[cols:] = grad_out[pooled - 1]
    for message, p, g in ((first_col, 0, 0), (last_col, cols - 16, half - 16)):
        at = 0 if p == 0 else 15
        hold[rows + pooled:] = jnp.zeros((hold.shape[0] - rows - pooled, c1), F32)
        for r in range(rows):
            hold[r:r + 1] = pre[r, p:p + 16].astype(F32)[at:at + 1]
        for i in range(pooled):
            hold[rows + i:rows + i + 1] = grad_out[i, g:g + 16].astype(F32)[at:at + 1]
        message[...] = hold[...].astype(BF16)


def one_at(where):
    return jnp.where(where, 1.0, 0.0).astype(BF16)


def local_kernel(pre, fields, w_first, w_second, slope, act_t, fields_t, taps_first, taps_second,
                 line, act_s, turned):
    rows, cols, c1 = pre.shape
    c0 = fields.shape[1]
    half = cols // 2

    def one_row(r, carry):
        line[...] = pre[r].astype(F32)
        for pc in range(2):
            value = line[pl.ds(pc, half, stride=2), :]
            cdf = cdf_of(value)
            act_s[r % 2, r // 2, :, pc * c1:(pc + 1) * c1] = (value * cdf).astype(BF16)
            slope[r, :, pc * c1:(pc + 1) * c1] = slope_of(value, cdf)
        return carry

    lax.fori_loop(0, rows, one_row, 0)
    for pr in range(2):
        act_t[pr] = act_s[pr].reshape(rows // 2 * half, 2 * c1).T
    col = lax.broadcasted_iota(jnp.int32, (cols, 2 * cols), 0)
    lane = lax.broadcasted_iota(jnp.int32, (cols, 2 * cols), 1)
    turn = lane // cols
    parity = (lane % cols) // half
    parity = parity + turn - 2 * parity * turn
    order = one_at(col == 2 * (lane % half) + parity)
    turned[...] = dot(fields[...].reshape(rows * c0, cols), order).astype(BF16).reshape(rows, c0, 2 * cols)
    low = lax.broadcasted_iota(jnp.int32, (c0, cols), 1) < half
    for q in range(rows // 2):
        fields_t[:c0, q * cols:(q + 1) * cols] = jnp.where(low, turned[2 * q, :, :cols], turned[2 * q + 1, :, cols:])
        fields_t[c0:, q * cols:(q + 1) * cols] = jnp.where(low, turned[2 * q, :, cols:], turned[2 * q + 1, :, :cols])
    taps_second[...] = jnp.zeros_like(taps_second)
    taps_first[...] = jnp.zeros_like(taps_first)
    for a in range(3):
        for pc, blocks in ((0, (2, 1, None, 0)), (1, (None, 2, 0, 1))):
            for k, b in enumerate(blocks):
                if b is not None:
                    taps_second[a, pc * c1:(pc + 1) * c1, k * c1:(k + 1) * c1] = w_second[a, b]
        for pc, blocks in ((0, (2, 1, 0, None)), (1, (None, 2, 1, 0))):
            for k, b in enumerate(blocks):
                if b is not None:
                    start = (2 * a + pc) * c0
                    taps_first[start:start + c0, k * c1:(k + 1) * c1] = w_first[a, b]


def middle_kernel(flags, grad_out, top, bottom, left, right, slope, act_t, fields_t, taps,
                  spread, own, other,
                  grid, wide, prods, ends, line, side, sides, sums, corner, keep):
    first, last, core = flags[0], flags[1], flags[2]
    rows, half, c2 = slope.shape
    c1 = c2 // 2
    pooled = rows // 2
    c0 = fields_t.shape[0] // 2
    cells = pooled * half

    grid[:, half:, :] = jnp.zeros((pooled + 2, EDGE, c1), F32)
    grid[1:pooled + 1, :half, :] = grad_out[...].astype(F32)
    grid[0, :half, :] = top[2 * half:, :].astype(F32)
    grid[pooled + 1, :half, :] = bottom[2 * half:, :].astype(F32)
    side[0] = left[...].astype(F32)
    side[1] = right[...].astype(F32)
    for i in range(pooled + 2):
        at = rows + i - 1
        if i == 0:
            at = rows + pooled + 2
        if i == pooled + 1:
            at = rows + pooled + 3
        grid[i, half:half + 1, :] = side[1, at:at + 1, :]
        grid[i, half + EDGE - 1:half + EDGE, :] = side[0, at:at + 1, :]
    for i in range(pooled + 2):
        here = grid[i]
        wide[i, :, :c1] = pltpu.roll(here, 1, 0).astype(BF16)
        wide[i, :, c1:2 * c1] = here.astype(BF16)
        wide[i, :, 2 * c1:3 * c1] = pltpu.roll(here, half + EDGE - 1, 0).astype(BF16)
        wide[i, :, 3 * c1:] = here.astype(BF16)

    flat = wide[1:pooled + 1].reshape(pooled * (half + EDGE), 4 * c1)
    for a in range(3):
        prods[a] = dot_nt(flat, taps[a]).reshape(pooled, half + EDGE, c2)
    fold = jnp.where(first == 1, taps[0], taps[2])
    ends[0] = dot_nt(wide[0], fold)
    ends[1] = dot_nt(wide[0], taps[1])
    ends[2] = dot_nt(wide[pooled + 1], taps[0])
    ends[3] = dot_nt(wide[pooled + 1], taps[1])

    for s in range(2):
        sides[s] = slope_of(side[s], cdf_of(side[s]))

    def place(r, total, incline, edge):
        inner = total[:half] * incline
        rim = total[half:]
        after = rim[:1, :c1] * sides[1, pl.ds(edge, 1), :]
        before = rim[EDGE - 1:, c1:] * sides[0, pl.ds(edge, 1), :]
        even, odd = inner[:, :c1], inner[:, c1:]
        at = lax.broadcasted_iota(jnp.int32, (half, c1), 0)
        spread[r, :, :c1] = jnp.where(at == 0, before, pltpu.roll(odd, 1, 0)).astype(BF16)
        spread[r, :, c1:2 * c1] = even.astype(BF16)
        spread[r, :, 2 * c1:3 * c1] = odd.astype(BF16)
        spread[r, :, 3 * c1:] = jnp.where(at == half - 1, after, pltpu.roll(even, half - 1, 0)).astype(BF16)

    def halo_slope(message):
        line[...] = message[:2 * half, :].astype(F32)
        both = [line[pl.ds(pc, half, stride=2), :] for pc in range(2)]
        return jnp.concatenate([slope_of(v, cdf_of(v)) for v in both], axis=1)

    place(0, ends[0] + ends[1] + prods[0, 0], halo_slope(top), rows + pooled)
    place(1, ends[0] + prods[1, 0] + prods[0, 0], slope[0], 0)

    def pair(i, carry):
        middle = prods[2, i] + prods[1, i]
        place(2 * i + 2, middle + prods[0, i + 1], slope[2 * i + 1], 2 * i + 1)
        place(2 * i + 3, prods[2, i] + prods[1, i + 1] + prods[0, i + 1], slope[2 * i + 2], 2 * i + 2)
        return carry

    lax.fori_loop(0, pooled - 1, pair, 0)
    final = prods[2, pooled - 1]
    place(rows, final + prods[1, pooled - 1] + ends[2], slope[rows - 1], rows - 1)
    outside = jnp.where(last == 1, 0.0, 1.0)
    place(rows + 1, (final + ends[3] + ends[2]) * outside, halo_slope(bottom), rows + pooled + 1)

    is_first = jnp.where(first == 1, 1.0, 0.0).astype(BF16)
    not_first = jnp.where(first == 1, 0.0, 1.0).astype(BF16)
    above = wide[0, :half, :3 * c1]
    wide[0, :half, :3 * c1] = above * not_first
    for n, (pr, start) in enumerate(((0, 0), (0, 1), (1, 1), (1, 2))):
        around = wide[start:start + pooled, :half, :3 * c1].reshape(cells, 3 * c1)
        sums[n] = dot(act_t[pr], around)
    corner[...] = dot(act_t[0, :, :half], above * is_first)

    unit = c0
    per_tap = c1 // unit
    count = 9 * per_tap + 9
    held = own.shape[0]

    def put(k, value):
        keep[k * unit:(k + 1) * unit, :] = value

    pieces = {0: ((0, 1), (1, 3)), 1: ((0, 1), (1, 2)), 2: ((0, 0), (1, 2))}
    for a in range(3):
        for b in range(3):
            total = None
            for pr, n in pieces[a]:
                for pc in range(2):
                    k = (pc + 1 - b) // 2 + 1
                    term = sums[n, pc * c1:(pc + 1) * c1, k * c1:(k + 1) * c1]
                    total = term if total is None else total + term
            if a == 0:
                for pc in range(2):
                    k = (pc + 1 - b) // 2 + 1
                    total = total + corner[pc * c1:(pc + 1) * c1, k * c1:(k + 1) * c1]
            total = total * 0.25
            for part in range(per_tap):
                put((3 * a + b) * per_tap + part, total[part * unit:(part + 1) * unit])

    head = spread[0]
    spread[0] = head * not_first
    spread[rows + 2] = head * is_first
    folded = dot(fields_t[:, :half], spread[rows + 2])
    for a in range(3):
        around = spread[2 - a:2 - a + rows].reshape(rows * half, 4 * c1)
        got = dot(fields_t[...], around)
        if a == 0:
            got = got + folded
        for b in range(3):
            even = got[:c0, (2 - b) * c1:(3 - b) * c1]
            odd = got[c0:, (3 - b) * c1:(4 - b) * c1]
            put(9 * per_tap + 3 * a + b, even + odd)
    keep[count * unit:] = jnp.zeros((2 * held - count * unit, c1), F32)
    own[...] = keep[pl.ds(pl.multiple_of(core * held, held), held), :]
    other[...] = keep[pl.ds(pl.multiple_of((1 - core) * held, held), held), :]


def last_kernel(spread, taps, out, total, turned):
    rows, c0, cols = out.shape
    half = cols // 2
    c2 = 2 * c0
    depth = spread.shape[2]
    result = dot_nt(taps[:c2], spread[2:rows + 2].reshape(rows * half, depth))
    for a in (1, 2):
        result = result + dot_nt(taps[a * c2:(a + 1) * c2],
                                 spread[2 - a:2 - a + rows].reshape(rows * half, depth))
    total[...] = result
    total[:, :half] = total[:, :half] + dot_nt(taps[:c2], spread[rows + 2])
    for q in range(rows // 2):
        pair = total[:, q * cols:(q + 1) * cols].astype(BF16)
        turned[q, :, :cols] = pair[:c0]
        turned[q, :, cols:] = pair[c0:]
    k = lax.broadcasted_iota(jnp.int32, (2 * cols, 2 * cols), 0)
    n = lax.broadcasted_iota(jnp.int32, (2 * cols, 2 * cols), 1)
    order = one_at(n == ((k % cols) // half) * cols + 2 * (k % half) + k // cols)
    found = dot(turned[...].reshape(rows // 2 * c0, 2 * cols), order).astype(BF16)
    for q in range(rows // 2):
        for rp in range(2):
            out[2 * q + rp] = found[q * c0:(q + 1) * c0, rp * cols:(rp + 1) * cols]


def gather_kernel(flags, mine, theirs, out_first, out_second):
    band, core = flags[3], flags[2]
    lats, count, rows, c1 = mine.shape
    size = out_second.shape[0]
    total = size + out_first.shape[0]
    for h in range(2):
        for i in range(lats):
            for j in range(count):
                at = ((h * lats + i) * count + j) * rows
                if at < total:
                    source = i ^ band
                    piece = jnp.where(core == h, mine[source, j], theirs[source, j]).astype(F32)
                    for out, base, end in ((out_second, 0, size), (out_first, size, total)):
                        low, high = max(at, base), min(at + rows, end)
                        if low < high:
                            out[low - base:high - base] = piece[low - at:high - at]


def vmem(count):
    return [pl.BlockSpec(memory_space=pltpu.VMEM)] * count


def params():
    return pltpu.CompilerParams(vmem_limit_bytes=48 * 1024 * 1024)


def shape(dims, kind):
    return jax.ShapeDtypeStruct(dims, kind)


def body(inputs, pre_first, grad_out, w_first, w_second):
    rows, cols, c1 = pre_first.shape
    c0 = inputs.shape[2]
    half, pooled = cols // 2, rows // 2
    lats, lons = lax.axis_size("lat"), lax.axis_size("lon")
    depths = lons // 2
    band, place = lax.axis_index("lat"), lax.axis_index("lon")
    core = lax.rem(place, 2)
    flags = jnp.stack([(band == 0).astype(jnp.int32), (band == lats - 1).astype(jnp.int32), core, band])

    edge = -(-(rows + pooled + 4) // 16) * 16
    head, tail, first_col, last_col = pl.pallas_call(
        pack_kernel,
        out_shape=(
            shape((cols + half, c1), BF16),
            shape((cols + half, c1), BF16),
            shape((edge, c1), BF16),
            shape((edge, c1), BF16),
        ),
        in_specs=vmem(2),
        out_specs=tuple(vmem(4)),
        scratch_shapes=[pltpu.VMEM((edge, c1), F32)],
        compiler_params=params(),
        cost_estimate=pl.CostEstimate(flops=1000, bytes_accessed=1 << 18, transcendentals=0),
    )(pre_first, grad_out)
    down = lax.ppermute(tail, "lat", [(i, i + 1) for i in range(lats - 1)])
    over = lax.ppermute(head, AREA, [(i, (i + lons // 2) % lons) for i in range(lons)])
    bottom = lax.ppermute(head, "lat", [(i + 1, i) for i in range(lats - 1)])
    top = jnp.where(band == 0, over, down)

    slope, act_t, fields_t, taps_first, taps_second = pl.pallas_call(
        local_kernel,
        out_shape=(
            shape((rows, half, 2 * c1), F32),
            shape((2, 2 * c1, pooled * half), BF16),
            shape((2 * c0, rows * half), BF16),
            shape((6 * c0, 4 * c1), BF16),
            shape((3, 2 * c1, 4 * c1), BF16),
        ),
        in_specs=vmem(4),
        out_specs=tuple(vmem(5)),
        scratch_shapes=[
            pltpu.VMEM((cols, c1), F32),
            pltpu.VMEM((2, pooled, half, 2 * c1), BF16),
            pltpu.VMEM((rows, c0, 2 * cols), BF16),
        ],
        compiler_params=params(),
        cost_estimate=pl.CostEstimate(flops=60 * rows * cols * c1, bytes_accessed=6 << 20,
                                      transcendentals=2 * rows * cols * c1),
    )(pre_first, jnp.transpose(inputs, (0, 2, 1)), w_first, w_second)

    def column(own_part, at):
        p, g = at * (cols - 1), cols + at * (half - 1)
        parts = [own_part[:rows + pooled], top[p:p + 1], bottom[p:p + 1], top[g:g + 1], bottom[g:g + 1]]
        return jnp.concatenate(parts + [jnp.zeros((edge - rows - pooled - 4, c1), BF16)], 0)

    left = lax.ppermute(column(last_col, 1), "lon", [(i, (i + 1) % lons) for i in range(lons)])
    right = lax.ppermute(column(first_col, 0), "lon", [(i, (i - 1) % lons) for i in range(lons)])

    chips = lats * depths
    size = 9 * (c1 + c0)
    piece = -(-size // (2 * chips * 16)) * 16
    held = chips * piece
    span = half + EDGE
    spread, own, other = pl.pallas_call(
        middle_kernel,
        out_shape=(
            shape((rows + 3, half, 4 * c1), BF16),
            shape((held, c1), F32),
            shape((held, c1), F32),
        ),
        in_specs=[pl.BlockSpec(memory_space=pltpu.SMEM)] + vmem(9),
        out_specs=tuple(vmem(3)),
        scratch_shapes=[
            pltpu.VMEM((pooled + 2, span, c1), F32),
            pltpu.VMEM((pooled + 2, span, 4 * c1), BF16),
            pltpu.VMEM((3, pooled, span, 2 * c1), F32),
            pltpu.VMEM((4, span, 2 * c1), F32),
            pltpu.VMEM((cols, c1), F32),
            pltpu.VMEM((2, edge, c1), F32),
            pltpu.VMEM((2, edge, c1), F32),
            pltpu.VMEM((4, 2 * c1, 3 * c1), F32),
            pltpu.VMEM((2 * c1, 3 * c1), F32),
            pltpu.VMEM((2 * held, c1), F32),
        ],
        compiler_params=params(),
        cost_estimate=pl.CostEstimate(flops=2 * rows * cols * c1 * 9 * (2 * c1 + c0), bytes_accessed=8 << 20,
                                      transcendentals=0),
    )(flags, grad_out, top, bottom, left, right, slope, act_t, fields_t, taps_second)

    swap = [(i, i ^ 1) for i in range(lons)]
    parts = (own + lax.ppermute(other, "lon", swap)).reshape(lats, depths * piece, c1)
    total = lax.dynamic_index_in_dim(parts, band, 0, False)
    for k in range(1, lats):
        sent = lax.dynamic_index_in_dim(parts, band ^ k, 0, False).astype(BF16)
        total = total + lax.ppermute(sent, "lat", [(i, i ^ k) for i in range(lats)]).astype(F32)
    groups = [[2 * i + k for i in range(depths)] for k in range(2)]
    line = lax.all_to_all(total.reshape(depths, piece, c1).astype(BF16), "lon", 0, 0,
                          axis_index_groups=groups, tiled=True)
    total = jnp.sum(line.astype(F32), 0).astype(BF16)
    line = lax.all_to_all(jnp.broadcast_to(total[None], line.shape), "lon", 0, 0,
                          axis_index_groups=groups, tiled=True)
    every = [line] + [lax.ppermute(line, "lat", [(i, i ^ k) for i in range(lats)]) for k in range(1, lats)]
    mine = jnp.stack(every, 0)
    theirs = lax.ppermute(mine, "lon", swap)

    grad_inputs = pl.pallas_call(
        last_kernel,
        out_shape=shape((rows, c0, cols), BF16),
        in_specs=vmem(2),
        out_specs=vmem(1)[0],
        scratch_shapes=[
            pltpu.VMEM((2 * c0, rows * half), F32),
            pltpu.VMEM((pooled, c0, 2 * cols), BF16),
        ],
        compiler_params=params(),
        cost_estimate=pl.CostEstimate(flops=2 * rows * cols * c1 * 9 * c0, bytes_accessed=3 << 20, transcendentals=0),
    )(spread, taps_first)

    grad_w_first, grad_w_second = pl.pallas_call(
        gather_kernel,
        out_shape=(shape((9 * c0, c1), F32), shape((9 * c1, c1), F32)),
        in_specs=[pl.BlockSpec(memory_space=pltpu.SMEM)] + vmem(2),
        out_specs=tuple(vmem(2)),
        compiler_params=params(),
        cost_estimate=pl.CostEstimate(flops=1000, bytes_accessed=3 << 19, transcendentals=0),
    )(flags, mine, theirs)
    return (jnp.transpose(grad_inputs, (0, 2, 1)), grad_w_first.reshape(w_first.shape),
            grad_w_second.reshape(w_second.shape))


def solution(mesh):
    in_specs = (P("lat", "lon", None), P("lat", "lon", None), P("lat", "lon", None), P(), P())
    out_specs = (P("lat", "lon", None), P(), P())
    return jax.shard_map(body, mesh=mesh, in_specs=in_specs, out_specs=out_specs, check_vma=False)
```

```python
import functools

import jax
import jax.numpy as jnp
from jax import lax
from jax.experimental import pallas as pl
from jax.experimental.pallas import tpu as pltpu
from jax.sharding import PartitionSpec as P

inv_root = 0.7071067811865476
density = 0.3989422804014327

F32 = jnp.float32
BF16 = jnp.bfloat16
EDGE = 16
AREA = ("lat", "lon")


def cdf_of(value):
    return 0.5 * (1.0 + lax.erf(value * inv_root))


def slope_of(value, cdf):
    return 0.25 * (cdf + value * jnp.exp(-0.5 * value * value) * density)


def dot(left, right):
    return jnp.dot(left, right, preferred_element_type=F32)


def dot_nt(left, right):
    return lax.dot_general(left, right, (((1,), (1,)), ((), ())), preferred_element_type=F32)


def pack_kernel(pre, grad_out, head, tail, first_col, last_col, hold):
    rows, cols, c1 = pre.shape
    pooled, half = grad_out.shape[:2]
    head[:cols] = pre[0]
    head[cols:] = grad_out[0]
    tail[:cols] = pre[rows - 1]
    tail[cols:] = grad_out[pooled - 1]
    for message, p, g in ((first_col, 0, 0), (last_col, cols - 16, half - 16)):
        at = 0 if p == 0 else 15
        hold[rows + pooled:] = jnp.zeros((hold.shape[0] - rows - pooled, c1), F32)
        for r in range(rows):
            hold[r:r + 1] = pre[r, p:p + 16].astype(F32)[at:at + 1]
        for i in range(pooled):
            hold[rows + i:rows + i + 1] = grad_out[i, g:g + 16].astype(F32)[at:at + 1]
        message[...] = hold[...].astype(BF16)


def one_at(where):
    return jnp.where(where, 1.0, 0.0).astype(BF16)


def local_kernel(pre, slope, act_t, line, act_s):
    rows, cols, c1 = pre.shape
    half = cols // 2

    def one_row(r, carry):
        line[...] = pre[r].astype(F32)
        for pc in range(2):
            value = line[pl.ds(pc, half, stride=2), :]
            cdf = cdf_of(value)
            act_s[r % 2, r // 2, :, pc * c1:(pc + 1) * c1] = (value * cdf).astype(BF16)
            slope[r, :, pc * c1:(pc + 1) * c1] = slope_of(value, cdf)
        return carry

    lax.fori_loop(0, rows, one_row, 0)
    for pr in range(2):
        act_t[pr] = act_s[pr].reshape(rows // 2 * half, 2 * c1).T


def layout_kernel(fields, w_first, w_second, fields_t, taps_first, taps_second, turned):
    rows, c0, cols = fields.shape
    c1 = w_first.shape[3]
    half = cols // 2
    col = lax.broadcasted_iota(jnp.int32, (cols, 2 * cols), 0)
    lane = lax.broadcasted_iota(jnp.int32, (cols, 2 * cols), 1)
    turn = lane // cols
    parity = (lane % cols) // half
    parity = parity + turn - 2 * parity * turn
    order = one_at(col == 2 * (lane % half) + parity)
    turned[...] = dot(fields[...].reshape(rows * c0, cols), order).astype(BF16).reshape(rows, c0, 2 * cols)
    low = lax.broadcasted_iota(jnp.int32, (c0, cols), 1) < half
    for q in range(rows // 2):
        fields_t[:c0, q * cols:(q + 1) * cols] = jnp.where(low, turned[2 * q, :, :cols], turned[2 * q + 1, :, cols:])
        fields_t[c0:, q * cols:(q + 1) * cols] = jnp.where(low, turned[2 * q, :, cols:], turned[2 * q + 1, :, :cols])
    taps_second[...] = jnp.zeros_like(taps_second)
    taps_first[...] = jnp.zeros_like(taps_first)
    for a in range(3):
        for pc, blocks in ((0, (2, 1, None, 0)), (1, (None, 2, 0, 1))):
            for k, b in enumerate(blocks):
                if b is not None:
                    taps_second[a, pc * c1:(pc + 1) * c1, k * c1:(k + 1) * c1] = w_second[a, b]
        for pc, blocks in ((0, (2, 1, 0, None)), (1, (None, 2, 1, 0))):
            for k, b in enumerate(blocks):
                if b is not None:
                    start = (2 * a + pc) * c0
                    taps_first[start:start + c0, k * c1:(k + 1) * c1] = w_first[a, b]


def steps(count, core):
    bits = count.bit_length() - 1
    return [1 << ((t + core) % bits) for t in range(bits)]


def distance(index, masks):
    return sum(m for t, m in enumerate(masks) if (index >> (len(masks) - 1 - t)) & 1)


def middle_kernel(lats, flags, grad_out, top, bottom, left, right, slope, act_t, fields_t, taps,
                  spread, own, other,
                  grid, wide, prods, ends, line, side, sides, sums, corner, keep):
    first, last, core = flags[0], flags[1], flags[2]
    rows, half, c2 = slope.shape
    c1 = c2 // 2
    pooled = rows // 2
    c0 = fields_t.shape[0] // 2
    cells = pooled * half

    grid[:, half:, :] = jnp.zeros((pooled + 2, EDGE, c1), F32)
    grid[1:pooled + 1, :half, :] = grad_out[...].astype(F32)
    grid[0, :half, :] = top[2 * half:, :].astype(F32)
    outside = jnp.where(last == 1, 0.0, 1.0)
    grid[pooled + 1, :half, :] = bottom[2 * half:, :].astype(F32) * outside
    side[0] = left[...].astype(F32)
    side[1] = right[...].astype(F32)
    for i in range(pooled + 2):
        at = rows + i - 1
        if i == 0:
            at = rows + pooled + 2
        if i == pooled + 1:
            at = rows + pooled + 3
        kept = outside if i == pooled + 1 else 1.0
        grid[i, half:half + 1, :] = side[1, at:at + 1, :] * kept
        grid[i, half + EDGE - 1:half + EDGE, :] = side[0, at:at + 1, :] * kept
    for i in range(pooled + 2):
        here = grid[i]
        wide[i, :, :c1] = pltpu.roll(here, 1, 0).astype(BF16)
        wide[i, :, c1:2 * c1] = here.astype(BF16)
        wide[i, :, 2 * c1:3 * c1] = pltpu.roll(here, half + EDGE - 1, 0).astype(BF16)
        wide[i, :, 3 * c1:] = here.astype(BF16)

    flat = wide[1:pooled + 1].reshape(pooled * (half + EDGE), 4 * c1)
    for a in range(3):
        prods[a] = dot_nt(flat, taps[a]).reshape(pooled, half + EDGE, c2)
    fold = jnp.where(first == 1, taps[0], taps[2])
    ends[0] = dot_nt(wide[0], fold)
    ends[1] = dot_nt(wide[0], taps[1])
    ends[2] = dot_nt(wide[pooled + 1], taps[0])
    ends[3] = dot_nt(wide[pooled + 1], taps[1])

    for s in range(2):
        sides[s] = slope_of(side[s], cdf_of(side[s]))

    def place(r, total, incline, edge):
        inner = total[:half] * incline
        rim = total[half:]
        after = rim[:1, :c1] * sides[1, pl.ds(edge, 1), :]
        before = rim[EDGE - 1:, c1:] * sides[0, pl.ds(edge, 1), :]
        even, odd = inner[:, :c1], inner[:, c1:]
        at = lax.broadcasted_iota(jnp.int32, (half, c1), 0)
        spread[r, :, :c1] = jnp.where(at == 0, before, pltpu.roll(odd, 1, 0)).astype(BF16)
        spread[r, :, c1:2 * c1] = even.astype(BF16)
        spread[r, :, 2 * c1:3 * c1] = odd.astype(BF16)
        spread[r, :, 3 * c1:] = jnp.where(at == half - 1, after, pltpu.roll(even, half - 1, 0)).astype(BF16)

    def halo_slope(message):
        line[...] = message[:2 * half, :].astype(F32)
        both = [line[pl.ds(pc, half, stride=2), :] for pc in range(2)]
        return jnp.concatenate([slope_of(v, cdf_of(v)) for v in both], axis=1)

    place(0, ends[0] + ends[1] + prods[0, 0], halo_slope(top), rows + pooled)
    place(1, ends[0] + prods[1, 0] + prods[0, 0], slope[0], 0)

    def pair(i, carry):
        middle = prods[2, i] + prods[1, i]
        place(2 * i + 2, middle + prods[0, i + 1], slope[2 * i + 1], 2 * i + 1)
        place(2 * i + 3, prods[2, i] + prods[1, i + 1] + prods[0, i + 1], slope[2 * i + 2], 2 * i + 2)
        return carry

    lax.fori_loop(0, pooled - 1, pair, 0)
    final = prods[2, pooled - 1]
    place(rows, final + prods[1, pooled - 1] + ends[2], slope[rows - 1], rows - 1)
    place(rows + 1, (final + ends[3] + ends[2]) * outside, halo_slope(bottom), rows + pooled + 1)

    is_first = jnp.where(first == 1, 1.0, 0.0).astype(BF16)
    not_first = jnp.where(first == 1, 0.0, 1.0).astype(BF16)
    above = wide[0, :half, :3 * c1]
    wide[0, :half, :3 * c1] = above * not_first
    for n, (pr, start) in enumerate(((0, 0), (0, 1), (1, 1), (1, 2))):
        around = wide[start:start + pooled, :half, :3 * c1].reshape(cells, 3 * c1)
        sums[n] = dot(act_t[pr], around)
    corner[...] = dot(act_t[0, :, :half], above * is_first)

    unit = c0
    per_tap = c1 // unit
    count = 9 * per_tap + 9
    held = own.shape[0]

    def put(k, value):
        keep[k * unit:(k + 1) * unit, :] = value

    pieces = {0: ((0, 1), (1, 3)), 1: ((0, 1), (1, 2)), 2: ((0, 0), (1, 2))}
    for a in range(3):
        for b in range(3):
            total = None
            for pr, n in pieces[a]:
                for pc in range(2):
                    k = (pc + 1 - b) // 2 + 1
                    term = sums[n, pc * c1:(pc + 1) * c1, k * c1:(k + 1) * c1]
                    total = term if total is None else total + term
            if a == 0:
                for pc in range(2):
                    k = (pc + 1 - b) // 2 + 1
                    total = total + corner[pc * c1:(pc + 1) * c1, k * c1:(k + 1) * c1]
            total = total * 0.25
            for part in range(per_tap):
                put((3 * a + b) * per_tap + part, total[part * unit:(part + 1) * unit])

    head = spread[0]
    spread[0] = head * not_first
    spread[rows + 2] = head * is_first
    folded = dot(fields_t[:, :half], spread[rows + 2])
    for a in range(3):
        around = spread[2 - a:2 - a + rows].reshape(rows * half, 4 * c1)
        got = dot(fields_t[...], around)
        if a == 0:
            got = got + folded
        for b in range(3):
            even = got[:c0, (2 - b) * c1:(3 - b) * c1]
            odd = got[c0:, (3 - b) * c1:(4 - b) * c1]
            put(9 * per_tap + 3 * a + b, even + odd)
    keep[count * unit:] = jnp.zeros((2 * held - count * unit, c1), F32)
    band = flags[3]
    block = held // lats
    orders = [steps(lats, k) for k in range(2)]
    for index in range(lats):
        far = [distance(index, masks) for masks in orders]
        for target, half_of in ((own, core), (other, 1 - core)):
            piece_at = half_of * lats + (band ^ jnp.where(half_of == 0, far[0], far[1]))
            target[index * block:(index + 1) * block] = keep[pl.ds(pl.multiple_of(piece_at * block, block), block), :]


def last_kernel(spread, taps, out, total, turned):
    rows, c0, cols = out.shape
    half = cols // 2
    c2 = 2 * c0
    depth = spread.shape[2]
    result = dot_nt(taps[:c2], spread[2:rows + 2].reshape(rows * half, depth))
    for a in (1, 2):
        result = result + dot_nt(taps[a * c2:(a + 1) * c2],
                                 spread[2 - a:2 - a + rows].reshape(rows * half, depth))
    total[...] = result
    total[:, :half] = total[:, :half] + dot_nt(taps[:c2], spread[rows + 2])
    for q in range(rows // 2):
        pair = total[:, q * cols:(q + 1) * cols].astype(BF16)
        turned[q, :, :cols] = pair[:c0]
        turned[q, :, cols:] = pair[c0:]
    k = lax.broadcasted_iota(jnp.int32, (2 * cols, 2 * cols), 0)
    n = lax.broadcasted_iota(jnp.int32, (2 * cols, 2 * cols), 1)
    order = one_at(n == ((k % cols) // half) * cols + 2 * (k % half) + k // cols)
    found = dot(turned[...].reshape(rows // 2 * c0, 2 * cols), order).astype(BF16)
    for q in range(rows // 2):
        for rp in range(2):
            out[2 * q + rp] = found[q * c0:(q + 1) * c0, rp * cols:(rp + 1) * cols]


def gather_kernel(flags, mine, theirs, out_first, out_second):
    band, core = flags[3], flags[2]
    lats, rows, c1 = mine.shape
    size = out_second.shape[0]
    total = size + out_first.shape[0]
    for h in range(2):
        masks = steps(lats, h)
        for i in range(lats):
            at = (h * lats + i) * rows
            far = i ^ band
            source = 0
            for m in masks:
                source = 2 * source + (far // m) % 2
            for out, base, end in ((out_second, 0, size), (out_first, size, total)):
                low, high = max(at, base), min(at + rows, end)
                if low < high:
                    here, there = (x[source, low - at:high - at] for x in (mine, theirs))
                    out[low - base:high - base] = jnp.where(core == h, here, there).astype(F32)


def vmem(count):
    return [pl.BlockSpec(memory_space=pltpu.VMEM)] * count


def params(mib):
    return pltpu.CompilerParams(vmem_limit_bytes=mib * 1024 * 1024)


def shape(dims, kind):
    return jax.ShapeDtypeStruct(dims, kind)


def body(inputs, pre_first, grad_out, w_first, w_second):
    rows, cols, c1 = pre_first.shape
    c0 = inputs.shape[2]
    half, pooled = cols // 2, rows // 2
    lats, lons = lax.axis_size("lat"), lax.axis_size("lon")
    depths = lons // 2
    band, place = lax.axis_index("lat"), lax.axis_index("lon")
    core = lax.rem(place, 2)
    flags = jnp.stack([(band == 0).astype(jnp.int32), (band == lats - 1).astype(jnp.int32), core, band])

    edge = -(-(rows + pooled + 4) // 16) * 16
    head, tail, first_col, last_col = pl.pallas_call(
        pack_kernel,
        out_shape=(
            shape((cols + half, c1), BF16),
            shape((cols + half, c1), BF16),
            shape((edge, c1), BF16),
            shape((edge, c1), BF16),
        ),
        in_specs=vmem(2),
        out_specs=tuple(vmem(4)),
        scratch_shapes=[
            pltpu.VMEM((edge, c1), F32),
        ],
        compiler_params=params(50),
        cost_estimate=pl.CostEstimate(flops=1000, bytes_accessed=1 << 18, transcendentals=0),
    )(pre_first, grad_out)
    over = lax.ppermute(head, AREA, [(i, (i + lons // 2) % lons) for i in range(lons)])
    down = lax.ppermute(tail, "lat", [(i, (i + 1) % lats) for i in range(lats)])
    bottom = lax.ppermute(head, "lat", [(i, (i - 1) % lats) for i in range(lats)])

    slope, act_t = pl.pallas_call(
        local_kernel,
        out_shape=(
            shape((rows, half, 2 * c1), F32),
            shape((2, 2 * c1, pooled * half), BF16),
        ),
        in_specs=vmem(1),
        out_specs=tuple(vmem(2)),
        scratch_shapes=[
            pltpu.VMEM((cols, c1), F32),
            pltpu.VMEM((2, pooled, half, 2 * c1), BF16),
        ],
        compiler_params=params(16),
        cost_estimate=pl.CostEstimate(flops=60 * rows * cols * c1, bytes_accessed=2 << 20,
                                      transcendentals=2 * rows * cols * c1),
    )(pre_first)

    fields = jnp.transpose(inputs, (0, 2, 1))
    over, down, bottom, slope, fields = lax.optimization_barrier((over, down, bottom, slope, fields))
    top = jnp.where(band == 0, over, down)

    def column(own_part, at):
        p, g = at * (cols - 1), cols + at * (half - 1)
        parts = [own_part[:rows + pooled], top[p:p + 1], bottom[p:p + 1], top[g:g + 1], bottom[g:g + 1]]
        return jnp.concatenate(parts + [jnp.zeros((edge - rows - pooled - 4, c1), BF16)], 0)

    left = lax.ppermute(column(last_col, 1), "lon", [(i, (i + 1) % lons) for i in range(lons)])
    right = lax.ppermute(column(first_col, 0), "lon", [(i, (i - 1) % lons) for i in range(lons)])

    fields_t, taps_first, taps_second = pl.pallas_call(
        layout_kernel,
        out_shape=(
            shape((2 * c0, rows * half), BF16),
            shape((6 * c0, 4 * c1), BF16),
            shape((3, 2 * c1, 4 * c1), BF16),
        ),
        in_specs=vmem(3),
        out_specs=tuple(vmem(3)),
        scratch_shapes=[pltpu.VMEM((rows, c0, 2 * cols), BF16)],
        compiler_params=params(16),
        cost_estimate=pl.CostEstimate(flops=4 * rows * cols * c0 * cols, bytes_accessed=3 << 20, transcendentals=0),
    )(fields, w_first, w_second)
    left, right, fields_t = lax.optimization_barrier((left, right, fields_t))

    chips = lats * depths
    size = 9 * (c1 + c0)
    piece = -(-size // (2 * chips * 16)) * 16
    held = chips * piece
    span = half + EDGE
    spread, own, other = pl.pallas_call(
        functools.partial(middle_kernel, lats),
        out_shape=(
            shape((rows + 3, half, 4 * c1), BF16),
            shape((held, c1), F32),
            shape((held, c1), F32),
        ),
        in_specs=[pl.BlockSpec(memory_space=pltpu.SMEM)] + vmem(9),
        out_specs=tuple(vmem(3)),
        scratch_shapes=[
            pltpu.VMEM((pooled + 2, span, c1), F32),
            pltpu.VMEM((pooled + 2, span, 4 * c1), BF16),
            pltpu.VMEM((3, pooled, span, 2 * c1), F32),
            pltpu.VMEM((4, span, 2 * c1), F32),
            pltpu.VMEM((cols, c1), F32),
            pltpu.VMEM((2, edge, c1), F32),
            pltpu.VMEM((2, edge, c1), F32),
            pltpu.VMEM((4, 2 * c1, 3 * c1), F32),
            pltpu.VMEM((2 * c1, 3 * c1), F32),
            pltpu.VMEM((2 * held, c1), F32),
        ],
        compiler_params=params(16),
        cost_estimate=pl.CostEstimate(flops=2 * rows * cols * c1 * 9 * (2 * c1 + c0), bytes_accessed=8 << 20,
                                      transcendentals=0),
    )(flags, grad_out, top, bottom, left, right, slope, act_t, fields_t, taps_second)

    swap = [(i, i ^ 1) for i in range(lons)]
    orders = [steps(lats, k) for k in range(2)]

    def along_lat(t, block):
        pairs = [(i * lons + j, (i ^ orders[j % 2][t]) * lons + j) for i in range(lats) for j in range(lons)]
        return lax.ppermute(block, AREA, pairs)

    total = (own + lax.ppermute(other, "lon", swap)).reshape(lats, held // lats, c1)
    rounds = lats.bit_length() - 1
    for t in range(rounds):
        count = total.shape[0] // 2
        sent = total[count:].astype(BF16)
        if t == 0:
            sent, spread = lax.optimization_barrier((sent, spread))
        got = along_lat(t, sent)
        if t == 0:
            grad_inputs = pl.pallas_call(
                last_kernel,
                out_shape=shape((rows, c0, cols), BF16),
                in_specs=vmem(2),
                out_specs=vmem(1)[0],
                scratch_shapes=[
                    pltpu.VMEM((2 * c0, rows * half), F32),
                    pltpu.VMEM((pooled, c0, 2 * cols), BF16),
                ],
                compiler_params=params(12),
                cost_estimate=pl.CostEstimate(flops=2 * rows * cols * c1 * 9 * c0, bytes_accessed=3 << 20, transcendentals=0),
            )(spread, taps_first)
            got, grad_inputs = lax.optimization_barrier((got, grad_inputs))
        total = total[:count] + got.astype(F32)
    step = 2
    while step < lons:
        part = total.astype(BF16)
        total = part.astype(F32) + lax.ppermute(part, "lon", [(i, i ^ step) for i in range(lons)]).astype(F32)
        step *= 2
    mine = total.astype(BF16)
    for t in reversed(range(rounds)):
        mine = jnp.concatenate([mine, along_lat(t, mine)], 0)
    theirs = lax.ppermute(mine, "lon", swap)

    grad_w_first, grad_w_second = pl.pallas_call(
        gather_kernel,
        out_shape=(shape((9 * c0, c1), F32), shape((9 * c1, c1), F32)),
        in_specs=[pl.BlockSpec(memory_space=pltpu.SMEM)] + vmem(2),
        out_specs=tuple(vmem(2)),
        compiler_params=params(8),
        cost_estimate=pl.CostEstimate(flops=1000, bytes_accessed=3 << 19, transcendentals=0),
    )(flags, mine, theirs)
    return (jnp.transpose(grad_inputs, (0, 2, 1)), grad_w_first.reshape(w_first.shape),
            grad_w_second.reshape(w_second.shape))


def solution(mesh):
    in_specs = (P("lat", "lon", None), P("lat", "lon", None), P("lat", "lon", None), P(), P())
    out_specs = (P("lat", "lon", None), P(), P())
    return jax.shard_map(body, mesh=mesh, in_specs=in_specs, out_specs=out_specs, check_vma=False)
```

```python
import functools

import jax
import jax.numpy as jnp
from jax import lax
from jax.experimental import pallas as pl
from jax.experimental.pallas import tpu as pltpu
from jax.sharding import PartitionSpec as P

inv_root = 0.7071067811865476
density = 0.3989422804014327

F32 = jnp.float32
BF16 = jnp.bfloat16
EDGE = 16
AREA = ("lat", "lon")


def cdf_of(value):
    return 0.5 * (1.0 + lax.erf(value * inv_root))


def slope_of(value, cdf):
    return 0.25 * (cdf + value * jnp.exp(-0.5 * value * value) * density)


def dot(left, right):
    return jnp.dot(left, right, preferred_element_type=F32)


def dot_nt(left, right):
    return lax.dot_general(left, right, (((1,), (1,)), ((), ())), preferred_element_type=F32)


def pack_kernel(pre, grad_out, head, tail, first_col, last_col, hold):
    rows, cols, c1 = pre.shape
    pooled, half = grad_out.shape[:2]
    head[:cols] = pre[0]
    head[cols:] = grad_out[0]
    tail[:cols] = pre[rows - 1]
    tail[cols:] = grad_out[pooled - 1]
    for message, p, g in ((first_col, 0, 0), (last_col, cols - 16, half - 16)):
        at = 0 if p == 0 else 15
        hold[rows + pooled:] = jnp.zeros((hold.shape[0] - rows - pooled, c1), F32)
        for r in range(rows):
            hold[r:r + 1] = pre[r, p:p + 16].astype(F32)[at:at + 1]
        for i in range(pooled):
            hold[rows + i:rows + i + 1] = grad_out[i, g:g + 16].astype(F32)[at:at + 1]
        message[...] = hold[...].astype(BF16)


def one_at(where):
    return jnp.where(where, 1.0, 0.0).astype(BF16)


def local_kernel(pre, slope, act_t, line, act_s):
    rows, cols, c1 = pre.shape
    half = cols // 2

    def one_row(r, carry):
        line[...] = pre[r].astype(F32)
        for pc in range(2):
            value = line[pl.ds(pc, half, stride=2), :]
            cdf = cdf_of(value)
            act_s[r % 2, r // 2, :, pc * c1:(pc + 1) * c1] = (value * cdf).astype(BF16)
            slope[r, :, pc * c1:(pc + 1) * c1] = slope_of(value, cdf)
        return carry

    lax.fori_loop(0, rows, one_row, 0)
    for pr in range(2):
        act_t[pr] = act_s[pr].reshape(rows // 2 * half, 2 * c1).T


def layout_kernel(fields, w_first, w_second, fields_t, taps_first, taps_second, turned):
    rows, c0, cols = fields.shape
    c1 = w_first.shape[3]
    half = cols // 2
    col = lax.broadcasted_iota(jnp.int32, (cols, 2 * cols), 0)
    lane = lax.broadcasted_iota(jnp.int32, (cols, 2 * cols), 1)
    turn = lane // cols
    parity = (lane % cols) // half
    parity = parity + turn - 2 * parity * turn
    order = one_at(col == 2 * (lane % half) + parity)
    turned[...] = dot(fields[...].reshape(rows * c0, cols), order).astype(BF16).reshape(rows, c0, 2 * cols)
    low = lax.broadcasted_iota(jnp.int32, (c0, cols), 1) < half
    for q in range(rows // 2):
        fields_t[:c0, q * cols:(q + 1) * cols] = jnp.where(low, turned[2 * q, :, :cols], turned[2 * q + 1, :, cols:])
        fields_t[c0:, q * cols:(q + 1) * cols] = jnp.where(low, turned[2 * q, :, cols:], turned[2 * q + 1, :, :cols])
    taps_second[...] = jnp.zeros_like(taps_second)
    taps_first[...] = jnp.zeros_like(taps_first)
    for a in range(3):
        for pc, blocks in ((0, (2, 1, None, 0)), (1, (None, 2, 0, 1))):
            for k, b in enumerate(blocks):
                if b is not None:
                    taps_second[a, pc * c1:(pc + 1) * c1, k * c1:(k + 1) * c1] = w_second[a, b]
        for pc, blocks in ((0, (2, 1, 0, None)), (1, (None, 2, 1, 0))):
            for k, b in enumerate(blocks):
                if b is not None:
                    start = (2 * a + pc) * c0
                    taps_first[start:start + c0, k * c1:(k + 1) * c1] = w_first[a, b]


def steps(count, core):
    bits = count.bit_length() - 1
    return [1 << ((t + core) % bits) for t in range(bits)]


def distance(index, masks):
    return sum(m for t, m in enumerate(masks) if (index >> (len(masks) - 1 - t)) & 1)


def middle_kernel(lats, flags, grad_out, top, bottom, left, right, slope, act_t, fields_t, taps,
                  spread, own, other,
                  grid, wide, prods, ends, line, side, sides, sums, corner, keep):
    first, last, core = flags[0], flags[1], flags[2]
    rows, half, c2 = slope.shape
    c1 = c2 // 2
    pooled = rows // 2
    c0 = fields_t.shape[0] // 2
    cells = pooled * half

    grid[:, half:, :] = jnp.zeros((pooled + 2, EDGE, c1), F32)
    grid[1:pooled + 1, :half, :] = grad_out[...].astype(F32)
    grid[0, :half, :] = top[2 * half:, :].astype(F32)
    outside = jnp.where(last == 1, 0.0, 1.0)
    grid[pooled + 1, :half, :] = bottom[2 * half:, :].astype(F32) * outside
    side[0] = left[...].astype(F32)
    side[1] = right[...].astype(F32)
    for i in range(pooled + 2):
        at = rows + i - 1
        if i == 0:
            at = rows + pooled + 2
        if i == pooled + 1:
            at = rows + pooled + 3
        kept = outside if i == pooled + 1 else 1.0
        grid[i, half:half + 1, :] = side[1, at:at + 1, :] * kept
        grid[i, half + EDGE - 1:half + EDGE, :] = side[0, at:at + 1, :] * kept
    for i in range(pooled + 2):
        here = grid[i]
        wide[i, :, :c1] = pltpu.roll(here, 1, 0).astype(BF16)
        wide[i, :, c1:2 * c1] = here.astype(BF16)
        wide[i, :, 2 * c1:3 * c1] = pltpu.roll(here, half + EDGE - 1, 0).astype(BF16)
        wide[i, :, 3 * c1:] = here.astype(BF16)

    flat = wide[1:pooled + 1].reshape(pooled * (half + EDGE), 4 * c1)
    for a in range(3):
        prods[a] = dot_nt(flat, taps[a]).reshape(pooled, half + EDGE, c2)
    fold = jnp.where(first == 1, taps[0], taps[2])
    ends[0] = dot_nt(wide[0], fold)
    ends[1] = dot_nt(wide[0], taps[1])
    ends[2] = dot_nt(wide[pooled + 1], taps[0])
    ends[3] = dot_nt(wide[pooled + 1], taps[1])

    for s in range(2):
        sides[s] = slope_of(side[s], cdf_of(side[s]))

    def place(r, total, incline, edge):
        inner = total[:half] * incline
        rim = total[half:]
        after = rim[:1, :c1] * sides[1, pl.ds(edge, 1), :]
        before = rim[EDGE - 1:, c1:] * sides[0, pl.ds(edge, 1), :]
        even, odd = inner[:, :c1], inner[:, c1:]
        at = lax.broadcasted_iota(jnp.int32, (half, c1), 0)
        spread[r, :, :c1] = jnp.where(at == 0, before, pltpu.roll(odd, 1, 0)).astype(BF16)
        spread[r, :, c1:2 * c1] = even.astype(BF16)
        spread[r, :, 2 * c1:3 * c1] = odd.astype(BF16)
        spread[r, :, 3 * c1:] = jnp.where(at == half - 1, after, pltpu.roll(even, half - 1, 0)).astype(BF16)

    def halo_slope(message):
        line[...] = message[:2 * half, :].astype(F32)
        both = [line[pl.ds(pc, half, stride=2), :] for pc in range(2)]
        return jnp.concatenate([slope_of(v, cdf_of(v)) for v in both], axis=1)

    place(0, ends[0] + ends[1] + prods[0, 0], halo_slope(top), rows + pooled)
    place(1, ends[0] + prods[1, 0] + prods[0, 0], slope[0], 0)

    def pair(i, carry):
        middle = prods[2, i] + prods[1, i]
        place(2 * i + 2, middle + prods[0, i + 1], slope[2 * i + 1], 2 * i + 1)
        place(2 * i + 3, prods[2, i] + prods[1, i + 1] + prods[0, i + 1], slope[2 * i + 2], 2 * i + 2)
        return carry

    lax.fori_loop(0, pooled - 1, pair, 0)
    final = prods[2, pooled - 1]
    place(rows, final + prods[1, pooled - 1] + ends[2], slope[rows - 1], rows - 1)
    place(rows + 1, (final + ends[3] + ends[2]) * outside, halo_slope(bottom), rows + pooled + 1)

    is_first = jnp.where(first == 1, 1.0, 0.0).astype(BF16)
    not_first = jnp.where(first == 1, 0.0, 1.0).astype(BF16)
    above = wide[0, :half, :3 * c1]
    wide[0, :half, :3 * c1] = above * not_first
    for n, (pr, start) in enumerate(((0, 0), (0, 1), (1, 1), (1, 2))):
        around = wide[start:start + pooled, :half, :3 * c1].reshape(cells, 3 * c1)
        sums[n] = dot(act_t[pr], around)
    corner[...] = dot(act_t[0, :, :half], above * is_first)

    unit = c0
    per_tap = c1 // unit
    count = 9 * per_tap + 9
    held = own.shape[0]

    def put(k, value):
        keep[k * unit:(k + 1) * unit, :] = value

    pieces = {0: ((0, 1), (1, 3)), 1: ((0, 1), (1, 2)), 2: ((0, 0), (1, 2))}
    for a in range(3):
        for b in range(3):
            total = None
            for pr, n in pieces[a]:
                for pc in range(2):
                    k = (pc + 1 - b) // 2 + 1
                    term = sums[n, pc * c1:(pc + 1) * c1, k * c1:(k + 1) * c1]
                    total = term if total is None else total + term
            if a == 0:
                for pc in range(2):
                    k = (pc + 1 - b) // 2 + 1
                    total = total + corner[pc * c1:(pc + 1) * c1, k * c1:(k + 1) * c1]
            total = total * 0.25
            for part in range(per_tap):
                put((3 * a + b) * per_tap + part, total[part * unit:(part + 1) * unit])

    head = spread[0]
    spread[0] = head * not_first
    spread[rows + 2] = head * is_first
    folded = dot(fields_t[:, :half], spread[rows + 2])
    for a in range(3):
        around = spread[2 - a:2 - a + rows].reshape(rows * half, 4 * c1)
        got = dot(fields_t[...], around)
        if a == 0:
            got = got + folded
        for b in range(3):
            even = got[:c0, (2 - b) * c1:(3 - b) * c1]
            odd = got[c0:, (3 - b) * c1:(4 - b) * c1]
            put(9 * per_tap + 3 * a + b, even + odd)
    keep[count * unit:] = jnp.zeros((2 * held - count * unit, c1), F32)
    band = flags[3]
    block = held // lats
    orders = [steps(lats, k) for k in range(2)]
    for index in range(lats):
        far = [distance(index, masks) for masks in orders]
        for target, half_of in ((own, core), (other, 1 - core)):
            piece_at = half_of * lats + (band ^ jnp.where(half_of == 0, far[0], far[1]))
            target[index * block:(index + 1) * block] = keep[pl.ds(pl.multiple_of(piece_at * block, block), block), :]


def last_kernel(spread, taps, out, total, turned):
    rows, c0, cols = out.shape
    half = cols // 2
    c2 = 2 * c0
    depth = spread.shape[2]
    result = dot_nt(taps[:c2], spread[2:rows + 2].reshape(rows * half, depth))
    for a in (1, 2):
        result = result + dot_nt(taps[a * c2:(a + 1) * c2],
                                 spread[2 - a:2 - a + rows].reshape(rows * half, depth))
    total[...] = result
    total[:, :half] = total[:, :half] + dot_nt(taps[:c2], spread[rows + 2])
    for q in range(rows // 2):
        pair = total[:, q * cols:(q + 1) * cols].astype(BF16)
        turned[q, :, :cols] = pair[:c0]
        turned[q, :, cols:] = pair[c0:]
    k = lax.broadcasted_iota(jnp.int32, (2 * cols, 2 * cols), 0)
    n = lax.broadcasted_iota(jnp.int32, (2 * cols, 2 * cols), 1)
    order = one_at(n == ((k % cols) // half) * cols + 2 * (k % half) + k // cols)
    found = dot(turned[...].reshape(rows // 2 * c0, 2 * cols), order).astype(BF16)
    for q in range(rows // 2):
        for rp in range(2):
            out[2 * q + rp] = found[q * c0:(q + 1) * c0, rp * cols:(rp + 1) * cols]


def gather_kernel(flags, mine, theirs, out_first, out_second):
    band, core = flags[3], flags[2]
    lats, rows, c1 = mine.shape
    size = out_second.shape[0]
    total = size + out_first.shape[0]
    for h in range(2):
        masks = steps(lats, h)
        for i in range(lats):
            at = (h * lats + i) * rows
            far = i ^ band
            source = 0
            for m in masks:
                source = 2 * source + (far // m) % 2
            for out, base, end in ((out_second, 0, size), (out_first, size, total)):
                low, high = max(at, base), min(at + rows, end)
                if low < high:
                    here, there = (x[source, low - at:high - at] for x in (mine, theirs))
                    out[low - base:high - base] = jnp.where(core == h, here, there).astype(F32)


def vmem(count):
    return [pl.BlockSpec(memory_space=pltpu.VMEM)] * count


def params(mib):
    return pltpu.CompilerParams(vmem_limit_bytes=mib * 1024 * 1024)


def shape(dims, kind):
    return jax.ShapeDtypeStruct(dims, kind)


def body(inputs, pre_first, grad_out, w_first, w_second):
    rows, cols, c1 = pre_first.shape
    c0 = inputs.shape[2]
    half, pooled = cols // 2, rows // 2
    lats, lons = lax.axis_size("lat"), lax.axis_size("lon")
    depths = lons // 2
    band, place = lax.axis_index("lat"), lax.axis_index("lon")
    core = lax.rem(place, 2)
    flags = jnp.stack([(band == 0).astype(jnp.int32), (band == lats - 1).astype(jnp.int32), core, band])

    edge = -(-(rows + pooled + 4) // 16) * 16
    head, tail, first_col, last_col = pl.pallas_call(
        pack_kernel,
        out_shape=(
            shape((cols + half, c1), BF16),
            shape((cols + half, c1), BF16),
            shape((edge, c1), BF16),
            shape((edge, c1), BF16),
        ),
        in_specs=vmem(2),
        out_specs=tuple(vmem(4)),
        scratch_shapes=[
            pltpu.VMEM((edge, c1), F32),
        ],
        compiler_params=params(50),
        cost_estimate=pl.CostEstimate(flops=1000, bytes_accessed=1 << 18, transcendentals=0),
    )(pre_first, grad_out)
    over = lax.ppermute(head, AREA, [(i, (i + lons // 2) % lons) for i in range(lons)])
    down = lax.ppermute(tail, "lat", [(i, (i + 1) % lats) for i in range(lats)])
    bottom = lax.ppermute(head, "lat", [(i, (i - 1) % lats) for i in range(lats)])

    slope, act_t = pl.pallas_call(
        local_kernel,
        out_shape=(
            shape((rows, half, 2 * c1), F32),
            shape((2, 2 * c1, pooled * half), BF16),
        ),
        in_specs=vmem(1),
        out_specs=tuple(vmem(2)),
        scratch_shapes=[
            pltpu.VMEM((cols, c1), F32),
            pltpu.VMEM((2, pooled, half, 2 * c1), BF16),
        ],
        compiler_params=params(16),
        cost_estimate=pl.CostEstimate(flops=60 * rows * cols * c1, bytes_accessed=2 << 20,
                                      transcendentals=2 * rows * cols * c1),
    )(pre_first)

    fields = jnp.transpose(inputs, (0, 2, 1))
    over, down, bottom, slope, fields = lax.optimization_barrier((over, down, bottom, slope, fields))
    top = jnp.where(band == 0, over, down)

    def column(own_part, at):
        p, g = at * (cols - 1), cols + at * (half - 1)
        parts = [own_part[:rows + pooled], top[p:p + 1], bottom[p:p + 1], top[g:g + 1], bottom[g:g + 1]]
        return jnp.concatenate(parts + [jnp.zeros((edge - rows - pooled - 4, c1), BF16)], 0)

    left = lax.ppermute(column(last_col, 1), "lon", [(i, (i + 1) % lons) for i in range(lons)])
    right = lax.ppermute(column(first_col, 0), "lon", [(i, (i - 1) % lons) for i in range(lons)])

    fields_t, taps_first, taps_second = pl.pallas_call(
        layout_kernel,
        out_shape=(
            shape((2 * c0, rows * half), BF16),
            shape((6 * c0, 4 * c1), BF16),
            shape((3, 2 * c1, 4 * c1), BF16),
        ),
        in_specs=vmem(3),
        out_specs=tuple(vmem(3)),
        scratch_shapes=[pltpu.VMEM((rows, c0, 2 * cols), BF16)],
        compiler_params=params(16),
        cost_estimate=pl.CostEstimate(flops=4 * rows * cols * c0 * cols, bytes_accessed=3 << 20, transcendentals=0),
    )(fields, w_first, w_second)
    left, right, fields_t = lax.optimization_barrier((left, right, fields_t))

    chips = lats * depths
    size = 9 * (c1 + c0)
    piece = -(-size // (2 * chips * 16)) * 16
    held = chips * piece
    span = half + EDGE
    spread, own, other = pl.pallas_call(
        functools.partial(middle_kernel, lats),
        out_shape=(
            shape((rows + 3, half, 4 * c1), BF16),
            shape((held, c1), F32),
            shape((held, c1), F32),
        ),
        in_specs=[pl.BlockSpec(memory_space=pltpu.SMEM)] + vmem(9),
        out_specs=tuple(vmem(3)),
        scratch_shapes=[
            pltpu.VMEM((pooled + 2, span, c1), F32),
            pltpu.VMEM((pooled + 2, span, 4 * c1), BF16),
            pltpu.VMEM((3, pooled, span, 2 * c1), F32),
            pltpu.VMEM((4, span, 2 * c1), F32),
            pltpu.VMEM((cols, c1), F32),
            pltpu.VMEM((2, edge, c1), F32),
            pltpu.VMEM((2, edge, c1), F32),
            pltpu.VMEM((4, 2 * c1, 3 * c1), F32),
            pltpu.VMEM((2 * c1, 3 * c1), F32),
            pltpu.VMEM((2 * held, c1), F32),
        ],
        compiler_params=params(16),
        cost_estimate=pl.CostEstimate(flops=2 * rows * cols * c1 * 9 * (2 * c1 + c0), bytes_accessed=8 << 20,
                                      transcendentals=0),
    )(flags, grad_out, top, bottom, left, right, slope, act_t, fields_t, taps_second)

    swap = [(i, i ^ 1) for i in range(lons)]
    orders = [steps(lats, k) for k in range(2)]

    def along_lat(t, block):
        far = [distance(t, masks) for masks in orders]
        pairs = [(i * lons + j, (i ^ far[j % 2]) * lons + j) for i in range(lats) for j in range(lons)]
        return lax.ppermute(block, AREA, pairs)

    parts = (own + lax.ppermute(other, "lon", swap)).reshape(lats, held // lats, c1)
    sent = [parts[t].astype(BF16) for t in range(1, lats)]
    *sent, spread = lax.optimization_barrier((*sent, spread))
    got = [along_lat(t + 1, block) for t, block in enumerate(sent)]
    grad_inputs = pl.pallas_call(
        last_kernel,
        out_shape=shape((rows, c0, cols), BF16),
        in_specs=vmem(2),
        out_specs=vmem(1)[0],
        scratch_shapes=[
            pltpu.VMEM((2 * c0, rows * half), F32),
            pltpu.VMEM((pooled, c0, 2 * cols), BF16),
        ],
        compiler_params=params(12),
        cost_estimate=pl.CostEstimate(flops=2 * rows * cols * c1 * 9 * c0, bytes_accessed=3 << 20, transcendentals=0),
    )(spread, taps_first)
    *got, grad_inputs = lax.optimization_barrier((*got, grad_inputs))
    total = parts[0]
    for block in got:
        total = total + block.astype(F32)
    part = total.astype(BF16)
    blocks = [part] + [lax.ppermute(part, "lon", [(i, i ^ (2 * k)) for i in range(lons)]) for k in range(1, depths)]
    blocks = [block.astype(F32) for block in blocks]
    while len(blocks) > 1:
        blocks = [blocks[k] + blocks[k + 1] for k in range(0, len(blocks), 2)]
    block = blocks[0].astype(BF16)
    mine = [block] + [along_lat(t, block) for t in range(1, lats)]
    theirs = [lax.ppermute(block, "lon", swap) for block in mine]
    mine, theirs = jnp.stack(mine, 0), jnp.stack(theirs, 0)

    grad_w_first, grad_w_second = pl.pallas_call(
        gather_kernel,
        out_shape=(shape((9 * c0, c1), F32), shape((9 * c1, c1), F32)),
        in_specs=[pl.BlockSpec(memory_space=pltpu.SMEM)] + vmem(2),
        out_specs=tuple(vmem(2)),
        compiler_params=params(8),
        cost_estimate=pl.CostEstimate(flops=1000, bytes_accessed=3 << 19, transcendentals=0),
    )(flags, mine, theirs)
    return (jnp.transpose(grad_inputs, (0, 2, 1)), grad_w_first.reshape(w_first.shape),
            grad_w_second.reshape(w_second.shape))


def solution(mesh):
    in_specs = (P("lat", "lon", None), P("lat", "lon", None), P("lat", "lon", None), P(), P())
    out_specs = (P("lat", "lon", None), P(), P())
    return jax.shard_map(body, mesh=mesh, in_specs=in_specs, out_specs=out_specs, check_vma=False)
```

```python
import functools

import jax
import jax.numpy as jnp
from jax import lax
from jax.experimental import pallas as pl
from jax.experimental.pallas import tpu as pltpu
from jax.sharding import PartitionSpec as P

inv_root = 0.7071067811865476
density = 0.3989422804014327

F32 = jnp.float32
BF16 = jnp.bfloat16
EDGE = 16
AREA = ("lat", "lon")


def cdf_of(value):
    return 0.5 * (1.0 + lax.erf(value * inv_root))


def slope_of(value, cdf):
    return 0.25 * (cdf + value * jnp.exp(-0.5 * value * value) * density)


def dot(left, right):
    return jnp.dot(left, right, preferred_element_type=F32)


def dot_nt(left, right):
    return lax.dot_general(left, right, (((1,), (1,)), ((), ())), preferred_element_type=F32)


def pack_kernel(flags, pre, grad_out, row_a, row_b, col_a, col_b, hold):
    rows, cols, c1 = pre.shape
    pooled, half = grad_out.shape[:2]
    core, even = flags[2], flags[4]
    for message, low in ((row_a, even == 0), (row_b, even == 1)):
        message[:cols] = pre[jnp.where(low, 0, rows - 1)]
        message[cols:] = grad_out[jnp.where(low, 0, pooled - 1)]
    hold[:, rows + pooled:] = jnp.zeros((2, hold.shape[1] - rows - pooled, c1), F32)
    for side, (p, g) in enumerate(((0, 0), (cols - 16, half - 16))):
        at = 15 * side
        for r in range(rows):
            hold[side, r:r + 1] = pre[r, p:p + 16].astype(F32)[at:at + 1]
        for i in range(pooled):
            hold[side, rows + i:rows + i + 1] = grad_out[i, g:g + 16].astype(F32)[at:at + 1]
    col_a[...] = hold[1 - core].astype(BF16)
    col_b[...] = hold[core].astype(BF16)


def one_at(where):
    return jnp.where(where, 1.0, 0.0).astype(BF16)


def local_kernel(pre, slope, act_t, line, act_s):
    rows, cols, c1 = pre.shape
    half = cols // 2

    def one_row(r, carry):
        line[...] = pre[r].astype(F32)
        for pc in range(2):
            value = line[pl.ds(pc, half, stride=2), :]
            cdf = cdf_of(value)
            act_s[r % 2, r // 2, :, pc * c1:(pc + 1) * c1] = (value * cdf).astype(BF16)
            slope[r, :, pc * c1:(pc + 1) * c1] = slope_of(value, cdf)
        return carry

    lax.fori_loop(0, rows, one_row, 0)
    for pr in range(2):
        act_t[pr] = act_s[pr].reshape(rows // 2 * half, 2 * c1).T


def layout_kernel(fields, w_first, w_second, fields_t, taps_first, taps_second, turned):
    rows, c0, cols = fields.shape
    c1 = w_first.shape[3]
    half = cols // 2
    col = lax.broadcasted_iota(jnp.int32, (cols, 2 * cols), 0)
    lane = lax.broadcasted_iota(jnp.int32, (cols, 2 * cols), 1)
    turn = lane // cols
    parity = (lane % cols) // half
    parity = parity + turn - 2 * parity * turn
    order = one_at(col == 2 * (lane % half) + parity)
    turned[...] = dot(fields[...].reshape(rows * c0, cols), order).astype(BF16).reshape(rows, c0, 2 * cols)
    low = lax.broadcasted_iota(jnp.int32, (c0, cols), 1) < half
    for q in range(rows // 2):
        fields_t[:c0, q * cols:(q + 1) * cols] = jnp.where(low, turned[2 * q, :, :cols], turned[2 * q + 1, :, cols:])
        fields_t[c0:, q * cols:(q + 1) * cols] = jnp.where(low, turned[2 * q, :, cols:], turned[2 * q + 1, :, :cols])
    taps_second[...] = jnp.zeros_like(taps_second)
    taps_first[...] = jnp.zeros_like(taps_first)
    for a in range(3):
        for pc, blocks in ((0, (2, 1, None, 0)), (1, (None, 2, 0, 1))):
            for k, b in enumerate(blocks):
                if b is not None:
                    taps_second[a, pc * c1:(pc + 1) * c1, k * c1:(k + 1) * c1] = w_second[a, b]
        for pc, blocks in ((0, (2, 1, 0, None)), (1, (None, 2, 1, 0))):
            for k, b in enumerate(blocks):
                if b is not None:
                    start = (2 * a + pc) * c0
                    taps_first[start:start + c0, k * c1:(k + 1) * c1] = w_first[a, b]


def steps(count, core):
    bits = count.bit_length() - 1
    return [1 << ((t + core) % bits) for t in range(bits)]


def distance(index, masks):
    return sum(m for t, m in enumerate(masks) if (index >> (len(masks) - 1 - t)) & 1)


def middle_kernel(lats, flags, grad_out, row_a, row_b, col_a, col_b, slope, act_t, fields_t, taps,
                  spread, own, *rest):
    sends, scratch = rest[:lats - 1], rest[lats - 1:]
    grid, wide, prods, ends, line, side, sides, sums, corner, keep = scratch
    first, last, core, band, even = (flags[k] for k in range(5))
    top = jnp.where(even == 1, row_b[...], row_a[...])
    bottom = jnp.where(even == 1, row_a[...], row_b[...])
    rows, half, c2 = slope.shape
    c1 = c2 // 2
    pooled = rows // 2
    c0 = fields_t.shape[0] // 2
    cells = pooled * half

    grid[:, half:, :] = jnp.zeros((pooled + 2, EDGE, c1), F32)
    grid[1:pooled + 1, :half, :] = grad_out[...].astype(F32)
    grid[0, :half, :] = top[2 * half:, :].astype(F32)
    outside = jnp.where(last == 1, 0.0, 1.0)
    grid[pooled + 1, :half, :] = bottom[2 * half:, :].astype(F32) * outside
    side[1 - core] = col_a[...].astype(F32)
    side[core] = col_b[...].astype(F32)
    for i in range(pooled + 2):
        at = rows + i - 1
        if i == 0:
            at = rows + pooled + 2
        if i == pooled + 1:
            at = rows + pooled + 3
        kept = outside if i == pooled + 1 else 1.0
        grid[i, half:half + 1, :] = side[1, at:at + 1, :] * kept
        grid[i, half + EDGE - 1:half + EDGE, :] = side[0, at:at + 1, :] * kept
    for i in range(pooled + 2):
        here = grid[i]
        wide[i, :, :c1] = pltpu.roll(here, 1, 0).astype(BF16)
        wide[i, :, c1:2 * c1] = here.astype(BF16)
        wide[i, :, 2 * c1:3 * c1] = pltpu.roll(here, half + EDGE - 1, 0).astype(BF16)
        wide[i, :, 3 * c1:] = here.astype(BF16)

    flat = wide[1:pooled + 1].reshape(pooled * (half + EDGE), 4 * c1)
    for a in range(3):
        prods[a] = dot_nt(flat, taps[a]).reshape(pooled, half + EDGE, c2)
    fold = jnp.where(first == 1, taps[0], taps[2])
    ends[0] = dot_nt(wide[0], fold)
    ends[1] = dot_nt(wide[0], taps[1])
    ends[2] = dot_nt(wide[pooled + 1], taps[0])
    ends[3] = dot_nt(wide[pooled + 1], taps[1])

    for s in range(2):
        sides[s] = slope_of(side[s], cdf_of(side[s]))

    def place(r, total, incline, edge):
        inner = total[:half] * incline
        rim = total[half:]
        after = rim[:1, :c1] * sides[1, pl.ds(edge, 1), :]
        before = rim[EDGE - 1:, c1:] * sides[0, pl.ds(edge, 1), :]
        even, odd = inner[:, :c1], inner[:, c1:]
        at = lax.broadcasted_iota(jnp.int32, (half, c1), 0)
        spread[r, :, :c1] = jnp.where(at == 0, before, pltpu.roll(odd, 1, 0)).astype(BF16)
        spread[r, :, c1:2 * c1] = even.astype(BF16)
        spread[r, :, 2 * c1:3 * c1] = odd.astype(BF16)
        spread[r, :, 3 * c1:] = jnp.where(at == half - 1, after, pltpu.roll(even, half - 1, 0)).astype(BF16)

    def halo_slope(message):
        line[...] = message[:2 * half, :].astype(F32)
        both = [line[pl.ds(pc, half, stride=2), :] for pc in range(2)]
        return jnp.concatenate([slope_of(v, cdf_of(v)) for v in both], axis=1)

    place(0, ends[0] + ends[1] + prods[0, 0], halo_slope(top), rows + pooled)
    place(1, ends[0] + prods[1, 0] + prods[0, 0], slope[0], 0)

    def pair(i, carry):
        middle = prods[2, i] + prods[1, i]
        place(2 * i + 2, middle + prods[0, i + 1], slope[2 * i + 1], 2 * i + 1)
        place(2 * i + 3, prods[2, i] + prods[1, i + 1] + prods[0, i + 1], slope[2 * i + 2], 2 * i + 2)
        return carry

    lax.fori_loop(0, pooled - 1, pair, 0)
    final = prods[2, pooled - 1]
    place(rows, final + prods[1, pooled - 1] + ends[2], slope[rows - 1], rows - 1)
    place(rows + 1, (final + ends[3] + ends[2]) * outside, halo_slope(bottom), rows + pooled + 1)

    is_first = jnp.where(first == 1, 1.0, 0.0).astype(BF16)
    not_first = jnp.where(first == 1, 0.0, 1.0).astype(BF16)
    above = wide[0, :half, :3 * c1]
    wide[0, :half, :3 * c1] = above * not_first
    for n, (pr, start) in enumerate(((0, 0), (0, 1), (1, 1), (1, 2))):
        around = wide[start:start + pooled, :half, :3 * c1].reshape(cells, 3 * c1)
        sums[n] = dot(act_t[pr], around)
    corner[...] = dot(act_t[0, :, :half], above * is_first)

    unit = c0
    per_tap = c1 // unit
    count = 9 * per_tap + 9
    block = own.shape[0]

    def put(k, value):
        keep[k * unit:(k + 1) * unit, :] = value

    pieces = {0: ((0, 1), (1, 3)), 1: ((0, 1), (1, 2)), 2: ((0, 0), (1, 2))}
    for a in range(3):
        for b in range(3):
            total = None
            for pr, n in pieces[a]:
                for pc in range(2):
                    k = (pc + 1 - b) // 2 + 1
                    term = sums[n, pc * c1:(pc + 1) * c1, k * c1:(k + 1) * c1]
                    total = term if total is None else total + term
            if a == 0:
                for pc in range(2):
                    k = (pc + 1 - b) // 2 + 1
                    total = total + corner[pc * c1:(pc + 1) * c1, k * c1:(k + 1) * c1]
            total = total * 0.25
            for part in range(per_tap):
                put((3 * a + b) * per_tap + part, total[part * unit:(part + 1) * unit])

    head = spread[0]
    spread[0] = head * not_first
    spread[rows + 2] = head * is_first
    folded = dot(fields_t[:, :half], spread[rows + 2])
    for a in range(3):
        around = spread[2 - a:2 - a + rows].reshape(rows * half, 4 * c1)
        got = dot(fields_t[...], around)
        if a == 0:
            got = got + folded
        for b in range(3):
            even = got[:c0, (2 - b) * c1:(3 - b) * c1]
            odd = got[c0:, (3 - b) * c1:(4 - b) * c1]
            put(9 * per_tap + 3 * a + b, even + odd)
    if lats * block > count * unit:
        keep[count * unit:] = jnp.zeros((lats * block - count * unit, c1), F32)
    orders = [steps(lats, k) for k in range(2)]
    for index in range(lats):
        far = [distance(index, masks) for masks in orders]
        at = (band ^ jnp.where(core == 0, far[0], far[1])) * block
        value = keep[pl.ds(pl.multiple_of(at, block), block), :]
        if index == 0:
            own[...] = value
        else:
            sends[index - 1][...] = value.astype(BF16)


def last_kernel(spread, taps, out, total, turned):
    rows, c0, cols = out.shape
    half = cols // 2
    c2 = 2 * c0
    depth = spread.shape[2]
    result = dot_nt(taps[:c2], spread[2:rows + 2].reshape(rows * half, depth))
    for a in (1, 2):
        result = result + dot_nt(taps[a * c2:(a + 1) * c2],
                                 spread[2 - a:2 - a + rows].reshape(rows * half, depth))
    total[...] = result
    total[:, :half] = total[:, :half] + dot_nt(taps[:c2], spread[rows + 2])
    for q in range(rows // 2):
        pair = total[:, q * cols:(q + 1) * cols].astype(BF16)
        turned[q, :, :cols] = pair[:c0]
        turned[q, :, cols:] = pair[c0:]
    k = lax.broadcasted_iota(jnp.int32, (2 * cols, 2 * cols), 0)
    n = lax.broadcasted_iota(jnp.int32, (2 * cols, 2 * cols), 1)
    order = one_at(n == ((k % cols) // half) * cols + 2 * (k % half) + k // cols)
    found = dot(turned[...].reshape(rows // 2 * c0, 2 * cols), order).astype(BF16)
    for q in range(rows // 2):
        for rp in range(2):
            out[2 * q + rp] = found[q * c0:(q + 1) * c0, rp * cols:(rp + 1) * cols]


def gather_kernel(flags, blocks, out_first, out_second):
    band, core = flags[3], flags[2]
    lats, rows, c1 = blocks.shape
    size = out_second.shape[0]
    total = size + out_first.shape[0]
    orders = [steps(lats, k) for k in range(2)]
    for i in range(lats):
        at = i * rows
        far = i ^ band
        places = []
        for masks in orders:
            place = 0
            for m in masks:
                place = 2 * place + (far // m) % 2
            places.append(place)
        source = jnp.where(core == 0, places[0], places[1])
        for out, base, end in ((out_second, 0, size), (out_first, size, total)):
            low, high = max(at, base), min(at + rows, end)
            if low < high:
                out[low - base:high - base] = blocks[source, low - at:high - at].astype(F32)


def vmem(count):
    return [pl.BlockSpec(memory_space=pltpu.VMEM)] * count


def params(mib):
    return pltpu.CompilerParams(vmem_limit_bytes=mib * 1024 * 1024)


def shape(dims, kind):
    return jax.ShapeDtypeStruct(dims, kind)


def body(inputs, pre_first, grad_out, w_first, w_second):
    rows, cols, c1 = pre_first.shape
    c0 = inputs.shape[2]
    half, pooled = cols // 2, rows // 2
    lats, lons = lax.axis_size("lat"), lax.axis_size("lon")
    depths = lons // 2
    band, place = lax.axis_index("lat"), lax.axis_index("lon")
    core = lax.rem(place, 2)
    even = lax.rem(band, 2) == 0
    flags = jnp.stack([(band == 0).astype(jnp.int32), (band == lats - 1).astype(jnp.int32), core, band,
                       even.astype(jnp.int32)])

    edge = -(-(rows + pooled + 4) // 16) * 16
    row_a, row_b, col_a, col_b = pl.pallas_call(
        pack_kernel,
        out_shape=(
            shape((cols + half, c1), BF16),
            shape((cols + half, c1), BF16),
            shape((edge, c1), BF16),
            shape((edge, c1), BF16),
        ),
        in_specs=[pl.BlockSpec(memory_space=pltpu.SMEM)] + vmem(2),
        out_specs=tuple(vmem(4)),
        scratch_shapes=[
            pltpu.VMEM((2, edge, c1), F32),
        ],
        compiler_params=params(50),
        cost_estimate=pl.CostEstimate(flops=1000, bytes_accessed=1 << 18, transcendentals=0),
    )(flags, pre_first, grad_out)
    pairs = [(j, (j + lons // 2) % lons) for j in range(lons)]
    for i in range(1, lats - 1, 2):
        for j in range(lons):
            pairs += [(i * lons + j, (i + 1) * lons + j), ((i + 1) * lons + j, i * lons + j)]
    row_b = lax.ppermute(row_b, AREA, pairs)
    row_a = lax.ppermute(row_a, "lat", [(i, i ^ 1) for i in range(lats)])

    slope, act_t = pl.pallas_call(
        local_kernel,
        out_shape=(
            shape((rows, half, 2 * c1), F32),
            shape((2, 2 * c1, pooled * half), BF16),
        ),
        in_specs=vmem(1),
        out_specs=tuple(vmem(2)),
        scratch_shapes=[
            pltpu.VMEM((cols, c1), F32),
            pltpu.VMEM((2, pooled, half, 2 * c1), BF16),
        ],
        compiler_params=params(16),
        cost_estimate=pl.CostEstimate(flops=60 * rows * cols * c1, bytes_accessed=2 << 20,
                                      transcendentals=2 * rows * cols * c1),
    )(pre_first)

    fields = jnp.transpose(inputs, (0, 2, 1))
    row_a, row_b, slope, fields = lax.optimization_barrier((row_a, row_b, slope, fields))

    def corners(at):
        places = (at * (cols - 1), cols + at * (half - 1))
        above, below = (jnp.where(even, one, two) for one, two in ((row_b, row_a), (row_a, row_b)))
        return jnp.concatenate([part[p:p + 1] for p in places for part in (above, below)], 0)

    low, high = corners(0), corners(1)
    pad = jnp.zeros((edge - rows - pooled - 4, c1), BF16)
    col_a = jnp.concatenate([col_a[:rows + pooled], jnp.where(core == 0, high, low), pad], 0)
    col_b = jnp.concatenate([col_b[:rows + pooled], jnp.where(core == 0, low, high), pad], 0)
    col_b = lax.ppermute(col_b, "lon", [(i, (i + 2 * (i % 2) - 1) % lons) for i in range(lons)])
    col_a = lax.ppermute(col_a, "lon", [(i, i ^ 1) for i in range(lons)])

    fields_t, taps_first, taps_second = pl.pallas_call(
        layout_kernel,
        out_shape=(
            shape((2 * c0, rows * half), BF16),
            shape((6 * c0, 4 * c1), BF16),
            shape((3, 2 * c1, 4 * c1), BF16),
        ),
        in_specs=vmem(3),
        out_specs=tuple(vmem(3)),
        scratch_shapes=[pltpu.VMEM((rows, c0, 2 * cols), BF16)],
        compiler_params=params(16),
        cost_estimate=pl.CostEstimate(flops=4 * rows * cols * c0 * cols, bytes_accessed=3 << 20, transcendentals=0),
    )(fields, w_first, w_second)
    col_a, col_b, fields_t = lax.optimization_barrier((col_a, col_b, fields_t))

    block = -(-9 * (c1 + c0) // (16 * lats)) * 16
    span = half + EDGE
    spread, own, *sends = pl.pallas_call(
        functools.partial(middle_kernel, lats),
        out_shape=(
            shape((rows + 3, half, 4 * c1), BF16),
            shape((block, c1), F32),
        ) + (shape((block, c1), BF16),) * (lats - 1),
        in_specs=[pl.BlockSpec(memory_space=pltpu.SMEM)] + vmem(9),
        out_specs=tuple(vmem(lats + 1)),
        scratch_shapes=[
            pltpu.VMEM((pooled + 2, span, c1), F32),
            pltpu.VMEM((pooled + 2, span, 4 * c1), BF16),
            pltpu.VMEM((3, pooled, span, 2 * c1), F32),
            pltpu.VMEM((4, span, 2 * c1), F32),
            pltpu.VMEM((cols, c1), F32),
            pltpu.VMEM((2, edge, c1), F32),
            pltpu.VMEM((2, edge, c1), F32),
            pltpu.VMEM((4, 2 * c1, 3 * c1), F32),
            pltpu.VMEM((2 * c1, 3 * c1), F32),
            pltpu.VMEM((lats * block, c1), F32),
        ],
        compiler_params=params(16),
        cost_estimate=pl.CostEstimate(flops=2 * rows * cols * c1 * 9 * (2 * c1 + c0), bytes_accessed=8 << 20,
                                      transcendentals=0),
    )(flags, grad_out, row_a, row_b, col_a, col_b, slope, act_t, fields_t, taps_second)

    orders = [steps(lats, k) for k in range(2)]

    def along_lat(t, value):
        far = [distance(t, masks) for masks in orders]
        return lax.ppermute(value, AREA, [
            (i * lons + j, (i ^ far[j % 2]) * lons + j) for i in range(lats) for j in range(lons)])

    got = [along_lat(t + 1, value) for t, value in enumerate(sends)]
    grad_inputs = pl.pallas_call(
        last_kernel,
        out_shape=shape((rows, c0, cols), BF16),
        in_specs=vmem(2),
        out_specs=vmem(1)[0],
        scratch_shapes=[
            pltpu.VMEM((2 * c0, rows * half), F32),
            pltpu.VMEM((pooled, c0, 2 * cols), BF16),
        ],
        compiler_params=params(12),
        cost_estimate=pl.CostEstimate(flops=2 * rows * cols * c1 * 9 * c0, bytes_accessed=3 << 20, transcendentals=0),
    )(spread, taps_first)
    *got, grad_inputs = lax.optimization_barrier((*got, grad_inputs))
    total = own
    for value in got:
        total = total + value.astype(F32)
    swap = [(i, i ^ 1) for i in range(lons)]
    low, high = total[:block // 2], total[block // 2:]
    total = jnp.where(core == 0, low, high) + lax.ppermute(jnp.where(core == 0, high, low), "lon", swap)
    part = total.astype(BF16)
    terms = [part] + [lax.ppermute(part, "lon", [(i, i ^ (2 * k)) for i in range(lons)]) for k in range(1, depths)]
    terms = [term.astype(F32) for term in terms]
    while len(terms) > 1:
        terms = [terms[k] + terms[k + 1] for k in range(0, len(terms), 2)]
    mine = terms[0].astype(BF16)
    theirs = lax.ppermute(mine, "lon", swap)
    whole = jnp.concatenate([jnp.where(core == 0, mine, theirs), jnp.where(core == 0, theirs, mine)], 0)
    blocks = jnp.stack([whole] + [along_lat(t, whole) for t in range(1, lats)], 0)

    grad_w_first, grad_w_second = pl.pallas_call(
        gather_kernel,
        out_shape=(shape((9 * c0, c1), F32), shape((9 * c1, c1), F32)),
        in_specs=[pl.BlockSpec(memory_space=pltpu.SMEM)] + vmem(1),
        out_specs=tuple(vmem(2)),
        compiler_params=params(8),
        cost_estimate=pl.CostEstimate(flops=1000, bytes_accessed=3 << 19, transcendentals=0),
    )(flags, blocks)
    return (jnp.transpose(grad_inputs, (0, 2, 1)), grad_w_first.reshape(w_first.shape),
            grad_w_second.reshape(w_second.shape))


def solution(mesh):
    in_specs = (P("lat", "lon", None), P("lat", "lon", None), P("lat", "lon", None), P(), P())
    out_specs = (P("lat", "lon", None), P(), P())
    return jax.shard_map(body, mesh=mesh, in_specs=in_specs, out_specs=out_specs, check_vma=False)
```

```python
import functools

import jax
import jax.numpy as jnp
from jax import lax
from jax.experimental import pallas as pl
from jax.experimental.pallas import tpu as pltpu
from jax.sharding import PartitionSpec as P

inv_root = 0.7071067811865476
density = 0.3989422804014327

F32 = jnp.float32
BF16 = jnp.bfloat16
EDGE = 16
AREA = ("lat", "lon")


def cdf_of(value):
    return 0.5 * (1.0 + lax.erf(value * inv_root))


def slope_of(value, cdf):
    return 0.25 * (cdf + value * jnp.exp(-0.5 * value * value) * density)


def dot(left, right):
    return jnp.dot(left, right, preferred_element_type=F32)


def dot_nt(left, right):
    return lax.dot_general(left, right, (((1,), (1,)), ((), ())), preferred_element_type=F32)


def position(lats):
    band, place = lax.axis_index("lat"), lax.axis_index("lon")
    return band, band == 0, band == lats - 1, lax.rem(band, 2) == 0, lax.rem(place, 2)


def pack_kernel(lats, pre, grad_out, row_a, row_b, col_a, col_b, hold):
    rows, cols, c1 = pre.shape
    pooled, half = grad_out.shape[:2]
    _, _, _, even, core = position(lats)
    for message, low in ((row_a, ~even), (row_b, even)):
        message[:cols] = pre[jnp.where(low, 0, rows - 1)]
        message[cols:] = grad_out[jnp.where(low, 0, pooled - 1)]
    hold[:, rows + pooled:] = jnp.zeros((2, hold.shape[1] - rows - pooled, c1), F32)
    for side, (p, g) in enumerate(((0, 0), (cols - 16, half - 16))):
        at = 15 * side
        for r in range(rows):
            hold[side, r:r + 1] = pre[r, p:p + 16].astype(F32)[at:at + 1]
        for i in range(pooled):
            hold[side, rows + i:rows + i + 1] = grad_out[i, g:g + 16].astype(F32)[at:at + 1]
    col_a[...] = hold[1 - core].astype(BF16)
    col_b[...] = hold[core].astype(BF16)


def one_at(where):
    return jnp.where(where, 1.0, 0.0).astype(BF16)


def local_kernel(pre, slope, act_t, line, act_s):
    rows, cols, c1 = pre.shape
    half = cols // 2

    def one_row(r, carry):
        line[...] = pre[r].astype(F32)
        for pc in range(2):
            value = line[pl.ds(pc, half, stride=2), :]
            cdf = cdf_of(value)
            act_s[r % 2, r // 2, :, pc * c1:(pc + 1) * c1] = (value * cdf).astype(BF16)
            slope[r, :, pc * c1:(pc + 1) * c1] = slope_of(value, cdf)
        return carry

    lax.fori_loop(0, rows, one_row, 0)
    for pr in range(2):
        act_t[pr] = act_s[pr].reshape(rows // 2 * half, 2 * c1).T


def layout_kernel(fields, w_first, w_second, fields_t, taps_first, taps_second, turned):
    rows, c0, cols = fields.shape
    c1 = w_first.shape[3]
    half = cols // 2
    col = lax.broadcasted_iota(jnp.int32, (cols, 2 * cols), 0)
    lane = lax.broadcasted_iota(jnp.int32, (cols, 2 * cols), 1)
    turn = lane // cols
    parity = (lane % cols) // half
    parity = parity + turn - 2 * parity * turn
    order = one_at(col == 2 * (lane % half) + parity)
    turned[...] = dot(fields[...].reshape(rows * c0, cols), order).astype(BF16).reshape(rows, c0, 2 * cols)
    low = lax.broadcasted_iota(jnp.int32, (c0, cols), 1) < half
    for q in range(rows // 2):
        fields_t[:c0, q * cols:(q + 1) * cols] = jnp.where(low, turned[2 * q, :, :cols], turned[2 * q + 1, :, cols:])
        fields_t[c0:, q * cols:(q + 1) * cols] = jnp.where(low, turned[2 * q, :, cols:], turned[2 * q + 1, :, :cols])
    taps_second[...] = jnp.zeros_like(taps_second)
    taps_first[...] = jnp.zeros_like(taps_first)
    for a in range(3):
        for pc, blocks in ((0, (2, 1, None, 0)), (1, (None, 2, 0, 1))):
            for k, b in enumerate(blocks):
                if b is not None:
                    taps_second[a, pc * c1:(pc + 1) * c1, k * c1:(k + 1) * c1] = w_second[a, b]
        for pc, blocks in ((0, (2, 1, 0, None)), (1, (None, 2, 1, 0))):
            for k, b in enumerate(blocks):
                if b is not None:
                    start = (2 * a + pc) * c0
                    taps_first[start:start + c0, k * c1:(k + 1) * c1] = w_first[a, b]


def middle_kernel(lats, grad_out, row_a, row_b, col_a, col_b, slope, act_t, fields_t, taps,
                  spread, own, other,
                  grid, wide, prods, ends, line, side, sides, sums, corner, keep):
    band, first, last, even, core = position(lats)
    top = jnp.where(even, row_b[...], row_a[...])
    bottom = jnp.where(even, row_a[...], row_b[...])
    rows, half, c2 = slope.shape
    c1 = c2 // 2
    pooled = rows // 2
    c0 = fields_t.shape[0] // 2
    cells = pooled * half

    grid[:, half:, :] = jnp.zeros((pooled + 2, EDGE, c1), F32)
    grid[1:pooled + 1, :half, :] = grad_out[...].astype(F32)
    grid[0, :half, :] = top[2 * half:, :].astype(F32)
    outside = jnp.where(last, 0.0, 1.0)
    grid[pooled + 1, :half, :] = bottom[2 * half:, :].astype(F32) * outside
    side[1 - core] = col_a[...].astype(F32)
    side[core] = col_b[...].astype(F32)
    for i in range(pooled + 2):
        at = rows + i - 1
        if i == 0:
            at = rows + pooled + 2
        if i == pooled + 1:
            at = rows + pooled + 3
        kept = outside if i == pooled + 1 else 1.0
        grid[i, half:half + 1, :] = side[1, at:at + 1, :] * kept
        grid[i, half + EDGE - 1:half + EDGE, :] = side[0, at:at + 1, :] * kept
    for i in range(pooled + 2):
        here = grid[i]
        wide[i, :, :c1] = pltpu.roll(here, 1, 0).astype(BF16)
        wide[i, :, c1:2 * c1] = here.astype(BF16)
        wide[i, :, 2 * c1:3 * c1] = pltpu.roll(here, half + EDGE - 1, 0).astype(BF16)
        wide[i, :, 3 * c1:] = here.astype(BF16)

    flat = wide[1:pooled + 1].reshape(pooled * (half + EDGE), 4 * c1)
    for a in range(3):
        prods[a] = dot_nt(flat, taps[a]).reshape(pooled, half + EDGE, c2)
    fold = jnp.where(first, taps[0], taps[2])
    ends[0] = dot_nt(wide[0], fold)
    ends[1] = dot_nt(wide[0], taps[1])
    ends[2] = dot_nt(wide[pooled + 1], taps[0])
    ends[3] = dot_nt(wide[pooled + 1], taps[1])

    for s in range(2):
        sides[s] = slope_of(side[s], cdf_of(side[s]))

    def place(r, total, incline, edge):
        inner = total[:half] * incline
        rim = total[half:]
        after = rim[:1, :c1] * sides[1, pl.ds(edge, 1), :]
        before = rim[EDGE - 1:, c1:] * sides[0, pl.ds(edge, 1), :]
        even, odd = inner[:, :c1], inner[:, c1:]
        at = lax.broadcasted_iota(jnp.int32, (half, c1), 0)
        spread[r, :, :c1] = jnp.where(at == 0, before, pltpu.roll(odd, 1, 0)).astype(BF16)
        spread[r, :, c1:2 * c1] = even.astype(BF16)
        spread[r, :, 2 * c1:3 * c1] = odd.astype(BF16)
        spread[r, :, 3 * c1:] = jnp.where(at == half - 1, after, pltpu.roll(even, half - 1, 0)).astype(BF16)

    def halo_slope(message):
        line[...] = message[:2 * half, :].astype(F32)
        both = [line[pl.ds(pc, half, stride=2), :] for pc in range(2)]
        return jnp.concatenate([slope_of(v, cdf_of(v)) for v in both], axis=1)

    place(0, ends[0] + ends[1] + prods[0, 0], halo_slope(top), rows + pooled)
    place(1, ends[0] + prods[1, 0] + prods[0, 0], slope[0], 0)

    def pair(i, carry):
        middle = prods[2, i] + prods[1, i]
        place(2 * i + 2, middle + prods[0, i + 1], slope[2 * i + 1], 2 * i + 1)
        place(2 * i + 3, prods[2, i] + prods[1, i + 1] + prods[0, i + 1], slope[2 * i + 2], 2 * i + 2)
        return carry

    lax.fori_loop(0, pooled - 1, pair, 0)
    final = prods[2, pooled - 1]
    place(rows, final + prods[1, pooled - 1] + ends[2], slope[rows - 1], rows - 1)
    place(rows + 1, (final + ends[3] + ends[2]) * outside, halo_slope(bottom), rows + pooled + 1)

    is_first = jnp.where(first, 1.0, 0.0).astype(BF16)
    not_first = jnp.where(first, 0.0, 1.0).astype(BF16)
    above = wide[0, :half, :3 * c1]
    wide[0, :half, :3 * c1] = above * not_first
    for n, (pr, start) in enumerate(((0, 0), (0, 1), (1, 1), (1, 2))):
        around = wide[start:start + pooled, :half, :3 * c1].reshape(cells, 3 * c1)
        sums[n] = dot(act_t[pr], around)
    corner[...] = dot(act_t[0, :, :half], above * is_first)

    unit = c0
    per_tap = c1 // unit
    count = 9 * per_tap + 9
    held = own.shape[0]
    block = held // lats

    def put(k, value):
        keep[k * unit:(k + 1) * unit, :] = value

    pieces = {0: ((0, 1), (1, 3)), 1: ((0, 1), (1, 2)), 2: ((0, 0), (1, 2))}
    for a in range(3):
        for b in range(3):
            total = None
            for pr, n in pieces[a]:
                for pc in range(2):
                    k = (pc + 1 - b) // 2 + 1
                    term = sums[n, pc * c1:(pc + 1) * c1, k * c1:(k + 1) * c1]
                    total = term if total is None else total + term
            if a == 0:
                for pc in range(2):
                    k = (pc + 1 - b) // 2 + 1
                    total = total + corner[pc * c1:(pc + 1) * c1, k * c1:(k + 1) * c1]
            total = total * 0.25
            for part in range(per_tap):
                put((3 * a + b) * per_tap + part, total[part * unit:(part + 1) * unit])

    head = spread[0]
    spread[0] = head * not_first
    spread[rows + 2] = head * is_first
    folded = dot(fields_t[:, :half], spread[rows + 2])
    for a in range(3):
        around = spread[2 - a:2 - a + rows].reshape(rows * half, 4 * c1)
        got = dot(fields_t[...], around)
        if a == 0:
            got = got + folded
        for b in range(3):
            even = got[:c0, (2 - b) * c1:(3 - b) * c1]
            odd = got[c0:, (3 - b) * c1:(4 - b) * c1]
            put(9 * per_tap + 3 * a + b, even + odd)
    if 2 * held > count * unit:
        keep[count * unit:] = jnp.zeros((2 * held - count * unit, c1), F32)
    for target, half_of in ((own, core), (other, 1 - core)):
        for far in range(lats):
            at = half_of * held + (band ^ far) * block
            target[far * block:(far + 1) * block] = keep[pl.ds(pl.multiple_of(at, block), block), :]


def last_kernel(spread, taps, out, total, turned):
    rows, c0, cols = out.shape
    half = cols // 2
    c2 = 2 * c0
    depth = spread.shape[2]
    result = dot_nt(taps[:c2], spread[2:rows + 2].reshape(rows * half, depth))
    for a in (1, 2):
        result = result + dot_nt(taps[a * c2:(a + 1) * c2],
                                 spread[2 - a:2 - a + rows].reshape(rows * half, depth))
    total[...] = result
    total[:, :half] = total[:, :half] + dot_nt(taps[:c2], spread[rows + 2])
    for q in range(rows // 2):
        pair = total[:, q * cols:(q + 1) * cols].astype(BF16)
        turned[q, :, :cols] = pair[:c0]
        turned[q, :, cols:] = pair[c0:]
    k = lax.broadcasted_iota(jnp.int32, (2 * cols, 2 * cols), 0)
    n = lax.broadcasted_iota(jnp.int32, (2 * cols, 2 * cols), 1)
    order = one_at(n == ((k % cols) // half) * cols + 2 * (k % half) + k // cols)
    found = dot(turned[...].reshape(rows // 2 * c0, 2 * cols), order).astype(BF16)
    for q in range(rows // 2):
        for rp in range(2):
            out[2 * q + rp] = found[q * c0:(q + 1) * c0, rp * cols:(rp + 1) * cols]


def gather_kernel(mine, theirs, out_first, out_second):
    lats, rows, c1 = mine.shape
    band, _, _, _, core = position(lats)
    size = out_second.shape[0]
    total = size + out_first.shape[0]
    for h in range(2):
        for i in range(lats):
            at = (h * lats + i) * rows
            for out, base, end in ((out_second, 0, size), (out_first, size, total)):
                low, high = max(at, base), min(at + rows, end)
                if low < high:
                    here, there = (x[i ^ band, low - at:high - at] for x in (mine, theirs))
                    out[low - base:high - base] = jnp.where(core == h, here, there).astype(F32)


def vmem(count):
    return [pl.BlockSpec(memory_space=pltpu.VMEM)] * count


def params(mib):
    return pltpu.CompilerParams(vmem_limit_bytes=mib * 1024 * 1024)


def shape(dims, kind):
    return jax.ShapeDtypeStruct(dims, kind)


def body(inputs, pre_first, grad_out, w_first, w_second):
    rows, cols, c1 = pre_first.shape
    c0 = inputs.shape[2]
    half, pooled = cols // 2, rows // 2
    lats, lons = lax.axis_size("lat"), lax.axis_size("lon")
    depths = lons // 2
    band, place = lax.axis_index("lat"), lax.axis_index("lon")
    core = lax.rem(place, 2)
    even = lax.rem(band, 2) == 0

    edge = -(-(rows + pooled + 4) // 16) * 16
    row_a, row_b, col_a, col_b = pl.pallas_call(
        functools.partial(pack_kernel, lats),
        out_shape=(
            shape((cols + half, c1), BF16),
            shape((cols + half, c1), BF16),
            shape((edge, c1), BF16),
            shape((edge, c1), BF16),
        ),
        in_specs=vmem(2),
        out_specs=tuple(vmem(4)),
        scratch_shapes=[
            pltpu.VMEM((2, edge, c1), F32),
        ],
        compiler_params=params(50),
        cost_estimate=pl.CostEstimate(flops=1000, bytes_accessed=1 << 18, transcendentals=0),
    )(pre_first, grad_out)
    pairs = [(j, (j + lons // 2) % lons) for j in range(lons)]
    for i in range(1, lats - 1, 2):
        for j in range(lons):
            pairs += [(i * lons + j, (i + 1) * lons + j), ((i + 1) * lons + j, i * lons + j)]
    row_b = lax.ppermute(row_b, AREA, pairs)
    row_a = lax.ppermute(row_a, "lat", [(i, i ^ 1) for i in range(lats)])

    slope, act_t = pl.pallas_call(
        local_kernel,
        out_shape=(
            shape((rows, half, 2 * c1), F32),
            shape((2, 2 * c1, pooled * half), BF16),
        ),
        in_specs=vmem(1),
        out_specs=tuple(vmem(2)),
        scratch_shapes=[
            pltpu.VMEM((cols, c1), F32),
            pltpu.VMEM((2, pooled, half, 2 * c1), BF16),
        ],
        compiler_params=params(16),
        cost_estimate=pl.CostEstimate(flops=60 * rows * cols * c1, bytes_accessed=2 << 20,
                                      transcendentals=2 * rows * cols * c1),
    )(pre_first)

    fields = jnp.transpose(inputs, (0, 2, 1))
    row_a, row_b, slope, fields = lax.optimization_barrier((row_a, row_b, slope, fields))

    def corners(at):
        places = (at * (cols - 1), cols + at * (half - 1))
        above, below = (jnp.where(even, one, two) for one, two in ((row_b, row_a), (row_a, row_b)))
        return jnp.concatenate([part[p:p + 1] for p in places for part in (above, below)], 0)

    low, high = corners(0), corners(1)
    pad = jnp.zeros((edge - rows - pooled - 4, c1), BF16)
    col_a = jnp.concatenate([col_a[:rows + pooled], jnp.where(core == 0, high, low), pad], 0)
    col_b = jnp.concatenate([col_b[:rows + pooled], jnp.where(core == 0, low, high), pad], 0)
    col_b = lax.ppermute(col_b, "lon", [(i, (i + 2 * (i % 2) - 1) % lons) for i in range(lons)])
    col_a = lax.ppermute(col_a, "lon", [(i, i ^ 1) for i in range(lons)])

    fields_t, taps_first, taps_second = pl.pallas_call(
        layout_kernel,
        out_shape=(
            shape((2 * c0, rows * half), BF16),
            shape((6 * c0, 4 * c1), BF16),
            shape((3, 2 * c1, 4 * c1), BF16),
        ),
        in_specs=vmem(3),
        out_specs=tuple(vmem(3)),
        scratch_shapes=[pltpu.VMEM((rows, c0, 2 * cols), BF16)],
        compiler_params=params(16),
        cost_estimate=pl.CostEstimate(flops=4 * rows * cols * c0 * cols, bytes_accessed=3 << 20, transcendentals=0),
    )(fields, w_first, w_second)
    col_a, col_b, fields_t = lax.optimization_barrier((col_a, col_b, fields_t))

    block = -(-9 * (c1 + c0) // (32 * lats)) * 16
    held = lats * block
    span = half + EDGE
    spread, own, other = pl.pallas_call(
        functools.partial(middle_kernel, lats),
        out_shape=(
            shape((rows + 3, half, 4 * c1), BF16),
            shape((held, c1), F32),
            shape((held, c1), F32),
        ),
        in_specs=vmem(9),
        out_specs=tuple(vmem(3)),
        scratch_shapes=[
            pltpu.VMEM((pooled + 2, span, c1), F32),
            pltpu.VMEM((pooled + 2, span, 4 * c1), BF16),
            pltpu.VMEM((3, pooled, span, 2 * c1), F32),
            pltpu.VMEM((4, span, 2 * c1), F32),
            pltpu.VMEM((cols, c1), F32),
            pltpu.VMEM((2, edge, c1), F32),
            pltpu.VMEM((2, edge, c1), F32),
            pltpu.VMEM((4, 2 * c1, 3 * c1), F32),
            pltpu.VMEM((2 * c1, 3 * c1), F32),
            pltpu.VMEM((2 * held, c1), F32),
        ],
        compiler_params=params(16),
        cost_estimate=pl.CostEstimate(flops=2 * rows * cols * c1 * 9 * (2 * c1 + c0), bytes_accessed=8 << 20,
                                      transcendentals=0),
    )(grad_out, row_a, row_b, col_a, col_b, slope, act_t, fields_t, taps_second)

    swap = [(i, i ^ 1) for i in range(lons)]

    def along_lat(far, value):
        return lax.ppermute(value, "lat", [(i, i ^ far) for i in range(lats)])

    parts = (own + lax.ppermute(other, "lon", swap)).reshape(lats, block, c1)
    sent = [parts[far].astype(BF16) for far in range(1, lats)]
    *sent, spread = lax.optimization_barrier((*sent, spread))
    got = [along_lat(far + 1, value) for far, value in enumerate(sent)]
    grad_inputs = pl.pallas_call(
        last_kernel,
        out_shape=shape((rows, c0, cols), BF16),
        in_specs=vmem(2),
        out_specs=vmem(1)[0],
        scratch_shapes=[
            pltpu.VMEM((2 * c0, rows * half), F32),
            pltpu.VMEM((pooled, c0, 2 * cols), BF16),
        ],
        compiler_params=params(12),
        cost_estimate=pl.CostEstimate(flops=2 * rows * cols * c1 * 9 * c0, bytes_accessed=3 << 20, transcendentals=0),
    )(spread, taps_first)
    *got, grad_inputs = lax.optimization_barrier((*got, grad_inputs))
    total = parts[0]
    for value in got:
        total = total + value.astype(F32)
    part = total.astype(BF16)
    terms = [part] + [lax.ppermute(part, "lon", [(i, i ^ (2 * k)) for i in range(lons)]) for k in range(1, depths)]
    terms = [term.astype(F32) for term in terms]
    while len(terms) > 1:
        terms = [terms[k] + terms[k + 1] for k in range(0, len(terms), 2)]
    part = terms[0].astype(BF16)
    mine = jnp.stack([part] + [along_lat(far, part) for far in range(1, lats)], 0)
    theirs = lax.ppermute(mine, "lon", swap)

    grad_w_first, grad_w_second = pl.pallas_call(
        gather_kernel,
        out_shape=(shape((9 * c0, c1), F32), shape((9 * c1, c1), F32)),
        in_specs=vmem(2),
        out_specs=tuple(vmem(2)),
        compiler_params=params(8),
        cost_estimate=pl.CostEstimate(flops=1000, bytes_accessed=3 << 19, transcendentals=0),
    )(mine, theirs)
    return (jnp.transpose(grad_inputs, (0, 2, 1)), grad_w_first.reshape(w_first.shape),
            grad_w_second.reshape(w_second.shape))


def solution(mesh):
    in_specs = (P("lat", "lon", None), P("lat", "lon", None), P("lat", "lon", None), P(), P())
    out_specs = (P("lat", "lon", None), P(), P())
    return jax.shard_map(body, mesh=mesh, in_specs=in_specs, out_specs=out_specs, check_vma=False)
```

```python
import functools

import jax
import jax.numpy as jnp
from jax import lax
from jax.experimental import pallas as pl
from jax.experimental.pallas import tpu as pltpu
from jax.sharding import PartitionSpec as P

inv_root = 0.7071067811865476
density = 0.3989422804014327

F32 = jnp.float32
BF16 = jnp.bfloat16
EDGE = 16
AREA = ("lat", "lon")


def cdf_of(value):
    return 0.5 * (1.0 + lax.erf(value * inv_root))


def slope_of(value, cdf):
    return 0.25 * (cdf + value * jnp.exp(-0.5 * value * value) * density)


def dot(left, right):
    return jnp.dot(left, right, preferred_element_type=F32)


def dot_nt(left, right):
    return lax.dot_general(left, right, (((1,), (1,)), ((), ())), preferred_element_type=F32)


def position(lats):
    band, place = lax.axis_index("lat"), lax.axis_index("lon")
    return band, band == 0, band == lats - 1, lax.rem(band, 2) == 0, lax.rem(place, 2)


def bases(lats, depths):
    band, depth = lax.axis_index("lat"), lax.axis_index("lon") // 2
    return (band, depth if lats == depths else band)


def pack_kernel(lats, pre, grad_out, row_a, row_b, col_a, col_b, hold):
    rows, cols, c1 = pre.shape
    pooled, half = grad_out.shape[:2]
    _, _, _, even, core = position(lats)
    for message, low in ((row_a, ~even), (row_b, even)):
        message[:cols] = pre[jnp.where(low, 0, rows - 1)]
        message[cols:] = grad_out[jnp.where(low, 0, pooled - 1)]
    hold[:, rows + pooled:] = jnp.zeros((2, hold.shape[1] - rows - pooled, c1), F32)
    for side, (p, g) in enumerate(((0, 0), (cols - 16, half - 16))):
        at = 15 * side
        for r in range(rows):
            hold[side, r:r + 1] = pre[r, p:p + 16].astype(F32)[at:at + 1]
        for i in range(pooled):
            hold[side, rows + i:rows + i + 1] = grad_out[i, g:g + 16].astype(F32)[at:at + 1]
    col_a[...] = hold[1 - core].astype(BF16)
    col_b[...] = hold[core].astype(BF16)


def one_at(where):
    return jnp.where(where, 1.0, 0.0).astype(BF16)


def local_kernel(pre, slope, act_t, line, act_s):
    rows, cols, c1 = pre.shape
    half = cols // 2

    def one_row(r, carry):
        line[...] = pre[r].astype(F32)
        for pc in range(2):
            value = line[pl.ds(pc, half, stride=2), :]
            cdf = cdf_of(value)
            act_s[r % 2, r // 2, :, pc * c1:(pc + 1) * c1] = (value * cdf).astype(BF16)
            slope[r, :, pc * c1:(pc + 1) * c1] = slope_of(value, cdf)
        return carry

    lax.fori_loop(0, rows, one_row, 0)
    for pr in range(2):
        act_t[pr] = act_s[pr].reshape(rows // 2 * half, 2 * c1).T


def layout_kernel(fields, w_first, w_second, fields_t, taps_first, taps_second, turned):
    rows, c0, cols = fields.shape
    c1 = w_first.shape[3]
    half = cols // 2
    col = lax.broadcasted_iota(jnp.int32, (cols, 2 * cols), 0)
    lane = lax.broadcasted_iota(jnp.int32, (cols, 2 * cols), 1)
    turn = lane // cols
    parity = (lane % cols) // half
    parity = parity + turn - 2 * parity * turn
    order = one_at(col == 2 * (lane % half) + parity)
    turned[...] = dot(fields[...].reshape(rows * c0, cols), order).astype(BF16).reshape(rows, c0, 2 * cols)
    low = lax.broadcasted_iota(jnp.int32, (c0, cols), 1) < half
    for q in range(rows // 2):
        fields_t[:c0, q * cols:(q + 1) * cols] = jnp.where(low, turned[2 * q, :, :cols], turned[2 * q + 1, :, cols:])
        fields_t[c0:, q * cols:(q + 1) * cols] = jnp.where(low, turned[2 * q, :, cols:], turned[2 * q + 1, :, :cols])
    taps_second[...] = jnp.zeros_like(taps_second)
    taps_first[...] = jnp.zeros_like(taps_first)
    for a in range(3):
        for pc, blocks in ((0, (2, 1, None, 0)), (1, (None, 2, 0, 1))):
            for k, b in enumerate(blocks):
                if b is not None:
                    taps_second[a, pc * c1:(pc + 1) * c1, k * c1:(k + 1) * c1] = w_second[a, b]
        for pc, blocks in ((0, (2, 1, 0, None)), (1, (None, 2, 1, 0))):
            for k, b in enumerate(blocks):
                if b is not None:
                    start = (2 * a + pc) * c0
                    taps_first[start:start + c0, k * c1:(k + 1) * c1] = w_first[a, b]


def middle_kernel(lats, depths, grad_out, row_a, row_b, col_a, col_b, slope, act_t, fields_t, taps,
                  spread, own, other,
                  grid, wide, prods, ends, line, side, sides, sums, corner, keep):
    _, first, last, even, core = position(lats)
    top = jnp.where(even, row_b[...], row_a[...])
    bottom = jnp.where(even, row_a[...], row_b[...])
    rows, half, c2 = slope.shape
    c1 = c2 // 2
    pooled = rows // 2
    c0 = fields_t.shape[0] // 2
    cells = pooled * half

    grid[:, half:, :] = jnp.zeros((pooled + 2, EDGE, c1), F32)
    grid[1:pooled + 1, :half, :] = grad_out[...].astype(F32)
    grid[0, :half, :] = top[2 * half:, :].astype(F32)
    outside = jnp.where(last, 0.0, 1.0)
    grid[pooled + 1, :half, :] = bottom[2 * half:, :].astype(F32) * outside
    side[1 - core] = col_a[...].astype(F32)
    side[core] = col_b[...].astype(F32)
    for i in range(pooled + 2):
        at = rows + i - 1
        if i == 0:
            at = rows + pooled + 2
        if i == pooled + 1:
            at = rows + pooled + 3
        kept = outside if i == pooled + 1 else 1.0
        grid[i, half:half + 1, :] = side[1, at:at + 1, :] * kept
        grid[i, half + EDGE - 1:half + EDGE, :] = side[0, at:at + 1, :] * kept
    for i in range(pooled + 2):
        here = grid[i]
        wide[i, :, :c1] = pltpu.roll(here, 1, 0).astype(BF16)
        wide[i, :, c1:2 * c1] = here.astype(BF16)
        wide[i, :, 2 * c1:3 * c1] = pltpu.roll(here, half + EDGE - 1, 0).astype(BF16)
        wide[i, :, 3 * c1:] = here.astype(BF16)

    flat = wide[1:pooled + 1].reshape(pooled * (half + EDGE), 4 * c1)
    for a in range(3):
        prods[a] = dot_nt(flat, taps[a]).reshape(pooled, half + EDGE, c2)
    fold = jnp.where(first, taps[0], taps[2])
    ends[0] = dot_nt(wide[0], fold)
    ends[1] = dot_nt(wide[0], taps[1])
    ends[2] = dot_nt(wide[pooled + 1], taps[0])
    ends[3] = dot_nt(wide[pooled + 1], taps[1])

    for s in range(2):
        sides[s] = slope_of(side[s], cdf_of(side[s]))

    def place(r, total, incline, edge):
        inner = total[:half] * incline
        rim = total[half:]
        after = rim[:1, :c1] * sides[1, pl.ds(edge, 1), :]
        before = rim[EDGE - 1:, c1:] * sides[0, pl.ds(edge, 1), :]
        even, odd = inner[:, :c1], inner[:, c1:]
        at = lax.broadcasted_iota(jnp.int32, (half, c1), 0)
        spread[r, :, :c1] = jnp.where(at == 0, before, pltpu.roll(odd, 1, 0)).astype(BF16)
        spread[r, :, c1:2 * c1] = even.astype(BF16)
        spread[r, :, 2 * c1:3 * c1] = odd.astype(BF16)
        spread[r, :, 3 * c1:] = jnp.where(at == half - 1, after, pltpu.roll(even, half - 1, 0)).astype(BF16)

    def halo_slope(message):
        line[...] = message[:2 * half, :].astype(F32)
        both = [line[pl.ds(pc, half, stride=2), :] for pc in range(2)]
        return jnp.concatenate([slope_of(v, cdf_of(v)) for v in both], axis=1)

    place(0, ends[0] + ends[1] + prods[0, 0], halo_slope(top), rows + pooled)
    place(1, ends[0] + prods[1, 0] + prods[0, 0], slope[0], 0)

    def pair(i, carry):
        middle = prods[2, i] + prods[1, i]
        place(2 * i + 2, middle + prods[0, i + 1], slope[2 * i + 1], 2 * i + 1)
        place(2 * i + 3, prods[2, i] + prods[1, i + 1] + prods[0, i + 1], slope[2 * i + 2], 2 * i + 2)
        return carry

    lax.fori_loop(0, pooled - 1, pair, 0)
    final = prods[2, pooled - 1]
    place(rows, final + prods[1, pooled - 1] + ends[2], slope[rows - 1], rows - 1)
    place(rows + 1, (final + ends[3] + ends[2]) * outside, halo_slope(bottom), rows + pooled + 1)

    is_first = jnp.where(first, 1.0, 0.0).astype(BF16)
    not_first = jnp.where(first, 0.0, 1.0).astype(BF16)
    above = wide[0, :half, :3 * c1]
    wide[0, :half, :3 * c1] = above * not_first
    for n, (pr, start) in enumerate(((0, 0), (0, 1), (1, 1), (1, 2))):
        around = wide[start:start + pooled, :half, :3 * c1].reshape(cells, 3 * c1)
        sums[n] = dot(act_t[pr], around)
    corner[...] = dot(act_t[0, :, :half], above * is_first)

    unit = c0
    per_tap = c1 // unit
    count = 9 * per_tap + 9
    held = own.shape[0]
    block = held // lats

    def put(k, value):
        keep[k * unit:(k + 1) * unit, :] = value

    pieces = {0: ((0, 1), (1, 3)), 1: ((0, 1), (1, 2)), 2: ((0, 0), (1, 2))}
    for a in range(3):
        for b in range(3):
            total = None
            for pr, n in pieces[a]:
                for pc in range(2):
                    k = (pc + 1 - b) // 2 + 1
                    term = sums[n, pc * c1:(pc + 1) * c1, k * c1:(k + 1) * c1]
                    total = term if total is None else total + term
            if a == 0:
                for pc in range(2):
                    k = (pc + 1 - b) // 2 + 1
                    total = total + corner[pc * c1:(pc + 1) * c1, k * c1:(k + 1) * c1]
            total = total * 0.25
            for part in range(per_tap):
                put((3 * a + b) * per_tap + part, total[part * unit:(part + 1) * unit])

    head = spread[0]
    spread[0] = head * not_first
    spread[rows + 2] = head * is_first
    folded = dot(fields_t[:, :half], spread[rows + 2])
    for a in range(3):
        around = spread[2 - a:2 - a + rows].reshape(rows * half, 4 * c1)
        got = dot(fields_t[...], around)
        if a == 0:
            got = got + folded
        for b in range(3):
            even = got[:c0, (2 - b) * c1:(3 - b) * c1]
            odd = got[c0:, (3 - b) * c1:(4 - b) * c1]
            put(9 * per_tap + 3 * a + b, even + odd)
    if 2 * held > count * unit:
        keep[count * unit:] = jnp.zeros((2 * held - count * unit, c1), F32)
    base = bases(lats, depths)
    for target, half_of in ((own, core), (other, 1 - core)):
        for far in range(lats):
            at = half_of * held + (jnp.where(half_of == 0, base[0], base[1]) ^ far) * block
            target[far * block:(far + 1) * block] = keep[pl.ds(pl.multiple_of(at, block), block), :]


def last_kernel(spread, taps, out, total, turned):
    rows, c0, cols = out.shape
    half = cols // 2
    c2 = 2 * c0
    depth = spread.shape[2]
    result = dot_nt(taps[:c2], spread[2:rows + 2].reshape(rows * half, depth))
    for a in (1, 2):
        result = result + dot_nt(taps[a * c2:(a + 1) * c2],
                                 spread[2 - a:2 - a + rows].reshape(rows * half, depth))
    total[...] = result
    total[:, :half] = total[:, :half] + dot_nt(taps[:c2], spread[rows + 2])
    for q in range(rows // 2):
        pair = total[:, q * cols:(q + 1) * cols].astype(BF16)
        turned[q, :, :cols] = pair[:c0]
        turned[q, :, cols:] = pair[c0:]
    k = lax.broadcasted_iota(jnp.int32, (2 * cols, 2 * cols), 0)
    n = lax.broadcasted_iota(jnp.int32, (2 * cols, 2 * cols), 1)
    order = one_at(n == ((k % cols) // half) * cols + 2 * (k % half) + k // cols)
    found = dot(turned[...].reshape(rows // 2 * c0, 2 * cols), order).astype(BF16)
    for q in range(rows // 2):
        for rp in range(2):
            out[2 * q + rp] = found[q * c0:(q + 1) * c0, rp * cols:(rp + 1) * cols]


def gather_kernel(depths, mine, theirs, out_first, out_second):
    lats, rows, c1 = mine.shape
    core = position(lats)[4]
    places = bases(lats, depths)
    size = out_second.shape[0]
    total = size + out_first.shape[0]
    for h in range(2):
        for i in range(lats):
            at = (h * lats + i) * rows
            for out, base, end in ((out_second, 0, size), (out_first, size, total)):
                low, high = max(at, base), min(at + rows, end)
                if low < high:
                    here, there = (x[i ^ places[h], low - at:high - at] for x in (mine, theirs))
                    out[low - base:high - base] = jnp.where(core == h, here, there).astype(F32)


def vmem(count):
    return [pl.BlockSpec(memory_space=pltpu.VMEM)] * count


def params(mib):
    return pltpu.CompilerParams(vmem_limit_bytes=mib * 1024 * 1024)


def shape(dims, kind):
    return jax.ShapeDtypeStruct(dims, kind)


def body(inputs, pre_first, grad_out, w_first, w_second):
    rows, cols, c1 = pre_first.shape
    c0 = inputs.shape[2]
    half, pooled = cols // 2, rows // 2
    lats, lons = lax.axis_size("lat"), lax.axis_size("lon")
    depths = lons // 2
    band, place = lax.axis_index("lat"), lax.axis_index("lon")
    core = lax.rem(place, 2)
    even = lax.rem(band, 2) == 0

    edge = -(-(rows + pooled + 4) // 16) * 16
    row_a, row_b, col_a, col_b = pl.pallas_call(
        functools.partial(pack_kernel, lats),
        out_shape=(
            shape((cols + half, c1), BF16),
            shape((cols + half, c1), BF16),
            shape((edge, c1), BF16),
            shape((edge, c1), BF16),
        ),
        in_specs=vmem(2),
        out_specs=tuple(vmem(4)),
        scratch_shapes=[
            pltpu.VMEM((2, edge, c1), F32),
        ],
        compiler_params=params(50),
        cost_estimate=pl.CostEstimate(flops=1000, bytes_accessed=1 << 18, transcendentals=0),
    )(pre_first, grad_out)
    pairs = [(j, (j + lons // 2) % lons) for j in range(lons)]
    for i in range(1, lats - 1, 2):
        for j in range(lons):
            pairs += [(i * lons + j, (i + 1) * lons + j), ((i + 1) * lons + j, i * lons + j)]
    row_b = lax.ppermute(row_b, AREA, pairs)
    row_a = lax.ppermute(row_a, "lat", [(i, i ^ 1) for i in range(lats)])

    slope, act_t = pl.pallas_call(
        local_kernel,
        out_shape=(
            shape((rows, half, 2 * c1), F32),
            shape((2, 2 * c1, pooled * half), BF16),
        ),
        in_specs=vmem(1),
        out_specs=tuple(vmem(2)),
        scratch_shapes=[
            pltpu.VMEM((cols, c1), F32),
            pltpu.VMEM((2, pooled, half, 2 * c1), BF16),
        ],
        compiler_params=params(16),
        cost_estimate=pl.CostEstimate(flops=60 * rows * cols * c1, bytes_accessed=2 << 20,
                                      transcendentals=2 * rows * cols * c1),
    )(pre_first)

    fields = jnp.transpose(inputs, (0, 2, 1))
    row_a, row_b, slope, fields = lax.optimization_barrier((row_a, row_b, slope, fields))

    def corners(at):
        places = (at * (cols - 1), cols + at * (half - 1))
        above, below = (jnp.where(even, one, two) for one, two in ((row_b, row_a), (row_a, row_b)))
        return jnp.concatenate([part[p:p + 1] for p in places for part in (above, below)], 0)

    low, high = corners(0), corners(1)
    pad = jnp.zeros((edge - rows - pooled - 4, c1), BF16)
    col_a = jnp.concatenate([col_a[:rows + pooled], jnp.where(core == 0, high, low), pad], 0)
    col_b = jnp.concatenate([col_b[:rows + pooled], jnp.where(core == 0, low, high), pad], 0)
    col_b = lax.ppermute(col_b, "lon", [(i, (i + 2 * (i % 2) - 1) % lons) for i in range(lons)])
    col_a = lax.ppermute(col_a, "lon", [(i, i ^ 1) for i in range(lons)])

    fields_t, taps_first, taps_second = pl.pallas_call(
        layout_kernel,
        out_shape=(
            shape((2 * c0, rows * half), BF16),
            shape((6 * c0, 4 * c1), BF16),
            shape((3, 2 * c1, 4 * c1), BF16),
        ),
        in_specs=vmem(3),
        out_specs=tuple(vmem(3)),
        scratch_shapes=[pltpu.VMEM((rows, c0, 2 * cols), BF16)],
        compiler_params=params(16),
        cost_estimate=pl.CostEstimate(flops=4 * rows * cols * c0 * cols, bytes_accessed=3 << 20, transcendentals=0),
    )(fields, w_first, w_second)
    col_a, col_b, fields_t = lax.optimization_barrier((col_a, col_b, fields_t))

    block = -(-9 * (c1 + c0) // (32 * lats)) * 16
    held = lats * block
    span = half + EDGE
    spread, own, other = pl.pallas_call(
        functools.partial(middle_kernel, lats, depths),
        out_shape=(
            shape((rows + 3, half, 4 * c1), BF16),
            shape((held, c1), F32),
            shape((held, c1), F32),
        ),
        in_specs=vmem(9),
        out_specs=tuple(vmem(3)),
        scratch_shapes=[
            pltpu.VMEM((pooled + 2, span, c1), F32),
            pltpu.VMEM((pooled + 2, span, 4 * c1), BF16),
            pltpu.VMEM((3, pooled, span, 2 * c1), F32),
            pltpu.VMEM((4, span, 2 * c1), F32),
            pltpu.VMEM((cols, c1), F32),
            pltpu.VMEM((2, edge, c1), F32),
            pltpu.VMEM((2, edge, c1), F32),
            pltpu.VMEM((4, 2 * c1, 3 * c1), F32),
            pltpu.VMEM((2 * c1, 3 * c1), F32),
            pltpu.VMEM((2 * held, c1), F32),
        ],
        compiler_params=params(16),
        cost_estimate=pl.CostEstimate(flops=2 * rows * cols * c1 * 9 * (2 * c1 + c0), bytes_accessed=8 << 20,
                                      transcendentals=0),
    )(grad_out, row_a, row_b, col_a, col_b, slope, act_t, fields_t, taps_second)

    swap = [(i, i ^ 1) for i in range(lons)]
    crossed = lats == depths

    def exchange(value, far, outer):
        pairs = []
        for i in range(lats):
            for j in range(lons):
                over_lat = outer != (crossed and j % 2 == 1)
                target = (i ^ far, j) if over_lat else (i, j ^ (2 * far))
                pairs.append((i * lons + j, target[0] * lons + target[1]))
        return lax.ppermute(value, AREA, pairs)

    parts = (own + lax.ppermute(other, "lon", swap)).reshape(lats, block, c1)
    sent = [parts[far].astype(BF16) for far in range(1, lats)]
    *sent, spread = lax.optimization_barrier((*sent, spread))
    got = [exchange(value, far + 1, True) for far, value in enumerate(sent)]
    grad_inputs = pl.pallas_call(
        last_kernel,
        out_shape=shape((rows, c0, cols), BF16),
        in_specs=vmem(2),
        out_specs=vmem(1)[0],
        scratch_shapes=[
            pltpu.VMEM((2 * c0, rows * half), F32),
            pltpu.VMEM((pooled, c0, 2 * cols), BF16),
        ],
        compiler_params=params(12),
        cost_estimate=pl.CostEstimate(flops=2 * rows * cols * c1 * 9 * c0, bytes_accessed=3 << 20, transcendentals=0),
    )(spread, taps_first)
    *got, grad_inputs = lax.optimization_barrier((*got, grad_inputs))
    total = parts[0]
    for value in got:
        total = total + value.astype(F32)
    part = total.astype(BF16)
    terms = [part] + [exchange(part, far, False) for far in range(1, depths)]
    terms = [term.astype(F32) for term in terms]
    while len(terms) > 1:
        terms = [terms[k] + terms[k + 1] for k in range(0, len(terms), 2)]
    part = terms[0].astype(BF16)
    mine = jnp.stack([part] + [exchange(part, far, True) for far in range(1, lats)], 0)
    theirs = lax.ppermute(mine, "lon", swap)

    grad_w_first, grad_w_second = pl.pallas_call(
        functools.partial(gather_kernel, depths),
        out_shape=(shape((9 * c0, c1), F32), shape((9 * c1, c1), F32)),
        in_specs=vmem(2),
        out_specs=tuple(vmem(2)),
        compiler_params=params(8),
        cost_estimate=pl.CostEstimate(flops=1000, bytes_accessed=3 << 19, transcendentals=0),
    )(mine, theirs)
    return (jnp.transpose(grad_inputs, (0, 2, 1)), grad_w_first.reshape(w_first.shape),
            grad_w_second.reshape(w_second.shape))


def solution(mesh):
    in_specs = (P("lat", "lon", None), P("lat", "lon", None), P("lat", "lon", None), P(), P())
    out_specs = (P("lat", "lon", None), P(), P())
    return jax.shard_map(body, mesh=mesh, in_specs=in_specs, out_specs=out_specs, check_vma=False)
```

```python
import functools

import jax
import jax.numpy as jnp
from jax import lax
from jax.experimental import pallas as pl
from jax.experimental.pallas import tpu as pltpu
from jax.sharding import PartitionSpec as P

inv_root = 0.7071067811865476
density = 0.3989422804014327

F32 = jnp.float32
BF16 = jnp.bfloat16
EDGE = 16
AREA = ("lat", "lon")


def cdf_of(value):
    return 0.5 * (1.0 + lax.erf(value * inv_root))


def slope_of(value, cdf):
    return 0.25 * (cdf + value * jnp.exp(-0.5 * value * value) * density)


def dot(left, right):
    return jnp.dot(left, right, preferred_element_type=F32)


def dot_nt(left, right):
    return lax.dot_general(left, right, (((1,), (1,)), ((), ())), preferred_element_type=F32)


def position(lats):
    band, place = lax.axis_index("lat"), lax.axis_index("lon")
    return band, band == 0, band == lats - 1, lax.rem(band, 2) == 0, lax.rem(place, 2)


def pack_kernel(lats, pre, grad_out, row_a, row_b, col_a, col_b, held, hold):
    rows, cols, c1 = pre.shape
    pooled, half = grad_out.shape[:2]
    _, _, _, even, core = position(lats)
    for message, low in ((row_a, ~even), (row_b, even)):
        message[:cols] = pre[jnp.where(low, 0, rows - 1)]
        message[cols:] = grad_out[jnp.where(low, 0, pooled - 1)]
    hold[:, rows + pooled:] = jnp.zeros((2, hold.shape[1] - rows - pooled, c1), F32)
    for side, (p, g) in enumerate(((0, 0), (cols - 16, half - 16))):
        at = 15 * side
        for r in range(rows):
            hold[side, r:r + 1] = pre[r, p:p + 16].astype(F32)[at:at + 1]
        for i in range(pooled):
            hold[side, rows + i:rows + i + 1] = grad_out[i, g:g + 16].astype(F32)[at:at + 1]
    col_a[...] = hold[1 - core].astype(BF16)
    col_b[...] = hold[core].astype(BF16)
    held[...] = pre[...]


def one_at(where):
    return jnp.where(where, 1.0, 0.0).astype(BF16)


def local_kernel(pre, slope, act_t, line, act_s):
    rows, cols, c1 = pre.shape
    half = cols // 2

    def one_row(r, carry):
        line[...] = pre[r].astype(F32)
        for pc in range(2):
            value = line[pl.ds(pc, half, stride=2), :]
            cdf = cdf_of(value)
            act_s[r % 2, r // 2, :, pc * c1:(pc + 1) * c1] = (value * cdf).astype(BF16)
            slope[r, :, pc * c1:(pc + 1) * c1] = slope_of(value, cdf)
        return carry

    lax.fori_loop(0, rows, one_row, 0)
    for pr in range(2):
        act_t[pr] = act_s[pr].reshape(rows // 2 * half, 2 * c1).T


def layout_kernel(fields, w_first, w_second, fields_t, taps_first, taps_second, turned):
    rows, c0, cols = fields.shape
    c1 = w_first.shape[3]
    half = cols // 2
    col = lax.broadcasted_iota(jnp.int32, (cols, 2 * cols), 0)
    lane = lax.broadcasted_iota(jnp.int32, (cols, 2 * cols), 1)
    turn = lane // cols
    parity = (lane % cols) // half
    parity = parity + turn - 2 * parity * turn
    order = one_at(col == 2 * (lane % half) + parity)
    turned[...] = dot(fields[...].reshape(rows * c0, cols), order).astype(BF16).reshape(rows, c0, 2 * cols)
    low = lax.broadcasted_iota(jnp.int32, (c0, cols), 1) < half
    for q in range(rows // 2):
        fields_t[:c0, q * cols:(q + 1) * cols] = jnp.where(low, turned[2 * q, :, :cols], turned[2 * q + 1, :, cols:])
        fields_t[c0:, q * cols:(q + 1) * cols] = jnp.where(low, turned[2 * q, :, cols:], turned[2 * q + 1, :, :cols])
    taps_second[...] = jnp.zeros_like(taps_second)
    taps_first[...] = jnp.zeros_like(taps_first)
    for a in range(3):
        for pc, blocks in ((0, (2, 1, None, 0)), (1, (None, 2, 0, 1))):
            for k, b in enumerate(blocks):
                if b is not None:
                    taps_second[a, pc * c1:(pc + 1) * c1, k * c1:(k + 1) * c1] = w_second[a, b]
        for pc, blocks in ((0, (2, 1, 0, None)), (1, (None, 2, 1, 0))):
            for k, b in enumerate(blocks):
                if b is not None:
                    start = (2 * a + pc) * c0
                    taps_first[start:start + c0, k * c1:(k + 1) * c1] = w_first[a, b]


def middle_kernel(lats, grad_out, row_a, row_b, col_a, col_b, slope, act_t, fields_t, taps,
                  spread, own, other,
                  grid, wide, prods, ends, line, side, sides, sums, corner, keep):
    band, first, last, even, core = position(lats)
    top = jnp.where(even, row_b[...], row_a[...])
    bottom = jnp.where(even, row_a[...], row_b[...])
    rows, half, c2 = slope.shape
    c1 = c2 // 2
    pooled = rows // 2
    c0 = fields_t.shape[0] // 2
    cells = pooled * half

    grid[:, half:, :] = jnp.zeros((pooled + 2, EDGE, c1), F32)
    grid[1:pooled + 1, :half, :] = grad_out[...].astype(F32)
    grid[0, :half, :] = top[2 * half:, :].astype(F32)
    outside = jnp.where(last, 0.0, 1.0)
    grid[pooled + 1, :half, :] = bottom[2 * half:, :].astype(F32) * outside
    side[1 - core] = col_a[...].astype(F32)
    side[core] = col_b[...].astype(F32)
    for i in range(pooled + 2):
        at = rows + i - 1
        if i == 0:
            at = rows + pooled + 2
        if i == pooled + 1:
            at = rows + pooled + 3
        kept = outside if i == pooled + 1 else 1.0
        grid[i, half:half + 1, :] = side[1, at:at + 1, :] * kept
        grid[i, half + EDGE - 1:half + EDGE, :] = side[0, at:at + 1, :] * kept
    for i in range(pooled + 2):
        here = grid[i]
        wide[i, :, :c1] = pltpu.roll(here, 1, 0).astype(BF16)
        wide[i, :, c1:2 * c1] = here.astype(BF16)
        wide[i, :, 2 * c1:3 * c1] = pltpu.roll(here, half + EDGE - 1, 0).astype(BF16)
        wide[i, :, 3 * c1:] = here.astype(BF16)

    flat = wide[1:pooled + 1].reshape(pooled * (half + EDGE), 4 * c1)
    for a in range(3):
        prods[a] = dot_nt(flat, taps[a]).reshape(pooled, half + EDGE, c2)
    fold = jnp.where(first, taps[0], taps[2])
    ends[0] = dot_nt(wide[0], fold)
    ends[1] = dot_nt(wide[0], taps[1])
    ends[2] = dot_nt(wide[pooled + 1], taps[0])
    ends[3] = dot_nt(wide[pooled + 1], taps[1])

    for s in range(2):
        sides[s] = slope_of(side[s], cdf_of(side[s]))

    def place(r, total, incline, edge):
        inner = total[:half] * incline
        rim = total[half:]
        after = rim[:1, :c1] * sides[1, pl.ds(edge, 1), :]
        before = rim[EDGE - 1:, c1:] * sides[0, pl.ds(edge, 1), :]
        even, odd = inner[:, :c1], inner[:, c1:]
        at = lax.broadcasted_iota(jnp.int32, (half, c1), 0)
        spread[r, :, :c1] = jnp.where(at == 0, before, pltpu.roll(odd, 1, 0)).astype(BF16)
        spread[r, :, c1:2 * c1] = even.astype(BF16)
        spread[r, :, 2 * c1:3 * c1] = odd.astype(BF16)
        spread[r, :, 3 * c1:] = jnp.where(at == half - 1, after, pltpu.roll(even, half - 1, 0)).astype(BF16)

    def halo_slope(message):
        line[...] = message[:2 * half, :].astype(F32)
        both = [line[pl.ds(pc, half, stride=2), :] for pc in range(2)]
        return jnp.concatenate([slope_of(v, cdf_of(v)) for v in both], axis=1)

    place(0, ends[0] + ends[1] + prods[0, 0], halo_slope(top), rows + pooled)
    place(1, ends[0] + prods[1, 0] + prods[0, 0], slope[0], 0)

    def pair(i, carry):
        middle = prods[2, i] + prods[1, i]
        place(2 * i + 2, middle + prods[0, i + 1], slope[2 * i + 1], 2 * i + 1)
        place(2 * i + 3, prods[2, i] + prods[1, i + 1] + prods[0, i + 1], slope[2 * i + 2], 2 * i + 2)
        return carry

    lax.fori_loop(0, pooled - 1, pair, 0)
    final = prods[2, pooled - 1]
    place(rows, final + prods[1, pooled - 1] + ends[2], slope[rows - 1], rows - 1)
    place(rows + 1, (final + ends[3] + ends[2]) * outside, halo_slope(bottom), rows + pooled + 1)

    is_first = jnp.where(first, 1.0, 0.0).astype(BF16)
    not_first = jnp.where(first, 0.0, 1.0).astype(BF16)
    above = wide[0, :half, :3 * c1]
    wide[0, :half, :3 * c1] = above * not_first
    for n, (pr, start) in enumerate(((0, 0), (0, 1), (1, 1), (1, 2))):
        around = wide[start:start + pooled, :half, :3 * c1].reshape(cells, 3 * c1)
        sums[n] = dot(act_t[pr], around)
    corner[...] = dot(act_t[0, :, :half], above * is_first)

    unit = c0
    per_tap = c1 // unit
    count = 9 * per_tap + 9
    held = own.shape[0]
    block = held // lats

    def put(k, value):
        keep[k * unit:(k + 1) * unit, :] = value

    pieces = {0: ((0, 1), (1, 3)), 1: ((0, 1), (1, 2)), 2: ((0, 0), (1, 2))}
    for a in range(3):
        for b in range(3):
            total = None
            for pr, n in pieces[a]:
                for pc in range(2):
                    k = (pc + 1 - b) // 2 + 1
                    term = sums[n, pc * c1:(pc + 1) * c1, k * c1:(k + 1) * c1]
                    total = term if total is None else total + term
            if a == 0:
                for pc in range(2):
                    k = (pc + 1 - b) // 2 + 1
                    total = total + corner[pc * c1:(pc + 1) * c1, k * c1:(k + 1) * c1]
            total = total * 0.25
            for part in range(per_tap):
                put((3 * a + b) * per_tap + part, total[part * unit:(part + 1) * unit])

    head = spread[0]
    spread[0] = head * not_first
    spread[rows + 2] = head * is_first
    folded = dot(fields_t[:, :half], spread[rows + 2])
    for a in range(3):
        around = spread[2 - a:2 - a + rows].reshape(rows * half, 4 * c1)
        got = dot(fields_t[...], around)
        if a == 0:
            got = got + folded
        for b in range(3):
            even = got[:c0, (2 - b) * c1:(3 - b) * c1]
            odd = got[c0:, (3 - b) * c1:(4 - b) * c1]
            put(9 * per_tap + 3 * a + b, even + odd)
    if 2 * held > count * unit:
        keep[count * unit:] = jnp.zeros((2 * held - count * unit, c1), F32)
    for target, half_of in ((own, core), (other, 1 - core)):
        for far in range(lats):
            at = half_of * held + (band ^ far) * block
            target[far * block:(far + 1) * block] = keep[pl.ds(pl.multiple_of(at, block), block), :]


def last_kernel(spread, taps, out, total, turned):
    rows, c0, cols = out.shape
    half = cols // 2
    c2 = 2 * c0
    depth = spread.shape[2]
    result = dot_nt(taps[:c2], spread[2:rows + 2].reshape(rows * half, depth))
    for a in (1, 2):
        result = result + dot_nt(taps[a * c2:(a + 1) * c2],
                                 spread[2 - a:2 - a + rows].reshape(rows * half, depth))
    total[...] = result
    total[:, :half] = total[:, :half] + dot_nt(taps[:c2], spread[rows + 2])
    for q in range(rows // 2):
        pair = total[:, q * cols:(q + 1) * cols].astype(BF16)
        turned[q, :, :cols] = pair[:c0]
        turned[q, :, cols:] = pair[c0:]
    k = lax.broadcasted_iota(jnp.int32, (2 * cols, 2 * cols), 0)
    n = lax.broadcasted_iota(jnp.int32, (2 * cols, 2 * cols), 1)
    order = one_at(n == ((k % cols) // half) * cols + 2 * (k % half) + k // cols)
    found = dot(turned[...].reshape(rows // 2 * c0, 2 * cols), order).astype(BF16)
    for q in range(rows // 2):
        for rp in range(2):
            out[2 * q + rp] = found[q * c0:(q + 1) * c0, rp * cols:(rp + 1) * cols]


def gather_kernel(mine, theirs, out_first, out_second):
    lats, rows, c1 = mine.shape
    band, _, _, _, core = position(lats)
    size = out_second.shape[0]
    total = size + out_first.shape[0]
    for h in range(2):
        for i in range(lats):
            at = (h * lats + i) * rows
            for out, base, end in ((out_second, 0, size), (out_first, size, total)):
                low, high = max(at, base), min(at + rows, end)
                if low < high:
                    here, there = (x[i ^ band, low - at:high - at] for x in (mine, theirs))
                    out[low - base:high - base] = jnp.where(core == h, here, there).astype(F32)


def vmem(count):
    return [pl.BlockSpec(memory_space=pltpu.VMEM)] * count


def params(mib):
    return pltpu.CompilerParams(vmem_limit_bytes=mib * 1024 * 1024)


def shape(dims, kind):
    return jax.ShapeDtypeStruct(dims, kind)


def body(inputs, pre_first, grad_out, w_first, w_second):
    rows, cols, c1 = pre_first.shape
    c0 = inputs.shape[2]
    half, pooled = cols // 2, rows // 2
    lats, lons = lax.axis_size("lat"), lax.axis_size("lon")
    depths = lons // 2
    band, place = lax.axis_index("lat"), lax.axis_index("lon")
    core = lax.rem(place, 2)
    even = lax.rem(band, 2) == 0

    edge = -(-(rows + pooled + 4) // 16) * 16
    row_a, row_b, col_a, col_b, held_pre = pl.pallas_call(
        functools.partial(pack_kernel, lats),
        out_shape=(
            shape((cols + half, c1), BF16),
            shape((cols + half, c1), BF16),
            shape((edge, c1), BF16),
            shape((edge, c1), BF16),
            shape(pre_first.shape, BF16),
        ),
        in_specs=vmem(2),
        out_specs=tuple(vmem(5)),
        scratch_shapes=[
            pltpu.VMEM((2, edge, c1), F32),
        ],
        compiler_params=params(50),
        cost_estimate=pl.CostEstimate(flops=1000, bytes_accessed=1 << 18, transcendentals=0),
    )(pre_first, grad_out)
    pairs = [(j, (j + lons // 2) % lons) for j in range(lons)]
    for i in range(1, lats - 1, 2):
        for j in range(lons):
            pairs += [(i * lons + j, (i + 1) * lons + j), ((i + 1) * lons + j, i * lons + j)]
    every = [(i * lons + j, (i ^ 1) * lons + j) for i in range(lats) for j in range(lons)]
    row_b = lax.ppermute(row_b, AREA, pairs)
    row_a = lax.ppermute(row_a, AREA, every)

    slope, act_t = pl.pallas_call(
        local_kernel,
        out_shape=(
            shape((rows, half, 2 * c1), F32),
            shape((2, 2 * c1, pooled * half), BF16),
        ),
        in_specs=vmem(1),
        out_specs=tuple(vmem(2)),
        scratch_shapes=[
            pltpu.VMEM((cols, c1), F32),
            pltpu.VMEM((2, pooled, half, 2 * c1), BF16),
        ],
        compiler_params=params(16),
        cost_estimate=pl.CostEstimate(flops=60 * rows * cols * c1, bytes_accessed=2 << 20,
                                      transcendentals=2 * rows * cols * c1),
    )(held_pre)

    fields = jnp.transpose(inputs, (0, 2, 1))
    row_b, row_a, slope, fields = lax.optimization_barrier((row_b, row_a, slope, fields))

    def corners(at):
        places = (at * (cols - 1), cols + at * (half - 1))
        above, below = (jnp.where(even, one, two) for one, two in ((row_b, row_a), (row_a, row_b)))
        return jnp.concatenate([part[p:p + 1] for p in places for part in (above, below)], 0)

    low, high = corners(0), corners(1)
    pad = jnp.zeros((edge - rows - pooled - 4, c1), BF16)
    col_a = jnp.concatenate([col_a[:rows + pooled], jnp.where(core == 0, high, low), pad], 0)
    col_b = jnp.concatenate([col_b[:rows + pooled], jnp.where(core == 0, low, high), pad], 0)
    col_b = lax.ppermute(col_b, "lon", [(i, (i + 2 * (i % 2) - 1) % lons) for i in range(lons)])
    col_a = lax.ppermute(col_a, "lon", [(i, i ^ 1) for i in range(lons)])

    fields_t, taps_first, taps_second = pl.pallas_call(
        layout_kernel,
        out_shape=(
            shape((2 * c0, rows * half), BF16),
            shape((6 * c0, 4 * c1), BF16),
            shape((3, 2 * c1, 4 * c1), BF16),
        ),
        in_specs=vmem(3),
        out_specs=tuple(vmem(3)),
        scratch_shapes=[pltpu.VMEM((rows, c0, 2 * cols), BF16)],
        compiler_params=params(16),
        cost_estimate=pl.CostEstimate(flops=4 * rows * cols * c0 * cols, bytes_accessed=3 << 20, transcendentals=0),
    )(fields, w_first, w_second)
    col_a, col_b, fields_t = lax.optimization_barrier((col_a, col_b, fields_t))

    block = -(-9 * (c1 + c0) // (32 * lats)) * 16
    held = lats * block
    span = half + EDGE
    spread, own, other = pl.pallas_call(
        functools.partial(middle_kernel, lats),
        out_shape=(
            shape((rows + 3, half, 4 * c1), BF16),
            shape((held, c1), F32),
            shape((held, c1), F32),
        ),
        in_specs=vmem(9),
        out_specs=tuple(vmem(3)),
        scratch_shapes=[
            pltpu.VMEM((pooled + 2, span, c1), F32),
            pltpu.VMEM((pooled + 2, span, 4 * c1), BF16),
            pltpu.VMEM((3, pooled, span, 2 * c1), F32),
            pltpu.VMEM((4, span, 2 * c1), F32),
            pltpu.VMEM((cols, c1), F32),
            pltpu.VMEM((2, edge, c1), F32),
            pltpu.VMEM((2, edge, c1), F32),
            pltpu.VMEM((4, 2 * c1, 3 * c1), F32),
            pltpu.VMEM((2 * c1, 3 * c1), F32),
            pltpu.VMEM((2 * held, c1), F32),
        ],
        compiler_params=params(16),
        cost_estimate=pl.CostEstimate(flops=2 * rows * cols * c1 * 9 * (2 * c1 + c0), bytes_accessed=8 << 20,
                                      transcendentals=0),
    )(grad_out, row_a, row_b, col_a, col_b, slope, act_t, fields_t, taps_second)

    swap = [(i, i ^ 1) for i in range(lons)]

    def along_lat(far, value):
        return lax.ppermute(value, "lat", [(i, i ^ far) for i in range(lats)])

    parts = (own + lax.ppermute(other, "lon", swap)).reshape(lats, block, c1)
    sent = [parts[far].astype(BF16) for far in range(1, lats)]
    *sent, spread = lax.optimization_barrier((*sent, spread))
    got = [along_lat(far + 1, value) for far, value in enumerate(sent)]
    grad_inputs = pl.pallas_call(
        last_kernel,
        out_shape=shape((rows, c0, cols), BF16),
        in_specs=vmem(2),
        out_specs=vmem(1)[0],
        scratch_shapes=[
            pltpu.VMEM((2 * c0, rows * half), F32),
            pltpu.VMEM((pooled, c0, 2 * cols), BF16),
        ],
        compiler_params=params(12),
        cost_estimate=pl.CostEstimate(flops=2 * rows * cols * c1 * 9 * c0, bytes_accessed=3 << 20, transcendentals=0),
    )(spread, taps_first)
    *got, grad_inputs = lax.optimization_barrier((*got, grad_inputs))
    total = parts[0]
    for value in got:
        total = total + value.astype(F32)
    part = total.astype(BF16)
    terms = [part] + [lax.ppermute(part, "lon", [(i, i ^ (2 * k)) for i in range(lons)]) for k in range(1, depths)]
    terms = [term.astype(F32) for term in terms]
    while len(terms) > 1:
        terms = [terms[k] + terms[k + 1] for k in range(0, len(terms), 2)]
    part = terms[0].astype(BF16)
    mine = jnp.stack([part] + [along_lat(far, part) for far in range(1, lats)], 0)
    theirs = lax.ppermute(mine, "lon", swap)

    grad_w_first, grad_w_second = pl.pallas_call(
        gather_kernel,
        out_shape=(shape((9 * c0, c1), F32), shape((9 * c1, c1), F32)),
        in_specs=vmem(2),
        out_specs=tuple(vmem(2)),
        compiler_params=params(8),
        cost_estimate=pl.CostEstimate(flops=1000, bytes_accessed=3 << 19, transcendentals=0),
    )(mine, theirs)
    return (jnp.transpose(grad_inputs, (0, 2, 1)), grad_w_first.reshape(w_first.shape),
            grad_w_second.reshape(w_second.shape))


def solution(mesh):
    in_specs = (P("lat", "lon", None), P("lat", "lon", None), P("lat", "lon", None), P(), P())
    out_specs = (P("lat", "lon", None), P(), P())
    return jax.shard_map(body, mesh=mesh, in_specs=in_specs, out_specs=out_specs, check_vma=False)
```

```python
import functools

import jax
import jax.numpy as jnp
from jax import lax
from jax.experimental import pallas as pl
from jax.experimental.pallas import tpu as pltpu
from jax.sharding import PartitionSpec as P

inv_root = 0.7071067811865476
density = 0.3989422804014327

F32 = jnp.float32
BF16 = jnp.bfloat16
EDGE = 16
AREA = ("lat", "lon")


def cdf_of(value):
    return 0.5 * (1.0 + lax.erf(value * inv_root))


def slope_of(value, cdf):
    return 0.25 * (cdf + value * jnp.exp(-0.5 * value * value) * density)


def dot(left, right):
    return jnp.dot(left, right, preferred_element_type=F32)


def dot_nt(left, right):
    return lax.dot_general(left, right, (((1,), (1,)), ((), ())), preferred_element_type=F32)


def position(lats):
    band, place = lax.axis_index("lat"), lax.axis_index("lon")
    return band, band == 0, band == lats - 1, lax.rem(band, 2) == 0, lax.rem(place, 2)


def pack_kernel(lats, pre, grad_out, row_a, row_b, col_a, col_b, held, hold):
    rows, cols, c1 = pre.shape
    pooled, half = grad_out.shape[:2]
    _, _, _, even, core = position(lats)
    for message, low in ((row_a, ~even), (row_b, even)):
        message[:cols] = pre[jnp.where(low, 0, rows - 1)]
        message[cols:] = grad_out[jnp.where(low, 0, pooled - 1)]
    hold[:, rows + pooled:] = jnp.zeros((2, hold.shape[1] - rows - pooled, c1), F32)
    for side, (p, g) in enumerate(((0, 0), (cols - 16, half - 16))):
        at = 15 * side
        for r in range(rows):
            hold[side, r:r + 1] = pre[r, p:p + 16].astype(F32)[at:at + 1]
        for i in range(pooled):
            hold[side, rows + i:rows + i + 1] = grad_out[i, g:g + 16].astype(F32)[at:at + 1]
    col_a[...] = hold[1 - core].astype(BF16)
    col_b[...] = hold[core].astype(BF16)
    held[...] = pre[...]


def one_at(where):
    return jnp.where(where, 1.0, 0.0).astype(BF16)


def local_kernel(pre, slope, act_t, line, act_s):
    rows, cols, c1 = pre.shape
    half = cols // 2

    def one_row(r, carry):
        line[...] = pre[r].astype(F32)
        for pc in range(2):
            value = line[pl.ds(pc, half, stride=2), :]
            cdf = cdf_of(value)
            act_s[r % 2, r // 2, :, pc * c1:(pc + 1) * c1] = (value * cdf).astype(BF16)
            slope[r, :, pc * c1:(pc + 1) * c1] = slope_of(value, cdf)
        return carry

    lax.fori_loop(0, rows, one_row, 0)
    for pr in range(2):
        act_t[pr] = act_s[pr].reshape(rows // 2 * half, 2 * c1).T


def layout_kernel(fields, w_first, w_second, fields_t, taps_first, taps_second, turned):
    rows, c0, cols = fields.shape
    c1 = w_first.shape[3]
    half = cols // 2
    col = lax.broadcasted_iota(jnp.int32, (cols, 2 * cols), 0)
    lane = lax.broadcasted_iota(jnp.int32, (cols, 2 * cols), 1)
    turn = lane // cols
    parity = (lane % cols) // half
    parity = parity + turn - 2 * parity * turn
    order = one_at(col == 2 * (lane % half) + parity)
    turned[...] = dot(fields[...].reshape(rows * c0, cols), order).astype(BF16).reshape(rows, c0, 2 * cols)
    low = lax.broadcasted_iota(jnp.int32, (c0, cols), 1) < half
    for q in range(rows // 2):
        fields_t[:c0, q * cols:(q + 1) * cols] = jnp.where(low, turned[2 * q, :, :cols], turned[2 * q + 1, :, cols:])
        fields_t[c0:, q * cols:(q + 1) * cols] = jnp.where(low, turned[2 * q, :, cols:], turned[2 * q + 1, :, :cols])
    taps_second[...] = jnp.zeros_like(taps_second)
    taps_first[...] = jnp.zeros_like(taps_first)
    for a in range(3):
        for pc, blocks in ((0, (2, 1, None, 0)), (1, (None, 2, 0, 1))):
            for k, b in enumerate(blocks):
                if b is not None:
                    taps_second[a, pc * c1:(pc + 1) * c1, k * c1:(k + 1) * c1] = w_second[a, b]
        for pc, blocks in ((0, (2, 1, 0, None)), (1, (None, 2, 1, 0))):
            for k, b in enumerate(blocks):
                if b is not None:
                    start = (2 * a + pc) * c0
                    taps_first[start:start + c0, k * c1:(k + 1) * c1] = w_first[a, b]


def middle_kernel(lats, grad_out, row_a, row_b, col_a, col_b, slope, act_t, fields_t, taps,
                  spread, own, other,
                  grid, wide, prods, ends, line, side, sides, sums, corner, keep):
    band, first, last, even, core = position(lats)
    top = jnp.where(even, row_b[...], row_a[...])
    bottom = jnp.where(even, row_a[...], row_b[...])
    rows, half, c2 = slope.shape
    c1 = c2 // 2
    pooled = rows // 2
    c0 = fields_t.shape[0] // 2
    cells = pooled * half

    grid[:, half:, :] = jnp.zeros((pooled + 2, EDGE, c1), F32)
    grid[1:pooled + 1, :half, :] = grad_out[...].astype(F32)
    grid[0, :half, :] = top[2 * half:, :].astype(F32)
    outside = jnp.where(last, 0.0, 1.0)
    grid[pooled + 1, :half, :] = bottom[2 * half:, :].astype(F32) * outside
    side[1 - core] = col_a[...].astype(F32)
    side[core] = col_b[...].astype(F32)
    for i in range(pooled + 2):
        at = rows + i - 1
        if i == 0:
            at = rows + pooled + 2
        if i == pooled + 1:
            at = rows + pooled + 3
        kept = outside if i == pooled + 1 else 1.0
        grid[i, half:half + 1, :] = side[1, at:at + 1, :] * kept
        grid[i, half + EDGE - 1:half + EDGE, :] = side[0, at:at + 1, :] * kept
    for i in range(pooled + 2):
        here = grid[i]
        wide[i, :, :c1] = pltpu.roll(here, 1, 0).astype(BF16)
        wide[i, :, c1:2 * c1] = here.astype(BF16)
        wide[i, :, 2 * c1:3 * c1] = pltpu.roll(here, half + EDGE - 1, 0).astype(BF16)
        wide[i, :, 3 * c1:] = here.astype(BF16)

    flat = wide[1:pooled + 1].reshape(pooled * (half + EDGE), 4 * c1)
    for a in range(3):
        prods[a] = dot_nt(flat, taps[a]).reshape(pooled, half + EDGE, c2)
    fold = jnp.where(first, taps[0], taps[2])
    ends[0] = dot_nt(wide[0], fold)
    ends[1] = dot_nt(wide[0], taps[1])
    ends[2] = dot_nt(wide[pooled + 1], taps[0])
    ends[3] = dot_nt(wide[pooled + 1], taps[1])

    for s in range(2):
        sides[s] = slope_of(side[s], cdf_of(side[s]))

    def place(r, total, incline, edge):
        inner = total[:half] * incline
        rim = total[half:]
        after = rim[:1, :c1] * sides[1, pl.ds(edge, 1), :]
        before = rim[EDGE - 1:, c1:] * sides[0, pl.ds(edge, 1), :]
        even, odd = inner[:, :c1], inner[:, c1:]
        at = lax.broadcasted_iota(jnp.int32, (half, c1), 0)
        spread[r, :, :c1] = jnp.where(at == 0, before, pltpu.roll(odd, 1, 0)).astype(BF16)
        spread[r, :, c1:2 * c1] = even.astype(BF16)
        spread[r, :, 2 * c1:3 * c1] = odd.astype(BF16)
        spread[r, :, 3 * c1:] = jnp.where(at == half - 1, after, pltpu.roll(even, half - 1, 0)).astype(BF16)

    def halo_slope(message):
        line[...] = message[:2 * half, :].astype(F32)
        both = [line[pl.ds(pc, half, stride=2), :] for pc in range(2)]
        return jnp.concatenate([slope_of(v, cdf_of(v)) for v in both], axis=1)

    place(0, ends[0] + ends[1] + prods[0, 0], halo_slope(top), rows + pooled)
    place(1, ends[0] + prods[1, 0] + prods[0, 0], slope[0], 0)

    def pair(i, carry):
        middle = prods[2, i] + prods[1, i]
        place(2 * i + 2, middle + prods[0, i + 1], slope[2 * i + 1], 2 * i + 1)
        place(2 * i + 3, prods[2, i] + prods[1, i + 1] + prods[0, i + 1], slope[2 * i + 2], 2 * i + 2)
        return carry

    lax.fori_loop(0, pooled - 1, pair, 0)
    final = prods[2, pooled - 1]
    place(rows, final + prods[1, pooled - 1] + ends[2], slope[rows - 1], rows - 1)
    place(rows + 1, (final + ends[3] + ends[2]) * outside, halo_slope(bottom), rows + pooled + 1)

    is_first = jnp.where(first, 1.0, 0.0).astype(BF16)
    not_first = jnp.where(first, 0.0, 1.0).astype(BF16)
    above = wide[0, :half, :3 * c1]
    wide[0, :half, :3 * c1] = above * not_first
    for n, (pr, start) in enumerate(((0, 0), (0, 1), (1, 1), (1, 2))):
        around = wide[start:start + pooled, :half, :3 * c1].reshape(cells, 3 * c1)
        sums[n] = dot(act_t[pr], around)
    corner[...] = dot(act_t[0, :, :half], above * is_first)

    unit = c0
    per_tap = c1 // unit
    count = 9 * per_tap + 9
    held = own.shape[0]
    block = held // lats

    def put(k, value):
        keep[k * unit:(k + 1) * unit, :] = value

    pieces = {0: ((0, 1), (1, 3)), 1: ((0, 1), (1, 2)), 2: ((0, 0), (1, 2))}
    for a in range(3):
        for b in range(3):
            total = None
            for pr, n in pieces[a]:
                for pc in range(2):
                    k = (pc + 1 - b) // 2 + 1
                    term = sums[n, pc * c1:(pc + 1) * c1, k * c1:(k + 1) * c1]
                    total = term if total is None else total + term
            if a == 0:
                for pc in range(2):
                    k = (pc + 1 - b) // 2 + 1
                    total = total + corner[pc * c1:(pc + 1) * c1, k * c1:(k + 1) * c1]
            total = total * 0.25
            for part in range(per_tap):
                put((3 * a + b) * per_tap + part, total[part * unit:(part + 1) * unit])

    head = spread[0]
    spread[0] = head * not_first
    spread[rows + 2] = head * is_first
    folded = dot(fields_t[:, :half], spread[rows + 2])
    for a in range(3):
        around = spread[2 - a:2 - a + rows].reshape(rows * half, 4 * c1)
        got = dot(fields_t[...], around)
        if a == 0:
            got = got + folded
        for b in range(3):
            even = got[:c0, (2 - b) * c1:(3 - b) * c1]
            odd = got[c0:, (3 - b) * c1:(4 - b) * c1]
            put(9 * per_tap + 3 * a + b, even + odd)
    if 2 * held > count * unit:
        keep[count * unit:] = jnp.zeros((2 * held - count * unit, c1), F32)
    for target, half_of in ((own, core), (other, 1 - core)):
        for far in range(lats):
            at = half_of * held + (band ^ far) * block
            target[far * block:(far + 1) * block] = keep[pl.ds(pl.multiple_of(at, block), block), :]


def last_kernel(spread, taps, out, total, turned):
    rows, c0, cols = out.shape
    half = cols // 2
    c2 = 2 * c0
    depth = spread.shape[2]
    result = dot_nt(taps[:c2], spread[2:rows + 2].reshape(rows * half, depth))
    for a in (1, 2):
        result = result + dot_nt(taps[a * c2:(a + 1) * c2],
                                 spread[2 - a:2 - a + rows].reshape(rows * half, depth))
    total[...] = result
    total[:, :half] = total[:, :half] + dot_nt(taps[:c2], spread[rows + 2])
    for q in range(rows // 2):
        pair = total[:, q * cols:(q + 1) * cols].astype(BF16)
        turned[q, :, :cols] = pair[:c0]
        turned[q, :, cols:] = pair[c0:]
    k = lax.broadcasted_iota(jnp.int32, (2 * cols, 2 * cols), 0)
    n = lax.broadcasted_iota(jnp.int32, (2 * cols, 2 * cols), 1)
    order = one_at(n == ((k % cols) // half) * cols + 2 * (k % half) + k // cols)
    found = dot(turned[...].reshape(rows // 2 * c0, 2 * cols), order).astype(BF16)
    for q in range(rows // 2):
        for rp in range(2):
            out[2 * q + rp] = found[q * c0:(q + 1) * c0, rp * cols:(rp + 1) * cols]


def gather_kernel(mine, theirs, out_first, out_second):
    lats, rows, c1 = mine.shape
    band, _, _, _, core = position(lats)
    size = out_second.shape[0]
    total = size + out_first.shape[0]
    for h in range(2):
        for i in range(lats):
            at = (h * lats + i) * rows
            for out, base, end in ((out_second, 0, size), (out_first, size, total)):
                low, high = max(at, base), min(at + rows, end)
                if low < high:
                    here, there = (x[i ^ band, low - at:high - at] for x in (mine, theirs))
                    out[low - base:high - base] = jnp.where(core == h, here, there).astype(F32)


def vmem(count):
    return [pl.BlockSpec(memory_space=pltpu.VMEM)] * count


def params(mib):
    return pltpu.CompilerParams(vmem_limit_bytes=mib * 1024 * 1024)


def shape(dims, kind):
    return jax.ShapeDtypeStruct(dims, kind)


def body(inputs, pre_first, grad_out, w_first, w_second):
    rows, cols, c1 = pre_first.shape
    c0 = inputs.shape[2]
    half, pooled = cols // 2, rows // 2
    lats, lons = lax.axis_size("lat"), lax.axis_size("lon")
    depths = lons // 2
    band, place = lax.axis_index("lat"), lax.axis_index("lon")
    core = lax.rem(place, 2)
    even = lax.rem(band, 2) == 0

    edge = -(-(rows + pooled + 4) // 16) * 16
    row_a, row_b, col_a, col_b, held_pre = pl.pallas_call(
        functools.partial(pack_kernel, lats),
        out_shape=(
            shape((cols + half, c1), BF16),
            shape((cols + half, c1), BF16),
            shape((edge, c1), BF16),
            shape((edge, c1), BF16),
            shape(pre_first.shape, BF16),
        ),
        in_specs=vmem(2),
        out_specs=tuple(vmem(5)),
        scratch_shapes=[
            pltpu.VMEM((2, edge, c1), F32),
        ],
        compiler_params=params(50),
        cost_estimate=pl.CostEstimate(flops=1000, bytes_accessed=1 << 18, transcendentals=0),
    )(pre_first, grad_out)
    pairs = [(i * lons + j, i * lons + (j + lons // 2) % lons) for i in (0, lats - 1) for j in range(lons)]
    for i in range(1, lats - 1, 2):
        for j in range(lons):
            pairs += [(i * lons + j, (i + 1) * lons + j), ((i + 1) * lons + j, i * lons + j)]
    every = [(i * lons + j, (i ^ 1) * lons + j) for i in range(lats) for j in range(lons)]
    row_b = lax.ppermute(row_b, AREA, pairs)
    row_a = lax.ppermute(row_a, AREA, every)

    slope, act_t = pl.pallas_call(
        local_kernel,
        out_shape=(
            shape((rows, half, 2 * c1), F32),
            shape((2, 2 * c1, pooled * half), BF16),
        ),
        in_specs=vmem(1),
        out_specs=tuple(vmem(2)),
        scratch_shapes=[
            pltpu.VMEM((cols, c1), F32),
            pltpu.VMEM((2, pooled, half, 2 * c1), BF16),
        ],
        compiler_params=params(16),
        cost_estimate=pl.CostEstimate(flops=60 * rows * cols * c1, bytes_accessed=2 << 20,
                                      transcendentals=2 * rows * cols * c1),
    )(held_pre)

    fields = jnp.transpose(inputs, (0, 2, 1))
    row_b, row_a, slope, fields = lax.optimization_barrier((row_b, row_a, slope, fields))

    def corners(at):
        places = (at * (cols - 1), cols + at * (half - 1))
        above, below = (jnp.where(even, one, two) for one, two in ((row_b, row_a), (row_a, row_b)))
        return jnp.concatenate([part[p:p + 1] for p in places for part in (above, below)], 0)

    low, high = corners(0), corners(1)
    pad = jnp.zeros((edge - rows - pooled - 4, c1), BF16)
    col_a = jnp.concatenate([col_a[:rows + pooled], jnp.where(core == 0, high, low), pad], 0)
    col_b = jnp.concatenate([col_b[:rows + pooled], jnp.where(core == 0, low, high), pad], 0)
    col_b = lax.ppermute(col_b, "lon", [(i, (i + 2 * (i % 2) - 1) % lons) for i in range(lons)])
    col_a = lax.ppermute(col_a, "lon", [(i, i ^ 1) for i in range(lons)])

    fields_t, taps_first, taps_second = pl.pallas_call(
        layout_kernel,
        out_shape=(
            shape((2 * c0, rows * half), BF16),
            shape((6 * c0, 4 * c1), BF16),
            shape((3, 2 * c1, 4 * c1), BF16),
        ),
        in_specs=vmem(3),
        out_specs=tuple(vmem(3)),
        scratch_shapes=[pltpu.VMEM((rows, c0, 2 * cols), BF16)],
        compiler_params=params(16),
        cost_estimate=pl.CostEstimate(flops=4 * rows * cols * c0 * cols, bytes_accessed=3 << 20, transcendentals=0),
    )(fields, w_first, w_second)
    col_a, col_b, fields_t = lax.optimization_barrier((col_a, col_b, fields_t))

    block = -(-9 * (c1 + c0) // (32 * lats)) * 16
    held = lats * block
    span = half + EDGE
    spread, own, other = pl.pallas_call(
        functools.partial(middle_kernel, lats),
        out_shape=(
            shape((rows + 3, half, 4 * c1), BF16),
            shape((held, c1), F32),
            shape((held, c1), F32),
        ),
        in_specs=vmem(9),
        out_specs=tuple(vmem(3)),
        scratch_shapes=[
            pltpu.VMEM((pooled + 2, span, c1), F32),
            pltpu.VMEM((pooled + 2, span, 4 * c1), BF16),
            pltpu.VMEM((3, pooled, span, 2 * c1), F32),
            pltpu.VMEM((4, span, 2 * c1), F32),
            pltpu.VMEM((cols, c1), F32),
            pltpu.VMEM((2, edge, c1), F32),
            pltpu.VMEM((2, edge, c1), F32),
            pltpu.VMEM((4, 2 * c1, 3 * c1), F32),
            pltpu.VMEM((2 * c1, 3 * c1), F32),
            pltpu.VMEM((2 * held, c1), F32),
        ],
        compiler_params=params(16),
        cost_estimate=pl.CostEstimate(flops=2 * rows * cols * c1 * 9 * (2 * c1 + c0), bytes_accessed=8 << 20,
                                      transcendentals=0),
    )(grad_out, row_a, row_b, col_a, col_b, slope, act_t, fields_t, taps_second)

    swap = [(i, i ^ 1) for i in range(lons)]

    def along_lat(far, value):
        return lax.ppermute(value, "lat", [(i, i ^ far) for i in range(lats)])

    parts = (own + lax.ppermute(other, "lon", swap)).reshape(lats, block, c1)
    sent = [parts[far].astype(BF16) for far in range(1, lats)]
    *sent, spread = lax.optimization_barrier((*sent, spread))
    got = [along_lat(far + 1, value) for far, value in enumerate(sent)]
    grad_inputs = pl.pallas_call(
        last_kernel,
        out_shape=shape((rows, c0, cols), BF16),
        in_specs=vmem(2),
        out_specs=vmem(1)[0],
        scratch_shapes=[
            pltpu.VMEM((2 * c0, rows * half), F32),
            pltpu.VMEM((pooled, c0, 2 * cols), BF16),
        ],
        compiler_params=params(12),
        cost_estimate=pl.CostEstimate(flops=2 * rows * cols * c1 * 9 * c0, bytes_accessed=3 << 20, transcendentals=0),
    )(spread, taps_first)
    *got, grad_inputs = lax.optimization_barrier((*got, grad_inputs))
    total = parts[0]
    for value in got:
        total = total + value.astype(F32)
    part = total.astype(BF16)
    terms = [part] + [lax.ppermute(part, "lon", [(i, i ^ (2 * k)) for i in range(lons)]) for k in range(1, depths)]
    terms = [term.astype(F32) for term in terms]
    while len(terms) > 1:
        terms = [terms[k] + terms[k + 1] for k in range(0, len(terms), 2)]
    part = terms[0].astype(BF16)
    mine = jnp.stack([part] + [along_lat(far, part) for far in range(1, lats)], 0)
    theirs = lax.ppermute(mine, "lon", swap)

    grad_w_first, grad_w_second = pl.pallas_call(
        gather_kernel,
        out_shape=(shape((9 * c0, c1), F32), shape((9 * c1, c1), F32)),
        in_specs=vmem(2),
        out_specs=tuple(vmem(2)),
        compiler_params=params(8),
        cost_estimate=pl.CostEstimate(flops=1000, bytes_accessed=3 << 19, transcendentals=0),
    )(mine, theirs)
    return (jnp.transpose(grad_inputs, (0, 2, 1)), grad_w_first.reshape(w_first.shape),
            grad_w_second.reshape(w_second.shape))


def solution(mesh):
    in_specs = (P("lat", "lon", None), P("lat", "lon", None), P("lat", "lon", None), P(), P())
    out_specs = (P("lat", "lon", None), P(), P())
    return jax.shard_map(body, mesh=mesh, in_specs=in_specs, out_specs=out_specs, check_vma=False)
```

```python
import functools

import jax
import jax.numpy as jnp
from jax import lax
from jax.experimental import pallas as pl
from jax.experimental.pallas import tpu as pltpu
from jax.sharding import PartitionSpec as P

inv_root = 0.7071067811865476
density = 0.3989422804014327

F32 = jnp.float32
BF16 = jnp.bfloat16
EDGE = 16
AREA = ("lat", "lon")


def cdf_of(value):
    return 0.5 * (1.0 + lax.erf(value * inv_root))


def slope_of(value, cdf):
    return 0.25 * (cdf + value * jnp.exp(-0.5 * value * value) * density)


def dot(left, right):
    return jnp.dot(left, right, preferred_element_type=F32)


def dot_nt(left, right):
    return lax.dot_general(left, right, (((1,), (1,)), ((), ())), preferred_element_type=F32)


def position(lats):
    band, place = lax.axis_index("lat"), lax.axis_index("lon")
    return band, band == 0, band == lats - 1, lax.rem(band, 2) == 0, lax.rem(place, 2)


def pack_kernel(lats, pre, grad_out, row_a, row_b, col_a, col_b, held, hold):
    rows, cols, c1 = pre.shape
    pooled, half = grad_out.shape[:2]
    _, _, _, even, core = position(lats)
    for message, low in ((row_a, ~even), (row_b, even)):
        message[:cols] = pre[jnp.where(low, 0, rows - 1)]
        message[cols:] = grad_out[jnp.where(low, 0, pooled - 1)]
    hold[:, rows + pooled:] = jnp.zeros((2, hold.shape[1] - rows - pooled, c1), F32)
    for side, (p, g) in enumerate(((0, 0), (cols - 16, half - 16))):
        at = 15 * side
        for r in range(rows):
            hold[side, r:r + 1] = pre[r, p:p + 16].astype(F32)[at:at + 1]
        for i in range(pooled):
            hold[side, rows + i:rows + i + 1] = grad_out[i, g:g + 16].astype(F32)[at:at + 1]
    col_a[...] = hold[1 - core].astype(BF16)
    col_b[...] = hold[core].astype(BF16)
    held[...] = pre[...]


def one_at(where):
    return jnp.where(where, 1.0, 0.0).astype(BF16)


def local_kernel(pre, slope, act_t, line, act_s):
    rows, cols, c1 = pre.shape
    half = cols // 2

    def one_row(r, carry):
        line[...] = pre[r].astype(F32)
        for pc in range(2):
            value = line[pl.ds(pc, half, stride=2), :]
            cdf = cdf_of(value)
            act_s[r % 2, r // 2, :, pc * c1:(pc + 1) * c1] = (value * cdf).astype(BF16)
            slope[r, :, pc * c1:(pc + 1) * c1] = slope_of(value, cdf)
        return carry

    lax.fori_loop(0, rows, one_row, 0)
    for pr in range(2):
        act_t[pr] = act_s[pr].reshape(rows // 2 * half, 2 * c1).T


def layout_kernel(fields, w_first, w_second, fields_t, taps_first, taps_second, turned):
    rows, c0, cols = fields.shape
    c1 = w_first.shape[3]
    half = cols // 2
    col = lax.broadcasted_iota(jnp.int32, (cols, 2 * cols), 0)
    lane = lax.broadcasted_iota(jnp.int32, (cols, 2 * cols), 1)
    turn = lane // cols
    parity = (lane % cols) // half
    parity = parity + turn - 2 * parity * turn
    order = one_at(col == 2 * (lane % half) + parity)
    turned[...] = dot(fields[...].reshape(rows * c0, cols), order).astype(BF16).reshape(rows, c0, 2 * cols)
    low = lax.broadcasted_iota(jnp.int32, (c0, cols), 1) < half
    for q in range(rows // 2):
        fields_t[:c0, q * cols:(q + 1) * cols] = jnp.where(low, turned[2 * q, :, :cols], turned[2 * q + 1, :, cols:])
        fields_t[c0:, q * cols:(q + 1) * cols] = jnp.where(low, turned[2 * q, :, cols:], turned[2 * q + 1, :, :cols])
    taps_second[...] = jnp.zeros_like(taps_second)
    taps_first[...] = jnp.zeros_like(taps_first)
    for a in range(3):
        for pc, blocks in ((0, (2, 1, None, 0)), (1, (None, 2, 0, 1))):
            for k, b in enumerate(blocks):
                if b is not None:
                    taps_second[a, pc * c1:(pc + 1) * c1, k * c1:(k + 1) * c1] = w_second[a, b]
        for pc, blocks in ((0, (2, 1, 0, None)), (1, (None, 2, 1, 0))):
            for k, b in enumerate(blocks):
                if b is not None:
                    start = (2 * a + pc) * c0
                    taps_first[start:start + c0, k * c1:(k + 1) * c1] = w_first[a, b]


def middle_kernel(lats, grad_out, row_a, row_b, col_a, col_b, slope, act_t, fields_t, taps,
                  spread, *rest):
    parts, scratch = rest[:lats], rest[lats:]
    grid, wide, prods, ends, line, side, sides, sums, corner, keep = scratch
    band, first, last, even, core = position(lats)
    top = jnp.where(even, row_b[...], row_a[...])
    bottom = jnp.where(even, row_a[...], row_b[...])
    rows, half, c2 = slope.shape
    c1 = c2 // 2
    pooled = rows // 2
    c0 = fields_t.shape[0] // 2
    cells = pooled * half

    grid[:, half:, :] = jnp.zeros((pooled + 2, EDGE, c1), F32)
    grid[1:pooled + 1, :half, :] = grad_out[...].astype(F32)
    grid[0, :half, :] = top[2 * half:, :].astype(F32)
    outside = jnp.where(last, 0.0, 1.0)
    grid[pooled + 1, :half, :] = bottom[2 * half:, :].astype(F32) * outside
    side[1 - core] = col_a[...].astype(F32)
    side[core] = col_b[...].astype(F32)
    for i in range(pooled + 2):
        at = rows + i - 1
        if i == 0:
            at = rows + pooled + 2
        if i == pooled + 1:
            at = rows + pooled + 3
        kept = outside if i == pooled + 1 else 1.0
        grid[i, half:half + 1, :] = side[1, at:at + 1, :] * kept
        grid[i, half + EDGE - 1:half + EDGE, :] = side[0, at:at + 1, :] * kept
    for i in range(pooled + 2):
        here = grid[i]
        wide[i, :, :c1] = pltpu.roll(here, 1, 0).astype(BF16)
        wide[i, :, c1:2 * c1] = here.astype(BF16)
        wide[i, :, 2 * c1:3 * c1] = pltpu.roll(here, half + EDGE - 1, 0).astype(BF16)
        wide[i, :, 3 * c1:] = here.astype(BF16)

    flat = wide[1:pooled + 1].reshape(pooled * (half + EDGE), 4 * c1)
    for a in range(3):
        prods[a] = dot_nt(flat, taps[a]).reshape(pooled, half + EDGE, c2)
    fold = jnp.where(first, taps[0], taps[2])
    ends[0] = dot_nt(wide[0], fold)
    ends[1] = dot_nt(wide[0], taps[1])
    ends[2] = dot_nt(wide[pooled + 1], taps[0])
    ends[3] = dot_nt(wide[pooled + 1], taps[1])

    for s in range(2):
        sides[s] = slope_of(side[s], cdf_of(side[s]))

    def place(r, total, incline, edge):
        inner = total[:half] * incline
        rim = total[half:]
        after = rim[:1, :c1] * sides[1, pl.ds(edge, 1), :]
        before = rim[EDGE - 1:, c1:] * sides[0, pl.ds(edge, 1), :]
        even, odd = inner[:, :c1], inner[:, c1:]
        at = lax.broadcasted_iota(jnp.int32, (half, c1), 0)
        spread[r, :, :c1] = jnp.where(at == 0, before, pltpu.roll(odd, 1, 0)).astype(BF16)
        spread[r, :, c1:2 * c1] = even.astype(BF16)
        spread[r, :, 2 * c1:3 * c1] = odd.astype(BF16)
        spread[r, :, 3 * c1:] = jnp.where(at == half - 1, after, pltpu.roll(even, half - 1, 0)).astype(BF16)

    def halo_slope(message):
        line[...] = message[:2 * half, :].astype(F32)
        both = [line[pl.ds(pc, half, stride=2), :] for pc in range(2)]
        return jnp.concatenate([slope_of(v, cdf_of(v)) for v in both], axis=1)

    place(0, ends[0] + ends[1] + prods[0, 0], halo_slope(top), rows + pooled)
    place(1, ends[0] + prods[1, 0] + prods[0, 0], slope[0], 0)

    def pair(i, carry):
        middle = prods[2, i] + prods[1, i]
        place(2 * i + 2, middle + prods[0, i + 1], slope[2 * i + 1], 2 * i + 1)
        place(2 * i + 3, prods[2, i] + prods[1, i + 1] + prods[0, i + 1], slope[2 * i + 2], 2 * i + 2)
        return carry

    lax.fori_loop(0, pooled - 1, pair, 0)
    final = prods[2, pooled - 1]
    place(rows, final + prods[1, pooled - 1] + ends[2], slope[rows - 1], rows - 1)
    place(rows + 1, (final + ends[3] + ends[2]) * outside, halo_slope(bottom), rows + pooled + 1)

    is_first = jnp.where(first, 1.0, 0.0).astype(BF16)
    not_first = jnp.where(first, 0.0, 1.0).astype(BF16)
    above = wide[0, :half, :3 * c1]
    wide[0, :half, :3 * c1] = above * not_first
    for n, (pr, start) in enumerate(((0, 0), (0, 1), (1, 1), (1, 2))):
        around = wide[start:start + pooled, :half, :3 * c1].reshape(cells, 3 * c1)
        sums[n] = dot(act_t[pr], around)
    corner[...] = dot(act_t[0, :, :half], above * is_first)

    unit = c0
    per_tap = c1 // unit
    count = 9 * per_tap + 9
    block = parts[0].shape[0]

    def put(k, value):
        keep[k * unit:(k + 1) * unit, :] = value

    pieces = {0: ((0, 1), (1, 3)), 1: ((0, 1), (1, 2)), 2: ((0, 0), (1, 2))}
    for a in range(3):
        for b in range(3):
            total = None
            for pr, n in pieces[a]:
                for pc in range(2):
                    k = (pc + 1 - b) // 2 + 1
                    term = sums[n, pc * c1:(pc + 1) * c1, k * c1:(k + 1) * c1]
                    total = term if total is None else total + term
            if a == 0:
                for pc in range(2):
                    k = (pc + 1 - b) // 2 + 1
                    total = total + corner[pc * c1:(pc + 1) * c1, k * c1:(k + 1) * c1]
            total = total * 0.25
            for part in range(per_tap):
                put((3 * a + b) * per_tap + part, total[part * unit:(part + 1) * unit])

    head = spread[0]
    spread[0] = head * not_first
    spread[rows + 2] = head * is_first
    folded = dot(fields_t[:, :half], spread[rows + 2])
    for a in range(3):
        around = spread[2 - a:2 - a + rows].reshape(rows * half, 4 * c1)
        got = dot(fields_t[...], around)
        if a == 0:
            got = got + folded
        for b in range(3):
            even = got[:c0, (2 - b) * c1:(3 - b) * c1]
            odd = got[c0:, (3 - b) * c1:(4 - b) * c1]
            put(9 * per_tap + 3 * a + b, even + odd)
    if lats * block > count * unit:
        keep[count * unit:] = jnp.zeros((lats * block - count * unit, c1), F32)
    for far in range(lats):
        parts[far][...] = keep[pl.ds(pl.multiple_of((band ^ far) * block, block), block), :]


def last_kernel(spread, taps, out, total, turned):
    rows, c0, cols = out.shape
    half = cols // 2
    c2 = 2 * c0
    depth = spread.shape[2]
    result = dot_nt(taps[:c2], spread[2:rows + 2].reshape(rows * half, depth))
    for a in (1, 2):
        result = result + dot_nt(taps[a * c2:(a + 1) * c2],
                                 spread[2 - a:2 - a + rows].reshape(rows * half, depth))
    total[...] = result
    total[:, :half] = total[:, :half] + dot_nt(taps[:c2], spread[rows + 2])
    for q in range(rows // 2):
        pair = total[:, q * cols:(q + 1) * cols].astype(BF16)
        turned[q, :, :cols] = pair[:c0]
        turned[q, :, cols:] = pair[c0:]
    k = lax.broadcasted_iota(jnp.int32, (2 * cols, 2 * cols), 0)
    n = lax.broadcasted_iota(jnp.int32, (2 * cols, 2 * cols), 1)
    order = one_at(n == ((k % cols) // half) * cols + 2 * (k % half) + k // cols)
    found = dot(turned[...].reshape(rows // 2 * c0, 2 * cols), order).astype(BF16)
    for q in range(rows // 2):
        for rp in range(2):
            out[2 * q + rp] = found[q * c0:(q + 1) * c0, rp * cols:(rp + 1) * cols]


def gather_kernel(mine, theirs, out_first, out_second):
    lats, rows, c1 = mine.shape
    band, _, _, _, core = position(lats)
    size = out_second.shape[0]
    total = size + out_first.shape[0]
    for i in range(lats):
        at = i * rows
        for out, base, end in ((out_second, 0, size), (out_first, size, total)):
            low, high = max(at, base), min(at + rows, end)
            if low < high:
                here, there = (x[i ^ band, low - at:high - at] for x in (mine, theirs))
                out[low - base:high - base] = jnp.where(core == 1, here, there).astype(F32)


def vmem(count):
    return [pl.BlockSpec(memory_space=pltpu.VMEM)] * count


def params(mib):
    return pltpu.CompilerParams(vmem_limit_bytes=mib * 1024 * 1024)


def shape(dims, kind):
    return jax.ShapeDtypeStruct(dims, kind)


def body(inputs, pre_first, grad_out, w_first, w_second):
    rows, cols, c1 = pre_first.shape
    c0 = inputs.shape[2]
    half, pooled = cols // 2, rows // 2
    lats, lons = lax.axis_size("lat"), lax.axis_size("lon")
    depths = lons // 2
    band, place = lax.axis_index("lat"), lax.axis_index("lon")
    core = lax.rem(place, 2)
    even = lax.rem(band, 2) == 0

    edge = -(-(rows + pooled + 4) // 16) * 16
    row_a, row_b, col_a, col_b, held_pre = pl.pallas_call(
        functools.partial(pack_kernel, lats),
        out_shape=(
            shape((cols + half, c1), BF16),
            shape((cols + half, c1), BF16),
            shape((edge, c1), BF16),
            shape((edge, c1), BF16),
            shape(pre_first.shape, BF16),
        ),
        in_specs=vmem(2),
        out_specs=tuple(vmem(5)),
        scratch_shapes=[
            pltpu.VMEM((2, edge, c1), F32),
        ],
        compiler_params=params(50),
        cost_estimate=pl.CostEstimate(flops=1000, bytes_accessed=1 << 18, transcendentals=0),
    )(pre_first, grad_out)
    pairs = [(i * lons + j, i * lons + (j + lons // 2) % lons) for i in (0, lats - 1) for j in range(lons)]
    for i in range(1, lats - 1, 2):
        for j in range(lons):
            pairs += [(i * lons + j, (i + 1) * lons + j), ((i + 1) * lons + j, i * lons + j)]
    every = [(i * lons + j, (i ^ 1) * lons + j) for i in range(lats) for j in range(lons)]
    row_b = lax.ppermute(row_b, AREA, pairs)
    row_a = lax.ppermute(row_a, AREA, every)

    slope, act_t = pl.pallas_call(
        local_kernel,
        out_shape=(
            shape((rows, half, 2 * c1), F32),
            shape((2, 2 * c1, pooled * half), BF16),
        ),
        in_specs=vmem(1),
        out_specs=tuple(vmem(2)),
        scratch_shapes=[
            pltpu.VMEM((cols, c1), F32),
            pltpu.VMEM((2, pooled, half, 2 * c1), BF16),
        ],
        compiler_params=params(16),
        cost_estimate=pl.CostEstimate(flops=60 * rows * cols * c1, bytes_accessed=2 << 20,
                                      transcendentals=2 * rows * cols * c1),
    )(held_pre)

    fields = jnp.transpose(inputs, (0, 2, 1))
    row_b, row_a, slope, fields = lax.optimization_barrier((row_b, row_a, slope, fields))

    def corners(at):
        places = (at * (cols - 1), cols + at * (half - 1))
        above, below = (jnp.where(even, one, two) for one, two in ((row_b, row_a), (row_a, row_b)))
        return jnp.concatenate([part[p:p + 1] for p in places for part in (above, below)], 0)

    low, high = corners(0), corners(1)
    pad = jnp.zeros((edge - rows - pooled - 4, c1), BF16)
    col_a = jnp.concatenate([col_a[:rows + pooled], jnp.where(core == 0, high, low), pad], 0)
    col_b = jnp.concatenate([col_b[:rows + pooled], jnp.where(core == 0, low, high), pad], 0)
    col_b = lax.ppermute(col_b, "lon", [(i, (i + 2 * (i % 2) - 1) % lons) for i in range(lons)])
    col_a = lax.ppermute(col_a, "lon", [(i, i ^ 1) for i in range(lons)])

    fields_t, taps_first, taps_second = pl.pallas_call(
        layout_kernel,
        out_shape=(
            shape((2 * c0, rows * half), BF16),
            shape((6 * c0, 4 * c1), BF16),
            shape((3, 2 * c1, 4 * c1), BF16),
        ),
        in_specs=vmem(3),
        out_specs=tuple(vmem(3)),
        scratch_shapes=[pltpu.VMEM((rows, c0, 2 * cols), BF16)],
        compiler_params=params(16),
        cost_estimate=pl.CostEstimate(flops=4 * rows * cols * c0 * cols, bytes_accessed=3 << 20, transcendentals=0),
    )(fields, w_first, w_second)
    col_a, col_b, fields_t = lax.optimization_barrier((col_a, col_b, fields_t))

    block = -(-9 * (c1 + c0) // (16 * lats)) * 16
    span = half + EDGE
    spread, *parts = pl.pallas_call(
        functools.partial(middle_kernel, lats),
        out_shape=(
            shape((rows + 3, half, 4 * c1), BF16),
        ) + (shape((block, c1), F32),) * lats,
        in_specs=vmem(9),
        out_specs=tuple(vmem(lats + 1)),
        scratch_shapes=[
            pltpu.VMEM((pooled + 2, span, c1), F32),
            pltpu.VMEM((pooled + 2, span, 4 * c1), BF16),
            pltpu.VMEM((3, pooled, span, 2 * c1), F32),
            pltpu.VMEM((4, span, 2 * c1), F32),
            pltpu.VMEM((cols, c1), F32),
            pltpu.VMEM((2, edge, c1), F32),
            pltpu.VMEM((2, edge, c1), F32),
            pltpu.VMEM((4, 2 * c1, 3 * c1), F32),
            pltpu.VMEM((2 * c1, 3 * c1), F32),
            pltpu.VMEM((lats * block, c1), F32),
        ],
        compiler_params=params(16),
        cost_estimate=pl.CostEstimate(flops=2 * rows * cols * c1 * 9 * (2 * c1 + c0), bytes_accessed=8 << 20,
                                      transcendentals=0),
    )(grad_out, row_a, row_b, col_a, col_b, slope, act_t, fields_t, taps_second)

    def swapped(value):
        return lax.ppermute(value, "lon", [(i, i ^ 1) for i in range(lons)])

    def between_chips(value, over_lat, over_lon):
        return lax.ppermute(value, AREA, [
            (i * lons + j, (i ^ over_lat * (j % 2)) * lons + (j ^ 2 * over_lon * (j % 2)))
            for i in range(lats) for j in range(lons)])

    order = [*range(1, lats), 0]
    added = {far: swapped(parts[far]) for far in order}
    added = {far: parts[far] + added[far] for far in order}
    got = [between_chips(added[far].astype(BF16), far, 0) for far in range(1, lats)]
    grad_inputs = pl.pallas_call(
        last_kernel,
        out_shape=shape((rows, c0, cols), BF16),
        in_specs=vmem(2),
        out_specs=vmem(1)[0],
        scratch_shapes=[
            pltpu.VMEM((2 * c0, rows * half), F32),
            pltpu.VMEM((pooled, c0, 2 * cols), BF16),
        ],
        compiler_params=params(12),
        cost_estimate=pl.CostEstimate(flops=2 * rows * cols * c1 * 9 * c0, bytes_accessed=3 << 20, transcendentals=0),
    )(spread, taps_first)
    *got, grad_inputs = lax.optimization_barrier((*got, grad_inputs))
    total = added[0]
    for value in got:
        total = total + value.astype(F32)
    part = total.astype(BF16)
    terms = [part] + [between_chips(part, 0, far) for far in range(1, depths)]
    terms = [term.astype(F32) for term in terms]
    while len(terms) > 1:
        terms = [terms[k] + terms[k + 1] for k in range(0, len(terms), 2)]
    part = terms[0].astype(BF16)
    mine = [part] + [between_chips(part, far, 0) for far in range(1, lats)]
    theirs = [swapped(value) for value in mine]
    mine, theirs = jnp.stack(mine, 0), jnp.stack(theirs, 0)

    grad_w_first, grad_w_second = pl.pallas_call(
        gather_kernel,
        out_shape=(shape((9 * c0, c1), F32), shape((9 * c1, c1), F32)),
        in_specs=vmem(2),
        out_specs=tuple(vmem(2)),
        compiler_params=params(8),
        cost_estimate=pl.CostEstimate(flops=1000, bytes_accessed=3 << 19, transcendentals=0),
    )(mine, theirs)
    return (jnp.transpose(grad_inputs, (0, 2, 1)), grad_w_first.reshape(w_first.shape),
            grad_w_second.reshape(w_second.shape))


def solution(mesh):
    in_specs = (P("lat", "lon", None), P("lat", "lon", None), P("lat", "lon", None), P(), P())
    out_specs = (P("lat", "lon", None), P(), P())
    return jax.shard_map(body, mesh=mesh, in_specs=in_specs, out_specs=out_specs, check_vma=False)
```

```python
import functools

import jax
import jax.numpy as jnp
from jax import lax
from jax.experimental import pallas as pl
from jax.experimental.pallas import tpu as pltpu
from jax.sharding import PartitionSpec as P

inv_root = 0.7071067811865476
density = 0.3989422804014327

F32 = jnp.float32
BF16 = jnp.bfloat16
EDGE = 16
AREA = ("lat", "lon")


def cdf_of(value):
    return 0.5 * (1.0 + lax.erf(value * inv_root))


def slope_of(value, cdf):
    return 0.25 * (cdf + value * jnp.exp(-0.5 * value * value) * density)


def dot(left, right):
    return jnp.dot(left, right, preferred_element_type=F32)


def dot_nt(left, right):
    return lax.dot_general(left, right, (((1,), (1,)), ((), ())), preferred_element_type=F32)


def position(lats):
    band, place = lax.axis_index("lat"), lax.axis_index("lon")
    return band, band == 0, band == lats - 1, lax.rem(band, 2) == 0, lax.rem(place, 2)


def odd(value):
    for shift in (4, 2, 1):
        value = value ^ (value >> shift)
    return value & 1


def half_held():
    band, place = lax.axis_index("lat"), lax.axis_index("lon")
    return odd(band) ^ odd(place // 2) ^ (place % 2)


def pack_kernel(lats, pre, grad_out, row_a, row_b, col_a, col_b, held, hold):
    rows, cols, c1 = pre.shape
    pooled, half = grad_out.shape[:2]
    _, _, _, even, core = position(lats)
    for message, low in ((row_a, ~even), (row_b, even)):
        message[:cols] = pre[jnp.where(low, 0, rows - 1)]
        message[cols:] = grad_out[jnp.where(low, 0, pooled - 1)]
    hold[:, rows + pooled:] = jnp.zeros((2, hold.shape[1] - rows - pooled, c1), F32)
    for side, (p, g) in enumerate(((0, 0), (cols - 16, half - 16))):
        at = 15 * side
        for r in range(rows):
            hold[side, r:r + 1] = pre[r, p:p + 16].astype(F32)[at:at + 1]
        for i in range(pooled):
            hold[side, rows + i:rows + i + 1] = grad_out[i, g:g + 16].astype(F32)[at:at + 1]
    col_a[...] = hold[1 - core].astype(BF16)
    col_b[...] = hold[core].astype(BF16)
    held[...] = pre[...]


def one_at(where):
    return jnp.where(where, 1.0, 0.0).astype(BF16)


def local_kernel(pre, slope, act_t, line, act_s):
    rows, cols, c1 = pre.shape
    half = cols // 2

    def one_row(r, carry):
        line[...] = pre[r].astype(F32)
        for pc in range(2):
            value = line[pl.ds(pc, half, stride=2), :]
            cdf = cdf_of(value)
            act_s[r % 2, r // 2, :, pc * c1:(pc + 1) * c1] = (value * cdf).astype(BF16)
            slope[r, :, pc * c1:(pc + 1) * c1] = slope_of(value, cdf)
        return carry

    lax.fori_loop(0, rows, one_row, 0)
    for pr in range(2):
        act_t[pr] = act_s[pr].reshape(rows // 2 * half, 2 * c1).T


def layout_kernel(fields, w_first, w_second, fields_t, taps_first, taps_second, turned):
    rows, c0, cols = fields.shape
    c1 = w_first.shape[3]
    half = cols // 2
    col = lax.broadcasted_iota(jnp.int32, (cols, 2 * cols), 0)
    lane = lax.broadcasted_iota(jnp.int32, (cols, 2 * cols), 1)
    turn = lane // cols
    parity = (lane % cols) // half
    parity = parity + turn - 2 * parity * turn
    order = one_at(col == 2 * (lane % half) + parity)
    turned[...] = dot(fields[...].reshape(rows * c0, cols), order).astype(BF16).reshape(rows, c0, 2 * cols)
    low = lax.broadcasted_iota(jnp.int32, (c0, cols), 1) < half
    for q in range(rows // 2):
        fields_t[:c0, q * cols:(q + 1) * cols] = jnp.where(low, turned[2 * q, :, :cols], turned[2 * q + 1, :, cols:])
        fields_t[c0:, q * cols:(q + 1) * cols] = jnp.where(low, turned[2 * q, :, cols:], turned[2 * q + 1, :, :cols])
    taps_second[...] = jnp.zeros_like(taps_second)
    taps_first[...] = jnp.zeros_like(taps_first)
    for a in range(3):
        for pc, blocks in ((0, (2, 1, None, 0)), (1, (None, 2, 0, 1))):
            for k, b in enumerate(blocks):
                if b is not None:
                    taps_second[a, pc * c1:(pc + 1) * c1, k * c1:(k + 1) * c1] = w_second[a, b]
        for pc, blocks in ((0, (2, 1, 0, None)), (1, (None, 2, 1, 0))):
            for k, b in enumerate(blocks):
                if b is not None:
                    start = (2 * a + pc) * c0
                    taps_first[start:start + c0, k * c1:(k + 1) * c1] = w_first[a, b]


def middle_kernel(lats, grad_out, row_a, row_b, col_a, col_b, slope, act_t, fields_t, taps,
                  spread, own, other,
                  grid, wide, prods, ends, line, side, sides, sums, corner, keep):
    band, first, last, even, core = position(lats)
    top = jnp.where(even, row_b[...], row_a[...])
    bottom = jnp.where(even, row_a[...], row_b[...])
    rows, half, c2 = slope.shape
    c1 = c2 // 2
    pooled = rows // 2
    c0 = fields_t.shape[0] // 2
    cells = pooled * half

    grid[:, half:, :] = jnp.zeros((pooled + 2, EDGE, c1), F32)
    grid[1:pooled + 1, :half, :] = grad_out[...].astype(F32)
    grid[0, :half, :] = top[2 * half:, :].astype(F32)
    outside = jnp.where(last, 0.0, 1.0)
    grid[pooled + 1, :half, :] = bottom[2 * half:, :].astype(F32) * outside
    side[1 - core] = col_a[...].astype(F32)
    side[core] = col_b[...].astype(F32)
    for i in range(pooled + 2):
        at = rows + i - 1
        if i == 0:
            at = rows + pooled + 2
        if i == pooled + 1:
            at = rows + pooled + 3
        kept = outside if i == pooled + 1 else 1.0
        grid[i, half:half + 1, :] = side[1, at:at + 1, :] * kept
        grid[i, half + EDGE - 1:half + EDGE, :] = side[0, at:at + 1, :] * kept
    for i in range(pooled + 2):
        here = grid[i]
        wide[i, :, :c1] = pltpu.roll(here, 1, 0).astype(BF16)
        wide[i, :, c1:2 * c1] = here.astype(BF16)
        wide[i, :, 2 * c1:3 * c1] = pltpu.roll(here, half + EDGE - 1, 0).astype(BF16)
        wide[i, :, 3 * c1:] = here.astype(BF16)

    flat = wide[1:pooled + 1].reshape(pooled * (half + EDGE), 4 * c1)
    for a in range(3):
        prods[a] = dot_nt(flat, taps[a]).reshape(pooled, half + EDGE, c2)
    fold = jnp.where(first, taps[0], taps[2])
    ends[0] = dot_nt(wide[0], fold)
    ends[1] = dot_nt(wide[0], taps[1])
    ends[2] = dot_nt(wide[pooled + 1], taps[0])
    ends[3] = dot_nt(wide[pooled + 1], taps[1])

    for s in range(2):
        sides[s] = slope_of(side[s], cdf_of(side[s]))

    def place(r, total, incline, edge):
        inner = total[:half] * incline
        rim = total[half:]
        after = rim[:1, :c1] * sides[1, pl.ds(edge, 1), :]
        before = rim[EDGE - 1:, c1:] * sides[0, pl.ds(edge, 1), :]
        even, odd = inner[:, :c1], inner[:, c1:]
        at = lax.broadcasted_iota(jnp.int32, (half, c1), 0)
        spread[r, :, :c1] = jnp.where(at == 0, before, pltpu.roll(odd, 1, 0)).astype(BF16)
        spread[r, :, c1:2 * c1] = even.astype(BF16)
        spread[r, :, 2 * c1:3 * c1] = odd.astype(BF16)
        spread[r, :, 3 * c1:] = jnp.where(at == half - 1, after, pltpu.roll(even, half - 1, 0)).astype(BF16)

    def halo_slope(message):
        line[...] = message[:2 * half, :].astype(F32)
        both = [line[pl.ds(pc, half, stride=2), :] for pc in range(2)]
        return jnp.concatenate([slope_of(v, cdf_of(v)) for v in both], axis=1)

    place(0, ends[0] + ends[1] + prods[0, 0], halo_slope(top), rows + pooled)
    place(1, ends[0] + prods[1, 0] + prods[0, 0], slope[0], 0)

    def pair(i, carry):
        middle = prods[2, i] + prods[1, i]
        place(2 * i + 2, middle + prods[0, i + 1], slope[2 * i + 1], 2 * i + 1)
        place(2 * i + 3, prods[2, i] + prods[1, i + 1] + prods[0, i + 1], slope[2 * i + 2], 2 * i + 2)
        return carry

    lax.fori_loop(0, pooled - 1, pair, 0)
    final = prods[2, pooled - 1]
    place(rows, final + prods[1, pooled - 1] + ends[2], slope[rows - 1], rows - 1)
    place(rows + 1, (final + ends[3] + ends[2]) * outside, halo_slope(bottom), rows + pooled + 1)

    is_first = jnp.where(first, 1.0, 0.0).astype(BF16)
    not_first = jnp.where(first, 0.0, 1.0).astype(BF16)
    above = wide[0, :half, :3 * c1]
    wide[0, :half, :3 * c1] = above * not_first
    for n, (pr, start) in enumerate(((0, 0), (0, 1), (1, 1), (1, 2))):
        around = wide[start:start + pooled, :half, :3 * c1].reshape(cells, 3 * c1)
        sums[n] = dot(act_t[pr], around)
    corner[...] = dot(act_t[0, :, :half], above * is_first)

    unit = c0
    per_tap = c1 // unit
    count = 9 * per_tap + 9
    held = own.shape[0]
    block = held // lats

    def put(k, value):
        keep[k * unit:(k + 1) * unit, :] = value

    pieces = {0: ((0, 1), (1, 3)), 1: ((0, 1), (1, 2)), 2: ((0, 0), (1, 2))}
    for a in range(3):
        for b in range(3):
            total = None
            for pr, n in pieces[a]:
                for pc in range(2):
                    k = (pc + 1 - b) // 2 + 1
                    term = sums[n, pc * c1:(pc + 1) * c1, k * c1:(k + 1) * c1]
                    total = term if total is None else total + term
            if a == 0:
                for pc in range(2):
                    k = (pc + 1 - b) // 2 + 1
                    total = total + corner[pc * c1:(pc + 1) * c1, k * c1:(k + 1) * c1]
            total = total * 0.25
            for part in range(per_tap):
                put((3 * a + b) * per_tap + part, total[part * unit:(part + 1) * unit])

    head = spread[0]
    spread[0] = head * not_first
    spread[rows + 2] = head * is_first
    folded = dot(fields_t[:, :half], spread[rows + 2])
    for a in range(3):
        around = spread[2 - a:2 - a + rows].reshape(rows * half, 4 * c1)
        got = dot(fields_t[...], around)
        if a == 0:
            got = got + folded
        for b in range(3):
            even = got[:c0, (2 - b) * c1:(3 - b) * c1]
            odd = got[c0:, (3 - b) * c1:(4 - b) * c1]
            put(9 * per_tap + 3 * a + b, even + odd)
    if 2 * held > count * unit:
        keep[count * unit:] = jnp.zeros((2 * held - count * unit, c1), F32)
    mine = half_held()
    for target, half_of in ((own, mine), (other, 1 - mine)):
        for far in range(lats):
            at = half_of * held + (band ^ far) * block
            target[far * block:(far + 1) * block] = keep[pl.ds(pl.multiple_of(at, block), block), :]


def last_kernel(spread, taps, out, total, turned):
    rows, c0, cols = out.shape
    half = cols // 2
    c2 = 2 * c0
    depth = spread.shape[2]
    result = dot_nt(taps[:c2], spread[2:rows + 2].reshape(rows * half, depth))
    for a in (1, 2):
        result = result + dot_nt(taps[a * c2:(a + 1) * c2],
                                 spread[2 - a:2 - a + rows].reshape(rows * half, depth))
    total[...] = result
    total[:, :half] = total[:, :half] + dot_nt(taps[:c2], spread[rows + 2])
    for q in range(rows // 2):
        pair = total[:, q * cols:(q + 1) * cols].astype(BF16)
        turned[q, :, :cols] = pair[:c0]
        turned[q, :, cols:] = pair[c0:]
    k = lax.broadcasted_iota(jnp.int32, (2 * cols, 2 * cols), 0)
    n = lax.broadcasted_iota(jnp.int32, (2 * cols, 2 * cols), 1)
    order = one_at(n == ((k % cols) // half) * cols + 2 * (k % half) + k // cols)
    found = dot(turned[...].reshape(rows // 2 * c0, 2 * cols), order).astype(BF16)
    for q in range(rows // 2):
        for rp in range(2):
            out[2 * q + rp] = found[q * c0:(q + 1) * c0, rp * cols:(rp + 1) * cols]


def gather_kernel(mine, theirs, out_first, out_second):
    lats, rows, c1 = mine.shape
    band, held = lax.axis_index("lat"), half_held()
    size = out_second.shape[0]
    total = size + out_first.shape[0]
    for h in range(2):
        for i in range(lats):
            at = (h * lats + i) * rows
            for out, base, end in ((out_second, 0, size), (out_first, size, total)):
                low, high = max(at, base), min(at + rows, end)
                if low < high:
                    here, there = (x[i ^ band, low - at:high - at] for x in (mine, theirs))
                    out[low - base:high - base] = jnp.where(held == h, here, there).astype(F32)


def vmem(count):
    return [pl.BlockSpec(memory_space=pltpu.VMEM)] * count


def params(mib):
    return pltpu.CompilerParams(vmem_limit_bytes=mib * 1024 * 1024)


def shape(dims, kind):
    return jax.ShapeDtypeStruct(dims, kind)


def body(inputs, pre_first, grad_out, w_first, w_second):
    rows, cols, c1 = pre_first.shape
    c0 = inputs.shape[2]
    half, pooled = cols // 2, rows // 2
    lats, lons = lax.axis_size("lat"), lax.axis_size("lon")
    depths = lons // 2
    band, place = lax.axis_index("lat"), lax.axis_index("lon")
    core = lax.rem(place, 2)
    even = lax.rem(band, 2) == 0

    edge = -(-(rows + pooled + 4) // 16) * 16
    row_a, row_b, col_a, col_b, held_pre = pl.pallas_call(
        functools.partial(pack_kernel, lats),
        out_shape=(
            shape((cols + half, c1), BF16),
            shape((cols + half, c1), BF16),
            shape((edge, c1), BF16),
            shape((edge, c1), BF16),
            shape(pre_first.shape, BF16),
        ),
        in_specs=vmem(2),
        out_specs=tuple(vmem(5)),
        scratch_shapes=[
            pltpu.VMEM((2, edge, c1), F32),
        ],
        compiler_params=params(50),
        cost_estimate=pl.CostEstimate(flops=1000, bytes_accessed=1 << 18, transcendentals=0),
    )(pre_first, grad_out)
    pairs = [(i * lons + j, i * lons + (j + lons // 2) % lons) for i in (0, lats - 1) for j in range(lons)]
    for i in range(1, lats - 1, 2):
        for j in range(lons):
            pairs += [(i * lons + j, (i + 1) * lons + j), ((i + 1) * lons + j, i * lons + j)]
    every = [(i * lons + j, (i ^ 1) * lons + j) for i in range(lats) for j in range(lons)]
    row_b = lax.ppermute(row_b, AREA, pairs)
    row_a = lax.ppermute(row_a, AREA, every)

    slope, act_t = pl.pallas_call(
        local_kernel,
        out_shape=(
            shape((rows, half, 2 * c1), F32),
            shape((2, 2 * c1, pooled * half), BF16),
        ),
        in_specs=vmem(1),
        out_specs=tuple(vmem(2)),
        scratch_shapes=[
            pltpu.VMEM((cols, c1), F32),
            pltpu.VMEM((2, pooled, half, 2 * c1), BF16),
        ],
        compiler_params=params(16),
        cost_estimate=pl.CostEstimate(flops=60 * rows * cols * c1, bytes_accessed=2 << 20,
                                      transcendentals=2 * rows * cols * c1),
    )(held_pre)

    fields = jnp.transpose(inputs, (0, 2, 1))
    row_b, row_a, slope, fields = lax.optimization_barrier((row_b, row_a, slope, fields))

    def corners(at):
        places = (at * (cols - 1), cols + at * (half - 1))
        above, below = (jnp.where(even, one, two) for one, two in ((row_b, row_a), (row_a, row_b)))
        return jnp.concatenate([part[p:p + 1] for p in places for part in (above, below)], 0)

    low, high = corners(0), corners(1)
    pad = jnp.zeros((edge - rows - pooled - 4, c1), BF16)
    col_a = jnp.concatenate([col_a[:rows + pooled], jnp.where(core == 0, high, low), pad], 0)
    col_b = jnp.concatenate([col_b[:rows + pooled], jnp.where(core == 0, low, high), pad], 0)
    col_b = lax.ppermute(col_b, "lon", [(i, (i + 2 * (i % 2) - 1) % lons) for i in range(lons)])
    col_a = lax.ppermute(col_a, "lon", [(i, i ^ 1) for i in range(lons)])

    fields_t, taps_first, taps_second = pl.pallas_call(
        layout_kernel,
        out_shape=(
            shape((2 * c0, rows * half), BF16),
            shape((6 * c0, 4 * c1), BF16),
            shape((3, 2 * c1, 4 * c1), BF16),
        ),
        in_specs=vmem(3),
        out_specs=tuple(vmem(3)),
        scratch_shapes=[pltpu.VMEM((rows, c0, 2 * cols), BF16)],
        compiler_params=params(16),
        cost_estimate=pl.CostEstimate(flops=4 * rows * cols * c0 * cols, bytes_accessed=3 << 20, transcendentals=0),
    )(fields, w_first, w_second)
    col_a, col_b, fields_t = lax.optimization_barrier((col_a, col_b, fields_t))

    block = -(-9 * (c1 + c0) // (32 * lats)) * 16
    held = lats * block
    span = half + EDGE
    spread, own, other = pl.pallas_call(
        functools.partial(middle_kernel, lats),
        out_shape=(
            shape((rows + 3, half, 4 * c1), BF16),
            shape((held, c1), F32),
            shape((held, c1), F32),
        ),
        in_specs=vmem(9),
        out_specs=tuple(vmem(3)),
        scratch_shapes=[
            pltpu.VMEM((pooled + 2, span, c1), F32),
            pltpu.VMEM((pooled + 2, span, 4 * c1), BF16),
            pltpu.VMEM((3, pooled, span, 2 * c1), F32),
            pltpu.VMEM((4, span, 2 * c1), F32),
            pltpu.VMEM((cols, c1), F32),
            pltpu.VMEM((2, edge, c1), F32),
            pltpu.VMEM((2, edge, c1), F32),
            pltpu.VMEM((4, 2 * c1, 3 * c1), F32),
            pltpu.VMEM((2 * c1, 3 * c1), F32),
            pltpu.VMEM((2 * held, c1), F32),
        ],
        compiler_params=params(16),
        cost_estimate=pl.CostEstimate(flops=2 * rows * cols * c1 * 9 * (2 * c1 + c0), bytes_accessed=8 << 20,
                                      transcendentals=0),
    )(grad_out, row_a, row_b, col_a, col_b, slope, act_t, fields_t, taps_second)

    swap = [(i, i ^ 1) for i in range(lons)]

    def between_chips(value, over_lat, over_lon):
        turn = odd(over_lat) ^ odd(over_lon)
        return lax.ppermute(value, AREA, [
            (i * lons + j, (i ^ over_lat) * lons + (j ^ (2 * over_lon) ^ turn)) for i in range(lats) for j in range(lons)])

    parts = (own + lax.ppermute(other, "lon", swap)).reshape(lats, block, c1)
    sent = [parts[far].astype(BF16) for far in range(1, lats)]
    *sent, spread = lax.optimization_barrier((*sent, spread))
    got = [between_chips(sent[far - 1], far, 0) for far in reversed(range(1, lats))]
    grad_inputs = pl.pallas_call(
        last_kernel,
        out_shape=shape((rows, c0, cols), BF16),
        in_specs=vmem(2),
        out_specs=vmem(1)[0],
        scratch_shapes=[
            pltpu.VMEM((2 * c0, rows * half), F32),
            pltpu.VMEM((pooled, c0, 2 * cols), BF16),
        ],
        compiler_params=params(12),
        cost_estimate=pl.CostEstimate(flops=2 * rows * cols * c1 * 9 * c0, bytes_accessed=3 << 20, transcendentals=0),
    )(spread, taps_first)
    *got, grad_inputs = lax.optimization_barrier((*got, grad_inputs))
    total = parts[0]
    for value in got:
        total = total + value.astype(F32)
    part = total.astype(BF16)
    terms = [part] + [between_chips(part, 0, far) for far in range(1, depths)]
    terms = [term.astype(F32) for term in terms]
    while len(terms) > 1:
        terms = [terms[k] + terms[k + 1] for k in range(0, len(terms), 2)]
    part = terms[0].astype(BF16)
    mine = jnp.stack([part] + [between_chips(part, far, 0) for far in range(1, lats)], 0)
    theirs = lax.ppermute(mine, "lon", swap)

    grad_w_first, grad_w_second = pl.pallas_call(
        gather_kernel,
        out_shape=(shape((9 * c0, c1), F32), shape((9 * c1, c1), F32)),
        in_specs=vmem(2),
        out_specs=tuple(vmem(2)),
        compiler_params=params(8),
        cost_estimate=pl.CostEstimate(flops=1000, bytes_accessed=3 << 19, transcendentals=0),
    )(mine, theirs)
    return (jnp.transpose(grad_inputs, (0, 2, 1)), grad_w_first.reshape(w_first.shape),
            grad_w_second.reshape(w_second.shape))


def solution(mesh):
    in_specs = (P("lat", "lon", None), P("lat", "lon", None), P("lat", "lon", None), P(), P())
    out_specs = (P("lat", "lon", None), P(), P())
    return jax.shard_map(body, mesh=mesh, in_specs=in_specs, out_specs=out_specs, check_vma=False)
```

```python
import functools

import jax
import jax.numpy as jnp
from jax import lax
from jax.experimental import pallas as pl
from jax.experimental.pallas import tpu as pltpu
from jax.sharding import PartitionSpec as P

inv_root = 0.7071067811865476
density = 0.3989422804014327

F32 = jnp.float32
BF16 = jnp.bfloat16
EDGE = 16
AREA = ("lat", "lon")


def cdf_of(value):
    return 0.5 * (1.0 + lax.erf(value * inv_root))


def slope_of(value, cdf):
    return 0.25 * (cdf + value * jnp.exp(-0.5 * value * value) * density)


def dot(left, right):
    return jnp.dot(left, right, preferred_element_type=F32)


def dot_nt(left, right):
    return lax.dot_general(left, right, (((1,), (1,)), ((), ())), preferred_element_type=F32)


def position(lats):
    band, place = lax.axis_index("lat"), lax.axis_index("lon")
    return band, band == 0, band == lats - 1, lax.rem(band, 2) == 0, lax.rem(place, 2)


def odd(value):
    for shift in (4, 2, 1):
        value = value ^ (value >> shift)
    return value & 1


def half_held():
    band, place = lax.axis_index("lat"), lax.axis_index("lon")
    return odd(band) ^ odd(place // 2) ^ (place % 2)


def pack_kernel(lats, pre_far, grad_far, row_a, row_b, col_a, col_b, pre, hold, grad_out, sems):
    copies = [pltpu.make_async_copy(pre_far, pre, sems.at[0]), pltpu.make_async_copy(grad_far, grad_out, sems.at[1])]
    for copy in copies:
        copy.start()
    for copy in copies:
        copy.wait()
    rows, cols, c1 = pre.shape
    pooled, half = grad_out.shape[:2]
    _, _, _, even, core = position(lats)
    for message, low in ((row_a, ~even), (row_b, even)):
        message[:cols] = pre[jnp.where(low, 0, rows - 1)]
        message[cols:] = grad_out[jnp.where(low, 0, pooled - 1)]
    hold[:, rows + pooled:] = jnp.zeros((2, hold.shape[1] - rows - pooled, c1), F32)
    for side, (p, g) in enumerate(((0, 0), (cols - 16, half - 16))):
        at = 15 * side
        for r in range(rows):
            hold[side, r:r + 1] = pre[r, p:p + 16].astype(F32)[at:at + 1]
        for i in range(pooled):
            hold[side, rows + i:rows + i + 1] = grad_out[i, g:g + 16].astype(F32)[at:at + 1]
    col_a[...] = hold[1 - core].astype(BF16)
    col_b[...] = hold[core].astype(BF16)


def one_at(where):
    return jnp.where(where, 1.0, 0.0).astype(BF16)


def local_kernel(pre, slope, act_t, line, act_s):
    rows, cols, c1 = pre.shape
    half = cols // 2

    def one_row(r, carry):
        line[...] = pre[r].astype(F32)
        for pc in range(2):
            value = line[pl.ds(pc, half, stride=2), :]
            cdf = cdf_of(value)
            act_s[r % 2, r // 2, :, pc * c1:(pc + 1) * c1] = (value * cdf).astype(BF16)
            slope[r, :, pc * c1:(pc + 1) * c1] = slope_of(value, cdf)
        return carry

    lax.fori_loop(0, rows, one_row, 0)
    for pr in range(2):
        act_t[pr] = act_s[pr].reshape(rows // 2 * half, 2 * c1).T


def layout_kernel(fields, w_first, w_second, fields_t, taps_first, taps_second, turned):
    rows, c0, cols = fields.shape
    c1 = w_first.shape[3]
    half = cols // 2
    col = lax.broadcasted_iota(jnp.int32, (cols, 2 * cols), 0)
    lane = lax.broadcasted_iota(jnp.int32, (cols, 2 * cols), 1)
    turn = lane // cols
    parity = (lane % cols) // half
    parity = parity + turn - 2 * parity * turn
    order = one_at(col == 2 * (lane % half) + parity)
    turned[...] = dot(fields[...].reshape(rows * c0, cols), order).astype(BF16).reshape(rows, c0, 2 * cols)
    low = lax.broadcasted_iota(jnp.int32, (c0, cols), 1) < half
    for q in range(rows // 2):
        fields_t[:c0, q * cols:(q + 1) * cols] = jnp.where(low, turned[2 * q, :, :cols], turned[2 * q + 1, :, cols:])
        fields_t[c0:, q * cols:(q + 1) * cols] = jnp.where(low, turned[2 * q, :, cols:], turned[2 * q + 1, :, :cols])
    taps_second[...] = jnp.zeros_like(taps_second)
    taps_first[...] = jnp.zeros_like(taps_first)
    for a in range(3):
        for pc, blocks in ((0, (2, 1, None, 0)), (1, (None, 2, 0, 1))):
            for k, b in enumerate(blocks):
                if b is not None:
                    taps_second[a, pc * c1:(pc + 1) * c1, k * c1:(k + 1) * c1] = w_second[a, b]
        for pc, blocks in ((0, (2, 1, 0, None)), (1, (None, 2, 1, 0))):
            for k, b in enumerate(blocks):
                if b is not None:
                    start = (2 * a + pc) * c0
                    taps_first[start:start + c0, k * c1:(k + 1) * c1] = w_first[a, b]


def middle_kernel(lats, grad_out, row_a, row_b, col_a, col_b, slope, act_t, fields_t, taps,
                  spread, own, other,
                  grid, wide, prods, ends, line, side, sides, sums, corner, keep):
    band, first, last, even, core = position(lats)
    top = jnp.where(even, row_b[...], row_a[...])
    bottom = jnp.where(even, row_a[...], row_b[...])
    rows, half, c2 = slope.shape
    c1 = c2 // 2
    pooled = rows // 2
    c0 = fields_t.shape[0] // 2
    cells = pooled * half

    grid[:, half:, :] = jnp.zeros((pooled + 2, EDGE, c1), F32)
    grid[1:pooled + 1, :half, :] = grad_out[...].astype(F32)
    grid[0, :half, :] = top[2 * half:, :].astype(F32)
    outside = jnp.where(last, 0.0, 1.0)
    grid[pooled + 1, :half, :] = bottom[2 * half:, :].astype(F32) * outside
    side[1 - core] = col_a[...].astype(F32)
    side[core] = col_b[...].astype(F32)
    for i in range(pooled + 2):
        at = rows + i - 1
        if i == 0:
            at = rows + pooled + 2
        if i == pooled + 1:
            at = rows + pooled + 3
        kept = outside if i == pooled + 1 else 1.0
        grid[i, half:half + 1, :] = side[1, at:at + 1, :] * kept
        grid[i, half + EDGE - 1:half + EDGE, :] = side[0, at:at + 1, :] * kept
    for i in range(pooled + 2):
        here = grid[i]
        wide[i, :, :c1] = pltpu.roll(here, 1, 0).astype(BF16)
        wide[i, :, c1:2 * c1] = here.astype(BF16)
        wide[i, :, 2 * c1:3 * c1] = pltpu.roll(here, half + EDGE - 1, 0).astype(BF16)
        wide[i, :, 3 * c1:] = here.astype(BF16)

    flat = wide[1:pooled + 1].reshape(pooled * (half + EDGE), 4 * c1)
    for a in range(3):
        prods[a] = dot_nt(flat, taps[a]).reshape(pooled, half + EDGE, c2)
    fold = jnp.where(first, taps[0], taps[2])
    ends[0] = dot_nt(wide[0], fold)
    ends[1] = dot_nt(wide[0], taps[1])
    ends[2] = dot_nt(wide[pooled + 1], taps[0])
    ends[3] = dot_nt(wide[pooled + 1], taps[1])

    for s in range(2):
        sides[s] = slope_of(side[s], cdf_of(side[s]))

    def place(r, total, incline, edge):
        inner = total[:half] * incline
        rim = total[half:]
        after = rim[:1, :c1] * sides[1, pl.ds(edge, 1), :]
        before = rim[EDGE - 1:, c1:] * sides[0, pl.ds(edge, 1), :]
        even, odd = inner[:, :c1], inner[:, c1:]
        at = lax.broadcasted_iota(jnp.int32, (half, c1), 0)
        spread[r, :, :c1] = jnp.where(at == 0, before, pltpu.roll(odd, 1, 0)).astype(BF16)
        spread[r, :, c1:2 * c1] = even.astype(BF16)
        spread[r, :, 2 * c1:3 * c1] = odd.astype(BF16)
        spread[r, :, 3 * c1:] = jnp.where(at == half - 1, after, pltpu.roll(even, half - 1, 0)).astype(BF16)

    def halo_slope(message):
        line[...] = message[:2 * half, :].astype(F32)
        both = [line[pl.ds(pc, half, stride=2), :] for pc in range(2)]
        return jnp.concatenate([slope_of(v, cdf_of(v)) for v in both], axis=1)

    place(0, ends[0] + ends[1] + prods[0, 0], halo_slope(top), rows + pooled)
    place(1, ends[0] + prods[1, 0] + prods[0, 0], slope[0], 0)

    def pair(i, carry):
        middle = prods[2, i] + prods[1, i]
        place(2 * i + 2, middle + prods[0, i + 1], slope[2 * i + 1], 2 * i + 1)
        place(2 * i + 3, prods[2, i] + prods[1, i + 1] + prods[0, i + 1], slope[2 * i + 2], 2 * i + 2)
        return carry

    lax.fori_loop(0, pooled - 1, pair, 0)
    final = prods[2, pooled - 1]
    place(rows, final + prods[1, pooled - 1] + ends[2], slope[rows - 1], rows - 1)
    place(rows + 1, (final + ends[3] + ends[2]) * outside, halo_slope(bottom), rows + pooled + 1)

    is_first = jnp.where(first, 1.0, 0.0).astype(BF16)
    not_first = jnp.where(first, 0.0, 1.0).astype(BF16)
    above = wide[0, :half, :3 * c1]
    wide[0, :half, :3 * c1] = above * not_first
    for n, (pr, start) in enumerate(((0, 0), (0, 1), (1, 1), (1, 2))):
        around = wide[start:start + pooled, :half, :3 * c1].reshape(cells, 3 * c1)
        sums[n] = dot(act_t[pr], around)
    corner[...] = dot(act_t[0, :, :half], above * is_first)

    unit = c0
    per_tap = c1 // unit
    count = 9 * per_tap + 9
    held = own.shape[0]
    block = held // lats

    def put(k, value):
        keep[k * unit:(k + 1) * unit, :] = value

    pieces = {0: ((0, 1), (1, 3)), 1: ((0, 1), (1, 2)), 2: ((0, 0), (1, 2))}
    for a in range(3):
        for b in range(3):
            total = None
            for pr, n in pieces[a]:
                for pc in range(2):
                    k = (pc + 1 - b) // 2 + 1
                    term = sums[n, pc * c1:(pc + 1) * c1, k * c1:(k + 1) * c1]
                    total = term if total is None else total + term
            if a == 0:
                for pc in range(2):
                    k = (pc + 1 - b) // 2 + 1
                    total = total + corner[pc * c1:(pc + 1) * c1, k * c1:(k + 1) * c1]
            total = total * 0.25
            for part in range(per_tap):
                put((3 * a + b) * per_tap + part, total[part * unit:(part + 1) * unit])

    head = spread[0]
    spread[0] = head * not_first
    spread[rows + 2] = head * is_first
    folded = dot(fields_t[:, :half], spread[rows + 2])
    for a in range(3):
        around = spread[2 - a:2 - a + rows].reshape(rows * half, 4 * c1)
        got = dot(fields_t[...], around)
        if a == 0:
            got = got + folded
        for b in range(3):
            even = got[:c0, (2 - b) * c1:(3 - b) * c1]
            odd = got[c0:, (3 - b) * c1:(4 - b) * c1]
            put(9 * per_tap + 3 * a + b, even + odd)
    if 2 * held > count * unit:
        keep[count * unit:] = jnp.zeros((2 * held - count * unit, c1), F32)
    mine = half_held()
    for target, half_of in ((own, mine), (other, 1 - mine)):
        for far in range(lats):
            at = half_of * held + (band ^ far) * block
            target[far * block:(far + 1) * block] = keep[pl.ds(pl.multiple_of(at, block), block), :]


def last_kernel(spread, taps, out, total, turned):
    rows, c0, cols = out.shape
    half = cols // 2
    c2 = 2 * c0
    depth = spread.shape[2]
    result = dot_nt(taps[:c2], spread[2:rows + 2].reshape(rows * half, depth))
    for a in (1, 2):
        result = result + dot_nt(taps[a * c2:(a + 1) * c2],
                                 spread[2 - a:2 - a + rows].reshape(rows * half, depth))
    total[...] = result
    total[:, :half] = total[:, :half] + dot_nt(taps[:c2], spread[rows + 2])
    for q in range(rows // 2):
        pair = total[:, q * cols:(q + 1) * cols].astype(BF16)
        turned[q, :, :cols] = pair[:c0]
        turned[q, :, cols:] = pair[c0:]
    k = lax.broadcasted_iota(jnp.int32, (2 * cols, 2 * cols), 0)
    n = lax.broadcasted_iota(jnp.int32, (2 * cols, 2 * cols), 1)
    order = one_at(n == ((k % cols) // half) * cols + 2 * (k % half) + k // cols)
    found = dot(turned[...].reshape(rows // 2 * c0, 2 * cols), order).astype(BF16)
    for q in range(rows // 2):
        for rp in range(2):
            out[2 * q + rp] = found[q * c0:(q + 1) * c0, rp * cols:(rp + 1) * cols]


def gather_kernel(mine, theirs, out_first, out_second):
    lats, rows, c1 = mine.shape
    band, held = lax.axis_index("lat"), half_held()
    size = out_second.shape[0]
    total = size + out_first.shape[0]
    for h in range(2):
        for i in range(lats):
            at = (h * lats + i) * rows
            for out, base, end in ((out_second, 0, size), (out_first, size, total)):
                low, high = max(at, base), min(at + rows, end)
                if low < high:
                    here, there = (x[i ^ band, low - at:high - at] for x in (mine, theirs))
                    out[low - base:high - base] = jnp.where(held == h, here, there).astype(F32)


def vmem(count):
    return [pl.BlockSpec(memory_space=pltpu.VMEM)] * count


def far(count):
    return [pl.BlockSpec(memory_space=pl.ANY)] * count


def params(mib):
    return pltpu.CompilerParams(vmem_limit_bytes=mib * 1024 * 1024)


def shape(dims, kind):
    return jax.ShapeDtypeStruct(dims, kind)


def body(inputs, pre_first, grad_out, w_first, w_second):
    rows, cols, c1 = pre_first.shape
    c0 = inputs.shape[2]
    half, pooled = cols // 2, rows // 2
    lats, lons = lax.axis_size("lat"), lax.axis_size("lon")
    depths = lons // 2
    band, place = lax.axis_index("lat"), lax.axis_index("lon")
    core = lax.rem(place, 2)
    even = lax.rem(band, 2) == 0

    edge = -(-(rows + pooled + 4) // 16) * 16
    row_a, row_b, col_a, col_b, held_pre = pl.pallas_call(
        functools.partial(pack_kernel, lats),
        out_shape=(
            pltpu.VMEM((cols + half, c1), BF16),
            pltpu.VMEM((cols + half, c1), BF16),
            pltpu.VMEM((edge, c1), BF16),
            pltpu.VMEM((edge, c1), BF16),
            pltpu.VMEM(pre_first.shape, BF16),
        ),
        in_specs=far(2),
        out_specs=tuple(vmem(5)),
        scratch_shapes=[
            pltpu.VMEM((2, edge, c1), F32),
            pltpu.VMEM(grad_out.shape, BF16),
            pltpu.SemaphoreType.DMA((2,)),
        ],
        compiler_params=params(58),
        cost_estimate=pl.CostEstimate(flops=1000, bytes_accessed=1 << 18, transcendentals=0),
    )(pre_first, grad_out)
    pairs = [(i * lons + j, i * lons + (j + lons // 2) % lons) for i in (0, lats - 1) for j in range(lons)]
    for i in range(1, lats - 1, 2):
        for j in range(lons):
            pairs += [(i * lons + j, (i + 1) * lons + j), ((i + 1) * lons + j, i * lons + j)]
    every = [(i * lons + j, (i ^ 1) * lons + j) for i in range(lats) for j in range(lons)]
    row_b = lax.ppermute(row_b, AREA, pairs)
    row_a = lax.ppermute(row_a, AREA, every)

    slope, act_t = pl.pallas_call(
        local_kernel,
        out_shape=(
            shape((rows, half, 2 * c1), F32),
            shape((2, 2 * c1, pooled * half), BF16),
        ),
        in_specs=vmem(1),
        out_specs=tuple(vmem(2)),
        scratch_shapes=[
            pltpu.VMEM((cols, c1), F32),
            pltpu.VMEM((2, pooled, half, 2 * c1), BF16),
        ],
        compiler_params=params(16),
        cost_estimate=pl.CostEstimate(flops=60 * rows * cols * c1, bytes_accessed=2 << 20,
                                      transcendentals=2 * rows * cols * c1),
    )(held_pre)

    fields = jnp.transpose(inputs, (0, 2, 1))
    row_b, row_a, slope, fields = lax.optimization_barrier((row_b, row_a, slope, fields))

    def corners(at):
        places = (at * (cols - 1), cols + at * (half - 1))
        above, below = (jnp.where(even, one, two) for one, two in ((row_b, row_a), (row_a, row_b)))
        return jnp.concatenate([part[p:p + 1] for p in places for part in (above, below)], 0)

    low, high = corners(0), corners(1)
    pad = jnp.zeros((edge - rows - pooled - 4, c1), BF16)
    col_a = jnp.concatenate([col_a[:rows + pooled], jnp.where(core == 0, high, low), pad], 0)
    col_b = jnp.concatenate([col_b[:rows + pooled], jnp.where(core == 0, low, high), pad], 0)
    col_b = lax.ppermute(col_b, "lon", [(i, (i + 2 * (i % 2) - 1) % lons) for i in range(lons)])
    col_a = lax.ppermute(col_a, "lon", [(i, i ^ 1) for i in range(lons)])

    fields_t, taps_first, taps_second = pl.pallas_call(
        layout_kernel,
        out_shape=(
            shape((2 * c0, rows * half), BF16),
            shape((6 * c0, 4 * c1), BF16),
            shape((3, 2 * c1, 4 * c1), BF16),
        ),
        in_specs=vmem(3),
        out_specs=tuple(vmem(3)),
        scratch_shapes=[pltpu.VMEM((rows, c0, 2 * cols), BF16)],
        compiler_params=params(16),
        cost_estimate=pl.CostEstimate(flops=4 * rows * cols * c0 * cols, bytes_accessed=3 << 20, transcendentals=0),
    )(fields, w_first, w_second)
    col_a, col_b, fields_t = lax.optimization_barrier((col_a, col_b, fields_t))

    block = -(-9 * (c1 + c0) // (32 * lats)) * 16
    held = lats * block
    span = half + EDGE
    spread, own, other = pl.pallas_call(
        functools.partial(middle_kernel, lats),
        out_shape=(
            shape((rows + 3, half, 4 * c1), BF16),
            shape((held, c1), F32),
            shape((held, c1), F32),
        ),
        in_specs=vmem(9),
        out_specs=tuple(vmem(3)),
        scratch_shapes=[
            pltpu.VMEM((pooled + 2, span, c1), F32),
            pltpu.VMEM((pooled + 2, span, 4 * c1), BF16),
            pltpu.VMEM((3, pooled, span, 2 * c1), F32),
            pltpu.VMEM((4, span, 2 * c1), F32),
            pltpu.VMEM((cols, c1), F32),
            pltpu.VMEM((2, edge, c1), F32),
            pltpu.VMEM((2, edge, c1), F32),
            pltpu.VMEM((4, 2 * c1, 3 * c1), F32),
            pltpu.VMEM((2 * c1, 3 * c1), F32),
            pltpu.VMEM((2 * held, c1), F32),
        ],
        compiler_params=params(16),
        cost_estimate=pl.CostEstimate(flops=2 * rows * cols * c1 * 9 * (2 * c1 + c0), bytes_accessed=8 << 20,
                                      transcendentals=0),
    )(grad_out, row_a, row_b, col_a, col_b, slope, act_t, fields_t, taps_second)

    swap = [(i, i ^ 1) for i in range(lons)]

    def between_chips(value, over_lat, over_lon):
        turn = odd(over_lat) ^ odd(over_lon)
        return lax.ppermute(value, AREA, [
            (i * lons + j, (i ^ over_lat) * lons + (j ^ (2 * over_lon) ^ turn)) for i in range(lats) for j in range(lons)])

    parts = (own + lax.ppermute(other, "lon", swap)).reshape(lats, block, c1)
    sent = [parts[far].astype(BF16) for far in range(1, lats)]
    *sent, spread = lax.optimization_barrier((*sent, spread))
    got = [between_chips(sent[far - 1], far, 0) for far in reversed(range(1, lats))]
    grad_inputs = pl.pallas_call(
        last_kernel,
        out_shape=shape((rows, c0, cols), BF16),
        in_specs=vmem(2),
        out_specs=vmem(1)[0],
        scratch_shapes=[
            pltpu.VMEM((2 * c0, rows * half), F32),
            pltpu.VMEM((pooled, c0, 2 * cols), BF16),
        ],
        compiler_params=params(12),
        cost_estimate=pl.CostEstimate(flops=2 * rows * cols * c1 * 9 * c0, bytes_accessed=3 << 20, transcendentals=0),
    )(spread, taps_first)
    *got, grad_inputs = lax.optimization_barrier((*got, grad_inputs))
    total = parts[0]
    for value in got:
        total = total + value.astype(F32)
    part = total.astype(BF16)
    terms = [part] + [between_chips(part, 0, far) for far in range(1, depths)]
    terms = [term.astype(F32) for term in terms]
    while len(terms) > 1:
        terms = [terms[k] + terms[k + 1] for k in range(0, len(terms), 2)]
    part = terms[0].astype(BF16)
    mine = jnp.stack([part] + [between_chips(part, far, 0) for far in range(1, lats)], 0)
    theirs = lax.ppermute(mine, "lon", swap)

    grad_w_first, grad_w_second = pl.pallas_call(
        gather_kernel,
        out_shape=(shape((9 * c0, c1), F32), shape((9 * c1, c1), F32)),
        in_specs=vmem(2),
        out_specs=tuple(vmem(2)),
        compiler_params=params(8),
        cost_estimate=pl.CostEstimate(flops=1000, bytes_accessed=3 << 19, transcendentals=0),
    )(mine, theirs)
    return (jnp.transpose(grad_inputs, (0, 2, 1)), grad_w_first.reshape(w_first.shape),
            grad_w_second.reshape(w_second.shape))


def solution(mesh):
    in_specs = (P("lat", "lon", None), P("lat", "lon", None), P("lat", "lon", None), P(), P())
    out_specs = (P("lat", "lon", None), P(), P())
    return jax.shard_map(body, mesh=mesh, in_specs=in_specs, out_specs=out_specs, check_vma=False)
```

```python
import functools

import jax
import jax.numpy as jnp
from jax import lax
from jax.experimental import pallas as pl
from jax.experimental.pallas import tpu as pltpu
from jax.sharding import PartitionSpec as P

inv_root = 0.7071067811865476
density = 0.3989422804014327

F32 = jnp.float32
BF16 = jnp.bfloat16
AREA = ("lat", "lon")


def cdf_of(value):
    return 0.5 * (1.0 + lax.erf(value * inv_root))


def slope_of(value, cdf):
    return 0.25 * (cdf + value * jnp.exp(-0.5 * value * value) * density)


def dot(left, right):
    return jnp.dot(left, right, preferred_element_type=F32)


def dot_nt(left, right):
    return lax.dot_general(left, right, (((1,), (1,)), ((), ())), preferred_element_type=F32)


def position(lats):
    band, place = lax.axis_index("lat"), lax.axis_index("lon")
    return band, band == 0, band == lats - 1, lax.rem(band, 2) == 0, lax.rem(place, 2)


def odd(value):
    for shift in (4, 2, 1):
        value = value ^ (value >> shift)
    return value & 1


def half_held():
    band, place = lax.axis_index("lat"), lax.axis_index("lon")
    return odd(band) ^ odd(place // 2) ^ (place % 2)


def pack_kernel(lats, pre_far, grad_far, row_a, row_b, col_a, col_b, pre, hold, grad_out, sems):
    copies = [pltpu.make_async_copy(pre_far, pre, sems.at[0]), pltpu.make_async_copy(grad_far, grad_out, sems.at[1])]
    for copy in copies:
        copy.start()
    for copy in copies:
        copy.wait()
    rows, cols, c1 = pre.shape
    pooled, half = grad_out.shape[:2]
    _, _, _, even, core = position(lats)
    for message, low in ((row_a, ~even), (row_b, even)):
        message[:cols] = pre[jnp.where(low, 0, rows - 1)]
        message[cols:] = grad_out[jnp.where(low, 0, pooled - 1)]
    hold[:, rows + pooled:] = jnp.zeros((2, hold.shape[1] - rows - pooled, c1), F32)
    for side, (p, g) in enumerate(((0, 0), (cols - 16, half - 16))):
        at = 15 * side
        for r in range(rows):
            hold[side, r:r + 1] = pre[r, p:p + 16].astype(F32)[at:at + 1]
        for i in range(pooled):
            hold[side, rows + i:rows + i + 1] = grad_out[i, g:g + 16].astype(F32)[at:at + 1]
    col_a[...] = hold[1 - core].astype(BF16)
    col_b[...] = hold[core].astype(BF16)


def one_at(where):
    return jnp.where(where, 1.0, 0.0).astype(BF16)


def local_kernel(pre, slope, act_t, act_ends, line, act_s):
    rows, cols, c1 = pre.shape
    half = cols // 2

    def one_row(r, carry):
        line[...] = pre[r].astype(F32)
        for pc in range(2):
            value = line[pl.ds(pc, half, stride=2), :]
            cdf = cdf_of(value)
            act = value * cdf
            act_s[r % 2, r // 2, :, pc * c1:(pc + 1) * c1] = act.astype(BF16)
            act_ends[pc, pl.ds(r, 1), :] = act[pc * (half - 1):pc * (half - 1) + 1]
            slope[r, :, pc * c1:(pc + 1) * c1] = slope_of(value, cdf)
        return carry

    lax.fori_loop(0, rows, one_row, 0)
    for pr in range(2):
        act_t[pr] = act_s[pr].reshape(rows // 2 * half, 2 * c1).T


def layout_kernel(fields, w_first, w_second, fields_t, field_ends, taps_first, taps_second, turned):
    rows, c0, cols = fields.shape
    c1 = w_first.shape[3]
    half = cols // 2
    col = lax.broadcasted_iota(jnp.int32, (cols, 2 * cols), 0)
    lane = lax.broadcasted_iota(jnp.int32, (cols, 2 * cols), 1)
    turn = lane // cols
    parity = (lane % cols) // half
    parity = parity + turn - 2 * parity * turn
    order = one_at(col == 2 * (lane % half) + parity)
    turned[...] = dot(fields[...].reshape(rows * c0, cols), order).astype(BF16).reshape(rows, c0, 2 * cols)
    low = lax.broadcasted_iota(jnp.int32, (c0, cols), 1) < half
    for q in range(rows // 2):
        fields_t[:c0, q * cols:(q + 1) * cols] = jnp.where(low, turned[2 * q, :, :cols], turned[2 * q + 1, :, cols:])
        fields_t[c0:, q * cols:(q + 1) * cols] = jnp.where(low, turned[2 * q, :, cols:], turned[2 * q + 1, :, :cols])
    cell = lax.broadcasted_iota(jnp.int32, (rows * half, 2 * rows), 0)
    n = lax.broadcasted_iota(jnp.int32, (rows * half, 2 * rows), 1)
    pick = one_at(cell == (n % rows) * half + (n // rows) * (half - 1))
    field_ends[...] = dot(fields_t[...], pick).astype(BF16)
    taps_second[...] = jnp.zeros_like(taps_second)
    taps_first[...] = jnp.zeros_like(taps_first)
    for a in range(3):
        for pc, blocks in ((0, (2, 1, None, 0)), (1, (None, 2, 0, 1))):
            for k, b in enumerate(blocks):
                if b is not None:
                    taps_second[a, pc * c1:(pc + 1) * c1, k * c1:(k + 1) * c1] = w_second[a, b]
        for pc, blocks in ((0, (2, 1, 0, None)), (1, (None, 2, 1, 0))):
            for k, b in enumerate(blocks):
                if b is not None:
                    start = (2 * a + pc) * c0
                    taps_first[start:start + c0, k * c1:(k + 1) * c1] = w_first[a, b]


def middle_kernel(lats, grad_out, row_a, row_b, slope, act_t, fields_t, taps,
                  spread, keep, raw_ends, slope_ends, out_ends,
                  grid, wide, prods, ends, line, sums, corner):
    _, first, last, even, _ = position(lats)
    top = jnp.where(even, row_b[...], row_a[...])
    bottom = jnp.where(even, row_a[...], row_b[...])
    rows, half, c2 = slope.shape
    c1 = c2 // 2
    pooled = rows // 2
    c0 = fields_t.shape[0] // 2
    cells = pooled * half
    raw_ends[...] = jnp.zeros_like(raw_ends)
    slope_ends[...] = jnp.zeros_like(slope_ends)
    out_ends[...] = jnp.zeros_like(out_ends)

    grid[1:pooled + 1] = grad_out[...].astype(F32)
    grid[0] = top[2 * half:, :].astype(F32)
    outside = jnp.where(last, 0.0, 1.0)
    grid[pooled + 1] = bottom[2 * half:, :].astype(F32) * outside
    at = lax.broadcasted_iota(jnp.int32, (half, c1), 0)
    for i in range(pooled + 2):
        here = grid[i]
        out_ends[0, i:i + 1] = here[:1]
        out_ends[1, i:i + 1] = here[half - 1:]
        wide[i, :, :c1] = jnp.where(at == 0, 0.0, pltpu.roll(here, 1, 0)).astype(BF16)
        wide[i, :, c1:2 * c1] = here.astype(BF16)
        wide[i, :, 2 * c1:3 * c1] = jnp.where(at == half - 1, 0.0, pltpu.roll(here, half - 1, 0)).astype(BF16)
        wide[i, :, 3 * c1:] = here.astype(BF16)

    flat = wide[1:pooled + 1].reshape(cells, 4 * c1)
    for a in range(3):
        prods[a] = dot_nt(flat, taps[a]).reshape(pooled, half, c2)
    fold = jnp.where(first, taps[0], taps[2])
    ends[0] = dot_nt(wide[0], fold)
    ends[1] = dot_nt(wide[0], taps[1])
    ends[2] = dot_nt(wide[pooled + 1], taps[0])
    ends[3] = dot_nt(wide[pooled + 1], taps[1])

    def place(r, total, incline):
        inner = total * incline
        raw_ends[0, pl.ds(r, 1), :] = total[:1, :c1]
        raw_ends[1, pl.ds(r, 1), :] = total[half - 1:, c1:]
        slope_ends[0, pl.ds(r, 1), :] = incline[:1, :c1]
        slope_ends[1, pl.ds(r, 1), :] = incline[half - 1:, c1:]
        even, odd = inner[:, :c1], inner[:, c1:]
        spread[r, :, :c1] = jnp.where(at == 0, 0.0, pltpu.roll(odd, 1, 0)).astype(BF16)
        spread[r, :, c1:2 * c1] = jnp.where(at == 0, 0.0, even).astype(BF16)
        spread[r, :, 2 * c1:3 * c1] = jnp.where(at == half - 1, 0.0, odd).astype(BF16)
        spread[r, :, 3 * c1:] = jnp.where(at == half - 1, 0.0, pltpu.roll(even, half - 1, 0)).astype(BF16)

    def halo_slope(message):
        line[...] = message[:2 * half, :].astype(F32)
        both = [line[pl.ds(pc, half, stride=2), :] for pc in range(2)]
        return jnp.concatenate([slope_of(v, cdf_of(v)) for v in both], axis=1)

    place(0, ends[0] + ends[1] + prods[0, 0], halo_slope(top))
    place(1, ends[0] + prods[1, 0] + prods[0, 0], slope[0])

    def pair(i, carry):
        middle = prods[2, i] + prods[1, i]
        place(2 * i + 2, middle + prods[0, i + 1], slope[2 * i + 1])
        place(2 * i + 3, prods[2, i] + prods[1, i + 1] + prods[0, i + 1], slope[2 * i + 2])
        return carry

    lax.fori_loop(0, pooled - 1, pair, 0)
    final = prods[2, pooled - 1]
    place(rows, final + prods[1, pooled - 1] + ends[2], slope[rows - 1])
    place(rows + 1, (final + ends[3] + ends[2]) * outside, halo_slope(bottom))

    is_first = jnp.where(first, 1.0, 0.0).astype(BF16)
    not_first = jnp.where(first, 0.0, 1.0).astype(BF16)
    above = wide[0, :, :3 * c1]
    wide[0, :, :3 * c1] = above * not_first
    for n, (pr, start) in enumerate(((0, 0), (0, 1), (1, 1), (1, 2))):
        around = wide[start:start + pooled, :, :3 * c1].reshape(cells, 3 * c1)
        sums[n] = dot(act_t[pr], around)
    corner[...] = dot(act_t[0, :, :half], above * is_first)

    unit = c0
    per_tap = c1 // unit
    count = 9 * per_tap + 9

    def put(k, value):
        keep[k * unit:(k + 1) * unit, :] = value

    pieces = {0: ((0, 1), (1, 3)), 1: ((0, 1), (1, 2)), 2: ((0, 0), (1, 2))}
    for a in range(3):
        for b in range(3):
            total = None
            for pr, n in pieces[a]:
                for pc in range(2):
                    k = (pc + 1 - b) // 2 + 1
                    term = sums[n, pc * c1:(pc + 1) * c1, k * c1:(k + 1) * c1]
                    total = term if total is None else total + term
            if a == 0:
                for pc in range(2):
                    k = (pc + 1 - b) // 2 + 1
                    total = total + corner[pc * c1:(pc + 1) * c1, k * c1:(k + 1) * c1]
            total = total * 0.25
            for part in range(per_tap):
                put((3 * a + b) * per_tap + part, total[part * unit:(part + 1) * unit])

    head = spread[0]
    spread[0] = head * not_first
    spread[rows + 2] = head * is_first
    folded = dot(fields_t[:, :half], spread[rows + 2])
    for a in range(3):
        around = spread[2 - a:2 - a + rows].reshape(rows * half, 4 * c1)
        got = dot(fields_t[...], around)
        if a == 0:
            got = got + folded
        for b in range(3):
            even = got[:c0, (2 - b) * c1:(3 - b) * c1]
            odd = got[c0:, (3 - b) * c1:(4 - b) * c1]
            put(9 * per_tap + 3 * a + b, even + odd)
    if keep.shape[0] > count * unit:
        keep[count * unit:] = jnp.zeros((keep.shape[0] - count * unit, c1), F32)


def columns_kernel(lats, col_a, col_b, act_ends, field_ends, taps, keep, raw_ends, slope_ends, out_ends,
                   ends, own, other, lhs, values, right_hand, total):
    band, first, last, _, core = position(lats)
    c1 = act_ends.shape[2]
    rows = act_ends.shape[1]
    pooled = rows // 2
    c0 = field_ends.shape[0] // 2
    span, size = raw_ends.shape[1], col_a.shape[0]
    got_a, got_b = col_a[...].astype(F32), col_b[...].astype(F32)
    message = jnp.concatenate([jnp.where(core == 0, got_b, got_a), jnp.where(core == 0, got_a, got_b)], 1)
    at = lax.broadcasted_iota(jnp.int32, (size, 2 * c1), 0)
    message = jnp.where(jnp.logical_and(at == rows + pooled + 3, last), 0.0, message).astype(BF16)

    n = lax.broadcasted_iota(jnp.int32, (3 * span, size), 0)
    k = lax.broadcasted_iota(jnp.int32, (3 * span, size), 1)
    row = n % span
    want = (row - n // span + 2) // 2 - 1
    place = jnp.where(want < 0, rows + pooled + 2, jnp.where(want == pooled, rows + pooled + 3, rows + want))
    beside = dot(one_at(jnp.logical_and(k == place, row < rows + 2)), message)
    n = lax.broadcasted_iota(jnp.int32, (3 * span, out_ends.shape[1]), 0)
    k = lax.broadcasted_iota(jnp.int32, (3 * span, out_ends.shape[1]), 1)
    row = n % span
    want = (row - n // span + 2) // 2
    pick = one_at(jnp.logical_and(k == want, row < rows + 2))
    within = dot(pick, jnp.concatenate([out_ends[0], out_ends[1]], 1).astype(BF16))
    n = lax.broadcasted_iota(jnp.int32, (span, size), 0)
    k = lax.broadcasted_iota(jnp.int32, (span, size), 1)
    place = jnp.where(n == 0, rows + pooled, jnp.where(n == rows + 1, rows + pooled + 1, n - 1))
    saved = dot(one_at(jnp.logical_and(k == place, n < rows + 2)), message)
    incline = slope_of(saved, cdf_of(saved))

    head = lax.broadcasted_iota(jnp.int32, (span, 2 * c1), 0) < 2
    turned = jnp.logical_and(head, first)
    lhs[...] = jnp.zeros_like(lhs)
    rights = []
    for a in range(4):
        sides, inner = (x[min(a, 2) * span:(min(a, 2) + 1) * span] for x in (beside, within))
        if a == 2:
            sides, inner = jnp.where(turned, 0.0, sides), jnp.where(turned, 0.0, inner)
        if a == 3:
            sides, inner = jnp.where(turned, sides, 0.0), jnp.where(turned, inner, 0.0)
        rights.append(sides)
        sides, inner = sides.astype(BF16), inner.astype(BF16)
        left, right = sides[:, :c1], sides[:, c1:]
        lhs[a, :span, c1:2 * c1] = left
        lhs[a, :span, 2 * c1:3 * c1] = inner[:, :c1]
        lhs[a, :span, 3 * c1:] = left
        lhs[a, span:2 * span, :c1] = left
        lhs[a, 2 * span:3 * span, :c1] = inner[:, c1:]
        lhs[a, 2 * span:3 * span, c1:2 * c1] = right
        lhs[a, 2 * span:3 * span, 3 * c1:] = right
        lhs[a, 3 * span:, 2 * c1:3 * c1] = right
    found = dot_nt(lhs[0], taps[0]) + dot_nt(lhs[1], taps[1]) + dot_nt(lhs[2], taps[2]) + dot_nt(lhs[3], taps[0])
    row = lax.broadcasted_iota(jnp.int32, (span, c1), 0)
    inside = jnp.where(jnp.logical_or(row > rows + 1, jnp.logical_and(row == rows + 1, last)), 0.0, 1.0)
    values[0] = found[:span, c1:] * incline[:, :c1] * inside
    values[1] = (raw_ends[0] + found[span:2 * span, :c1]) * slope_ends[0] * inside
    values[2] = (raw_ends[1] + found[3 * span:, c1:]) * slope_ends[1] * inside
    values[3] = found[2 * span:3 * span, :c1] * incline[:, c1:] * inside
    ends[...] = values[...].astype(BF16)

    total[...] = keep[...]
    for side, b in ((0, 2), (1, 0)):
        around = jnp.concatenate([x[1:rows + 1, side * c1:(side + 1) * c1] for x in rights], 1).astype(BF16)
        terms = lax.dot_general(act_ends[side].astype(BF16), around, (((0,), (0,)), ((), ())),
                                preferred_element_type=F32) * 0.25
        for a in range(3):
            term = terms[:, a * c1:(a + 1) * c1]
            if a == 0:
                term = term + terms[:, 3 * c1:]
            low = (3 * a + b) * c1
            total[low:low + c1] = total[low:low + c1] + term
    right_hand[...] = jnp.zeros_like(right_hand)
    top = lax.broadcasted_iota(jnp.int32, (rows, c1), 0) == 0
    over = jnp.logical_and(top, first)
    for a in range(4):
        for j in range(4):
            value = values[j, 2 - min(a, 2):2 - min(a, 2) + rows]
            if a == 2:
                value = jnp.where(over, 0.0, value)
            if a == 3:
                value = jnp.where(over, value, 0.0)
            right_hand[a, j // 2 * rows:(j // 2 + 1) * rows, j * c1:(j + 1) * c1] = value.astype(BF16)
    for a in range(3):
        got = dot(field_ends[...], right_hand[a])
        if a == 0:
            got = got + dot(field_ends[...], right_hand[3])
        for b in range(3):
            even = got[:c0, (2 - b) * c1:(3 - b) * c1]
            odd = got[c0:, (3 - b) * c1:(4 - b) * c1]
            low = 9 * c1 + (3 * a + b) * c0
            total[low:low + c0] = total[low:low + c0] + even + odd

    held = own.shape[0]
    block = held // lats
    mine = half_held()
    for target, half_of in ((own, mine), (other, 1 - mine)):
        for far in range(lats):
            start = half_of * held + (band ^ far) * block
            target[far * block:(far + 1) * block] = total[pl.ds(pl.multiple_of(start, block), block), :]


def last_kernel(lats, part, ends, taps, out, spread, values, total, turned):
    rows, c0, cols = out.shape
    half = cols // 2
    c2 = 2 * c0
    depth = spread.shape[2]
    first = position(lats)[1]
    spread[...] = part[...]
    c1 = depth // 4
    for j in range(4):
        values[:, j * c1:(j + 1) * c1] = ends[j].astype(F32)
    at = lax.broadcasted_iota(jnp.int32, (16, 2 * c1), 0)
    for r in range(rows + 3):
        n = 0 if r == rows + 2 else r
        for side, (low, spot) in enumerate(((0, 0), (half - 16, 15))):
            lanes = slice(2 * side * c1, 2 * (side + 1) * c1)
            new = values[n:n + 1, lanes]
            if n == 0:
                new = jnp.where(first == (r != 0), new, 0.0)
            tile = spread[r, low:low + 16, lanes].astype(F32)
            spread[r, low:low + 16, lanes] = jnp.where(at == spot, new, tile).astype(BF16)
    result = dot_nt(taps[:c2], spread[2:rows + 2].reshape(rows * half, depth))
    for a in (1, 2):
        result = result + dot_nt(taps[a * c2:(a + 1) * c2],
                                 spread[2 - a:2 - a + rows].reshape(rows * half, depth))
    total[...] = result
    total[:, :half] = total[:, :half] + dot_nt(taps[:c2], spread[rows + 2])
    for q in range(rows // 2):
        pair = total[:, q * cols:(q + 1) * cols].astype(BF16)
        turned[q, :, :cols] = pair[:c0]
        turned[q, :, cols:] = pair[c0:]
    k = lax.broadcasted_iota(jnp.int32, (2 * cols, 2 * cols), 0)
    n = lax.broadcasted_iota(jnp.int32, (2 * cols, 2 * cols), 1)
    order = one_at(n == ((k % cols) // half) * cols + 2 * (k % half) + k // cols)
    found = dot(turned[...].reshape(rows // 2 * c0, 2 * cols), order).astype(BF16)
    for q in range(rows // 2):
        for rp in range(2):
            out[2 * q + rp] = found[q * c0:(q + 1) * c0, rp * cols:(rp + 1) * cols]


def gather_kernel(mine, theirs, out_first, out_second):
    lats, rows, c1 = mine.shape
    band, held = lax.axis_index("lat"), half_held()
    size = out_second.shape[0]
    total = size + out_first.shape[0]
    for h in range(2):
        for i in range(lats):
            at = (h * lats + i) * rows
            for out, base, end in ((out_second, 0, size), (out_first, size, total)):
                low, high = max(at, base), min(at + rows, end)
                if low < high:
                    here, there = (x[i ^ band, low - at:high - at] for x in (mine, theirs))
                    out[low - base:high - base] = jnp.where(held == h, here, there).astype(F32)


def vmem(count):
    return [pl.BlockSpec(memory_space=pltpu.VMEM)] * count


def far(count):
    return [pl.BlockSpec(memory_space=pl.ANY)] * count


def params(mib):
    return pltpu.CompilerParams(vmem_limit_bytes=mib * 1024 * 1024)


def shape(dims, kind):
    return jax.ShapeDtypeStruct(dims, kind)


def body(inputs, pre_first, grad_out, w_first, w_second):
    rows, cols, c1 = pre_first.shape
    c0 = inputs.shape[2]
    half, pooled = cols // 2, rows // 2
    lats, lons = lax.axis_size("lat"), lax.axis_size("lon")
    depths = lons // 2
    band, place = lax.axis_index("lat"), lax.axis_index("lon")
    core = lax.rem(place, 2)
    even = lax.rem(band, 2) == 0

    edge = -(-(rows + pooled + 4) // 16) * 16
    row_a, row_b, col_a, col_b, held_pre = pl.pallas_call(
        functools.partial(pack_kernel, lats),
        out_shape=(
            pltpu.VMEM((cols + half, c1), BF16),
            pltpu.VMEM((cols + half, c1), BF16),
            pltpu.VMEM((edge, c1), BF16),
            pltpu.VMEM((edge, c1), BF16),
            pltpu.VMEM(pre_first.shape, BF16),
        ),
        in_specs=far(2),
        out_specs=tuple(vmem(5)),
        scratch_shapes=[
            pltpu.VMEM((2, edge, c1), F32),
            pltpu.VMEM(grad_out.shape, BF16),
            pltpu.SemaphoreType.DMA((2,)),
        ],
        compiler_params=params(58),
        cost_estimate=pl.CostEstimate(flops=1000, bytes_accessed=1 << 18, transcendentals=0),
    )(pre_first, grad_out)
    pairs = [(i * lons + j, i * lons + (j + lons // 2) % lons) for i in (0, lats - 1) for j in range(lons)]
    for i in range(1, lats - 1, 2):
        for j in range(lons):
            pairs += [(i * lons + j, (i + 1) * lons + j), ((i + 1) * lons + j, i * lons + j)]
    every = [(i * lons + j, (i ^ 1) * lons + j) for i in range(lats) for j in range(lons)]
    row_b = lax.ppermute(row_b, AREA, pairs)
    row_a = lax.ppermute(row_a, AREA, every)

    slope, act_t, act_ends = pl.pallas_call(
        local_kernel,
        out_shape=(
            shape((rows, half, 2 * c1), F32),
            shape((2, 2 * c1, pooled * half), BF16),
            shape((2, rows, c1), F32),
        ),
        in_specs=vmem(1),
        out_specs=tuple(vmem(3)),
        scratch_shapes=[
            pltpu.VMEM((cols, c1), F32),
            pltpu.VMEM((2, pooled, half, 2 * c1), BF16),
        ],
        compiler_params=params(16),
        cost_estimate=pl.CostEstimate(flops=60 * rows * cols * c1, bytes_accessed=2 << 20,
                                      transcendentals=2 * rows * cols * c1),
    )(held_pre)

    fields_t, field_ends, taps_first, taps_second = pl.pallas_call(
        layout_kernel,
        out_shape=(
            shape((2 * c0, rows * half), BF16),
            shape((2 * c0, 2 * rows), BF16),
            shape((6 * c0, 4 * c1), BF16),
            shape((3, 2 * c1, 4 * c1), BF16),
        ),
        in_specs=vmem(3),
        out_specs=tuple(vmem(4)),
        scratch_shapes=[pltpu.VMEM((rows, c0, 2 * cols), BF16)],
        compiler_params=params(16),
        cost_estimate=pl.CostEstimate(flops=4 * rows * cols * c0 * cols, bytes_accessed=3 << 20, transcendentals=0),
    )(jnp.transpose(inputs, (0, 2, 1)), w_first, w_second)
    row_b, row_a, slope, fields_t = lax.optimization_barrier((row_b, row_a, slope, fields_t))

    def corners(at):
        places = (at * (cols - 1), cols + at * (half - 1))
        above, below = (jnp.where(even, one, two) for one, two in ((row_b, row_a), (row_a, row_b)))
        return jnp.concatenate([part[p:p + 1] for p in places for part in (above, below)], 0)

    low, high = corners(0), corners(1)
    pad = jnp.zeros((edge - rows - pooled - 4, c1), BF16)
    col_a = jnp.concatenate([col_a[:rows + pooled], jnp.where(core == 0, high, low), pad], 0)
    col_b = jnp.concatenate([col_b[:rows + pooled], jnp.where(core == 0, low, high), pad], 0)
    col_b = lax.ppermute(col_b, "lon", [(i, (i + 2 * (i % 2) - 1) % lons) for i in range(lons)])
    col_a = lax.ppermute(col_a, "lon", [(i, i ^ 1) for i in range(lons)])

    block = -(-9 * (c1 + c0) // (32 * lats)) * 16
    held = lats * block
    reach = -(-(rows + 2) // 16) * 16
    spread, keep, raw_ends, slope_ends, out_ends = pl.pallas_call(
        functools.partial(middle_kernel, lats),
        out_shape=(
            shape((rows + 3, half, 4 * c1), BF16),
            shape((2 * held, c1), F32),
            shape((2, reach, c1), F32),
            shape((2, reach, c1), F32),
            shape((2, -(-(pooled + 2) // 16) * 16, c1), F32),
        ),
        in_specs=vmem(7),
        out_specs=tuple(vmem(5)),
        scratch_shapes=[
            pltpu.VMEM((pooled + 2, half, c1), F32),
            pltpu.VMEM((pooled + 2, half, 4 * c1), BF16),
            pltpu.VMEM((3, pooled, half, 2 * c1), F32),
            pltpu.VMEM((4, half, 2 * c1), F32),
            pltpu.VMEM((cols, c1), F32),
            pltpu.VMEM((4, 2 * c1, 3 * c1), F32),
            pltpu.VMEM((2 * c1, 3 * c1), F32),
        ],
        compiler_params=params(16),
        cost_estimate=pl.CostEstimate(flops=2 * rows * cols * c1 * 9 * (2 * c1 + c0), bytes_accessed=8 << 20,
                                      transcendentals=0),
    )(grad_out, row_a, row_b, slope, act_t, fields_t, taps_second)
    col_a, col_b, keep = lax.optimization_barrier((col_a, col_b, keep))

    ends, own, other = pl.pallas_call(
        functools.partial(columns_kernel, lats),
        out_shape=(
            shape((4, reach, c1), BF16),
            shape((held, c1), F32),
            shape((held, c1), F32),
        ),
        in_specs=vmem(9),
        out_specs=tuple(vmem(3)),
        scratch_shapes=[
            pltpu.VMEM((4, 4 * reach, 4 * c1), BF16),
            pltpu.VMEM((4, reach, c1), F32),
            pltpu.VMEM((4, 2 * rows, 4 * c1), BF16),
            pltpu.VMEM((2 * held, c1), F32),
        ],
        compiler_params=params(16),
        cost_estimate=pl.CostEstimate(flops=1 << 28, bytes_accessed=3 << 20, transcendentals=0),
    )(col_a, col_b, act_ends, field_ends, taps_second, keep, raw_ends, slope_ends, out_ends)

    swap = [(i, i ^ 1) for i in range(lons)]

    def between_chips(value, over_lat, over_lon):
        turn = odd(over_lat) ^ odd(over_lon)
        return lax.ppermute(value, AREA, [
            (i * lons + j, (i ^ over_lat) * lons + (j ^ (2 * over_lon) ^ turn)) for i in range(lats) for j in range(lons)])

    parts = (own + lax.ppermute(other, "lon", swap)).reshape(lats, block, c1)
    sent = [parts[far].astype(BF16) for far in range(1, lats)]
    *sent, ends = lax.optimization_barrier((*sent, ends))
    got = [between_chips(sent[far - 1], far, 0) for far in reversed(range(1, lats))]
    grad_inputs = pl.pallas_call(
        functools.partial(last_kernel, lats),
        out_shape=shape((rows, c0, cols), BF16),
        in_specs=vmem(3),
        out_specs=vmem(1)[0],
        scratch_shapes=[
            pltpu.VMEM((rows + 3, half, 4 * c1), BF16),
            pltpu.VMEM((reach, 4 * c1), F32),
            pltpu.VMEM((2 * c0, rows * half), F32),
            pltpu.VMEM((pooled, c0, 2 * cols), BF16),
        ],
        compiler_params=params(12),
        cost_estimate=pl.CostEstimate(flops=2 * rows * cols * c1 * 9 * c0, bytes_accessed=3 << 20, transcendentals=0),
    )(spread, ends, taps_first)
    *got, grad_inputs = lax.optimization_barrier((*got, grad_inputs))
    total = parts[0]
    for value in got:
        total = total + value.astype(F32)
    part = total.astype(BF16)
    terms = [part] + [between_chips(part, 0, far) for far in range(1, depths)]
    terms = [term.astype(F32) for term in terms]
    while len(terms) > 1:
        terms = [terms[k] + terms[k + 1] for k in range(0, len(terms), 2)]
    part = terms[0].astype(BF16)
    mine = jnp.stack([part] + [between_chips(part, far, 0) for far in range(1, lats)], 0)
    theirs = lax.ppermute(mine, "lon", swap)

    grad_w_first, grad_w_second = pl.pallas_call(
        gather_kernel,
        out_shape=(shape((9 * c0, c1), F32), shape((9 * c1, c1), F32)),
        in_specs=vmem(2),
        out_specs=tuple(vmem(2)),
        compiler_params=params(8),
        cost_estimate=pl.CostEstimate(flops=1000, bytes_accessed=3 << 19, transcendentals=0),
    )(mine, theirs)
    return (jnp.transpose(grad_inputs, (0, 2, 1)), grad_w_first.reshape(w_first.shape),
            grad_w_second.reshape(w_second.shape))


def solution(mesh):
    in_specs = (P("lat", "lon", None), P("lat", "lon", None), P("lat", "lon", None), P(), P())
    out_specs = (P("lat", "lon", None), P(), P())
    return jax.shard_map(body, mesh=mesh, in_specs=in_specs, out_specs=out_specs, check_vma=False)
```

```python
import functools

import jax
import jax.numpy as jnp
from jax import lax
from jax.experimental import pallas as pl
from jax.experimental.pallas import tpu as pltpu
from jax.sharding import PartitionSpec as P

inv_root = 0.7071067811865476
density = 0.3989422804014327

F32 = jnp.float32
BF16 = jnp.bfloat16
AREA = ("lat", "lon")


def cdf_of(value):
    return 0.5 * (1.0 + lax.erf(value * inv_root))


def slope_of(value, cdf):
    return 0.25 * (cdf + value * jnp.exp(-0.5 * value * value) * density)


def dot(left, right):
    return jnp.dot(left, right, preferred_element_type=F32)


def dot_nt(left, right):
    return lax.dot_general(left, right, (((1,), (1,)), ((), ())), preferred_element_type=F32)


def position(lats):
    band, place = lax.axis_index("lat"), lax.axis_index("lon")
    return band, band == 0, band == lats - 1, lax.rem(band, 2) == 0, lax.rem(place, 2)


def odd(value):
    for shift in (4, 2, 1):
        value = value ^ (value >> shift)
    return value & 1


def half_held():
    band, place = lax.axis_index("lat"), lax.axis_index("lon")
    return odd(band) ^ odd(place // 2) ^ (place % 2)


def pack_kernel(lats, pre_far, grad_far, row_a, row_b, col_a, col_b, pre, hold, grad_out, sems):
    copies = [pltpu.make_async_copy(pre_far, pre, sems.at[0]), pltpu.make_async_copy(grad_far, grad_out, sems.at[1])]
    for copy in copies:
        copy.start()
    for copy in copies:
        copy.wait()
    rows, cols, c1 = pre.shape
    pooled, half = grad_out.shape[:2]
    _, _, _, even, core = position(lats)
    for message, low in ((row_a, ~even), (row_b, even)):
        message[:cols] = pre[jnp.where(low, 0, rows - 1)]
        message[cols:] = grad_out[jnp.where(low, 0, pooled - 1)]
    hold[:, rows + pooled:] = jnp.zeros((2, hold.shape[1] - rows - pooled, c1), F32)
    for side, (p, g) in enumerate(((0, 0), (cols - 16, half - 16))):
        at = 15 * side
        for r in range(rows):
            hold[side, r:r + 1] = pre[r, p:p + 16].astype(F32)[at:at + 1]
        for i in range(pooled):
            hold[side, rows + i:rows + i + 1] = grad_out[i, g:g + 16].astype(F32)[at:at + 1]
    col_a[...] = hold[1 - core].astype(BF16)
    col_b[...] = hold[core].astype(BF16)


def one_at(where):
    return jnp.where(where, 1.0, 0.0).astype(BF16)


def local_kernel(pre, slope, act_t, act_ends, line, act_s):
    rows, cols, c1 = pre.shape
    half = cols // 2

    def one_row(r, carry):
        line[...] = pre[r].astype(F32)
        for pc in range(2):
            value = line[pl.ds(pc, half, stride=2), :]
            cdf = cdf_of(value)
            act = value * cdf
            act_s[r % 2, r // 2, :, pc * c1:(pc + 1) * c1] = act.astype(BF16)
            act_ends[pc, pl.ds(r, 1), :] = act[pc * (half - 1):pc * (half - 1) + 1]
            slope[r, :, pc * c1:(pc + 1) * c1] = slope_of(value, cdf)
        return carry

    lax.fori_loop(0, rows, one_row, 0)
    for pr in range(2):
        act_t[pr] = act_s[pr].reshape(rows // 2 * half, 2 * c1).T


def layout_kernel(fields, w_first, w_second, fields_t, field_ends, taps_first, taps_second, turned):
    rows, c0, cols = fields.shape
    c1 = w_first.shape[3]
    half = cols // 2
    col = lax.broadcasted_iota(jnp.int32, (cols, 2 * cols), 0)
    lane = lax.broadcasted_iota(jnp.int32, (cols, 2 * cols), 1)
    turn = lane // cols
    parity = (lane % cols) // half
    parity = parity + turn - 2 * parity * turn
    order = one_at(col == 2 * (lane % half) + parity)
    turned[...] = dot(fields[...].reshape(rows * c0, cols), order).astype(BF16).reshape(rows, c0, 2 * cols)
    low = lax.broadcasted_iota(jnp.int32, (c0, cols), 1) < half
    for q in range(rows // 2):
        fields_t[:c0, q * cols:(q + 1) * cols] = jnp.where(low, turned[2 * q, :, :cols], turned[2 * q + 1, :, cols:])
        fields_t[c0:, q * cols:(q + 1) * cols] = jnp.where(low, turned[2 * q, :, cols:], turned[2 * q + 1, :, :cols])
    cell = lax.broadcasted_iota(jnp.int32, (rows * half, 2 * rows), 0)
    n = lax.broadcasted_iota(jnp.int32, (rows * half, 2 * rows), 1)
    pick = one_at(cell == (n % rows) * half + (n // rows) * (half - 1))
    field_ends[...] = dot(fields_t[...], pick).astype(BF16)
    taps_second[...] = jnp.zeros_like(taps_second)
    taps_first[...] = jnp.zeros_like(taps_first)
    for a in range(3):
        for pc, blocks in ((0, (2, 1, None, 0)), (1, (None, 2, 0, 1))):
            for k, b in enumerate(blocks):
                if b is not None:
                    taps_second[a, pc * c1:(pc + 1) * c1, k * c1:(k + 1) * c1] = w_second[a, b]
        for pc, blocks in ((0, (2, 1, 0, None)), (1, (None, 2, 1, 0))):
            for k, b in enumerate(blocks):
                if b is not None:
                    start = (2 * a + pc) * c0
                    taps_first[start:start + c0, k * c1:(k + 1) * c1] = w_first[a, b]


def middle_kernel(lats, grad_out, row_a, row_b, slope, act_t, fields_t, taps,
                  spread, keep, raw_ends, slope_ends, out_ends,
                  grid, wide, prods, ends, line, sums, corner):
    _, first, last, even, _ = position(lats)
    top = jnp.where(even, row_b[...], row_a[...])
    bottom = jnp.where(even, row_a[...], row_b[...])
    rows, half, c2 = slope.shape
    c1 = c2 // 2
    pooled = rows // 2
    c0 = fields_t.shape[0] // 2
    cells = pooled * half
    raw_ends[...] = jnp.zeros_like(raw_ends)
    slope_ends[...] = jnp.zeros_like(slope_ends)
    out_ends[...] = jnp.zeros_like(out_ends)

    grid[1:pooled + 1] = grad_out[...].astype(F32)
    grid[0] = top[2 * half:, :].astype(F32)
    outside = jnp.where(last, 0.0, 1.0)
    grid[pooled + 1] = bottom[2 * half:, :].astype(F32) * outside
    at = lax.broadcasted_iota(jnp.int32, (half, c1), 0)
    for i in range(pooled + 2):
        here = grid[i]
        out_ends[0, i:i + 1] = here[:1]
        out_ends[1, i:i + 1] = here[half - 1:]
        wide[i, :, :c1] = jnp.where(at == 0, 0.0, pltpu.roll(here, 1, 0)).astype(BF16)
        wide[i, :, c1:2 * c1] = here.astype(BF16)
        wide[i, :, 2 * c1:3 * c1] = jnp.where(at == half - 1, 0.0, pltpu.roll(here, half - 1, 0)).astype(BF16)
        wide[i, :, 3 * c1:] = here.astype(BF16)

    flat = wide[1:pooled + 1].reshape(cells, 4 * c1)
    for a in range(3):
        prods[a] = dot_nt(flat, taps[a]).reshape(pooled, half, c2)
    fold = jnp.where(first, taps[0], taps[2])
    ends[0] = dot_nt(wide[0], fold)
    ends[1] = dot_nt(wide[0], taps[1])
    ends[2] = dot_nt(wide[pooled + 1], taps[0])
    ends[3] = dot_nt(wide[pooled + 1], taps[1])

    def place(r, total, incline):
        inner = total * incline
        raw_ends[0, pl.ds(r, 1), :] = total[:1, :c1]
        raw_ends[1, pl.ds(r, 1), :] = total[half - 1:, c1:]
        slope_ends[0, pl.ds(r, 1), :] = incline[:1, :c1]
        slope_ends[1, pl.ds(r, 1), :] = incline[half - 1:, c1:]
        even, odd = inner[:, :c1], inner[:, c1:]
        spread[r, :, :c1] = jnp.where(at == 0, 0.0, pltpu.roll(odd, 1, 0)).astype(BF16)
        spread[r, :, c1:2 * c1] = jnp.where(at == 0, 0.0, even).astype(BF16)
        spread[r, :, 2 * c1:3 * c1] = jnp.where(at == half - 1, 0.0, odd).astype(BF16)
        spread[r, :, 3 * c1:] = jnp.where(at == half - 1, 0.0, pltpu.roll(even, half - 1, 0)).astype(BF16)

    def halo_slope(message):
        line[...] = message[:2 * half, :].astype(F32)
        both = [line[pl.ds(pc, half, stride=2), :] for pc in range(2)]
        return jnp.concatenate([slope_of(v, cdf_of(v)) for v in both], axis=1)

    place(0, ends[0] + ends[1] + prods[0, 0], halo_slope(top))
    place(1, ends[0] + prods[1, 0] + prods[0, 0], slope[0])

    def pair(i, carry):
        middle = prods[2, i] + prods[1, i]
        place(2 * i + 2, middle + prods[0, i + 1], slope[2 * i + 1])
        place(2 * i + 3, prods[2, i] + prods[1, i + 1] + prods[0, i + 1], slope[2 * i + 2])
        return carry

    lax.fori_loop(0, pooled - 1, pair, 0)
    final = prods[2, pooled - 1]
    place(rows, final + prods[1, pooled - 1] + ends[2], slope[rows - 1])
    place(rows + 1, (final + ends[3] + ends[2]) * outside, halo_slope(bottom))

    is_first = jnp.where(first, 1.0, 0.0).astype(BF16)
    not_first = jnp.where(first, 0.0, 1.0).astype(BF16)
    above = wide[0, :, :3 * c1]
    wide[0, :, :3 * c1] = above * not_first
    for n, (pr, start) in enumerate(((0, 0), (0, 1), (1, 1), (1, 2))):
        around = wide[start:start + pooled, :, :3 * c1].reshape(cells, 3 * c1)
        sums[n] = dot(act_t[pr], around)
    corner[...] = dot(act_t[0, :, :half], above * is_first)

    unit = c0
    per_tap = c1 // unit
    count = 9 * per_tap + 9

    def put(k, value):
        keep[k * unit:(k + 1) * unit, :] = value

    pieces = {0: ((0, 1), (1, 3)), 1: ((0, 1), (1, 2)), 2: ((0, 0), (1, 2))}
    for a in range(3):
        for b in range(3):
            total = None
            for pr, n in pieces[a]:
                for pc in range(2):
                    k = (pc + 1 - b) // 2 + 1
                    term = sums[n, pc * c1:(pc + 1) * c1, k * c1:(k + 1) * c1]
                    total = term if total is None else total + term
            if a == 0:
                for pc in range(2):
                    k = (pc + 1 - b) // 2 + 1
                    total = total + corner[pc * c1:(pc + 1) * c1, k * c1:(k + 1) * c1]
            total = total * 0.25
            for part in range(per_tap):
                put((3 * a + b) * per_tap + part, total[part * unit:(part + 1) * unit])

    head = spread[0]
    spread[0] = head * not_first
    spread[rows + 2] = head * is_first
    folded = dot(fields_t[:, :half], spread[rows + 2])
    for a in range(3):
        around = spread[2 - a:2 - a + rows].reshape(rows * half, 4 * c1)
        got = dot(fields_t[...], around)
        if a == 0:
            got = got + folded
        for b in range(3):
            even = got[:c0, (2 - b) * c1:(3 - b) * c1]
            odd = got[c0:, (3 - b) * c1:(4 - b) * c1]
            put(9 * per_tap + 3 * a + b, even + odd)
    if keep.shape[0] > count * unit:
        keep[count * unit:] = jnp.zeros((keep.shape[0] - count * unit, c1), F32)


def columns_kernel(lats, col_a, col_b, act_ends, field_ends, taps, keep, raw_ends, slope_ends, out_ends,
                   ends, own, other, lhs, values, right_hand, total):
    band, first, last, _, core = position(lats)
    c1 = act_ends.shape[2]
    rows = act_ends.shape[1]
    pooled = rows // 2
    c0 = field_ends.shape[0] // 2
    span, size = raw_ends.shape[1], col_a.shape[0]
    got_a, got_b = col_a[...].astype(F32), col_b[...].astype(F32)
    message = jnp.concatenate([jnp.where(core == 0, got_b, got_a), jnp.where(core == 0, got_a, got_b)], 1)
    at = lax.broadcasted_iota(jnp.int32, (size, 2 * c1), 0)
    message = jnp.where(jnp.logical_and(at == rows + pooled + 3, last), 0.0, message).astype(BF16)

    n = lax.broadcasted_iota(jnp.int32, (3 * span, size), 0)
    k = lax.broadcasted_iota(jnp.int32, (3 * span, size), 1)
    row = n % span
    want = (row - n // span + 2) // 2 - 1
    place = jnp.where(want < 0, rows + pooled + 2, jnp.where(want == pooled, rows + pooled + 3, rows + want))
    beside = dot(one_at(jnp.logical_and(k == place, row < rows + 2)), message)
    n = lax.broadcasted_iota(jnp.int32, (3 * span, out_ends.shape[1]), 0)
    k = lax.broadcasted_iota(jnp.int32, (3 * span, out_ends.shape[1]), 1)
    row = n % span
    want = (row - n // span + 2) // 2
    pick = one_at(jnp.logical_and(k == want, row < rows + 2))
    within = dot(pick, jnp.concatenate([out_ends[0], out_ends[1]], 1).astype(BF16))
    n = lax.broadcasted_iota(jnp.int32, (span, size), 0)
    k = lax.broadcasted_iota(jnp.int32, (span, size), 1)
    place = jnp.where(n == 0, rows + pooled, jnp.where(n == rows + 1, rows + pooled + 1, n - 1))
    saved = dot(one_at(jnp.logical_and(k == place, n < rows + 2)), message)
    incline = slope_of(saved, cdf_of(saved))

    head = lax.broadcasted_iota(jnp.int32, (span, 2 * c1), 0) < 2
    turned = jnp.logical_and(head, first)
    lhs[...] = jnp.zeros_like(lhs)
    rights = []
    for a in range(4):
        sides, inner = (x[min(a, 2) * span:(min(a, 2) + 1) * span] for x in (beside, within))
        if a == 2:
            sides, inner = jnp.where(turned, 0.0, sides), jnp.where(turned, 0.0, inner)
        if a == 3:
            sides, inner = jnp.where(turned, sides, 0.0), jnp.where(turned, inner, 0.0)
        rights.append(sides)
        sides, inner = sides.astype(BF16), inner.astype(BF16)
        left, right = sides[:, :c1], sides[:, c1:]
        lhs[a, :span, c1:2 * c1] = left
        lhs[a, :span, 2 * c1:3 * c1] = inner[:, :c1]
        lhs[a, :span, 3 * c1:] = left
        lhs[a, span:2 * span, :c1] = left
        lhs[a, 2 * span:3 * span, :c1] = inner[:, c1:]
        lhs[a, 2 * span:3 * span, c1:2 * c1] = right
        lhs[a, 2 * span:3 * span, 3 * c1:] = right
        lhs[a, 3 * span:, 2 * c1:3 * c1] = right
    found = dot_nt(lhs[0], taps[0]) + dot_nt(lhs[1], taps[1]) + dot_nt(lhs[2], taps[2]) + dot_nt(lhs[3], taps[0])
    row = lax.broadcasted_iota(jnp.int32, (span, c1), 0)
    inside = jnp.where(jnp.logical_or(row > rows + 1, jnp.logical_and(row == rows + 1, last)), 0.0, 1.0)
    values[0] = found[:span, c1:] * incline[:, :c1] * inside
    values[1] = (raw_ends[0] + found[span:2 * span, :c1]) * slope_ends[0] * inside
    values[2] = (raw_ends[1] + found[3 * span:, c1:]) * slope_ends[1] * inside
    values[3] = found[2 * span:3 * span, :c1] * incline[:, c1:] * inside
    ends[...] = values[...].astype(BF16)

    total[...] = keep[...]
    for side, b in ((0, 2), (1, 0)):
        around = jnp.concatenate([x[1:rows + 1, side * c1:(side + 1) * c1] for x in rights], 1).astype(BF16)
        terms = lax.dot_general(act_ends[side].astype(BF16), around, (((0,), (0,)), ((), ())),
                                preferred_element_type=F32) * 0.25
        for a in range(3):
            term = terms[:, a * c1:(a + 1) * c1]
            if a == 0:
                term = term + terms[:, 3 * c1:]
            low = (3 * a + b) * c1
            total[low:low + c1] = total[low:low + c1] + term
    right_hand[...] = jnp.zeros_like(right_hand)
    top = lax.broadcasted_iota(jnp.int32, (rows, c1), 0) == 0
    over = jnp.logical_and(top, first)
    for a in range(4):
        for j in range(4):
            value = values[j, 2 - min(a, 2):2 - min(a, 2) + rows]
            if a == 2:
                value = jnp.where(over, 0.0, value)
            if a == 3:
                value = jnp.where(over, value, 0.0)
            right_hand[a, j // 2 * rows:(j // 2 + 1) * rows, j * c1:(j + 1) * c1] = value.astype(BF16)
    for a in range(3):
        got = dot(field_ends[...], right_hand[a])
        if a == 0:
            got = got + dot(field_ends[...], right_hand[3])
        for b in range(3):
            even = got[:c0, (2 - b) * c1:(3 - b) * c1]
            odd = got[c0:, (3 - b) * c1:(4 - b) * c1]
            low = 9 * c1 + (3 * a + b) * c0
            total[low:low + c0] = total[low:low + c0] + even + odd

    held = own.shape[0]
    block = held // lats
    mine = half_held()
    for target, half_of in ((own, mine), (other, 1 - mine)):
        for far in range(lats):
            start = half_of * held + (band ^ far) * block
            target[far * block:(far + 1) * block] = total[pl.ds(pl.multiple_of(start, block), block), :]


def last_kernel(lats, part, ends, taps, out, spread, values, total, turned):
    rows, c0, cols = out.shape
    half = cols // 2
    c2 = 2 * c0
    depth = spread.shape[2]
    first = position(lats)[1]
    spread[...] = part[...]
    c1 = depth // 4
    for j in range(4):
        values[:, j * c1:(j + 1) * c1] = ends[j].astype(F32)
    at = lax.broadcasted_iota(jnp.int32, (16, 2 * c1), 0)
    for r in range(rows + 3):
        n = 0 if r == rows + 2 else r
        for side, (low, spot) in enumerate(((0, 0), (half - 16, 15))):
            lanes = slice(2 * side * c1, 2 * (side + 1) * c1)
            new = values[n:n + 1, lanes]
            if n == 0:
                new = jnp.where(first == (r != 0), new, 0.0)
            tile = spread[r, low:low + 16, lanes].astype(F32)
            spread[r, low:low + 16, lanes] = jnp.where(at == spot, new, tile).astype(BF16)
    result = dot_nt(taps[:c2], spread[2:rows + 2].reshape(rows * half, depth))
    for a in (1, 2):
        result = result + dot_nt(taps[a * c2:(a + 1) * c2],
                                 spread[2 - a:2 - a + rows].reshape(rows * half, depth))
    total[...] = result
    total[:, :half] = total[:, :half] + dot_nt(taps[:c2], spread[rows + 2])
    for q in range(rows // 2):
        pair = total[:, q * cols:(q + 1) * cols].astype(BF16)
        turned[q, :, :cols] = pair[:c0]
        turned[q, :, cols:] = pair[c0:]
    k = lax.broadcasted_iota(jnp.int32, (2 * cols, 2 * cols), 0)
    n = lax.broadcasted_iota(jnp.int32, (2 * cols, 2 * cols), 1)
    order = one_at(n == ((k % cols) // half) * cols + 2 * (k % half) + k // cols)
    found = dot(turned[...].reshape(rows // 2 * c0, 2 * cols), order).astype(BF16)
    for q in range(rows // 2):
        for rp in range(2):
            out[2 * q + rp] = found[q * c0:(q + 1) * c0, rp * cols:(rp + 1) * cols]


def gather_kernel(mine, theirs, out_first, out_second, whole, sems):
    lats, rows, c1 = mine.shape
    band, held = lax.axis_index("lat"), half_held()
    size = out_second.shape[0]
    total = size + out_first.shape[0]
    copies = []
    for h in range(2):
        for i in range(lats):
            at = (h * lats + i) * rows
            here, there = (x[i ^ band].astype(F32) for x in (mine, theirs))
            whole[at:at + rows] = jnp.where(held == h, here, there)
            for out, base, end in ((out_second, 0, size), (out_first, size, total)):
                low, high = max(at, base), min(at + rows, end)
                if low < high:
                    copies.append(pltpu.make_async_copy(whole.at[pl.ds(low, high - low)],
                                                        out.at[pl.ds(low - base, high - low)], sems.at[len(copies)]))
                    copies[-1].start()
    for copy in copies:
        copy.wait()


def vmem(count):
    return [pl.BlockSpec(memory_space=pltpu.VMEM)] * count


def far(count):
    return [pl.BlockSpec(memory_space=pl.ANY)] * count


def params(mib):
    return pltpu.CompilerParams(vmem_limit_bytes=mib * 1024 * 1024)


def shape(dims, kind):
    return jax.ShapeDtypeStruct(dims, kind)


def body(inputs, pre_first, grad_out, w_first, w_second):
    rows, cols, c1 = pre_first.shape
    c0 = inputs.shape[2]
    half, pooled = cols // 2, rows // 2
    lats, lons = lax.axis_size("lat"), lax.axis_size("lon")
    depths = lons // 2
    band, place = lax.axis_index("lat"), lax.axis_index("lon")
    core = lax.rem(place, 2)
    even = lax.rem(band, 2) == 0

    edge = -(-(rows + pooled + 4) // 16) * 16
    row_a, row_b, col_a, col_b, held_pre = pl.pallas_call(
        functools.partial(pack_kernel, lats),
        out_shape=(
            pltpu.VMEM((cols + half, c1), BF16),
            pltpu.VMEM((cols + half, c1), BF16),
            pltpu.VMEM((edge, c1), BF16),
            pltpu.VMEM((edge, c1), BF16),
            pltpu.VMEM(pre_first.shape, BF16),
        ),
        in_specs=far(2),
        out_specs=tuple(vmem(5)),
        scratch_shapes=[
            pltpu.VMEM((2, edge, c1), F32),
            pltpu.VMEM(grad_out.shape, BF16),
            pltpu.SemaphoreType.DMA((2,)),
        ],
        compiler_params=params(58),
        cost_estimate=pl.CostEstimate(flops=1000, bytes_accessed=1 << 18, transcendentals=0),
    )(pre_first, grad_out)
    pairs = [(i * lons + j, i * lons + (j + lons // 2) % lons) for i in (0, lats - 1) for j in range(lons)]
    for i in range(1, lats - 1, 2):
        for j in range(lons):
            pairs += [(i * lons + j, (i + 1) * lons + j), ((i + 1) * lons + j, i * lons + j)]
    every = [(i * lons + j, (i ^ 1) * lons + j) for i in range(lats) for j in range(lons)]
    row_b = lax.ppermute(row_b, AREA, pairs)
    row_a = lax.ppermute(row_a, AREA, every)

    slope, act_t, act_ends = pl.pallas_call(
        local_kernel,
        out_shape=(
            shape((rows, half, 2 * c1), F32),
            shape((2, 2 * c1, pooled * half), BF16),
            shape((2, rows, c1), F32),
        ),
        in_specs=vmem(1),
        out_specs=tuple(vmem(3)),
        scratch_shapes=[
            pltpu.VMEM((cols, c1), F32),
            pltpu.VMEM((2, pooled, half, 2 * c1), BF16),
        ],
        compiler_params=params(16),
        cost_estimate=pl.CostEstimate(flops=60 * rows * cols * c1, bytes_accessed=2 << 20,
                                      transcendentals=2 * rows * cols * c1),
    )(held_pre)

    fields_t, field_ends, taps_first, taps_second = pl.pallas_call(
        layout_kernel,
        out_shape=(
            shape((2 * c0, rows * half), BF16),
            shape((2 * c0, 2 * rows), BF16),
            shape((6 * c0, 4 * c1), BF16),
            shape((3, 2 * c1, 4 * c1), BF16),
        ),
        in_specs=vmem(3),
        out_specs=tuple(vmem(4)),
        scratch_shapes=[pltpu.VMEM((rows, c0, 2 * cols), BF16)],
        compiler_params=params(16),
        cost_estimate=pl.CostEstimate(flops=4 * rows * cols * c0 * cols, bytes_accessed=3 << 20, transcendentals=0),
    )(jnp.transpose(inputs, (0, 2, 1)), w_first, w_second)
    row_b, row_a, slope, fields_t = lax.optimization_barrier((row_b, row_a, slope, fields_t))

    def corners(at):
        places = (at * (cols - 1), cols + at * (half - 1))
        above, below = (jnp.where(even, one, two) for one, two in ((row_b, row_a), (row_a, row_b)))
        return jnp.concatenate([part[p:p + 1] for p in places for part in (above, below)], 0)

    low, high = corners(0), corners(1)
    pad = jnp.zeros((edge - rows - pooled - 4, c1), BF16)
    col_a = jnp.concatenate([col_a[:rows + pooled], jnp.where(core == 0, high, low), pad], 0)
    col_b = jnp.concatenate([col_b[:rows + pooled], jnp.where(core == 0, low, high), pad], 0)
    col_b = lax.ppermute(col_b, "lon", [(i, (i + 2 * (i % 2) - 1) % lons) for i in range(lons)])
    col_a = lax.ppermute(col_a, "lon", [(i, i ^ 1) for i in range(lons)])

    block = -(-9 * (c1 + c0) // (32 * lats)) * 16
    held = lats * block
    reach = -(-(rows + 2) // 16) * 16
    spread, keep, raw_ends, slope_ends, out_ends = pl.pallas_call(
        functools.partial(middle_kernel, lats),
        out_shape=(
            shape((rows + 3, half, 4 * c1), BF16),
            shape((2 * held, c1), F32),
            shape((2, reach, c1), F32),
            shape((2, reach, c1), F32),
            shape((2, -(-(pooled + 2) // 16) * 16, c1), F32),
        ),
        in_specs=vmem(7),
        out_specs=tuple(vmem(5)),
        scratch_shapes=[
            pltpu.VMEM((pooled + 2, half, c1), F32),
            pltpu.VMEM((pooled + 2, half, 4 * c1), BF16),
            pltpu.VMEM((3, pooled, half, 2 * c1), F32),
            pltpu.VMEM((4, half, 2 * c1), F32),
            pltpu.VMEM((cols, c1), F32),
            pltpu.VMEM((4, 2 * c1, 3 * c1), F32),
            pltpu.VMEM((2 * c1, 3 * c1), F32),
        ],
        compiler_params=params(16),
        cost_estimate=pl.CostEstimate(flops=2 * rows * cols * c1 * 9 * (2 * c1 + c0), bytes_accessed=8 << 20,
                                      transcendentals=0),
    )(grad_out, row_a, row_b, slope, act_t, fields_t, taps_second)
    col_a, col_b, keep = lax.optimization_barrier((col_a, col_b, keep))

    ends, own, other = pl.pallas_call(
        functools.partial(columns_kernel, lats),
        out_shape=(
            shape((4, reach, c1), BF16),
            shape((held, c1), F32),
            shape((held, c1), F32),
        ),
        in_specs=vmem(9),
        out_specs=tuple(vmem(3)),
        scratch_shapes=[
            pltpu.VMEM((4, 4 * reach, 4 * c1), BF16),
            pltpu.VMEM((4, reach, c1), F32),
            pltpu.VMEM((4, 2 * rows, 4 * c1), BF16),
            pltpu.VMEM((2 * held, c1), F32),
        ],
        compiler_params=params(16),
        cost_estimate=pl.CostEstimate(flops=1 << 28, bytes_accessed=3 << 20, transcendentals=0),
    )(col_a, col_b, act_ends, field_ends, taps_second, keep, raw_ends, slope_ends, out_ends)

    swap = [(i, i ^ 1) for i in range(lons)]

    def between_chips(value, over_lat, over_lon):
        turn = odd(over_lat) ^ odd(over_lon)
        return lax.ppermute(value, AREA, [
            (i * lons + j, (i ^ over_lat) * lons + (j ^ (2 * over_lon) ^ turn)) for i in range(lats) for j in range(lons)])

    parts = (own + lax.ppermute(other, "lon", swap)).reshape(lats, block, c1)
    sent = [parts[far].astype(BF16) for far in range(1, lats)]
    *sent, ends = lax.optimization_barrier((*sent, ends))
    got = [between_chips(sent[far - 1], far, 0) for far in reversed(range(1, lats))]
    grad_inputs = pl.pallas_call(
        functools.partial(last_kernel, lats),
        out_shape=shape((rows, c0, cols), BF16),
        in_specs=vmem(3),
        out_specs=vmem(1)[0],
        scratch_shapes=[
            pltpu.VMEM((rows + 3, half, 4 * c1), BF16),
            pltpu.VMEM((reach, 4 * c1), F32),
            pltpu.VMEM((2 * c0, rows * half), F32),
            pltpu.VMEM((pooled, c0, 2 * cols), BF16),
        ],
        compiler_params=params(12),
        cost_estimate=pl.CostEstimate(flops=2 * rows * cols * c1 * 9 * c0, bytes_accessed=3 << 20, transcendentals=0),
    )(spread, ends, taps_first)
    *got, grad_inputs = lax.optimization_barrier((*got, grad_inputs))
    total = parts[0]
    for value in got:
        total = total + value.astype(F32)
    part = total.astype(BF16)
    terms = [part] + [between_chips(part, 0, far) for far in range(1, depths)]
    terms = [term.astype(F32) for term in terms]
    while len(terms) > 1:
        terms = [terms[k] + terms[k + 1] for k in range(0, len(terms), 2)]
    part = terms[0].astype(BF16)
    mine = [part] + [between_chips(part, far, 0) for far in range(1, lats)]
    theirs = [lax.ppermute(value, "lon", swap) for value in mine]
    mine, theirs = jnp.stack(mine, 0), jnp.stack(theirs, 0)

    grad_w_first, grad_w_second = pl.pallas_call(
        gather_kernel,
        out_shape=(shape((9 * c0, c1), F32), shape((9 * c1, c1), F32)),
        in_specs=vmem(2),
        out_specs=tuple(far(2)),
        scratch_shapes=[pltpu.VMEM((2 * held, c1), F32), pltpu.SemaphoreType.DMA((2 * lats + 2,))],
        compiler_params=params(8),
        cost_estimate=pl.CostEstimate(flops=1000, bytes_accessed=3 << 19, transcendentals=0),
    )(mine, theirs)
    return (jnp.transpose(grad_inputs, (0, 2, 1)), grad_w_first.reshape(w_first.shape),
            grad_w_second.reshape(w_second.shape))


def solution(mesh):
    in_specs = (P("lat", "lon", None), P("lat", "lon", None), P("lat", "lon", None), P(), P())
    out_specs = (P("lat", "lon", None), P(), P())
    return jax.shard_map(body, mesh=mesh, in_specs=in_specs, out_specs=out_specs, check_vma=False)
```

```python
import functools

import jax
import jax.numpy as jnp
from jax import lax
from jax.experimental import pallas as pl
from jax.experimental.pallas import tpu as pltpu
from jax.sharding import PartitionSpec as P

inv_root = 0.7071067811865476
density = 0.3989422804014327

F32 = jnp.float32
BF16 = jnp.bfloat16
AREA = ("lat", "lon")


def cdf_of(value):
    return 0.5 * (1.0 + lax.erf(value * inv_root))


def slope_of(value, cdf):
    return 0.25 * (cdf + value * jnp.exp(-0.5 * value * value) * density)


def dot(left, right):
    return jnp.dot(left, right, preferred_element_type=F32)


def dot_nt(left, right):
    return lax.dot_general(left, right, (((1,), (1,)), ((), ())), preferred_element_type=F32)


def position(lats):
    band, place = lax.axis_index("lat"), lax.axis_index("lon")
    return band, band == 0, band == lats - 1, lax.rem(band, 2) == 0, lax.rem(place, 2)


def odd(value):
    for shift in (4, 2, 1):
        value = value ^ (value >> shift)
    return value & 1


def half_held():
    band, place = lax.axis_index("lat"), lax.axis_index("lon")
    return odd(band) ^ odd(place // 2) ^ (place % 2)


def pack_kernel(lats, pre_far, grad_far, row_a, row_b, col_a, col_b, pre, hold, grad_out, sems):
    copies = [pltpu.make_async_copy(pre_far, pre, sems.at[0]), pltpu.make_async_copy(grad_far, grad_out, sems.at[1])]
    for copy in copies:
        copy.start()
    for copy in copies:
        copy.wait()
    rows, cols, c1 = pre.shape
    pooled, half = grad_out.shape[:2]
    _, _, _, even, core = position(lats)
    for message, low in ((row_a, ~even), (row_b, even)):
        message[:cols] = pre[jnp.where(low, 0, rows - 1)]
        message[cols:] = grad_out[jnp.where(low, 0, pooled - 1)]
    hold[:, rows + pooled:] = jnp.zeros((2, hold.shape[1] - rows - pooled, c1), F32)
    for side, (p, g) in enumerate(((0, 0), (cols - 16, half - 16))):
        at = 15 * side
        for r in range(rows):
            hold[side, r:r + 1] = pre[r, p:p + 16].astype(F32)[at:at + 1]
        for i in range(pooled):
            hold[side, rows + i:rows + i + 1] = grad_out[i, g:g + 16].astype(F32)[at:at + 1]
    col_a[...] = hold[1 - core].astype(BF16)
    col_b[...] = hold[core].astype(BF16)


def one_at(where):
    return jnp.where(where, 1.0, 0.0).astype(BF16)


def local_kernel(pre, slope, act_t, act_ends, line, act_s):
    rows, cols, c1 = pre.shape
    half = cols // 2

    def one_row(r, carry):
        line[...] = pre[r].astype(F32)
        for pc in range(2):
            value = line[pl.ds(pc, half, stride=2), :]
            cdf = cdf_of(value)
            act = value * cdf
            act_s[r % 2, r // 2, :, pc * c1:(pc + 1) * c1] = act.astype(BF16)
            act_ends[pc, pl.ds(r, 1), :] = act[pc * (half - 1):pc * (half - 1) + 1]
            slope[r, :, pc * c1:(pc + 1) * c1] = slope_of(value, cdf)
        return carry

    lax.fori_loop(0, rows, one_row, 0)
    for pr in range(2):
        act_t[pr] = act_s[pr].reshape(rows // 2 * half, 2 * c1).T


def layout_kernel(fields, w_first, w_second, fields_t, field_ends, taps_first, taps_second, turned):
    rows, c0, cols = fields.shape
    c1 = w_first.shape[3]
    half = cols // 2
    col = lax.broadcasted_iota(jnp.int32, (cols, 2 * cols), 0)
    lane = lax.broadcasted_iota(jnp.int32, (cols, 2 * cols), 1)
    turn = lane // cols
    parity = (lane % cols) // half
    parity = parity + turn - 2 * parity * turn
    order = one_at(col == 2 * (lane % half) + parity)
    turned[...] = dot(fields[...].reshape(rows * c0, cols), order).astype(BF16).reshape(rows, c0, 2 * cols)
    low = lax.broadcasted_iota(jnp.int32, (c0, cols), 1) < half
    for q in range(rows // 2):
        fields_t[:c0, q * cols:(q + 1) * cols] = jnp.where(low, turned[2 * q, :, :cols], turned[2 * q + 1, :, cols:])
        fields_t[c0:, q * cols:(q + 1) * cols] = jnp.where(low, turned[2 * q, :, cols:], turned[2 * q + 1, :, :cols])
    cell = lax.broadcasted_iota(jnp.int32, (rows * half, 2 * rows), 0)
    n = lax.broadcasted_iota(jnp.int32, (rows * half, 2 * rows), 1)
    pick = one_at(cell == (n % rows) * half + (n // rows) * (half - 1))
    field_ends[...] = dot(fields_t[...], pick).astype(BF16)
    taps_second[...] = jnp.zeros_like(taps_second)
    taps_first[...] = jnp.zeros_like(taps_first)
    for a in range(3):
        for pc, blocks in ((0, (2, 1, None, 0)), (1, (None, 2, 0, 1))):
            for k, b in enumerate(blocks):
                if b is not None:
                    taps_second[a, pc * c1:(pc + 1) * c1, k * c1:(k + 1) * c1] = w_second[a, b]
        for pc, blocks in ((0, (2, 1, 0, None)), (1, (None, 2, 1, 0))):
            for k, b in enumerate(blocks):
                if b is not None:
                    start = (2 * a + pc) * c0
                    taps_first[start:start + c0, k * c1:(k + 1) * c1] = w_first[a, b]


def middle_kernel(lats, grad_out, row_a, row_b, slope, act_t, fields_t, taps,
                  spread, keep, raw_ends, slope_ends, out_ends,
                  grid, wide, prods, ends, line, sums, corner):
    _, first, last, even, _ = position(lats)
    top = jnp.where(even, row_b[...], row_a[...])
    bottom = jnp.where(even, row_a[...], row_b[...])
    rows, half, c2 = slope.shape
    c1 = c2 // 2
    pooled = rows // 2
    c0 = fields_t.shape[0] // 2
    cells = pooled * half
    raw_ends[...] = jnp.zeros_like(raw_ends)
    slope_ends[...] = jnp.zeros_like(slope_ends)
    out_ends[...] = jnp.zeros_like(out_ends)

    grid[1:pooled + 1] = grad_out[...].astype(F32)
    grid[0] = top[2 * half:, :].astype(F32)
    outside = jnp.where(last, 0.0, 1.0)
    grid[pooled + 1] = bottom[2 * half:, :].astype(F32) * outside
    at = lax.broadcasted_iota(jnp.int32, (half, c1), 0)
    for i in range(pooled + 2):
        here = grid[i]
        out_ends[0, i:i + 1] = here[:1]
        out_ends[1, i:i + 1] = here[half - 1:]
        wide[i, :, :c1] = jnp.where(at == 0, 0.0, pltpu.roll(here, 1, 0)).astype(BF16)
        wide[i, :, c1:2 * c1] = here.astype(BF16)
        wide[i, :, 2 * c1:3 * c1] = jnp.where(at == half - 1, 0.0, pltpu.roll(here, half - 1, 0)).astype(BF16)
        wide[i, :, 3 * c1:] = here.astype(BF16)

    flat = wide[1:pooled + 1].reshape(cells, 4 * c1)
    for a in range(3):
        prods[a] = dot_nt(flat, taps[a]).reshape(pooled, half, c2)
    fold = jnp.where(first, taps[0], taps[2])
    ends[0] = dot_nt(wide[0], fold)
    ends[1] = dot_nt(wide[0], taps[1])
    ends[2] = dot_nt(wide[pooled + 1], taps[0])
    ends[3] = dot_nt(wide[pooled + 1], taps[1])

    def place(r, total, incline):
        inner = total * incline
        raw_ends[0, pl.ds(r, 1), :] = total[:1, :c1]
        raw_ends[1, pl.ds(r, 1), :] = total[half - 1:, c1:]
        slope_ends[0, pl.ds(r, 1), :] = incline[:1, :c1]
        slope_ends[1, pl.ds(r, 1), :] = incline[half - 1:, c1:]
        even, odd = inner[:, :c1], inner[:, c1:]
        spread[r, :, :c1] = jnp.where(at == 0, 0.0, pltpu.roll(odd, 1, 0)).astype(BF16)
        spread[r, :, c1:2 * c1] = jnp.where(at == 0, 0.0, even).astype(BF16)
        spread[r, :, 2 * c1:3 * c1] = jnp.where(at == half - 1, 0.0, odd).astype(BF16)
        spread[r, :, 3 * c1:] = jnp.where(at == half - 1, 0.0, pltpu.roll(even, half - 1, 0)).astype(BF16)

    def halo_slope(message):
        line[...] = message[:2 * half, :].astype(F32)
        both = [line[pl.ds(pc, half, stride=2), :] for pc in range(2)]
        return jnp.concatenate([slope_of(v, cdf_of(v)) for v in both], axis=1)

    place(0, ends[0] + ends[1] + prods[0, 0], halo_slope(top))
    place(1, ends[0] + prods[1, 0] + prods[0, 0], slope[0])

    def pair(i, carry):
        middle = prods[2, i] + prods[1, i]
        place(2 * i + 2, middle + prods[0, i + 1], slope[2 * i + 1])
        place(2 * i + 3, prods[2, i] + prods[1, i + 1] + prods[0, i + 1], slope[2 * i + 2])
        return carry

    lax.fori_loop(0, pooled - 1, pair, 0)
    final = prods[2, pooled - 1]
    place(rows, final + prods[1, pooled - 1] + ends[2], slope[rows - 1])
    place(rows + 1, (final + ends[3] + ends[2]) * outside, halo_slope(bottom))

    is_first = jnp.where(first, 1.0, 0.0).astype(BF16)
    not_first = jnp.where(first, 0.0, 1.0).astype(BF16)
    above = wide[0, :, :3 * c1]
    wide[0, :, :3 * c1] = above * not_first
    for n, (pr, start) in enumerate(((0, 0), (0, 1), (1, 1), (1, 2))):
        around = wide[start:start + pooled, :, :3 * c1].reshape(cells, 3 * c1)
        sums[n] = dot(act_t[pr], around)
    corner[...] = dot(act_t[0, :, :half], above * is_first)

    unit = c0
    per_tap = c1 // unit
    count = 9 * per_tap + 9

    def put(k, value):
        keep[k * unit:(k + 1) * unit, :] = value

    pieces = {0: ((0, 1), (1, 3)), 1: ((0, 1), (1, 2)), 2: ((0, 0), (1, 2))}
    for a in range(3):
        for b in range(3):
            total = None
            for pr, n in pieces[a]:
                for pc in range(2):
                    k = (pc + 1 - b) // 2 + 1
                    term = sums[n, pc * c1:(pc + 1) * c1, k * c1:(k + 1) * c1]
                    total = term if total is None else total + term
            if a == 0:
                for pc in range(2):
                    k = (pc + 1 - b) // 2 + 1
                    total = total + corner[pc * c1:(pc + 1) * c1, k * c1:(k + 1) * c1]
            total = total * 0.25
            for part in range(per_tap):
                put((3 * a + b) * per_tap + part, total[part * unit:(part + 1) * unit])

    head = spread[0]
    spread[0] = head * not_first
    spread[rows + 2] = head * is_first
    folded = dot(fields_t[:, :half], spread[rows + 2])
    for a in range(3):
        around = spread[2 - a:2 - a + rows].reshape(rows * half, 4 * c1)
        got = dot(fields_t[...], around)
        if a == 0:
            got = got + folded
        for b in range(3):
            even = got[:c0, (2 - b) * c1:(3 - b) * c1]
            odd = got[c0:, (3 - b) * c1:(4 - b) * c1]
            put(9 * per_tap + 3 * a + b, even + odd)
    if keep.shape[0] > count * unit:
        keep[count * unit:] = jnp.zeros((keep.shape[0] - count * unit, c1), F32)


def columns_kernel(lats, col_a, col_b, act_ends, field_ends, taps, keep, raw_ends, slope_ends, out_ends,
                   ends, own, other, lhs, values, right_hand, total):
    band, first, last, _, core = position(lats)
    c1 = act_ends.shape[2]
    rows = act_ends.shape[1]
    pooled = rows // 2
    c0 = field_ends.shape[0] // 2
    span, size = raw_ends.shape[1], col_a.shape[0]
    got_a, got_b = col_a[...].astype(F32), col_b[...].astype(F32)
    message = jnp.concatenate([jnp.where(core == 0, got_b, got_a), jnp.where(core == 0, got_a, got_b)], 1)
    at = lax.broadcasted_iota(jnp.int32, (size, 2 * c1), 0)
    message = jnp.where(jnp.logical_and(at == rows + pooled + 3, last), 0.0, message).astype(BF16)

    n = lax.broadcasted_iota(jnp.int32, (3 * span, size), 0)
    k = lax.broadcasted_iota(jnp.int32, (3 * span, size), 1)
    row = n % span
    want = (row - n // span + 2) // 2 - 1
    place = jnp.where(want < 0, rows + pooled + 2, jnp.where(want == pooled, rows + pooled + 3, rows + want))
    beside = dot(one_at(jnp.logical_and(k == place, row < rows + 2)), message)
    n = lax.broadcasted_iota(jnp.int32, (3 * span, out_ends.shape[1]), 0)
    k = lax.broadcasted_iota(jnp.int32, (3 * span, out_ends.shape[1]), 1)
    row = n % span
    want = (row - n // span + 2) // 2
    pick = one_at(jnp.logical_and(k == want, row < rows + 2))
    within = dot(pick, jnp.concatenate([out_ends[0], out_ends[1]], 1).astype(BF16))
    n = lax.broadcasted_iota(jnp.int32, (span, size), 0)
    k = lax.broadcasted_iota(jnp.int32, (span, size), 1)
    place = jnp.where(n == 0, rows + pooled, jnp.where(n == rows + 1, rows + pooled + 1, n - 1))
    saved = dot(one_at(jnp.logical_and(k == place, n < rows + 2)), message)
    incline = slope_of(saved, cdf_of(saved))

    head = lax.broadcasted_iota(jnp.int32, (span, 2 * c1), 0) < 2
    turned = jnp.logical_and(head, first)
    lhs[...] = jnp.zeros_like(lhs)
    rights = []
    for a in range(4):
        sides, inner = (x[min(a, 2) * span:(min(a, 2) + 1) * span] for x in (beside, within))
        if a == 2:
            sides, inner = jnp.where(turned, 0.0, sides), jnp.where(turned, 0.0, inner)
        if a == 3:
            sides, inner = jnp.where(turned, sides, 0.0), jnp.where(turned, inner, 0.0)
        rights.append(sides)
        sides, inner = sides.astype(BF16), inner.astype(BF16)
        left, right = sides[:, :c1], sides[:, c1:]
        lhs[a, :span, c1:2 * c1] = left
        lhs[a, :span, 2 * c1:3 * c1] = inner[:, :c1]
        lhs[a, :span, 3 * c1:] = left
        lhs[a, span:2 * span, :c1] = left
        lhs[a, 2 * span:3 * span, :c1] = inner[:, c1:]
        lhs[a, 2 * span:3 * span, c1:2 * c1] = right
        lhs[a, 2 * span:3 * span, 3 * c1:] = right
        lhs[a, 3 * span:, 2 * c1:3 * c1] = right
    found = dot_nt(lhs[0], taps[0]) + dot_nt(lhs[1], taps[1]) + dot_nt(lhs[2], taps[2]) + dot_nt(lhs[3], taps[0])
    row = lax.broadcasted_iota(jnp.int32, (span, c1), 0)
    inside = jnp.where(jnp.logical_or(row > rows + 1, jnp.logical_and(row == rows + 1, last)), 0.0, 1.0)
    values[0] = found[:span, c1:] * incline[:, :c1] * inside
    values[1] = (raw_ends[0] + found[span:2 * span, :c1]) * slope_ends[0] * inside
    values[2] = (raw_ends[1] + found[3 * span:, c1:]) * slope_ends[1] * inside
    values[3] = found[2 * span:3 * span, :c1] * incline[:, c1:] * inside
    ends[...] = values[...].astype(BF16)

    total[...] = keep[...]
    for side, b in ((0, 2), (1, 0)):
        around = jnp.concatenate([x[1:rows + 1, side * c1:(side + 1) * c1] for x in rights], 1).astype(BF16)
        terms = lax.dot_general(act_ends[side].astype(BF16), around, (((0,), (0,)), ((), ())),
                                preferred_element_type=F32) * 0.25
        for a in range(3):
            term = terms[:, a * c1:(a + 1) * c1]
            if a == 0:
                term = term + terms[:, 3 * c1:]
            low = (3 * a + b) * c1
            total[low:low + c1] = total[low:low + c1] + term
    right_hand[...] = jnp.zeros_like(right_hand)
    top = lax.broadcasted_iota(jnp.int32, (rows, c1), 0) == 0
    over = jnp.logical_and(top, first)
    for a in range(4):
        for j in range(4):
            value = values[j, 2 - min(a, 2):2 - min(a, 2) + rows]
            if a == 2:
                value = jnp.where(over, 0.0, value)
            if a == 3:
                value = jnp.where(over, value, 0.0)
            right_hand[a, j // 2 * rows:(j // 2 + 1) * rows, j * c1:(j + 1) * c1] = value.astype(BF16)
    for a in range(3):
        got = dot(field_ends[...], right_hand[a])
        if a == 0:
            got = got + dot(field_ends[...], right_hand[3])
        for b in range(3):
            even = got[:c0, (2 - b) * c1:(3 - b) * c1]
            odd = got[c0:, (3 - b) * c1:(4 - b) * c1]
            low = 9 * c1 + (3 * a + b) * c0
            total[low:low + c0] = total[low:low + c0] + even + odd

    held = own.shape[0]
    block = held // lats
    mine = half_held()
    for target, half_of in ((own, mine), (other, 1 - mine)):
        for far in range(lats):
            start = half_of * held + (band ^ far) * block
            target[far * block:(far + 1) * block] = total[pl.ds(pl.multiple_of(start, block), block), :]


def last_kernel(lats, part, ends, taps, out, spread, values, total, turned):
    rows, c0, cols = out.shape
    half = cols // 2
    c2 = 2 * c0
    depth = spread.shape[2]
    first = position(lats)[1]
    spread[...] = part[...]
    c1 = depth // 4
    for j in range(4):
        values[:, j * c1:(j + 1) * c1] = ends[j].astype(F32)
    at = lax.broadcasted_iota(jnp.int32, (16, 2 * c1), 0)
    for r in range(rows + 3):
        n = 0 if r == rows + 2 else r
        for side, (low, spot) in enumerate(((0, 0), (half - 16, 15))):
            lanes = slice(2 * side * c1, 2 * (side + 1) * c1)
            new = values[n:n + 1, lanes]
            if n == 0:
                new = jnp.where(first == (r != 0), new, 0.0)
            tile = spread[r, low:low + 16, lanes].astype(F32)
            spread[r, low:low + 16, lanes] = jnp.where(at == spot, new, tile).astype(BF16)
    result = dot_nt(taps[:c2], spread[2:rows + 2].reshape(rows * half, depth))
    for a in (1, 2):
        result = result + dot_nt(taps[a * c2:(a + 1) * c2],
                                 spread[2 - a:2 - a + rows].reshape(rows * half, depth))
    total[...] = result
    total[:, :half] = total[:, :half] + dot_nt(taps[:c2], spread[rows + 2])
    for q in range(rows // 2):
        pair = total[:, q * cols:(q + 1) * cols].astype(BF16)
        turned[q, :, :cols] = pair[:c0]
        turned[q, :, cols:] = pair[c0:]
    k = lax.broadcasted_iota(jnp.int32, (2 * cols, 2 * cols), 0)
    n = lax.broadcasted_iota(jnp.int32, (2 * cols, 2 * cols), 1)
    order = one_at(n == ((k % cols) // half) * cols + 2 * (k % half) + k // cols)
    found = dot(turned[...].reshape(rows // 2 * c0, 2 * cols), order).astype(BF16)
    for q in range(rows // 2):
        for rp in range(2):
            out[2 * q + rp] = found[q * c0:(q + 1) * c0, rp * cols:(rp + 1) * cols]


def gather_kernel(mine, theirs, out_first, out_second):
    lats, rows, c1 = mine.shape
    band, held = lax.axis_index("lat"), half_held()
    size = out_second.shape[0]
    total = size + out_first.shape[0]
    for h in range(2):
        for i in range(lats):
            at = (h * lats + i) * rows
            for out, base, end in ((out_second, 0, size), (out_first, size, total)):
                low, high = max(at, base), min(at + rows, end)
                if low < high:
                    here, there = (x[i ^ band, low - at:high - at] for x in (mine, theirs))
                    out[low - base:high - base] = jnp.where(held == h, here, there).astype(F32)


def vmem(count):
    return [pl.BlockSpec(memory_space=pltpu.VMEM)] * count


def far(count):
    return [pl.BlockSpec(memory_space=pl.ANY)] * count


def params(mib):
    return pltpu.CompilerParams(vmem_limit_bytes=mib * 1024 * 1024)


def shape(dims, kind):
    return jax.ShapeDtypeStruct(dims, kind)


def body(inputs, pre_first, grad_out, w_first, w_second):
    rows, cols, c1 = pre_first.shape
    c0 = inputs.shape[2]
    half, pooled = cols // 2, rows // 2
    lats, lons = lax.axis_size("lat"), lax.axis_size("lon")
    depths = lons // 2
    band, place = lax.axis_index("lat"), lax.axis_index("lon")
    core = lax.rem(place, 2)
    even = lax.rem(band, 2) == 0

    edge = -(-(rows + pooled + 4) // 16) * 16
    row_a, row_b, col_a, col_b, held_pre = pl.pallas_call(
        functools.partial(pack_kernel, lats),
        out_shape=(
            pltpu.VMEM((cols + half, c1), BF16),
            pltpu.VMEM((cols + half, c1), BF16),
            pltpu.VMEM((edge, c1), BF16),
            pltpu.VMEM((edge, c1), BF16),
            pltpu.VMEM(pre_first.shape, BF16),
        ),
        in_specs=far(2),
        out_specs=tuple(vmem(5)),
        scratch_shapes=[
            pltpu.VMEM((2, edge, c1), F32),
            pltpu.VMEM(grad_out.shape, BF16),
            pltpu.SemaphoreType.DMA((2,)),
        ],
        compiler_params=params(58),
        cost_estimate=pl.CostEstimate(flops=1000, bytes_accessed=1 << 18, transcendentals=0),
    )(pre_first, grad_out)
    pairs = [(i * lons + j, i * lons + (j + lons // 2) % lons) for i in (0, lats - 1) for j in range(lons)]
    for i in range(1, lats - 1, 2):
        for j in range(lons):
            pairs += [(i * lons + j, (i + 1) * lons + j), ((i + 1) * lons + j, i * lons + j)]
    every = [(i * lons + j, (i ^ 1) * lons + j) for i in range(lats) for j in range(lons)]
    row_b = lax.ppermute(row_b, AREA, pairs)
    row_a = lax.ppermute(row_a, AREA, every)

    slope, act_t, act_ends = pl.pallas_call(
        local_kernel,
        out_shape=(
            shape((rows, half, 2 * c1), F32),
            shape((2, 2 * c1, pooled * half), BF16),
            shape((2, rows, c1), F32),
        ),
        in_specs=vmem(1),
        out_specs=tuple(vmem(3)),
        scratch_shapes=[
            pltpu.VMEM((cols, c1), F32),
            pltpu.VMEM((2, pooled, half, 2 * c1), BF16),
        ],
        compiler_params=params(16),
        cost_estimate=pl.CostEstimate(flops=60 * rows * cols * c1, bytes_accessed=2 << 20,
                                      transcendentals=2 * rows * cols * c1),
    )(held_pre)

    fields_t, field_ends, taps_first, taps_second = pl.pallas_call(
        layout_kernel,
        out_shape=(
            shape((2 * c0, rows * half), BF16),
            shape((2 * c0, 2 * rows), BF16),
            shape((6 * c0, 4 * c1), BF16),
            shape((3, 2 * c1, 4 * c1), BF16),
        ),
        in_specs=vmem(3),
        out_specs=tuple(vmem(4)),
        scratch_shapes=[pltpu.VMEM((rows, c0, 2 * cols), BF16)],
        compiler_params=params(16),
        cost_estimate=pl.CostEstimate(flops=4 * rows * cols * c0 * cols, bytes_accessed=3 << 20, transcendentals=0),
    )(jnp.transpose(inputs, (0, 2, 1)), w_first, w_second)
    row_b, row_a, slope, fields_t = lax.optimization_barrier((row_b, row_a, slope, fields_t))

    def corners(at):
        places = (at * (cols - 1), cols + at * (half - 1))
        above, below = (jnp.where(even, one, two) for one, two in ((row_b, row_a), (row_a, row_b)))
        return jnp.concatenate([part[p:p + 1] for p in places for part in (above, below)], 0)

    low, high = corners(0), corners(1)
    pad = jnp.zeros((edge - rows - pooled - 4, c1), BF16)
    col_a = jnp.concatenate([col_a[:rows + pooled], jnp.where(core == 0, high, low), pad], 0)
    col_b = jnp.concatenate([col_b[:rows + pooled], jnp.where(core == 0, low, high), pad], 0)
    col_b = lax.ppermute(col_b, "lon", [(i, (i + 2 * (i % 2) - 1) % lons) for i in range(lons)])
    col_a = lax.ppermute(col_a, "lon", [(i, i ^ 1) for i in range(lons)])

    block = -(-9 * (c1 + c0) // (32 * lats)) * 16
    held = lats * block
    reach = -(-(rows + 2) // 16) * 16
    spread, keep, raw_ends, slope_ends, out_ends = pl.pallas_call(
        functools.partial(middle_kernel, lats),
        out_shape=(
            shape((rows + 3, half, 4 * c1), BF16),
            shape((2 * held, c1), F32),
            shape((2, reach, c1), F32),
            shape((2, reach, c1), F32),
            shape((2, -(-(pooled + 2) // 16) * 16, c1), F32),
        ),
        in_specs=vmem(7),
        out_specs=tuple(vmem(5)),
        scratch_shapes=[
            pltpu.VMEM((pooled + 2, half, c1), F32),
            pltpu.VMEM((pooled + 2, half, 4 * c1), BF16),
            pltpu.VMEM((3, pooled, half, 2 * c1), F32),
            pltpu.VMEM((4, half, 2 * c1), F32),
            pltpu.VMEM((cols, c1), F32),
            pltpu.VMEM((4, 2 * c1, 3 * c1), F32),
            pltpu.VMEM((2 * c1, 3 * c1), F32),
        ],
        compiler_params=params(16),
        cost_estimate=pl.CostEstimate(flops=2 * rows * cols * c1 * 9 * (2 * c1 + c0), bytes_accessed=8 << 20,
                                      transcendentals=0),
    )(grad_out, row_a, row_b, slope, act_t, fields_t, taps_second)
    col_a, col_b, keep = lax.optimization_barrier((col_a, col_b, keep))

    ends, own, other = pl.pallas_call(
        functools.partial(columns_kernel, lats),
        out_shape=(
            shape((4, reach, c1), BF16),
            shape((held, c1), F32),
            shape((held, c1), F32),
        ),
        in_specs=vmem(9),
        out_specs=tuple(vmem(3)),
        scratch_shapes=[
            pltpu.VMEM((4, 4 * reach, 4 * c1), BF16),
            pltpu.VMEM((4, reach, c1), F32),
            pltpu.VMEM((4, 2 * rows, 4 * c1), BF16),
            pltpu.VMEM((2 * held, c1), F32),
        ],
        compiler_params=params(16),
        cost_estimate=pl.CostEstimate(flops=1 << 28, bytes_accessed=3 << 20, transcendentals=0),
    )(col_a, col_b, act_ends, field_ends, taps_second, keep, raw_ends, slope_ends, out_ends)

    swap = [(i, i ^ 1) for i in range(lons)]

    def between_chips(value, over_lat, over_lon):
        turn = odd(over_lat) ^ odd(over_lon)
        return lax.ppermute(value, AREA, [
            (i * lons + j, (i ^ over_lat) * lons + (j ^ (2 * over_lon) ^ turn)) for i in range(lats) for j in range(lons)])

    parts = (own + lax.ppermute(other, "lon", swap)).reshape(lats, block, c1)
    sent = [parts[far].astype(BF16) for far in range(1, lats)]
    *sent, ends = lax.optimization_barrier((*sent, ends))
    got = [between_chips(sent[far - 1], far, 0) for far in range(1, lats)]
    grad_inputs = pl.pallas_call(
        functools.partial(last_kernel, lats),
        out_shape=shape((rows, c0, cols), BF16),
        in_specs=vmem(3),
        out_specs=vmem(1)[0],
        scratch_shapes=[
            pltpu.VMEM((rows + 3, half, 4 * c1), BF16),
            pltpu.VMEM((reach, 4 * c1), F32),
            pltpu.VMEM((2 * c0, rows * half), F32),
            pltpu.VMEM((pooled, c0, 2 * cols), BF16),
        ],
        compiler_params=params(12),
        cost_estimate=pl.CostEstimate(flops=2 * rows * cols * c1 * 9 * c0, bytes_accessed=3 << 20, transcendentals=0),
    )(spread, ends, taps_first)
    *got, grad_inputs = lax.optimization_barrier((*got, grad_inputs))
    total = parts[0]
    for value in got:
        total = total + value.astype(F32)
    part = total.astype(BF16)
    terms = [part] + [between_chips(part, 0, far) for far in range(1, depths)]
    terms = [term.astype(F32) for term in terms]
    while len(terms) > 1:
        terms = [terms[k + (k > 0)] + terms[k + (k == 0)] for k in range(0, len(terms), 2)]
    part = terms[0].astype(BF16)
    mine = jnp.stack([part] + [between_chips(part, far, 0) for far in range(1, lats)], 0)
    theirs = lax.ppermute(mine, "lon", swap)

    grad_w_first, grad_w_second = pl.pallas_call(
        gather_kernel,
        out_shape=(shape((9 * c0, c1), F32), shape((9 * c1, c1), F32)),
        in_specs=vmem(2),
        out_specs=tuple(vmem(2)),
        compiler_params=params(8),
        cost_estimate=pl.CostEstimate(flops=1000, bytes_accessed=3 << 19, transcendentals=0),
    )(mine, theirs)
    return (jnp.transpose(grad_inputs, (0, 2, 1)), grad_w_first.reshape(w_first.shape),
            grad_w_second.reshape(w_second.shape))


def solution(mesh):
    in_specs = (P("lat", "lon", None), P("lat", "lon", None), P("lat", "lon", None), P(), P())
    out_specs = (P("lat", "lon", None), P(), P())
    return jax.shard_map(body, mesh=mesh, in_specs=in_specs, out_specs=out_specs, check_vma=False)
```

```python
import functools

import jax
import jax.numpy as jnp
from jax import lax
from jax.experimental import pallas as pl
from jax.experimental.pallas import tpu as pltpu
from jax.sharding import PartitionSpec as P

inv_root = 0.7071067811865476
density = 0.3989422804014327

F32 = jnp.float32
BF16 = jnp.bfloat16
AREA = ("lat", "lon")


def cdf_of(value):
    return 0.5 * (1.0 + lax.erf(value * inv_root))


def slope_of(value, cdf):
    return 0.25 * (cdf + value * jnp.exp(-0.5 * value * value) * density)


def dot(left, right):
    return jnp.dot(left, right, preferred_element_type=F32)


def dot_nt(left, right):
    return lax.dot_general(left, right, (((1,), (1,)), ((), ())), preferred_element_type=F32)


def position(lats):
    band, place = lax.axis_index("lat"), lax.axis_index("lon")
    return band, band == 0, band == lats - 1, lax.rem(band, 2) == 0, lax.rem(place, 2)


def odd(value):
    for shift in (4, 2, 1):
        value = value ^ (value >> shift)
    return value & 1


def half_held():
    band, place = lax.axis_index("lat"), lax.axis_index("lon")
    return odd(band) ^ odd(place // 2) ^ (place % 2)


def pack_kernel(lats, pre_far, grad_far, row_a, row_b, col_a, col_b, pre, hold, grad_out, sems):
    copies = [pltpu.make_async_copy(pre_far, pre, sems.at[0]), pltpu.make_async_copy(grad_far, grad_out, sems.at[1])]
    for copy in copies:
        copy.start()
    for copy in copies:
        copy.wait()
    rows, cols, c1 = pre.shape
    pooled, half = grad_out.shape[:2]
    _, _, _, even, core = position(lats)
    for message, low in ((row_a, ~even), (row_b, even)):
        message[:cols] = pre[jnp.where(low, 0, rows - 1)]
        message[cols:] = grad_out[jnp.where(low, 0, pooled - 1)]
    hold[:, rows + pooled:] = jnp.zeros((2, hold.shape[1] - rows - pooled, c1), F32)
    for side, (p, g) in enumerate(((0, 0), (cols - 16, half - 16))):
        at = 15 * side
        for r in range(rows):
            hold[side, r:r + 1] = pre[r, p:p + 16].astype(F32)[at:at + 1]
        for i in range(pooled):
            hold[side, rows + i:rows + i + 1] = grad_out[i, g:g + 16].astype(F32)[at:at + 1]
    col_a[...] = hold[1 - core].astype(BF16)
    col_b[...] = hold[core].astype(BF16)


def one_at(where):
    return jnp.where(where, 1.0, 0.0).astype(BF16)


def local_kernel(pre, slope, act_t, act_ends, line, act_s):
    rows, cols, c1 = pre.shape
    half = cols // 2

    def one_row(r, carry):
        line[...] = pre[r].astype(F32)
        for pc in range(2):
            value = line[pl.ds(pc, half, stride=2), :]
            cdf = cdf_of(value)
            act = value * cdf
            act_s[r % 2, r // 2, :, pc * c1:(pc + 1) * c1] = act.astype(BF16)
            act_ends[pc, pl.ds(r, 1), :] = act[pc * (half - 1):pc * (half - 1) + 1]
            slope[r, :, pc * c1:(pc + 1) * c1] = slope_of(value, cdf)
        return carry

    lax.fori_loop(0, rows, one_row, 0)
    for pr in range(2):
        act_t[pr] = act_s[pr].reshape(rows // 2 * half, 2 * c1).T


def layout_kernel(fields, w_first, w_second, fields_t, field_ends, taps_first, taps_second, turned):
    rows, c0, cols = fields.shape
    c1 = w_first.shape[3]
    half = cols // 2
    col = lax.broadcasted_iota(jnp.int32, (cols, 2 * cols), 0)
    lane = lax.broadcasted_iota(jnp.int32, (cols, 2 * cols), 1)
    turn = lane // cols
    parity = (lane % cols) // half
    parity = parity + turn - 2 * parity * turn
    order = one_at(col == 2 * (lane % half) + parity)
    turned[...] = dot(fields[...].reshape(rows * c0, cols), order).astype(BF16).reshape(rows, c0, 2 * cols)
    low = lax.broadcasted_iota(jnp.int32, (c0, cols), 1) < half
    for q in range(rows // 2):
        fields_t[:c0, q * cols:(q + 1) * cols] = jnp.where(low, turned[2 * q, :, :cols], turned[2 * q + 1, :, cols:])
        fields_t[c0:, q * cols:(q + 1) * cols] = jnp.where(low, turned[2 * q, :, cols:], turned[2 * q + 1, :, :cols])
    cell = lax.broadcasted_iota(jnp.int32, (rows * half, 2 * rows), 0)
    n = lax.broadcasted_iota(jnp.int32, (rows * half, 2 * rows), 1)
    pick = one_at(cell == (n % rows) * half + (n // rows) * (half - 1))
    field_ends[...] = dot(fields_t[...], pick).astype(BF16)
    taps_second[...] = jnp.zeros_like(taps_second)
    taps_first[...] = jnp.zeros_like(taps_first)
    for a in range(3):
        for pc, blocks in ((0, (2, 1, None, 0)), (1, (None, 2, 0, 1))):
            for k, b in enumerate(blocks):
                if b is not None:
                    taps_second[a, pc * c1:(pc + 1) * c1, k * c1:(k + 1) * c1] = w_second[a, b]
        for pc, blocks in ((0, (2, 1, 0, None)), (1, (None, 2, 1, 0))):
            for k, b in enumerate(blocks):
                if b is not None:
                    start = (2 * a + pc) * c0
                    taps_first[start:start + c0, k * c1:(k + 1) * c1] = w_first[a, b]


def middle_kernel(lats, grad_out, row_a, row_b, slope, act_t, fields_t, taps,
                  spread, keep, raw_ends, slope_ends, out_ends,
                  grid, wide, prods, ends, line, sums, corner):
    _, first, last, even, _ = position(lats)
    top = jnp.where(even, row_b[...], row_a[...])
    bottom = jnp.where(even, row_a[...], row_b[...])
    rows, half, c2 = slope.shape
    c1 = c2 // 2
    pooled = rows // 2
    c0 = fields_t.shape[0] // 2
    cells = pooled * half
    raw_ends[...] = jnp.zeros_like(raw_ends)
    slope_ends[...] = jnp.zeros_like(slope_ends)
    out_ends[...] = jnp.zeros_like(out_ends)

    grid[1:pooled + 1] = grad_out[...].astype(F32)
    grid[0] = top[2 * half:, :].astype(F32)
    outside = jnp.where(last, 0.0, 1.0)
    grid[pooled + 1] = bottom[2 * half:, :].astype(F32) * outside
    at = lax.broadcasted_iota(jnp.int32, (half, c1), 0)
    for i in range(pooled + 2):
        here = grid[i]
        out_ends[0, i:i + 1] = here[:1]
        out_ends[1, i:i + 1] = here[half - 1:]
        wide[i, :, :c1] = jnp.where(at == 0, 0.0, pltpu.roll(here, 1, 0)).astype(BF16)
        wide[i, :, c1:2 * c1] = here.astype(BF16)
        wide[i, :, 2 * c1:3 * c1] = jnp.where(at == half - 1, 0.0, pltpu.roll(here, half - 1, 0)).astype(BF16)
        wide[i, :, 3 * c1:] = here.astype(BF16)

    flat = wide[1:pooled + 1].reshape(cells, 4 * c1)
    for a in range(3):
        prods[a] = dot_nt(flat, taps[a]).reshape(pooled, half, c2)
    fold = jnp.where(first, taps[0], taps[2])
    ends[0] = dot_nt(wide[0], fold)
    ends[1] = dot_nt(wide[0], taps[1])
    ends[2] = dot_nt(wide[pooled + 1], taps[0])
    ends[3] = dot_nt(wide[pooled + 1], taps[1])

    def place(r, total, incline):
        inner = total * incline
        raw_ends[0, pl.ds(r, 1), :] = total[:1, :c1]
        raw_ends[1, pl.ds(r, 1), :] = total[half - 1:, c1:]
        slope_ends[0, pl.ds(r, 1), :] = incline[:1, :c1]
        slope_ends[1, pl.ds(r, 1), :] = incline[half - 1:, c1:]
        even, odd = inner[:, :c1], inner[:, c1:]
        spread[r, :, :c1] = jnp.where(at == 0, 0.0, pltpu.roll(odd, 1, 0)).astype(BF16)
        spread[r, :, c1:2 * c1] = jnp.where(at == 0, 0.0, even).astype(BF16)
        spread[r, :, 2 * c1:3 * c1] = jnp.where(at == half - 1, 0.0, odd).astype(BF16)
        spread[r, :, 3 * c1:] = jnp.where(at == half - 1, 0.0, pltpu.roll(even, half - 1, 0)).astype(BF16)

    def halo_slope(message):
        line[...] = message[:2 * half, :].astype(F32)
        both = [line[pl.ds(pc, half, stride=2), :] for pc in range(2)]
        return jnp.concatenate([slope_of(v, cdf_of(v)) for v in both], axis=1)

    place(0, ends[0] + ends[1] + prods[0, 0], halo_slope(top))
    place(1, ends[0] + prods[1, 0] + prods[0, 0], slope[0])

    def pair(i, carry):
        middle = prods[2, i] + prods[1, i]
        place(2 * i + 2, middle + prods[0, i + 1], slope[2 * i + 1])
        place(2 * i + 3, prods[2, i] + prods[1, i + 1] + prods[0, i + 1], slope[2 * i + 2])
        return carry

    lax.fori_loop(0, pooled - 1, pair, 0)
    final = prods[2, pooled - 1]
    place(rows, final + prods[1, pooled - 1] + ends[2], slope[rows - 1])
    place(rows + 1, (final + ends[3] + ends[2]) * outside, halo_slope(bottom))

    is_first = jnp.where(first, 1.0, 0.0).astype(BF16)
    not_first = jnp.where(first, 0.0, 1.0).astype(BF16)
    above = wide[0, :, :3 * c1]
    wide[0, :, :3 * c1] = above * not_first
    for n, (pr, start) in enumerate(((0, 0), (0, 1), (1, 1), (1, 2))):
        around = wide[start:start + pooled, :, :3 * c1].reshape(cells, 3 * c1)
        sums[n] = dot(act_t[pr], around)
    corner[...] = dot(act_t[0, :, :half], above * is_first)

    unit = c0
    per_tap = c1 // unit
    count = 9 * per_tap + 9

    def put(k, value):
        keep[k * unit:(k + 1) * unit, :] = value

    pieces = {0: ((0, 1), (1, 3)), 1: ((0, 1), (1, 2)), 2: ((0, 0), (1, 2))}
    for a in range(3):
        for b in range(3):
            total = None
            for pr, n in pieces[a]:
                for pc in range(2):
                    k = (pc + 1 - b) // 2 + 1
                    term = sums[n, pc * c1:(pc + 1) * c1, k * c1:(k + 1) * c1]
                    total = term if total is None else total + term
            if a == 0:
                for pc in range(2):
                    k = (pc + 1 - b) // 2 + 1
                    total = total + corner[pc * c1:(pc + 1) * c1, k * c1:(k + 1) * c1]
            total = total * 0.25
            for part in range(per_tap):
                put((3 * a + b) * per_tap + part, total[part * unit:(part + 1) * unit])

    head = spread[0]
    spread[0] = head * not_first
    spread[rows + 2] = head * is_first
    folded = dot(fields_t[:, :half], spread[rows + 2])
    for a in range(3):
        around = spread[2 - a:2 - a + rows].reshape(rows * half, 4 * c1)
        got = dot(fields_t[...], around)
        if a == 0:
            got = got + folded
        for b in range(3):
            even = got[:c0, (2 - b) * c1:(3 - b) * c1]
            odd = got[c0:, (3 - b) * c1:(4 - b) * c1]
            put(9 * per_tap + 3 * a + b, even + odd)
    if keep.shape[0] > count * unit:
        keep[count * unit:] = jnp.zeros((keep.shape[0] - count * unit, c1), F32)


def columns_kernel(lats, col_a, col_b, act_ends, field_ends, taps, keep, raw_ends, slope_ends, out_ends,
                   ends, own, other, lhs, values, right_hand, total):
    band, first, last, _, core = position(lats)
    c1 = act_ends.shape[2]
    rows = act_ends.shape[1]
    pooled = rows // 2
    c0 = field_ends.shape[0] // 2
    span, size = raw_ends.shape[1], col_a.shape[0]
    got_a, got_b = col_a[...].astype(F32), col_b[...].astype(F32)
    message = jnp.concatenate([jnp.where(core == 0, got_b, got_a), jnp.where(core == 0, got_a, got_b)], 1)
    at = lax.broadcasted_iota(jnp.int32, (size, 2 * c1), 0)
    message = jnp.where(jnp.logical_and(at == rows + pooled + 3, last), 0.0, message).astype(BF16)

    n = lax.broadcasted_iota(jnp.int32, (3 * span, size), 0)
    k = lax.broadcasted_iota(jnp.int32, (3 * span, size), 1)
    row = n % span
    want = (row - n // span + 2) // 2 - 1
    place = jnp.where(want < 0, rows + pooled + 2, jnp.where(want == pooled, rows + pooled + 3, rows + want))
    beside = dot(one_at(jnp.logical_and(k == place, row < rows + 2)), message)
    n = lax.broadcasted_iota(jnp.int32, (3 * span, out_ends.shape[1]), 0)
    k = lax.broadcasted_iota(jnp.int32, (3 * span, out_ends.shape[1]), 1)
    row = n % span
    want = (row - n // span + 2) // 2
    pick = one_at(jnp.logical_and(k == want, row < rows + 2))
    within = dot(pick, jnp.concatenate([out_ends[0], out_ends[1]], 1).astype(BF16))
    n = lax.broadcasted_iota(jnp.int32, (span, size), 0)
    k = lax.broadcasted_iota(jnp.int32, (span, size), 1)
    place = jnp.where(n == 0, rows + pooled, jnp.where(n == rows + 1, rows + pooled + 1, n - 1))
    saved = dot(one_at(jnp.logical_and(k == place, n < rows + 2)), message)
    incline = slope_of(saved, cdf_of(saved))

    head = lax.broadcasted_iota(jnp.int32, (span, 2 * c1), 0) < 2
    turned = jnp.logical_and(head, first)
    lhs[...] = jnp.zeros_like(lhs)
    rights = []
    for a in range(4):
        sides, inner = (x[min(a, 2) * span:(min(a, 2) + 1) * span] for x in (beside, within))
        if a == 2:
            sides, inner = jnp.where(turned, 0.0, sides), jnp.where(turned, 0.0, inner)
        if a == 3:
            sides, inner = jnp.where(turned, sides, 0.0), jnp.where(turned, inner, 0.0)
        rights.append(sides)
        sides, inner = sides.astype(BF16), inner.astype(BF16)
        left, right = sides[:, :c1], sides[:, c1:]
        lhs[a, :span, c1:2 * c1] = left
        lhs[a, :span, 2 * c1:3 * c1] = inner[:, :c1]
        lhs[a, :span, 3 * c1:] = left
        lhs[a, span:2 * span, :c1] = left
        lhs[a, 2 * span:3 * span, :c1] = inner[:, c1:]
        lhs[a, 2 * span:3 * span, c1:2 * c1] = right
        lhs[a, 2 * span:3 * span, 3 * c1:] = right
        lhs[a, 3 * span:, 2 * c1:3 * c1] = right
    found = dot_nt(lhs[0], taps[0]) + dot_nt(lhs[1], taps[1]) + dot_nt(lhs[2], taps[2]) + dot_nt(lhs[3], taps[0])
    row = lax.broadcasted_iota(jnp.int32, (span, c1), 0)
    inside = jnp.where(jnp.logical_or(row > rows + 1, jnp.logical_and(row == rows + 1, last)), 0.0, 1.0)
    values[0] = found[:span, c1:] * incline[:, :c1] * inside
    values[1] = (raw_ends[0] + found[span:2 * span, :c1]) * slope_ends[0] * inside
    values[2] = (raw_ends[1] + found[3 * span:, c1:]) * slope_ends[1] * inside
    values[3] = found[2 * span:3 * span, :c1] * incline[:, c1:] * inside
    ends[...] = values[...].astype(BF16)

    total[...] = keep[...]
    for side, b in ((0, 2), (1, 0)):
        around = jnp.concatenate([x[1:rows + 1, side * c1:(side + 1) * c1] for x in rights], 1).astype(BF16)
        terms = lax.dot_general(act_ends[side].astype(BF16), around, (((0,), (0,)), ((), ())),
                                preferred_element_type=F32) * 0.25
        for a in range(3):
            term = terms[:, a * c1:(a + 1) * c1]
            if a == 0:
                term = term + terms[:, 3 * c1:]
            low = (3 * a + b) * c1
            total[low:low + c1] = total[low:low + c1] + term
    right_hand[...] = jnp.zeros_like(right_hand)
    top = lax.broadcasted_iota(jnp.int32, (rows, c1), 0) == 0
    over = jnp.logical_and(top, first)
    for a in range(4):
        for j in range(4):
            value = values[j, 2 - min(a, 2):2 - min(a, 2) + rows]
            if a == 2:
                value = jnp.where(over, 0.0, value)
            if a == 3:
                value = jnp.where(over, value, 0.0)
            right_hand[a, j // 2 * rows:(j // 2 + 1) * rows, j * c1:(j + 1) * c1] = value.astype(BF16)
    for a in range(3):
        got = dot(field_ends[...], right_hand[a])
        if a == 0:
            got = got + dot(field_ends[...], right_hand[3])
        for b in range(3):
            even = got[:c0, (2 - b) * c1:(3 - b) * c1]
            odd = got[c0:, (3 - b) * c1:(4 - b) * c1]
            low = 9 * c1 + (3 * a + b) * c0
            total[low:low + c0] = total[low:low + c0] + even + odd

    held = own.shape[0]
    block = held // lats
    mine = half_held()
    for target, half_of in ((own, mine), (other, 1 - mine)):
        for far in range(lats):
            start = half_of * held + (band ^ far) * block
            target[far * block:(far + 1) * block] = total[pl.ds(pl.multiple_of(start, block), block), :]


def last_kernel(lats, part, ends, taps, out, spread, values, total, turned):
    rows, c0, cols = out.shape
    half = cols // 2
    c2 = 2 * c0
    depth = spread.shape[2]
    first = position(lats)[1]
    spread[...] = part[...]
    c1 = depth // 4
    for j in range(4):
        values[:, j * c1:(j + 1) * c1] = ends[j].astype(F32)
    at = lax.broadcasted_iota(jnp.int32, (16, 2 * c1), 0)
    for r in range(rows + 3):
        n = 0 if r == rows + 2 else r
        for side, (low, spot) in enumerate(((0, 0), (half - 16, 15))):
            lanes = slice(2 * side * c1, 2 * (side + 1) * c1)
            new = values[n:n + 1, lanes]
            if n == 0:
                new = jnp.where(first == (r != 0), new, 0.0)
            tile = spread[r, low:low + 16, lanes].astype(F32)
            spread[r, low:low + 16, lanes] = jnp.where(at == spot, new, tile).astype(BF16)
    result = dot_nt(taps[:c2], spread[2:rows + 2].reshape(rows * half, depth))
    for a in (1, 2):
        result = result + dot_nt(taps[a * c2:(a + 1) * c2],
                                 spread[2 - a:2 - a + rows].reshape(rows * half, depth))
    total[...] = result
    total[:, :half] = total[:, :half] + dot_nt(taps[:c2], spread[rows + 2])
    for q in range(rows // 2):
        pair = total[:, q * cols:(q + 1) * cols].astype(BF16)
        turned[q, :, :cols] = pair[:c0]
        turned[q, :, cols:] = pair[c0:]
    k = lax.broadcasted_iota(jnp.int32, (2 * cols, 2 * cols), 0)
    n = lax.broadcasted_iota(jnp.int32, (2 * cols, 2 * cols), 1)
    order = one_at(n == ((k % cols) // half) * cols + 2 * (k % half) + k // cols)
    found = dot(turned[...].reshape(rows // 2 * c0, 2 * cols), order).astype(BF16)
    for q in range(rows // 2):
        for rp in range(2):
            out[2 * q + rp] = found[q * c0:(q + 1) * c0, rp * cols:(rp + 1) * cols]


def gather_kernel(mine, theirs, out_first, out_second):
    lats, rows, c1 = mine.shape
    band, held = lax.axis_index("lat"), half_held()
    size = out_second.shape[0]
    total = size + out_first.shape[0]
    for h in range(2):
        for i in range(lats):
            at = (h * lats + i) * rows
            for out, base, end in ((out_second, 0, size), (out_first, size, total)):
                low, high = max(at, base), min(at + rows, end)
                if low < high:
                    here, there = (x[i ^ band, low - at:high - at] for x in (mine, theirs))
                    out[low - base:high - base] = jnp.where(held == h, here, there).astype(F32)


def vmem(count):
    return [pl.BlockSpec(memory_space=pltpu.VMEM)] * count


def far(count):
    return [pl.BlockSpec(memory_space=pl.ANY)] * count


def params(mib):
    return pltpu.CompilerParams(vmem_limit_bytes=mib * 1024 * 1024)


def shape(dims, kind):
    return jax.ShapeDtypeStruct(dims, kind)


def body(inputs, pre_first, grad_out, w_first, w_second):
    rows, cols, c1 = pre_first.shape
    c0 = inputs.shape[2]
    half, pooled = cols // 2, rows // 2
    lats, lons = lax.axis_size("lat"), lax.axis_size("lon")
    depths = lons // 2
    band, place = lax.axis_index("lat"), lax.axis_index("lon")
    core = lax.rem(place, 2)
    even = lax.rem(band, 2) == 0

    edge = -(-(rows + pooled + 4) // 16) * 16
    row_a, row_b, col_a, col_b, held_pre = pl.pallas_call(
        functools.partial(pack_kernel, lats),
        out_shape=(
            pltpu.VMEM((cols + half, c1), BF16),
            pltpu.VMEM((cols + half, c1), BF16),
            pltpu.VMEM((edge, c1), BF16),
            pltpu.VMEM((edge, c1), BF16),
            pltpu.VMEM(pre_first.shape, BF16),
        ),
        in_specs=far(2),
        out_specs=tuple(vmem(5)),
        scratch_shapes=[
            pltpu.VMEM((2, edge, c1), F32),
            pltpu.VMEM(grad_out.shape, BF16),
            pltpu.SemaphoreType.DMA((2,)),
        ],
        compiler_params=params(58),
        cost_estimate=pl.CostEstimate(flops=1000, bytes_accessed=1 << 18, transcendentals=0),
    )(pre_first, grad_out)
    pairs = [(i * lons + j, i * lons + (j + lons // 2) % lons) for i in (0, lats - 1) for j in range(lons)]
    for i in range(1, lats - 1, 2):
        for j in range(lons):
            pairs += [(i * lons + j, (i + 1) * lons + j), ((i + 1) * lons + j, i * lons + j)]
    every = [(i * lons + j, (i ^ 1) * lons + j) for i in range(lats) for j in range(lons)]
    row_b = lax.ppermute(row_b, AREA, pairs)
    row_a = lax.ppermute(row_a, AREA, every)

    slope, act_t, act_ends = pl.pallas_call(
        local_kernel,
        out_shape=(
            shape((rows, half, 2 * c1), F32),
            shape((2, 2 * c1, pooled * half), BF16),
            shape((2, rows, c1), F32),
        ),
        in_specs=vmem(1),
        out_specs=tuple(vmem(3)),
        scratch_shapes=[
            pltpu.VMEM((cols, c1), F32),
            pltpu.VMEM((2, pooled, half, 2 * c1), BF16),
        ],
        compiler_params=params(16),
        cost_estimate=pl.CostEstimate(flops=60 * rows * cols * c1, bytes_accessed=2 << 20,
                                      transcendentals=2 * rows * cols * c1),
    )(held_pre)

    fields_t, field_ends, taps_first, taps_second = pl.pallas_call(
        layout_kernel,
        out_shape=(
            shape((2 * c0, rows * half), BF16),
            shape((2 * c0, 2 * rows), BF16),
            shape((6 * c0, 4 * c1), BF16),
            shape((3, 2 * c1, 4 * c1), BF16),
        ),
        in_specs=vmem(3),
        out_specs=tuple(vmem(4)),
        scratch_shapes=[pltpu.VMEM((rows, c0, 2 * cols), BF16)],
        compiler_params=params(16),
        cost_estimate=pl.CostEstimate(flops=4 * rows * cols * c0 * cols, bytes_accessed=3 << 20, transcendentals=0),
    )(jnp.transpose(inputs, (0, 2, 1)), w_first, w_second)
    row_b, row_a, slope, fields_t = lax.optimization_barrier((row_b, row_a, slope, fields_t))

    def corners(at):
        places = (at * (cols - 1), cols + at * (half - 1))
        above, below = (jnp.where(even, one, two) for one, two in ((row_b, row_a), (row_a, row_b)))
        return jnp.concatenate([part[p:p + 1] for p in places for part in (above, below)], 0)

    low, high = corners(0), corners(1)
    pad = jnp.zeros((edge - rows - pooled - 4, c1), BF16)
    col_a = jnp.concatenate([col_a[:rows + pooled], jnp.where(core == 0, high, low), pad], 0)
    col_b = jnp.concatenate([col_b[:rows + pooled], jnp.where(core == 0, low, high), pad], 0)
    col_b = lax.ppermute(col_b, "lon", [(i, (i + 2 * (i % 2) - 1) % lons) for i in range(lons)])
    col_a = lax.ppermute(col_a, "lon", [(i, i ^ 1) for i in range(lons)])

    block = -(-9 * (c1 + c0) // (32 * lats)) * 16
    held = lats * block
    reach = -(-(rows + 2) // 16) * 16
    spread, keep, raw_ends, slope_ends, out_ends = pl.pallas_call(
        functools.partial(middle_kernel, lats),
        out_shape=(
            shape((rows + 3, half, 4 * c1), BF16),
            shape((2 * held, c1), F32),
            shape((2, reach, c1), F32),
            shape((2, reach, c1), F32),
            shape((2, -(-(pooled + 2) // 16) * 16, c1), F32),
        ),
        in_specs=vmem(7),
        out_specs=tuple(vmem(5)),
        scratch_shapes=[
            pltpu.VMEM((pooled + 2, half, c1), F32),
            pltpu.VMEM((pooled + 2, half, 4 * c1), BF16),
            pltpu.VMEM((3, pooled, half, 2 * c1), F32),
            pltpu.VMEM((4, half, 2 * c1), F32),
            pltpu.VMEM((cols, c1), F32),
            pltpu.VMEM((4, 2 * c1, 3 * c1), F32),
            pltpu.VMEM((2 * c1, 3 * c1), F32),
        ],
        compiler_params=params(16),
        cost_estimate=pl.CostEstimate(flops=2 * rows * cols * c1 * 9 * (2 * c1 + c0), bytes_accessed=8 << 20,
                                      transcendentals=0),
    )(grad_out, row_a, row_b, slope, act_t, fields_t, taps_second)
    col_a, col_b, keep = lax.optimization_barrier((col_a, col_b, keep))

    ends, own, other = pl.pallas_call(
        functools.partial(columns_kernel, lats),
        out_shape=(
            shape((4, reach, c1), BF16),
            shape((held, c1), F32),
            shape((held, c1), F32),
        ),
        in_specs=vmem(9),
        out_specs=tuple(vmem(3)),
        scratch_shapes=[
            pltpu.VMEM((4, 4 * reach, 4 * c1), BF16),
            pltpu.VMEM((4, reach, c1), F32),
            pltpu.VMEM((4, 2 * rows, 4 * c1), BF16),
            pltpu.VMEM((2 * held, c1), F32),
        ],
        compiler_params=params(16),
        cost_estimate=pl.CostEstimate(flops=1 << 28, bytes_accessed=3 << 20, transcendentals=0),
    )(col_a, col_b, act_ends, field_ends, taps_second, keep, raw_ends, slope_ends, out_ends)

    swap = [(i, i ^ 1) for i in range(lons)]

    def between_chips(value, over_lat, over_lon):
        turn = odd(over_lat) ^ odd(over_lon)
        return lax.ppermute(value, AREA, [
            (i * lons + j, (i ^ over_lat) * lons + (j ^ (2 * over_lon) ^ turn)) for i in range(lats) for j in range(lons)])

    parts = (own + lax.ppermute(other, "lon", swap)).reshape(lats, block, c1)
    sent = [parts[far].astype(BF16) for far in range(1, lats)]
    *sent, ends = lax.optimization_barrier((*sent, ends))
    got = [between_chips(sent[far - 1], far, 0) for far in reversed(range(1, lats))]
    grad_inputs = pl.pallas_call(
        functools.partial(last_kernel, lats),
        out_shape=shape((rows, c0, cols), BF16),
        in_specs=vmem(3),
        out_specs=vmem(1)[0],
        scratch_shapes=[
            pltpu.VMEM((rows + 3, half, 4 * c1), BF16),
            pltpu.VMEM((reach, 4 * c1), F32),
            pltpu.VMEM((2 * c0, rows * half), F32),
            pltpu.VMEM((pooled, c0, 2 * cols), BF16),
        ],
        compiler_params=params(12),
        cost_estimate=pl.CostEstimate(flops=2 * rows * cols * c1 * 9 * c0, bytes_accessed=3 << 20, transcendentals=0),
    )(spread, ends, taps_first)
    *got, grad_inputs = lax.optimization_barrier((*got, grad_inputs))
    total = parts[0]
    for value in got:
        total = total + value.astype(F32)
    part = total.astype(BF16)
    terms = [part] + [between_chips(part, 0, far) for far in range(1, depths)]
    terms = [term.astype(F32) for term in terms]
    while len(terms) > 1:
        terms = [terms[k + (k > 0)] + terms[k + (k == 0)] for k in range(0, len(terms), 2)]
    part = terms[0].astype(BF16)
    mine = jnp.stack([part] + [between_chips(part, far, 0) for far in range(1, lats)], 0)
    theirs = lax.ppermute(mine, "lon", swap)

    grad_w_first, grad_w_second = pl.pallas_call(
        gather_kernel,
        out_shape=(shape((9 * c0, c1), F32), shape((9 * c1, c1), F32)),
        in_specs=vmem(2),
        out_specs=tuple(vmem(2)),
        compiler_params=params(8),
        cost_estimate=pl.CostEstimate(flops=1000, bytes_accessed=3 << 19, transcendentals=0),
    )(mine, theirs)
    return (jnp.transpose(grad_inputs, (0, 2, 1)), grad_w_first.reshape(w_first.shape),
            grad_w_second.reshape(w_second.shape))


def solution(mesh):
    in_specs = (P("lat", "lon", None), P("lat", "lon", None), P("lat", "lon", None), P(), P())
    out_specs = (P("lat", "lon", None), P(), P())
    return jax.shard_map(body, mesh=mesh, in_specs=in_specs, out_specs=out_specs, check_vma=False)
```

```python
import functools

import jax
import jax.numpy as jnp
from jax import lax
from jax.experimental import pallas as pl
from jax.experimental.pallas import tpu as pltpu
from jax.sharding import PartitionSpec as P

inv_root = 0.7071067811865476
density = 0.3989422804014327

F32 = jnp.float32
BF16 = jnp.bfloat16
AREA = ("lat", "lon")


def cdf_of(value):
    return 0.5 * (1.0 + lax.erf(value * inv_root))


def slope_of(value, cdf):
    return 0.25 * (cdf + value * jnp.exp(-0.5 * value * value) * density)


def dot(left, right):
    return jnp.dot(left, right, preferred_element_type=F32)


def dot_nt(left, right):
    return lax.dot_general(left, right, (((1,), (1,)), ((), ())), preferred_element_type=F32)


def position(lats):
    band, place = lax.axis_index("lat"), lax.axis_index("lon")
    return band, band == 0, band == lats - 1, lax.rem(band, 2) == 0, lax.rem(place, 2)


def odd(value):
    for shift in (4, 2, 1):
        value = value ^ (value >> shift)
    return value & 1


def half_held():
    band, place = lax.axis_index("lat"), lax.axis_index("lon")
    return odd(band) ^ odd(place // 2) ^ (place % 2)


def pack_kernel(lats, pre_far, grad_far, row_a, row_b, col_a, col_b, pre, hold, grad_out, sems):
    copies = [pltpu.make_async_copy(pre_far, pre, sems.at[0]), pltpu.make_async_copy(grad_far, grad_out, sems.at[1])]
    for copy in copies:
        copy.start()
    for copy in copies:
        copy.wait()
    rows, cols, c1 = pre.shape
    pooled, half = grad_out.shape[:2]
    _, _, _, even, core = position(lats)
    for message, low in ((row_a, ~even), (row_b, even)):
        message[:cols] = pre[jnp.where(low, 0, rows - 1)]
        message[cols:] = grad_out[jnp.where(low, 0, pooled - 1)]
    hold[:, rows + pooled:] = jnp.zeros((2, hold.shape[1] - rows - pooled, c1), F32)
    for side, (p, g) in enumerate(((0, 0), (cols - 16, half - 16))):
        at = 15 * side
        for r in range(rows):
            hold[side, r:r + 1] = pre[r, p:p + 16].astype(F32)[at:at + 1]
        for i in range(pooled):
            hold[side, rows + i:rows + i + 1] = grad_out[i, g:g + 16].astype(F32)[at:at + 1]
    col_a[...] = hold[1 - core].astype(BF16)
    col_b[...] = hold[core].astype(BF16)


def one_at(where):
    return jnp.where(where, 1.0, 0.0).astype(BF16)


def local_kernel(pre, slope, act_t, act_ends, line, act_s):
    rows, cols, c1 = pre.shape
    half = cols // 2

    def one_row(r, carry):
        line[...] = pre[r].astype(F32)
        for pc in range(2):
            value = line[pl.ds(pc, half, stride=2), :]
            cdf = cdf_of(value)
            act = value * cdf
            act_s[r % 2, r // 2, :, pc * c1:(pc + 1) * c1] = act.astype(BF16)
            act_ends[pc, pl.ds(r, 1), :] = act[pc * (half - 1):pc * (half - 1) + 1]
            slope[r, :, pc * c1:(pc + 1) * c1] = slope_of(value, cdf)
        return carry

    lax.fori_loop(0, rows, one_row, 0)
    for pr in range(2):
        act_t[pr] = act_s[pr].reshape(rows // 2 * half, 2 * c1).T


def layout_kernel(fields, w_first, w_second, fields_t, field_ends, taps_first, taps_second, turned):
    rows, c0, cols = fields.shape
    c1 = w_first.shape[3]
    half = cols // 2
    col = lax.broadcasted_iota(jnp.int32, (cols, 2 * cols), 0)
    lane = lax.broadcasted_iota(jnp.int32, (cols, 2 * cols), 1)
    turn = lane // cols
    parity = (lane % cols) // half
    parity = parity + turn - 2 * parity * turn
    order = one_at(col == 2 * (lane % half) + parity)
    turned[...] = dot(fields[...].reshape(rows * c0, cols), order).astype(BF16).reshape(rows, c0, 2 * cols)
    low = lax.broadcasted_iota(jnp.int32, (c0, cols), 1) < half
    for q in range(rows // 2):
        fields_t[:c0, q * cols:(q + 1) * cols] = jnp.where(low, turned[2 * q, :, :cols], turned[2 * q + 1, :, cols:])
        fields_t[c0:, q * cols:(q + 1) * cols] = jnp.where(low, turned[2 * q, :, cols:], turned[2 * q + 1, :, :cols])
    cell = lax.broadcasted_iota(jnp.int32, (rows * half, 2 * rows), 0)
    n = lax.broadcasted_iota(jnp.int32, (rows * half, 2 * rows), 1)
    pick = one_at(cell == (n % rows) * half + (n // rows) * (half - 1))
    field_ends[...] = dot(fields_t[...], pick).astype(BF16)
    taps_second[...] = jnp.zeros_like(taps_second)
    taps_first[...] = jnp.zeros_like(taps_first)
    for a in range(3):
        for pc, blocks in ((0, (2, 1, None, 0)), (1, (None, 2, 0, 1))):
            for k, b in enumerate(blocks):
                if b is not None:
                    taps_second[a, pc * c1:(pc + 1) * c1, k * c1:(k + 1) * c1] = w_second[a, b]
        for pc, blocks in ((0, (2, 1, 0, None)), (1, (None, 2, 1, 0))):
            for k, b in enumerate(blocks):
                if b is not None:
                    start = (2 * a + pc) * c0
                    taps_first[start:start + c0, k * c1:(k + 1) * c1] = w_first[a, b]


def middle_kernel(lats, grad_out, row_a, row_b, slope, act_t, fields_t, taps,
                  spread, keep, raw_ends, slope_ends, out_ends,
                  grid, wide, prods, ends, line, sums, corner):
    _, first, last, even, _ = position(lats)
    top = jnp.where(even, row_b[...], row_a[...])
    bottom = jnp.where(even, row_a[...], row_b[...])
    rows, half, c2 = slope.shape
    c1 = c2 // 2
    pooled = rows // 2
    c0 = fields_t.shape[0] // 2
    cells = pooled * half
    raw_ends[...] = jnp.zeros_like(raw_ends)
    slope_ends[...] = jnp.zeros_like(slope_ends)
    out_ends[...] = jnp.zeros_like(out_ends)

    grid[1:pooled + 1] = grad_out[...].astype(F32)
    grid[0] = top[2 * half:, :].astype(F32)
    outside = jnp.where(last, 0.0, 1.0)
    grid[pooled + 1] = bottom[2 * half:, :].astype(F32) * outside
    at = lax.broadcasted_iota(jnp.int32, (half, c1), 0)
    for i in range(pooled + 2):
        here = grid[i]
        out_ends[0, i:i + 1] = here[:1]
        out_ends[1, i:i + 1] = here[half - 1:]
        wide[i, :, :c1] = jnp.where(at == 0, 0.0, pltpu.roll(here, 1, 0)).astype(BF16)
        wide[i, :, c1:2 * c1] = here.astype(BF16)
        wide[i, :, 2 * c1:3 * c1] = jnp.where(at == half - 1, 0.0, pltpu.roll(here, half - 1, 0)).astype(BF16)
        wide[i, :, 3 * c1:] = here.astype(BF16)

    flat = wide[1:pooled + 1].reshape(cells, 4 * c1)
    for a in range(3):
        prods[a] = dot_nt(flat, taps[a]).reshape(pooled, half, c2)
    fold = jnp.where(first, taps[0], taps[2])
    ends[0] = dot_nt(wide[0], fold)
    ends[1] = dot_nt(wide[0], taps[1])
    ends[2] = dot_nt(wide[pooled + 1], taps[0])
    ends[3] = dot_nt(wide[pooled + 1], taps[1])

    def place(r, total, incline):
        inner = total * incline
        raw_ends[0, pl.ds(r, 1), :] = total[:1, :c1]
        raw_ends[1, pl.ds(r, 1), :] = total[half - 1:, c1:]
        slope_ends[0, pl.ds(r, 1), :] = incline[:1, :c1]
        slope_ends[1, pl.ds(r, 1), :] = incline[half - 1:, c1:]
        even, odd = inner[:, :c1], inner[:, c1:]
        spread[r, :, :c1] = jnp.where(at == 0, 0.0, pltpu.roll(odd, 1, 0)).astype(BF16)
        spread[r, :, c1:2 * c1] = jnp.where(at == 0, 0.0, even).astype(BF16)
        spread[r, :, 2 * c1:3 * c1] = jnp.where(at == half - 1, 0.0, odd).astype(BF16)
        spread[r, :, 3 * c1:] = jnp.where(at == half - 1, 0.0, pltpu.roll(even, half - 1, 0)).astype(BF16)

    def halo_slope(message):
        line[...] = message[:2 * half, :].astype(F32)
        both = [line[pl.ds(pc, half, stride=2), :] for pc in range(2)]
        return jnp.concatenate([slope_of(v, cdf_of(v)) for v in both], axis=1)

    place(0, ends[0] + ends[1] + prods[0, 0], halo_slope(top))
    place(1, ends[0] + prods[1, 0] + prods[0, 0], slope[0])

    def pair(i, carry):
        middle = prods[2, i] + prods[1, i]
        place(2 * i + 2, middle + prods[0, i + 1], slope[2 * i + 1])
        place(2 * i + 3, prods[2, i] + prods[1, i + 1] + prods[0, i + 1], slope[2 * i + 2])
        return carry

    lax.fori_loop(0, pooled - 1, pair, 0)
    final = prods[2, pooled - 1]
    place(rows, final + prods[1, pooled - 1] + ends[2], slope[rows - 1])
    place(rows + 1, (final + ends[3] + ends[2]) * outside, halo_slope(bottom))

    is_first = jnp.where(first, 1.0, 0.0).astype(BF16)
    not_first = jnp.where(first, 0.0, 1.0).astype(BF16)
    above = wide[0, :, :3 * c1]
    wide[0, :, :3 * c1] = above * not_first
    for n, (pr, start) in enumerate(((0, 0), (0, 1), (1, 1), (1, 2))):
        around = wide[start:start + pooled, :, :3 * c1].reshape(cells, 3 * c1)
        sums[n] = dot(act_t[pr], around)
    corner[...] = dot(act_t[0, :, :half], above * is_first)

    unit = c0
    per_tap = c1 // unit
    count = 9 * per_tap + 9

    def put(k, value):
        keep[k * unit:(k + 1) * unit, :] = value

    pieces = {0: ((0, 1), (1, 3)), 1: ((0, 1), (1, 2)), 2: ((0, 0), (1, 2))}
    for a in range(3):
        for b in range(3):
            total = None
            for pr, n in pieces[a]:
                for pc in range(2):
                    k = (pc + 1 - b) // 2 + 1
                    term = sums[n, pc * c1:(pc + 1) * c1, k * c1:(k + 1) * c1]
                    total = term if total is None else total + term
            if a == 0:
                for pc in range(2):
                    k = (pc + 1 - b) // 2 + 1
                    total = total + corner[pc * c1:(pc + 1) * c1, k * c1:(k + 1) * c1]
            total = total * 0.25
            for part in range(per_tap):
                put((3 * a + b) * per_tap + part, total[part * unit:(part + 1) * unit])

    head = spread[0]
    spread[0] = head * not_first
    spread[rows + 2] = head * is_first
    folded = dot(fields_t[:, :half], spread[rows + 2])
    for a in range(3):
        around = spread[2 - a:2 - a + rows].reshape(rows * half, 4 * c1)
        got = dot(fields_t[...], around)
        if a == 0:
            got = got + folded
        for b in range(3):
            even = got[:c0, (2 - b) * c1:(3 - b) * c1]
            odd = got[c0:, (3 - b) * c1:(4 - b) * c1]
            put(9 * per_tap + 3 * a + b, even + odd)
    if keep.shape[0] > count * unit:
        keep[count * unit:] = jnp.zeros((keep.shape[0] - count * unit, c1), F32)


def columns_kernel(lats, col_a, col_b, act_ends, field_ends, taps, keep, raw_ends, slope_ends, out_ends,
                   ends, own, other, lhs, values, right_hand, total):
    band, first, last, _, core = position(lats)
    c1 = act_ends.shape[2]
    rows = act_ends.shape[1]
    pooled = rows // 2
    c0 = field_ends.shape[0] // 2
    span, size = raw_ends.shape[1], col_a.shape[0]
    got_a, got_b = col_a[...].astype(F32), col_b[...].astype(F32)
    message = jnp.concatenate([jnp.where(core == 0, got_b, got_a), jnp.where(core == 0, got_a, got_b)], 1)
    at = lax.broadcasted_iota(jnp.int32, (size, 2 * c1), 0)
    message = jnp.where(jnp.logical_and(at == rows + pooled + 3, last), 0.0, message).astype(BF16)

    n = lax.broadcasted_iota(jnp.int32, (3 * span, size), 0)
    k = lax.broadcasted_iota(jnp.int32, (3 * span, size), 1)
    row = n % span
    want = (row - n // span + 2) // 2 - 1
    place = jnp.where(want < 0, rows + pooled + 2, jnp.where(want == pooled, rows + pooled + 3, rows + want))
    beside = dot(one_at(jnp.logical_and(k == place, row < rows + 2)), message)
    n = lax.broadcasted_iota(jnp.int32, (3 * span, out_ends.shape[1]), 0)
    k = lax.broadcasted_iota(jnp.int32, (3 * span, out_ends.shape[1]), 1)
    row = n % span
    want = (row - n // span + 2) // 2
    pick = one_at(jnp.logical_and(k == want, row < rows + 2))
    within = dot(pick, jnp.concatenate([out_ends[0], out_ends[1]], 1).astype(BF16))
    n = lax.broadcasted_iota(jnp.int32, (span, size), 0)
    k = lax.broadcasted_iota(jnp.int32, (span, size), 1)
    place = jnp.where(n == 0, rows + pooled, jnp.where(n == rows + 1, rows + pooled + 1, n - 1))
    saved = dot(one_at(jnp.logical_and(k == place, n < rows + 2)), message)
    incline = slope_of(saved, cdf_of(saved))

    head = lax.broadcasted_iota(jnp.int32, (span, 2 * c1), 0) < 2
    turned = jnp.logical_and(head, first)
    lhs[...] = jnp.zeros_like(lhs)
    rights = []
    for a in range(4):
        sides, inner = (x[min(a, 2) * span:(min(a, 2) + 1) * span] for x in (beside, within))
        if a == 2:
            sides, inner = jnp.where(turned, 0.0, sides), jnp.where(turned, 0.0, inner)
        if a == 3:
            sides, inner = jnp.where(turned, sides, 0.0), jnp.where(turned, inner, 0.0)
        rights.append(sides)
        sides, inner = sides.astype(BF16), inner.astype(BF16)
        left, right = sides[:, :c1], sides[:, c1:]
        lhs[a, :span, c1:2 * c1] = left
        lhs[a, :span, 2 * c1:3 * c1] = inner[:, :c1]
        lhs[a, :span, 3 * c1:] = left
        lhs[a, span:2 * span, :c1] = left
        lhs[a, 2 * span:3 * span, :c1] = inner[:, c1:]
        lhs[a, 2 * span:3 * span, c1:2 * c1] = right
        lhs[a, 2 * span:3 * span, 3 * c1:] = right
        lhs[a, 3 * span:, 2 * c1:3 * c1] = right
    found = dot_nt(lhs[0], taps[0]) + dot_nt(lhs[1], taps[1]) + dot_nt(lhs[2], taps[2]) + dot_nt(lhs[3], taps[0])
    row = lax.broadcasted_iota(jnp.int32, (span, c1), 0)
    inside = jnp.where(jnp.logical_or(row > rows + 1, jnp.logical_and(row == rows + 1, last)), 0.0, 1.0)
    values[0] = found[:span, c1:] * incline[:, :c1] * inside
    values[1] = (raw_ends[0] + found[span:2 * span, :c1]) * slope_ends[0] * inside
    values[2] = (raw_ends[1] + found[3 * span:, c1:]) * slope_ends[1] * inside
    values[3] = found[2 * span:3 * span, :c1] * incline[:, c1:] * inside
    ends[...] = values[...].astype(BF16)

    total[...] = keep[...]
    for side, b in ((0, 2), (1, 0)):
        around = jnp.concatenate([x[1:rows + 1, side * c1:(side + 1) * c1] for x in rights], 1).astype(BF16)
        terms = lax.dot_general(act_ends[side].astype(BF16), around, (((0,), (0,)), ((), ())),
                                preferred_element_type=F32) * 0.25
        for a in range(3):
            term = terms[:, a * c1:(a + 1) * c1]
            if a == 0:
                term = term + terms[:, 3 * c1:]
            low = (3 * a + b) * c1
            total[low:low + c1] = total[low:low + c1] + term
    right_hand[...] = jnp.zeros_like(right_hand)
    top = lax.broadcasted_iota(jnp.int32, (rows, c1), 0) == 0
    over = jnp.logical_and(top, first)
    for a in range(4):
        for j in range(4):
            value = values[j, 2 - min(a, 2):2 - min(a, 2) + rows]
            if a == 2:
                value = jnp.where(over, 0.0, value)
            if a == 3:
                value = jnp.where(over, value, 0.0)
            right_hand[a, j // 2 * rows:(j // 2 + 1) * rows, j * c1:(j + 1) * c1] = value.astype(BF16)
    for a in range(3):
        got = dot(field_ends[...], right_hand[a])
        if a == 0:
            got = got + dot(field_ends[...], right_hand[3])
        for b in range(3):
            even = got[:c0, (2 - b) * c1:(3 - b) * c1]
            odd = got[c0:, (3 - b) * c1:(4 - b) * c1]
            low = 9 * c1 + (3 * a + b) * c0
            total[low:low + c0] = total[low:low + c0] + even + odd

    held = own.shape[0]
    block = held // lats
    mine = half_held()
    for target, half_of in ((own, mine), (other, 1 - mine)):
        for far in range(lats):
            start = half_of * held + (band ^ far) * block
            target[far * block:(far + 1) * block] = total[pl.ds(pl.multiple_of(start, block), block), :]


def last_kernel(lats, part, ends, taps, out, spread, values, total, turned):
    rows, c0, cols = out.shape
    half = cols // 2
    c2 = 2 * c0
    depth = spread.shape[2]
    first = position(lats)[1]
    spread[...] = part[...]
    c1 = depth // 4
    for j in range(4):
        values[:, j * c1:(j + 1) * c1] = ends[j].astype(F32)
    at = lax.broadcasted_iota(jnp.int32, (16, 2 * c1), 0)
    for r in range(rows + 3):
        n = 0 if r == rows + 2 else r
        for side, (low, spot) in enumerate(((0, 0), (half - 16, 15))):
            lanes = slice(2 * side * c1, 2 * (side + 1) * c1)
            new = values[n:n + 1, lanes]
            if n == 0:
                new = jnp.where(first == (r != 0), new, 0.0)
            tile = spread[r, low:low + 16, lanes].astype(F32)
            spread[r, low:low + 16, lanes] = jnp.where(at == spot, new, tile).astype(BF16)
    result = dot_nt(taps[:c2], spread[2:rows + 2].reshape(rows * half, depth))
    for a in (1, 2):
        result = result + dot_nt(taps[a * c2:(a + 1) * c2],
                                 spread[2 - a:2 - a + rows].reshape(rows * half, depth))
    total[...] = result
    total[:, :half] = total[:, :half] + dot_nt(taps[:c2], spread[rows + 2])
    for q in range(rows // 2):
        pair = total[:, q * cols:(q + 1) * cols].astype(BF16)
        turned[q, :, :cols] = pair[:c0]
        turned[q, :, cols:] = pair[c0:]
    k = lax.broadcasted_iota(jnp.int32, (2 * cols, 2 * cols), 0)
    n = lax.broadcasted_iota(jnp.int32, (2 * cols, 2 * cols), 1)
    order = one_at(n == ((k % cols) // half) * cols + 2 * (k % half) + k // cols)
    found = dot(turned[...].reshape(rows // 2 * c0, 2 * cols), order).astype(BF16)
    for q in range(rows // 2):
        for rp in range(2):
            out[2 * q + rp] = found[q * c0:(q + 1) * c0, rp * cols:(rp + 1) * cols]


def gather_kernel(mine, theirs, out_first, out_second):
    lats, rows, c1 = mine.shape
    band, held = lax.axis_index("lat"), half_held()
    size = out_second.shape[0]
    total = size + out_first.shape[0]
    for h in range(2):
        for i in range(lats):
            at = (h * lats + i) * rows
            for out, base, end in ((out_second, 0, size), (out_first, size, total)):
                low, high = max(at, base), min(at + rows, end)
                if low < high:
                    here, there = (x[i ^ band, low - at:high - at] for x in (mine, theirs))
                    out[low - base:high - base] = jnp.where(held == h, here, there).astype(F32)


def vmem(count):
    return [pl.BlockSpec(memory_space=pltpu.VMEM)] * count


def far(count):
    return [pl.BlockSpec(memory_space=pl.ANY)] * count


def params(mib):
    return pltpu.CompilerParams(vmem_limit_bytes=mib * 1024 * 1024)


def shape(dims, kind):
    return jax.ShapeDtypeStruct(dims, kind)


def body(inputs, pre_first, grad_out, w_first, w_second):
    rows, cols, c1 = pre_first.shape
    c0 = inputs.shape[2]
    half, pooled = cols // 2, rows // 2
    lats, lons = lax.axis_size("lat"), lax.axis_size("lon")
    depths = lons // 2
    band, place = lax.axis_index("lat"), lax.axis_index("lon")
    core = lax.rem(place, 2)
    even = lax.rem(band, 2) == 0

    edge = -(-(rows + pooled + 4) // 16) * 16
    row_a, row_b, col_a, col_b, held_pre = pl.pallas_call(
        functools.partial(pack_kernel, lats),
        out_shape=(
            pltpu.VMEM((cols + half, c1), BF16),
            pltpu.VMEM((cols + half, c1), BF16),
            pltpu.VMEM((edge, c1), BF16),
            pltpu.VMEM((edge, c1), BF16),
            pltpu.VMEM(pre_first.shape, BF16),
        ),
        in_specs=far(2),
        out_specs=tuple(vmem(5)),
        scratch_shapes=[
            pltpu.VMEM((2, edge, c1), F32),
            pltpu.VMEM(grad_out.shape, BF16),
            pltpu.SemaphoreType.DMA((2,)),
        ],
        compiler_params=params(58),
        cost_estimate=pl.CostEstimate(flops=1000, bytes_accessed=1 << 18, transcendentals=0),
    )(pre_first, grad_out)
    pairs = [(j, (j + lons // 2) % lons) for j in range(lons)]
    pairs += [((lats - 1) * lons + j, (lats - 1) * lons + (j ^ 1)) for j in range(lons)]
    for i in range(1, lats - 1, 2):
        for j in range(lons):
            pairs += [(i * lons + j, (i + 1) * lons + j), ((i + 1) * lons + j, i * lons + j)]
    every = [(i * lons + j, (i ^ 1) * lons + j) for i in range(lats) for j in range(lons)]
    row_b = lax.ppermute(row_b, AREA, pairs)
    row_a = lax.ppermute(row_a, AREA, every)

    slope, act_t, act_ends = pl.pallas_call(
        local_kernel,
        out_shape=(
            shape((rows, half, 2 * c1), F32),
            shape((2, 2 * c1, pooled * half), BF16),
            shape((2, rows, c1), F32),
        ),
        in_specs=vmem(1),
        out_specs=tuple(vmem(3)),
        scratch_shapes=[
            pltpu.VMEM((cols, c1), F32),
            pltpu.VMEM((2, pooled, half, 2 * c1), BF16),
        ],
        compiler_params=params(16),
        cost_estimate=pl.CostEstimate(flops=60 * rows * cols * c1, bytes_accessed=2 << 20,
                                      transcendentals=2 * rows * cols * c1),
    )(held_pre)

    fields_t, field_ends, taps_first, taps_second = pl.pallas_call(
        layout_kernel,
        out_shape=(
            shape((2 * c0, rows * half), BF16),
            shape((2 * c0, 2 * rows), BF16),
            shape((6 * c0, 4 * c1), BF16),
            shape((3, 2 * c1, 4 * c1), BF16),
        ),
        in_specs=vmem(3),
        out_specs=tuple(vmem(4)),
        scratch_shapes=[pltpu.VMEM((rows, c0, 2 * cols), BF16)],
        compiler_params=params(16),
        cost_estimate=pl.CostEstimate(flops=4 * rows * cols * c0 * cols, bytes_accessed=3 << 20, transcendentals=0),
    )(jnp.transpose(inputs, (0, 2, 1)), w_first, w_second)
    row_b, row_a, slope, fields_t = lax.optimization_barrier((row_b, row_a, slope, fields_t))

    def corners(at):
        places = (at * (cols - 1), cols + at * (half - 1))
        above, below = (jnp.where(even, one, two) for one, two in ((row_b, row_a), (row_a, row_b)))
        return jnp.concatenate([part[p:p + 1] for p in places for part in (above, below)], 0)

    low, high = corners(0), corners(1)
    pad = jnp.zeros((edge - rows - pooled - 4, c1), BF16)
    col_a = jnp.concatenate([col_a[:rows + pooled], jnp.where(core == 0, high, low), pad], 0)
    col_b = jnp.concatenate([col_b[:rows + pooled], jnp.where(core == 0, low, high), pad], 0)
    col_b = lax.ppermute(col_b, "lon", [(i, (i + 2 * (i % 2) - 1) % lons) for i in range(lons)])
    col_a = lax.ppermute(col_a, "lon", [(i, i ^ 1) for i in range(lons)])

    block = -(-9 * (c1 + c0) // (32 * lats)) * 16
    held = lats * block
    reach = -(-(rows + 2) // 16) * 16
    spread, keep, raw_ends, slope_ends, out_ends = pl.pallas_call(
        functools.partial(middle_kernel, lats),
        out_shape=(
            shape((rows + 3, half, 4 * c1), BF16),
            shape((2 * held, c1), F32),
            shape((2, reach, c1), F32),
            shape((2, reach, c1), F32),
            shape((2, -(-(pooled + 2) // 16) * 16, c1), F32),
        ),
        in_specs=vmem(7),
        out_specs=tuple(vmem(5)),
        scratch_shapes=[
            pltpu.VMEM((pooled + 2, half, c1), F32),
            pltpu.VMEM((pooled + 2, half, 4 * c1), BF16),
            pltpu.VMEM((3, pooled, half, 2 * c1), F32),
            pltpu.VMEM((4, half, 2 * c1), F32),
            pltpu.VMEM((cols, c1), F32),
            pltpu.VMEM((4, 2 * c1, 3 * c1), F32),
            pltpu.VMEM((2 * c1, 3 * c1), F32),
        ],
        compiler_params=params(16),
        cost_estimate=pl.CostEstimate(flops=2 * rows * cols * c1 * 9 * (2 * c1 + c0), bytes_accessed=8 << 20,
                                      transcendentals=0),
    )(grad_out, row_a, row_b, slope, act_t, fields_t, taps_second)
    col_a, col_b, keep = lax.optimization_barrier((col_a, col_b, keep))

    ends, own, other = pl.pallas_call(
        functools.partial(columns_kernel, lats),
        out_shape=(
            shape((4, reach, c1), BF16),
            shape((held, c1), F32),
            shape((held, c1), F32),
        ),
        in_specs=vmem(9),
        out_specs=tuple(vmem(3)),
        scratch_shapes=[
            pltpu.VMEM((4, 4 * reach, 4 * c1), BF16),
            pltpu.VMEM((4, reach, c1), F32),
            pltpu.VMEM((4, 2 * rows, 4 * c1), BF16),
            pltpu.VMEM((2 * held, c1), F32),
        ],
        compiler_params=params(16),
        cost_estimate=pl.CostEstimate(flops=1 << 28, bytes_accessed=3 << 20, transcendentals=0),
    )(col_a, col_b, act_ends, field_ends, taps_second, keep, raw_ends, slope_ends, out_ends)

    swap = [(i, i ^ 1) for i in range(lons)]

    def between_chips(value, over_lat, over_lon):
        turn = odd(over_lat) ^ odd(over_lon)
        return lax.ppermute(value, AREA, [
            (i * lons + j, (i ^ over_lat) * lons + (j ^ (2 * over_lon) ^ turn)) for i in range(lats) for j in range(lons)])

    parts = (own + lax.ppermute(other, "lon", swap)).reshape(lats, block, c1)
    sent = [parts[far].astype(BF16) for far in range(1, lats)]
    *sent, ends = lax.optimization_barrier((*sent, ends))
    got = [between_chips(sent[far - 1], far, 0) for far in reversed(range(1, lats))]
    grad_inputs = pl.pallas_call(
        functools.partial(last_kernel, lats),
        out_shape=shape((rows, c0, cols), BF16),
        in_specs=vmem(3),
        out_specs=vmem(1)[0],
        scratch_shapes=[
            pltpu.VMEM((rows + 3, half, 4 * c1), BF16),
            pltpu.VMEM((reach, 4 * c1), F32),
            pltpu.VMEM((2 * c0, rows * half), F32),
            pltpu.VMEM((pooled, c0, 2 * cols), BF16),
        ],
        compiler_params=params(12),
        cost_estimate=pl.CostEstimate(flops=2 * rows * cols * c1 * 9 * c0, bytes_accessed=3 << 20, transcendentals=0),
    )(spread, ends, taps_first)
    *got, grad_inputs = lax.optimization_barrier((*got, grad_inputs))
    total = parts[0]
    for value in got:
        total = total + value.astype(F32)
    part = total.astype(BF16)
    terms = [part] + [between_chips(part, 0, far) for far in range(1, depths)]
    terms = [term.astype(F32) for term in terms]
    while len(terms) > 1:
        terms = [terms[k + (k > 0)] + terms[k + (k == 0)] for k in range(0, len(terms), 2)]
    part = terms[0].astype(BF16)
    mine = jnp.stack([part] + [between_chips(part, far, 0) for far in range(1, lats)], 0)
    theirs = lax.ppermute(mine, "lon", swap)

    grad_w_first, grad_w_second = pl.pallas_call(
        gather_kernel,
        out_shape=(shape((9 * c0, c1), F32), shape((9 * c1, c1), F32)),
        in_specs=vmem(2),
        out_specs=tuple(vmem(2)),
        compiler_params=params(8),
        cost_estimate=pl.CostEstimate(flops=1000, bytes_accessed=3 << 19, transcendentals=0),
    )(mine, theirs)
    return (jnp.transpose(grad_inputs, (0, 2, 1)), grad_w_first.reshape(w_first.shape),
            grad_w_second.reshape(w_second.shape))


def solution(mesh):
    in_specs = (P("lat", "lon", None), P("lat", "lon", None), P("lat", "lon", None), P(), P())
    out_specs = (P("lat", "lon", None), P(), P())
    return jax.shard_map(body, mesh=mesh, in_specs=in_specs, out_specs=out_specs, check_vma=False)
```

```python
import functools

import jax
import jax.numpy as jnp
from jax import lax
from jax.experimental import pallas as pl
from jax.experimental.pallas import tpu as pltpu
from jax.sharding import PartitionSpec as P

inv_root = 0.7071067811865476
density = 0.3989422804014327

F32 = jnp.float32
BF16 = jnp.bfloat16
AREA = ("lat", "lon")


def cdf_of(value):
    return 0.5 * (1.0 + lax.erf(value * inv_root))


def slope_of(value, cdf):
    return 0.25 * (cdf + value * jnp.exp(-0.5 * value * value) * density)


def dot(left, right):
    return jnp.dot(left, right, preferred_element_type=F32)


def dot_nt(left, right):
    return lax.dot_general(left, right, (((1,), (1,)), ((), ())), preferred_element_type=F32)


def position(lats):
    band, place = lax.axis_index("lat"), lax.axis_index("lon")
    return band, band == 0, band == lats - 1, lax.rem(band, 2) == 0, lax.rem(place, 2)


def odd(value):
    for shift in (4, 2, 1):
        value = value ^ (value >> shift)
    return value & 1


def half_held():
    band, place = lax.axis_index("lat"), lax.axis_index("lon")
    return odd(band) ^ odd(place // 2) ^ (place % 2)


def pack_kernel(lats, pre_far, grad_far, row_a, row_b, col_a, col_b, pre, hold, grad_out, sems):
    copies = [pltpu.make_async_copy(pre_far, pre, sems.at[0]), pltpu.make_async_copy(grad_far, grad_out, sems.at[1])]
    for copy in copies:
        copy.start()
    for copy in copies:
        copy.wait()
    rows, cols, c1 = pre.shape
    pooled, half = grad_out.shape[:2]
    _, _, _, even, core = position(lats)
    for message, low in ((row_a, ~even), (row_b, even)):
        message[:cols] = pre[jnp.where(low, 0, rows - 1)]
        message[cols:] = grad_out[jnp.where(low, 0, pooled - 1)]
    hold[:, rows + pooled:] = jnp.zeros((2, hold.shape[1] - rows - pooled, c1), F32)
    for side, (p, g) in enumerate(((0, 0), (cols - 16, half - 16))):
        at = 15 * side
        for r in range(rows):
            hold[side, r:r + 1] = pre[r, p:p + 16].astype(F32)[at:at + 1]
        for i in range(pooled):
            hold[side, rows + i:rows + i + 1] = grad_out[i, g:g + 16].astype(F32)[at:at + 1]
    col_a[...] = hold[1 - core].astype(BF16)
    col_b[...] = hold[core].astype(BF16)


def one_at(where):
    return jnp.where(where, 1.0, 0.0).astype(BF16)


def local_kernel(pre, slope, act_t, act_ends, line, act_s):
    rows, cols, c1 = pre.shape
    half = cols // 2

    def one_row(r, carry):
        line[...] = pre[r].astype(F32)
        for pc in range(2):
            value = line[pl.ds(pc, half, stride=2), :]
            cdf = cdf_of(value)
            act = value * cdf
            act_s[r % 2, r // 2, :, pc * c1:(pc + 1) * c1] = act.astype(BF16)
            act_ends[pc, pl.ds(r, 1), :] = act[pc * (half - 1):pc * (half - 1) + 1]
            slope[r, :, pc * c1:(pc + 1) * c1] = slope_of(value, cdf)
        return carry

    lax.fori_loop(0, rows, one_row, 0)
    for pr in range(2):
        act_t[pr] = act_s[pr].reshape(rows // 2 * half, 2 * c1).T


def layout_kernel(fields, w_first, w_second, fields_t, field_ends, taps_first, taps_second, turned):
    rows, c0, cols = fields.shape
    c1 = w_first.shape[3]
    half = cols // 2
    first = lax.axis_index("lat") == 0
    col = lax.broadcasted_iota(jnp.int32, (cols, 2 * cols), 0)
    lane = lax.broadcasted_iota(jnp.int32, (cols, 2 * cols), 1)
    turn = lane // cols
    parity = (lane % cols) // half
    parity = parity + turn - 2 * parity * turn
    order = one_at(col == 2 * (lane % half) + parity)
    turned[...] = dot(fields[...].reshape(rows * c0, cols), order).astype(BF16).reshape(rows, c0, 2 * cols)
    low = lax.broadcasted_iota(jnp.int32, (c0, cols), 1) < half
    none = jnp.zeros((c0, cols), BF16)
    for a in range(3):
        for q in range(rows // 2 + 1):
            for pc in range(2):
                near, away = (slice(0, cols), slice(cols, 2 * cols)) if pc == 0 else (slice(cols, 2 * cols), slice(0, cols))
                left, right = 2 * q - 2 + a, 2 * q - 1 + a
                one = turned[left, :, near] if 0 <= left < rows else none
                two = turned[right, :, away] if 0 <= right < rows else none
                if q == 0 and a != 1:
                    one = jnp.where(first == (a == 0), turned[0, :, near], none)
                start = (2 * a + pc) * c0
                fields_t[start:start + c0, q * cols:(q + 1) * cols] = jnp.where(low, one, two)
    reach = field_ends.shape[1] // 2
    cell = lax.broadcasted_iota(jnp.int32, ((rows + 2) * half, 2 * reach), 0)
    n = lax.broadcasted_iota(jnp.int32, ((rows + 2) * half, 2 * reach), 1)
    pick = one_at(cell == (n % reach) * half + (n // reach) * (half - 1))
    field_ends[...] = dot(fields_t[...], pick).astype(BF16)
    taps_second[...] = jnp.zeros_like(taps_second)
    taps_first[...] = jnp.zeros_like(taps_first)
    for a in range(3):
        for pc, blocks in ((0, (2, 1, None, 0)), (1, (None, 2, 0, 1))):
            for k, b in enumerate(blocks):
                if b is not None:
                    taps_second[a, pc * c1:(pc + 1) * c1, k * c1:(k + 1) * c1] = w_second[a, b]
        for pc, blocks in ((0, (2, 1, 0, None)), (1, (None, 2, 1, 0))):
            for k, b in enumerate(blocks):
                if b is not None:
                    start = (2 * a + pc) * c0
                    taps_first[start:start + c0, k * c1:(k + 1) * c1] = w_first[a, b]


def middle_kernel(lats, grad_out, row_a, row_b, slope, act_t, fields_t, taps,
                  spread, keep, raw_ends, slope_ends, out_ends,
                  grid, wide, prods, line, sums, corner):
    _, first, last, even, _ = position(lats)
    top = jnp.where(even, row_b[...], row_a[...])
    bottom = jnp.where(even, row_a[...], row_b[...])
    rows, half, c2 = slope.shape
    c1 = c2 // 2
    pooled = rows // 2
    c0 = fields_t.shape[0] // 6
    cells = pooled * half
    raw_ends[...] = jnp.zeros_like(raw_ends)
    slope_ends[...] = jnp.zeros_like(slope_ends)
    out_ends[...] = jnp.zeros_like(out_ends)

    grid[1:pooled + 1] = grad_out[...].astype(F32)
    grid[0] = top[2 * half:, :].astype(F32)
    outside = jnp.where(last, 0.0, 1.0)
    grid[pooled + 1] = bottom[2 * half:, :].astype(F32) * outside
    at = lax.broadcasted_iota(jnp.int32, (half, c1), 0)
    for i in range(pooled + 2):
        here = grid[i]
        out_ends[0, i:i + 1] = here[:1]
        out_ends[1, i:i + 1] = here[half - 1:]
        wide[i, :, :c1] = jnp.where(at == 0, 0.0, pltpu.roll(here, 1, 0)).astype(BF16)
        wide[i, :, c1:2 * c1] = here.astype(BF16)
        wide[i, :, 2 * c1:3 * c1] = jnp.where(at == half - 1, 0.0, pltpu.roll(here, half - 1, 0)).astype(BF16)
        wide[i, :, 3 * c1:] = here.astype(BF16)

    flat = wide[...].reshape((pooled + 2) * half, 4 * c1)
    for a in range(3):
        prods[a] = dot_nt(flat, taps[a]).reshape(pooled + 2, half, c2)
    fold = jnp.where(first, prods[0, 0], prods[2, 0])

    def place(r, total, incline):
        inner = total * incline
        raw_ends[0, pl.ds(r, 1), :] = total[:1, :c1]
        raw_ends[1, pl.ds(r, 1), :] = total[half - 1:, c1:]
        slope_ends[0, pl.ds(r, 1), :] = incline[:1, :c1]
        slope_ends[1, pl.ds(r, 1), :] = incline[half - 1:, c1:]
        even, odd = inner[:, :c1], inner[:, c1:]
        spread[r, :, :c1] = jnp.where(at == 0, 0.0, pltpu.roll(odd, 1, 0)).astype(BF16)
        spread[r, :, c1:2 * c1] = jnp.where(at == 0, 0.0, even).astype(BF16)
        spread[r, :, 2 * c1:3 * c1] = jnp.where(at == half - 1, 0.0, odd).astype(BF16)
        spread[r, :, 3 * c1:] = jnp.where(at == half - 1, 0.0, pltpu.roll(even, half - 1, 0)).astype(BF16)

    def halo_slope(message):
        line[...] = message[:2 * half, :].astype(F32)
        both = [line[pl.ds(pc, half, stride=2), :] for pc in range(2)]
        return jnp.concatenate([slope_of(v, cdf_of(v)) for v in both], axis=1)

    place(0, fold + prods[1, 0] + prods[0, 1], halo_slope(top))
    place(1, fold + prods[1, 1] + prods[0, 1], slope[0])

    def pair(i, carry):
        place(2 * i, prods[2, i] + prods[1, i] + prods[0, i + 1], slope[2 * i - 1])
        place(2 * i + 1, prods[2, i] + prods[1, i + 1] + prods[0, i + 1], slope[2 * i])
        return carry

    lax.fori_loop(1, pooled, pair, 0)
    final, below = prods[2, pooled], prods[0, pooled + 1]
    place(rows, final + prods[1, pooled] + below, slope[rows - 1])
    place(rows + 1, (final + prods[1, pooled + 1] + below) * outside, halo_slope(bottom))

    is_first = jnp.where(first, 1.0, 0.0).astype(BF16)
    not_first = jnp.where(first, 0.0, 1.0).astype(BF16)
    above = wide[0, :, :3 * c1]
    wide[0, :, :3 * c1] = above * not_first
    for n, (pr, start) in enumerate(((0, 0), (0, 1), (1, 1), (1, 2))):
        around = wide[start:start + pooled, :, :3 * c1].reshape(cells, 3 * c1)
        sums[n] = dot(act_t[pr], around)
    corner[...] = dot(act_t[0, :, :half], above * is_first)

    unit = c0
    per_tap = c1 // unit
    count = 9 * per_tap + 9

    def put(k, value):
        keep[k * unit:(k + 1) * unit, :] = value

    pieces = {0: ((0, 1), (1, 3)), 1: ((0, 1), (1, 2)), 2: ((0, 0), (1, 2))}
    for a in range(3):
        for b in range(3):
            total = None
            for pr, n in pieces[a]:
                for pc in range(2):
                    k = (pc + 1 - b) // 2 + 1
                    term = sums[n, pc * c1:(pc + 1) * c1, k * c1:(k + 1) * c1]
                    total = term if total is None else total + term
            if a == 0:
                for pc in range(2):
                    k = (pc + 1 - b) // 2 + 1
                    total = total + corner[pc * c1:(pc + 1) * c1, k * c1:(k + 1) * c1]
            total = total * 0.25
            for part in range(per_tap):
                put((3 * a + b) * per_tap + part, total[part * unit:(part + 1) * unit])

    got = dot(fields_t[...], spread[...].reshape((rows + 2) * half, 4 * c1))
    for a in range(3):
        for b in range(3):
            even = got[2 * a * c0:(2 * a + 1) * c0, (2 - b) * c1:(3 - b) * c1]
            odd = got[(2 * a + 1) * c0:(2 * a + 2) * c0, (3 - b) * c1:(4 - b) * c1]
            put(9 * per_tap + 3 * a + b, even + odd)
    if keep.shape[0] > count * unit:
        keep[count * unit:] = jnp.zeros((keep.shape[0] - count * unit, c1), F32)


def columns_kernel(lats, col_a, col_b, act_ends, field_ends, taps, keep, raw_ends, slope_ends, out_ends,
                   ends, own, other, lhs, values, right_hand, total):
    band, first, last, _, core = position(lats)
    c1 = act_ends.shape[2]
    rows = act_ends.shape[1]
    pooled = rows // 2
    c0 = field_ends.shape[0] // 6
    span, size = raw_ends.shape[1], col_a.shape[0]
    got_a, got_b = col_a[...].astype(F32), col_b[...].astype(F32)
    message = jnp.concatenate([jnp.where(core == 0, got_b, got_a), jnp.where(core == 0, got_a, got_b)], 1)
    at = lax.broadcasted_iota(jnp.int32, (size, 2 * c1), 0)
    message = jnp.where(jnp.logical_and(at == rows + pooled + 3, last), 0.0, message).astype(BF16)

    n = lax.broadcasted_iota(jnp.int32, (3 * span, size), 0)
    k = lax.broadcasted_iota(jnp.int32, (3 * span, size), 1)
    row = n % span
    want = (row - n // span + 2) // 2 - 1
    place = jnp.where(want < 0, rows + pooled + 2, jnp.where(want == pooled, rows + pooled + 3, rows + want))
    beside = dot(one_at(jnp.logical_and(k == place, row < rows + 2)), message)
    n = lax.broadcasted_iota(jnp.int32, (3 * span, out_ends.shape[1]), 0)
    k = lax.broadcasted_iota(jnp.int32, (3 * span, out_ends.shape[1]), 1)
    row = n % span
    want = (row - n // span + 2) // 2
    pick = one_at(jnp.logical_and(k == want, row < rows + 2))
    within = dot(pick, jnp.concatenate([out_ends[0], out_ends[1]], 1).astype(BF16))
    n = lax.broadcasted_iota(jnp.int32, (span, size), 0)
    k = lax.broadcasted_iota(jnp.int32, (span, size), 1)
    place = jnp.where(n == 0, rows + pooled, jnp.where(n == rows + 1, rows + pooled + 1, n - 1))
    saved = dot(one_at(jnp.logical_and(k == place, n < rows + 2)), message)
    incline = slope_of(saved, cdf_of(saved))

    row = lax.broadcasted_iota(jnp.int32, (span, 2 * c1), 0)
    turned = jnp.logical_and(row < 2, first)
    sides, inner = ([x[a * span:(a + 1) * span] for a in range(3)] for x in (beside, within))
    over, over_inner = (jnp.where(turned, x[2], 0.0) for x in (sides, inner))
    sides[2], inner[2] = (jnp.where(turned, 0.0, x[2]) for x in (sides, inner))
    rights = sides + [over]
    lhs[...] = jnp.zeros_like(lhs)
    for a in range(3):
        one, two = sides[a], inner[a]
        if a == 0:
            one, two = one + pltpu.roll(over, span - 8, 0), two + pltpu.roll(over_inner, span - 8, 0)
        one, two = one.astype(BF16), two.astype(BF16)
        left, right = one[:, :c1], one[:, c1:]
        lhs[a, :span, c1:2 * c1] = left
        lhs[a, :span, 2 * c1:3 * c1] = two[:, :c1]
        lhs[a, :span, 3 * c1:] = left
        lhs[a, span:2 * span, :c1] = left
        lhs[a, 2 * span:3 * span, :c1] = two[:, c1:]
        lhs[a, 2 * span:3 * span, c1:2 * c1] = right
        lhs[a, 2 * span:3 * span, 3 * c1:] = right
        lhs[a, 3 * span:, 2 * c1:3 * c1] = right
    found = dot_nt(lhs[0], taps[0]) + dot_nt(lhs[1], taps[1]) + dot_nt(lhs[2], taps[2])
    head = lax.broadcasted_iota(jnp.int32, (span, 2 * c1), 0) < 2
    found = [found[k * span:(k + 1) * span] for k in range(4)]
    found = [x + jnp.where(head, pltpu.roll(x, 8, 0), 0.0) for x in found]
    row = lax.broadcasted_iota(jnp.int32, (span, c1), 0)
    inside = jnp.where(jnp.logical_or(row > rows + 1, jnp.logical_and(row == rows + 1, last)), 0.0, 1.0)
    values[0] = found[0][:, c1:] * incline[:, :c1] * inside
    values[1] = (raw_ends[0] + found[1][:, :c1]) * slope_ends[0] * inside
    values[2] = (raw_ends[1] + found[3][:, c1:]) * slope_ends[1] * inside
    values[3] = found[2][:, :c1] * incline[:, c1:] * inside
    ends[...] = values[...].astype(BF16)

    total[...] = keep[...]
    for side, b in ((0, 2), (1, 0)):
        around = jnp.concatenate([x[1:rows + 1, side * c1:(side + 1) * c1] for x in rights], 1).astype(BF16)
        terms = lax.dot_general(act_ends[side].astype(BF16), around, (((0,), (0,)), ((), ())),
                                preferred_element_type=F32) * 0.25
        for a in range(3):
            term = terms[:, a * c1:(a + 1) * c1]
            if a == 0:
                term = term + terms[:, 3 * c1:]
            low = (3 * a + b) * c1
            total[low:low + c1] = total[low:low + c1] + term
    right_hand[...] = jnp.zeros_like(right_hand)
    for j in range(4):
        right_hand[j // 2 * span:(j // 2 + 1) * span, j * c1:(j + 1) * c1] = ends[j]
    got = dot(field_ends[...], right_hand[...])
    for a in range(3):
        for b in range(3):
            even = got[2 * a * c0:(2 * a + 1) * c0, (2 - b) * c1:(3 - b) * c1]
            odd = got[(2 * a + 1) * c0:(2 * a + 2) * c0, (3 - b) * c1:(4 - b) * c1]
            low = 9 * c1 + (3 * a + b) * c0
            total[low:low + c0] = total[low:low + c0] + even + odd

    held = own.shape[0]
    block = held // lats
    mine = half_held()
    for target, half_of in ((own, mine), (other, 1 - mine)):
        for far in range(lats):
            start = half_of * held + (band ^ far) * block
            target[far * block:(far + 1) * block] = total[pl.ds(pl.multiple_of(start, block), block), :]


def last_kernel(lats, part, ends, taps, out, spread, values, total, turned):
    rows, c0, cols = out.shape
    half = cols // 2
    c2 = 2 * c0
    depth = spread.shape[2]
    first = position(lats)[1]
    spread[:rows + 2] = part[...]
    spread[rows + 2] = part[0]
    c1 = depth // 4
    for j in range(4):
        values[:, j * c1:(j + 1) * c1] = ends[j].astype(F32)
    at = lax.broadcasted_iota(jnp.int32, (16, 2 * c1), 0)
    for r in range(rows + 3):
        n = 0 if r == rows + 2 else r
        for side, (low, spot) in enumerate(((0, 0), (half - 16, 15))):
            lanes = slice(2 * side * c1, 2 * (side + 1) * c1)
            new = values[n:n + 1, lanes]
            tile = spread[r, low:low + 16, lanes].astype(F32)
            spread[r, low:low + 16, lanes] = jnp.where(at == spot, new, tile).astype(BF16)
    spread[0] = spread[0] * one_at(~first)
    spread[rows + 2] = spread[rows + 2] * one_at(first)
    result = dot_nt(taps[:c2], spread[2:rows + 2].reshape(rows * half, depth))
    for a in (1, 2):
        result = result + dot_nt(taps[a * c2:(a + 1) * c2],
                                 spread[2 - a:2 - a + rows].reshape(rows * half, depth))
    total[...] = result
    total[:, :half] = total[:, :half] + dot_nt(taps[:c2], spread[rows + 2])
    for q in range(rows // 2):
        pair = total[:, q * cols:(q + 1) * cols].astype(BF16)
        turned[q, :, :cols] = pair[:c0]
        turned[q, :, cols:] = pair[c0:]
    k = lax.broadcasted_iota(jnp.int32, (2 * cols, 2 * cols), 0)
    n = lax.broadcasted_iota(jnp.int32, (2 * cols, 2 * cols), 1)
    order = one_at(n == ((k % cols) // half) * cols + 2 * (k % half) + k // cols)
    found = dot(turned[...].reshape(rows // 2 * c0, 2 * cols), order).astype(BF16)
    for q in range(rows // 2):
        for rp in range(2):
            out[2 * q + rp] = found[q * c0:(q + 1) * c0, rp * cols:(rp + 1) * cols]


def gather_kernel(mine, theirs, out_first, out_second):
    lats, rows, c1 = mine.shape
    band, held = lax.axis_index("lat"), half_held()
    size = out_second.shape[0]
    total = size + out_first.shape[0]
    for h in range(2):
        for i in range(lats):
            at = (h * lats + i) * rows
            for out, base, end in ((out_second, 0, size), (out_first, size, total)):
                low, high = max(at, base), min(at + rows, end)
                if low < high:
                    here, there = (x[i ^ band, low - at:high - at] for x in (mine, theirs))
                    out[low - base:high - base] = jnp.where(held == h, here, there).astype(F32)


def vmem(count):
    return [pl.BlockSpec(memory_space=pltpu.VMEM)] * count


def far(count):
    return [pl.BlockSpec(memory_space=pl.ANY)] * count


def params(mib):
    return pltpu.CompilerParams(vmem_limit_bytes=mib * 1024 * 1024)


def shape(dims, kind):
    return jax.ShapeDtypeStruct(dims, kind)


def body(inputs, pre_first, grad_out, w_first, w_second):
    rows, cols, c1 = pre_first.shape
    c0 = inputs.shape[2]
    half, pooled = cols // 2, rows // 2
    lats, lons = lax.axis_size("lat"), lax.axis_size("lon")
    depths = lons // 2
    band, place = lax.axis_index("lat"), lax.axis_index("lon")
    core = lax.rem(place, 2)
    even = lax.rem(band, 2) == 0

    edge = -(-(rows + pooled + 4) // 16) * 16
    reach = -(-(rows + 10) // 16) * 16
    row_a, row_b, col_a, col_b, held_pre = pl.pallas_call(
        functools.partial(pack_kernel, lats),
        out_shape=(
            pltpu.VMEM((cols + half, c1), BF16),
            pltpu.VMEM((cols + half, c1), BF16),
            pltpu.VMEM((edge, c1), BF16),
            pltpu.VMEM((edge, c1), BF16),
            pltpu.VMEM(pre_first.shape, BF16),
        ),
        in_specs=far(2),
        out_specs=tuple(vmem(5)),
        scratch_shapes=[
            pltpu.VMEM((2, edge, c1), F32),
            pltpu.VMEM(grad_out.shape, BF16),
            pltpu.SemaphoreType.DMA((2,)),
        ],
        compiler_params=params(58),
        cost_estimate=pl.CostEstimate(flops=1000, bytes_accessed=1 << 18, transcendentals=0),
    )(pre_first, grad_out)
    pairs = [(j, (j + lons // 2) % lons) for j in range(lons)]
    pairs += [((lats - 1) * lons + j, (lats - 1) * lons + (j ^ 1)) for j in range(lons)]
    for i in range(1, lats - 1, 2):
        for j in range(lons):
            pairs += [(i * lons + j, (i + 1) * lons + j), ((i + 1) * lons + j, i * lons + j)]
    every = [(i * lons + j, (i ^ 1) * lons + j) for i in range(lats) for j in range(lons)]
    row_b = lax.ppermute(row_b, AREA, pairs)
    row_a = lax.ppermute(row_a, AREA, every)

    slope, act_t, act_ends = pl.pallas_call(
        local_kernel,
        out_shape=(
            shape((rows, half, 2 * c1), F32),
            shape((2, 2 * c1, pooled * half), BF16),
            shape((2, rows, c1), F32),
        ),
        in_specs=vmem(1),
        out_specs=tuple(vmem(3)),
        scratch_shapes=[
            pltpu.VMEM((cols, c1), F32),
            pltpu.VMEM((2, pooled, half, 2 * c1), BF16),
        ],
        compiler_params=params(16),
        cost_estimate=pl.CostEstimate(flops=60 * rows * cols * c1, bytes_accessed=2 << 20,
                                      transcendentals=2 * rows * cols * c1),
    )(held_pre)

    fields_t, field_ends, taps_first, taps_second = pl.pallas_call(
        layout_kernel,
        out_shape=(
            shape((6 * c0, (rows + 2) * half), BF16),
            shape((6 * c0, 2 * reach), BF16),
            shape((6 * c0, 4 * c1), BF16),
            shape((3, 2 * c1, 4 * c1), BF16),
        ),
        in_specs=vmem(3),
        out_specs=tuple(vmem(4)),
        scratch_shapes=[pltpu.VMEM((rows, c0, 2 * cols), BF16)],
        compiler_params=params(16),
        cost_estimate=pl.CostEstimate(flops=4 * rows * cols * c0 * cols, bytes_accessed=3 << 20, transcendentals=0),
    )(jnp.transpose(inputs, (0, 2, 1)), w_first, w_second)
    row_b, row_a, slope, fields_t = lax.optimization_barrier((row_b, row_a, slope, fields_t))

    def corners(at):
        places = (at * (cols - 1), cols + at * (half - 1))
        above, below = (jnp.where(even, one, two) for one, two in ((row_b, row_a), (row_a, row_b)))
        return jnp.concatenate([part[p:p + 1] for p in places for part in (above, below)], 0)

    low, high = corners(0), corners(1)
    pad = jnp.zeros((edge - rows - pooled - 4, c1), BF16)
    col_a = jnp.concatenate([col_a[:rows + pooled], jnp.where(core == 0, high, low), pad], 0)
    col_b = jnp.concatenate([col_b[:rows + pooled], jnp.where(core == 0, low, high), pad], 0)
    col_b = lax.ppermute(col_b, "lon", [(i, (i + 2 * (i % 2) - 1) % lons) for i in range(lons)])
    col_a = lax.ppermute(col_a, "lon", [(i, i ^ 1) for i in range(lons)])

    block = -(-9 * (c1 + c0) // (32 * lats)) * 16
    held = lats * block
    spread, keep, raw_ends, slope_ends, out_ends = pl.pallas_call(
        functools.partial(middle_kernel, lats),
        out_shape=(
            shape((rows + 2, half, 4 * c1), BF16),
            shape((2 * held, c1), F32),
            shape((2, reach, c1), F32),
            shape((2, reach, c1), F32),
            shape((2, -(-(pooled + 2) // 16) * 16, c1), F32),
        ),
        in_specs=vmem(7),
        out_specs=tuple(vmem(5)),
        scratch_shapes=[
            pltpu.VMEM((pooled + 2, half, c1), F32),
            pltpu.VMEM((pooled + 2, half, 4 * c1), BF16),
            pltpu.VMEM((3, pooled + 2, half, 2 * c1), F32),
            pltpu.VMEM((cols, c1), F32),
            pltpu.VMEM((4, 2 * c1, 3 * c1), F32),
            pltpu.VMEM((2 * c1, 3 * c1), F32),
        ],
        compiler_params=params(16),
        cost_estimate=pl.CostEstimate(flops=2 * rows * cols * c1 * 9 * (2 * c1 + c0), bytes_accessed=8 << 20,
                                      transcendentals=0),
    )(grad_out, row_a, row_b, slope, act_t, fields_t, taps_second)
    col_a, col_b, keep = lax.optimization_barrier((col_a, col_b, keep))

    ends, own, other = pl.pallas_call(
        functools.partial(columns_kernel, lats),
        out_shape=(
            shape((4, reach, c1), BF16),
            shape((held, c1), F32),
            shape((held, c1), F32),
        ),
        in_specs=vmem(9),
        out_specs=tuple(vmem(3)),
        scratch_shapes=[
            pltpu.VMEM((3, 4 * reach, 4 * c1), BF16),
            pltpu.VMEM((4, reach, c1), F32),
            pltpu.VMEM((2 * reach, 4 * c1), BF16),
            pltpu.VMEM((2 * held, c1), F32),
        ],
        compiler_params=params(16),
        cost_estimate=pl.CostEstimate(flops=1 << 28, bytes_accessed=3 << 20, transcendentals=0),
    )(col_a, col_b, act_ends, field_ends, taps_second, keep, raw_ends, slope_ends, out_ends)

    swap = [(i, i ^ 1) for i in range(lons)]

    def between_chips(value, over_lat, over_lon):
        turn = odd(over_lat) ^ odd(over_lon)
        return lax.ppermute(value, AREA, [
            (i * lons + j, (i ^ over_lat) * lons + (j ^ (2 * over_lon) ^ turn)) for i in range(lats) for j in range(lons)])

    parts = (own + lax.ppermute(other, "lon", swap)).reshape(lats, block, c1)
    sent = [parts[far].astype(BF16) for far in range(1, lats)]
    *sent, ends = lax.optimization_barrier((*sent, ends))
    got = [between_chips(sent[far - 1], far, 0) for far in reversed(range(1, lats))]
    grad_inputs = pl.pallas_call(
        functools.partial(last_kernel, lats),
        out_shape=shape((rows, c0, cols), BF16),
        in_specs=vmem(3),
        out_specs=vmem(1)[0],
        scratch_shapes=[
            pltpu.VMEM((rows + 3, half, 4 * c1), BF16),
            pltpu.VMEM((reach, 4 * c1), F32),
            pltpu.VMEM((2 * c0, rows * half), F32),
            pltpu.VMEM((pooled, c0, 2 * cols), BF16),
        ],
        compiler_params=params(12),
        cost_estimate=pl.CostEstimate(flops=2 * rows * cols * c1 * 9 * c0, bytes_accessed=3 << 20, transcendentals=0),
    )(spread, ends, taps_first)
    *got, grad_inputs = lax.optimization_barrier((*got, grad_inputs))
    total = parts[0]
    for value in got:
        total = total + value.astype(F32)
    part = total.astype(BF16)
    terms = [part] + [between_chips(part, 0, far) for far in range(1, depths)]
    terms = [term.astype(F32) for term in terms]
    while len(terms) > 1:
        terms = [terms[k + (k > 0)] + terms[k + (k == 0)] for k in range(0, len(terms), 2)]
    part = terms[0].astype(BF16)
    mine = jnp.stack([part] + [between_chips(part, far, 0) for far in range(1, lats)], 0)
    theirs = lax.ppermute(mine, "lon", swap)

    grad_w_first, grad_w_second = pl.pallas_call(
        gather_kernel,
        out_shape=(shape((9 * c0, c1), F32), shape((9 * c1, c1), F32)),
        in_specs=vmem(2),
        out_specs=tuple(vmem(2)),
        compiler_params=params(8),
        cost_estimate=pl.CostEstimate(flops=1000, bytes_accessed=3 << 19, transcendentals=0),
    )(mine, theirs)
    return (jnp.transpose(grad_inputs, (0, 2, 1)), grad_w_first.reshape(w_first.shape),
            grad_w_second.reshape(w_second.shape))


def solution(mesh):
    in_specs = (P("lat", "lon", None), P("lat", "lon", None), P("lat", "lon", None), P(), P())
    out_specs = (P("lat", "lon", None), P(), P())
    return jax.shard_map(body, mesh=mesh, in_specs=in_specs, out_specs=out_specs, check_vma=False)
```

```python
import functools

import jax
import jax.numpy as jnp
from jax import lax
from jax.experimental import pallas as pl
from jax.experimental.pallas import tpu as pltpu
from jax.sharding import PartitionSpec as P

inv_root = 0.7071067811865476
density = 0.3989422804014327

F32 = jnp.float32
BF16 = jnp.bfloat16
AREA = ("lat", "lon")


def cdf_of(value):
    return 0.5 * (1.0 + lax.erf(value * inv_root))


def slope_of(value, cdf):
    return 0.25 * (cdf + value * jnp.exp(-0.5 * value * value) * density)


def dot(left, right):
    return jnp.dot(left, right, preferred_element_type=F32)


def dot_nt(left, right):
    return lax.dot_general(left, right, (((1,), (1,)), ((), ())), preferred_element_type=F32)


def position(lats):
    band, place = lax.axis_index("lat"), lax.axis_index("lon")
    return band, band == 0, band == lats - 1, lax.rem(band, 2) == 0, lax.rem(place, 2)


def odd(value):
    for shift in (4, 2, 1):
        value = value ^ (value >> shift)
    return value & 1


def half_held():
    band, place = lax.axis_index("lat"), lax.axis_index("lon")
    return odd(band) ^ odd(place // 2) ^ (place % 2)


def pack_kernel(lats, pre_far, grad_far, row_a, row_b, col_a, col_b, pre, hold, grad_out, sems):
    copies = [pltpu.make_async_copy(pre_far, pre, sems.at[0]), pltpu.make_async_copy(grad_far, grad_out, sems.at[1])]
    for copy in copies:
        copy.start()
    for copy in copies:
        copy.wait()
    rows, cols, c1 = pre.shape
    pooled, half = grad_out.shape[:2]
    _, _, _, even, core = position(lats)
    for message, low in ((row_a, ~even), (row_b, even)):
        message[:cols] = pre[jnp.where(low, 0, rows - 1)]
        message[cols:] = grad_out[jnp.where(low, 0, pooled - 1)]
    hold[:, rows + pooled:] = jnp.zeros((2, hold.shape[1] - rows - pooled, c1), F32)
    for side, (p, g) in enumerate(((0, 0), (cols - 16, half - 16))):
        at = 15 * side
        for r in range(rows):
            hold[side, r:r + 1] = pre[r, p:p + 16].astype(F32)[at:at + 1]
        for i in range(pooled):
            hold[side, rows + i:rows + i + 1] = grad_out[i, g:g + 16].astype(F32)[at:at + 1]
    col_a[...] = hold[1 - core].astype(BF16)
    col_b[...] = hold[core].astype(BF16)


def one_at(where):
    return jnp.where(where, 1.0, 0.0).astype(BF16)


def local_kernel(pre, slope, act_t, act_ends, line, act_s):
    rows, cols, c1 = pre.shape
    half = cols // 2

    def one_row(r, carry):
        line[...] = pre[r].astype(F32)
        for pc in range(2):
            value = line[pl.ds(pc, half, stride=2), :]
            cdf = cdf_of(value)
            act = value * cdf
            act_s[r % 2, r // 2, :, pc * c1:(pc + 1) * c1] = act.astype(BF16)
            act_ends[pc, pl.ds(r, 1), :] = act[pc * (half - 1):pc * (half - 1) + 1]
            slope[r, :, pc * c1:(pc + 1) * c1] = slope_of(value, cdf)
        return carry

    lax.fori_loop(0, rows, one_row, 0)
    for pr in range(2):
        act_t[pr] = act_s[pr].reshape(rows // 2 * half, 2 * c1).T


def layout_kernel(fields, w_first, w_second, fields_t, field_ends, taps_first, taps_second, turned):
    rows, c0, cols = fields.shape
    c1 = w_first.shape[3]
    half = cols // 2
    col = lax.broadcasted_iota(jnp.int32, (cols, 2 * cols), 0)
    lane = lax.broadcasted_iota(jnp.int32, (cols, 2 * cols), 1)
    turn = lane // cols
    parity = (lane % cols) // half
    parity = parity + turn - 2 * parity * turn
    order = one_at(col == 2 * (lane % half) + parity)
    turned[...] = dot(fields[...].reshape(rows * c0, cols), order).astype(BF16).reshape(rows, c0, 2 * cols)
    low = lax.broadcasted_iota(jnp.int32, (c0, cols), 1) < half
    for q in range(rows // 2):
        fields_t[:c0, q * cols:(q + 1) * cols] = jnp.where(low, turned[2 * q, :, :cols], turned[2 * q + 1, :, cols:])
        fields_t[c0:, q * cols:(q + 1) * cols] = jnp.where(low, turned[2 * q, :, cols:], turned[2 * q + 1, :, :cols])
    cell = lax.broadcasted_iota(jnp.int32, (rows * half, 2 * rows), 0)
    n = lax.broadcasted_iota(jnp.int32, (rows * half, 2 * rows), 1)
    pick = one_at(cell == (n % rows) * half + (n // rows) * (half - 1))
    field_ends[...] = dot(fields_t[...], pick).astype(BF16)
    taps_second[...] = jnp.zeros_like(taps_second)
    taps_first[...] = jnp.zeros_like(taps_first)
    for a in range(3):
        for pc, blocks in ((0, (2, 1, None, 0)), (1, (None, 2, 0, 1))):
            for k, b in enumerate(blocks):
                if b is not None:
                    taps_second[a, pc * c1:(pc + 1) * c1, k * c1:(k + 1) * c1] = w_second[a, b]
        for pc, blocks in ((0, (2, 1, 0, None)), (1, (None, 2, 1, 0))):
            for k, b in enumerate(blocks):
                if b is not None:
                    start = (2 * a + pc) * c0
                    taps_first[start:start + c0, k * c1:(k + 1) * c1] = w_first[a, b]


def middle_kernel(lats, grad_out, row_a, row_b, slope, act_t, fields_t, taps,
                  spread, keep, raw_ends, slope_ends, out_ends,
                  grid, wide, prods, ends, line, sums, corner):
    _, first, last, even, _ = position(lats)
    top = jnp.where(even, row_b[...], row_a[...])
    bottom = jnp.where(even, row_a[...], row_b[...])
    rows, half, c2 = slope.shape
    c1 = c2 // 2
    pooled = rows // 2
    c0 = fields_t.shape[0] // 2
    cells = pooled * half
    raw_ends[...] = jnp.zeros_like(raw_ends)
    slope_ends[...] = jnp.zeros_like(slope_ends)
    out_ends[...] = jnp.zeros_like(out_ends)

    grid[1:pooled + 1] = grad_out[...].astype(F32)
    grid[0] = top[2 * half:, :].astype(F32)
    outside = jnp.where(last, 0.0, 1.0)
    grid[pooled + 1] = bottom[2 * half:, :].astype(F32) * outside
    at = lax.broadcasted_iota(jnp.int32, (half, c1), 0)
    for i in range(pooled + 2):
        here = grid[i]
        out_ends[0, i:i + 1] = here[:1]
        out_ends[1, i:i + 1] = here[half - 1:]
        wide[i, :, :c1] = jnp.where(at == 0, 0.0, pltpu.roll(here, 1, 0)).astype(BF16)
        wide[i, :, c1:2 * c1] = here.astype(BF16)
        wide[i, :, 2 * c1:3 * c1] = jnp.where(at == half - 1, 0.0, pltpu.roll(here, half - 1, 0)).astype(BF16)
        wide[i, :, 3 * c1:] = here.astype(BF16)

    flat = wide[1:pooled + 1].reshape(cells, 4 * c1)
    for a in range(3):
        prods[a] = dot_nt(flat, taps[a]).reshape(pooled, half, c2)
    fold = jnp.where(first, taps[0], taps[2])
    ends[0] = dot_nt(wide[0], fold)
    ends[1] = dot_nt(wide[0], taps[1])
    ends[2] = dot_nt(wide[pooled + 1], taps[0])
    ends[3] = dot_nt(wide[pooled + 1], taps[1])

    def place(r, total, incline):
        inner = total * incline
        raw_ends[0, pl.ds(r, 1), :] = total[:1, :c1]
        raw_ends[1, pl.ds(r, 1), :] = total[half - 1:, c1:]
        slope_ends[0, pl.ds(r, 1), :] = incline[:1, :c1]
        slope_ends[1, pl.ds(r, 1), :] = incline[half - 1:, c1:]
        even, odd = inner[:, :c1], inner[:, c1:]
        spread[r, :, :c1] = jnp.where(at == 0, 0.0, pltpu.roll(odd, 1, 0)).astype(BF16)
        spread[r, :, c1:2 * c1] = jnp.where(at == 0, 0.0, even).astype(BF16)
        spread[r, :, 2 * c1:3 * c1] = jnp.where(at == half - 1, 0.0, odd).astype(BF16)
        spread[r, :, 3 * c1:] = jnp.where(at == half - 1, 0.0, pltpu.roll(even, half - 1, 0)).astype(BF16)

    def halo_slope(message):
        line[...] = message[:2 * half, :].astype(F32)
        both = [line[pl.ds(pc, half, stride=2), :] for pc in range(2)]
        return jnp.concatenate([slope_of(v, cdf_of(v)) for v in both], axis=1)

    place(0, ends[0] + ends[1] + prods[0, 0], halo_slope(top))
    place(1, ends[0] + prods[1, 0] + prods[0, 0], slope[0])

    def pair(i, carry):
        middle = prods[2, i] + prods[1, i]
        place(2 * i + 2, middle + prods[0, i + 1], slope[2 * i + 1])
        place(2 * i + 3, prods[2, i] + prods[1, i + 1] + prods[0, i + 1], slope[2 * i + 2])
        return carry

    lax.fori_loop(0, pooled - 1, pair, 0)
    final = prods[2, pooled - 1]
    place(rows, final + prods[1, pooled - 1] + ends[2], slope[rows - 1])
    place(rows + 1, (final + ends[3] + ends[2]) * outside, halo_slope(bottom))

    is_first = jnp.where(first, 1.0, 0.0).astype(BF16)
    not_first = jnp.where(first, 0.0, 1.0).astype(BF16)
    above = wide[0, :, :3 * c1]
    wide[0, :, :3 * c1] = above * not_first
    for n, (pr, start) in enumerate(((0, 0), (0, 1), (1, 1), (1, 2))):
        around = wide[start:start + pooled, :, :3 * c1].reshape(cells, 3 * c1)
        sums[n] = dot(act_t[pr], around)
    corner[...] = dot(act_t[0, :, :half], above * is_first)

    unit = c0
    per_tap = c1 // unit
    count = 9 * per_tap + 9

    def put(k, value):
        keep[k * unit:(k + 1) * unit, :] = value

    pieces = {0: ((0, 1), (1, 3)), 1: ((0, 1), (1, 2)), 2: ((0, 0), (1, 2))}
    for a in range(3):
        for b in range(3):
            total = None
            for pr, n in pieces[a]:
                for pc in range(2):
                    k = (pc + 1 - b) // 2 + 1
                    term = sums[n, pc * c1:(pc + 1) * c1, k * c1:(k + 1) * c1]
                    total = term if total is None else total + term
            if a == 0:
                for pc in range(2):
                    k = (pc + 1 - b) // 2 + 1
                    total = total + corner[pc * c1:(pc + 1) * c1, k * c1:(k + 1) * c1]
            total = total * 0.25
            for part in range(per_tap):
                put((3 * a + b) * per_tap + part, total[part * unit:(part + 1) * unit])

    head = spread[0]
    spread[0] = head * not_first
    spread[rows + 2] = head * is_first
    folded = dot(fields_t[:, :half], spread[rows + 2])
    for a in range(3):
        around = spread[2 - a:2 - a + rows].reshape(rows * half, 4 * c1)
        got = dot(fields_t[...], around)
        if a == 0:
            got = got + folded
        for b in range(3):
            even = got[:c0, (2 - b) * c1:(3 - b) * c1]
            odd = got[c0:, (3 - b) * c1:(4 - b) * c1]
            put(9 * per_tap + 3 * a + b, even + odd)
    if keep.shape[0] > count * unit:
        keep[count * unit:] = jnp.zeros((keep.shape[0] - count * unit, c1), F32)


def columns_kernel(lats, col_a, col_b, act_ends, field_ends, taps, keep, raw_ends, slope_ends, out_ends,
                   ends, *rest):
    own, other, (lhs, values, right_hand, total) = rest[:lats], rest[lats:2 * lats], rest[2 * lats:]
    band, first, last, _, core = position(lats)
    c1 = act_ends.shape[2]
    rows = act_ends.shape[1]
    pooled = rows // 2
    c0 = field_ends.shape[0] // 2
    span, size = raw_ends.shape[1], col_a.shape[0]
    got_a, got_b = col_a[...].astype(F32), col_b[...].astype(F32)
    message = jnp.concatenate([jnp.where(core == 0, got_b, got_a), jnp.where(core == 0, got_a, got_b)], 1)
    at = lax.broadcasted_iota(jnp.int32, (size, 2 * c1), 0)
    message = jnp.where(jnp.logical_and(at == rows + pooled + 3, last), 0.0, message).astype(BF16)

    n = lax.broadcasted_iota(jnp.int32, (3 * span, size), 0)
    k = lax.broadcasted_iota(jnp.int32, (3 * span, size), 1)
    row = n % span
    want = (row - n // span + 2) // 2 - 1
    place = jnp.where(want < 0, rows + pooled + 2, jnp.where(want == pooled, rows + pooled + 3, rows + want))
    beside = dot(one_at(jnp.logical_and(k == place, row < rows + 2)), message)
    n = lax.broadcasted_iota(jnp.int32, (3 * span, out_ends.shape[1]), 0)
    k = lax.broadcasted_iota(jnp.int32, (3 * span, out_ends.shape[1]), 1)
    row = n % span
    want = (row - n // span + 2) // 2
    pick = one_at(jnp.logical_and(k == want, row < rows + 2))
    within = dot(pick, jnp.concatenate([out_ends[0], out_ends[1]], 1).astype(BF16))
    n = lax.broadcasted_iota(jnp.int32, (span, size), 0)
    k = lax.broadcasted_iota(jnp.int32, (span, size), 1)
    place = jnp.where(n == 0, rows + pooled, jnp.where(n == rows + 1, rows + pooled + 1, n - 1))
    saved = dot(one_at(jnp.logical_and(k == place, n < rows + 2)), message)
    incline = slope_of(saved, cdf_of(saved))

    head = lax.broadcasted_iota(jnp.int32, (span, 2 * c1), 0) < 2
    turned = jnp.logical_and(head, first)
    lhs[...] = jnp.zeros_like(lhs)
    rights = []
    for a in range(4):
        sides, inner = (x[min(a, 2) * span:(min(a, 2) + 1) * span] for x in (beside, within))
        if a == 2:
            sides, inner = jnp.where(turned, 0.0, sides), jnp.where(turned, 0.0, inner)
        if a == 3:
            sides, inner = jnp.where(turned, sides, 0.0), jnp.where(turned, inner, 0.0)
        rights.append(sides)
        sides, inner = sides.astype(BF16), inner.astype(BF16)
        left, right = sides[:, :c1], sides[:, c1:]
        lhs[a, :span, c1:2 * c1] = left
        lhs[a, :span, 2 * c1:3 * c1] = inner[:, :c1]
        lhs[a, :span, 3 * c1:] = left
        lhs[a, span:2 * span, :c1] = left
        lhs[a, 2 * span:3 * span, :c1] = inner[:, c1:]
        lhs[a, 2 * span:3 * span, c1:2 * c1] = right
        lhs[a, 2 * span:3 * span, 3 * c1:] = right
        lhs[a, 3 * span:, 2 * c1:3 * c1] = right
    found = dot_nt(lhs[0], taps[0]) + dot_nt(lhs[1], taps[1]) + dot_nt(lhs[2], taps[2]) + dot_nt(lhs[3], taps[0])
    row = lax.broadcasted_iota(jnp.int32, (span, c1), 0)
    inside = jnp.where(jnp.logical_or(row > rows + 1, jnp.logical_and(row == rows + 1, last)), 0.0, 1.0)
    values[0] = found[:span, c1:] * incline[:, :c1] * inside
    values[1] = (raw_ends[0] + found[span:2 * span, :c1]) * slope_ends[0] * inside
    values[2] = (raw_ends[1] + found[3 * span:, c1:]) * slope_ends[1] * inside
    values[3] = found[2 * span:3 * span, :c1] * incline[:, c1:] * inside
    ends[...] = values[...].astype(BF16)

    total[...] = keep[...]
    for side, b in ((0, 2), (1, 0)):
        around = jnp.concatenate([x[1:rows + 1, side * c1:(side + 1) * c1] for x in rights], 1).astype(BF16)
        terms = lax.dot_general(act_ends[side].astype(BF16), around, (((0,), (0,)), ((), ())),
                                preferred_element_type=F32) * 0.25
        for a in range(3):
            term = terms[:, a * c1:(a + 1) * c1]
            if a == 0:
                term = term + terms[:, 3 * c1:]
            low = (3 * a + b) * c1
            total[low:low + c1] = total[low:low + c1] + term
    right_hand[...] = jnp.zeros_like(right_hand)
    top = lax.broadcasted_iota(jnp.int32, (rows, c1), 0) == 0
    over = jnp.logical_and(top, first)
    for a in range(4):
        for j in range(4):
            value = values[j, 2 - min(a, 2):2 - min(a, 2) + rows]
            if a == 2:
                value = jnp.where(over, 0.0, value)
            if a == 3:
                value = jnp.where(over, value, 0.0)
            right_hand[a, j // 2 * rows:(j // 2 + 1) * rows, j * c1:(j + 1) * c1] = value.astype(BF16)
    for a in range(3):
        got = dot(field_ends[...], right_hand[a])
        if a == 0:
            got = got + dot(field_ends[...], right_hand[3])
        for b in range(3):
            even = got[:c0, (2 - b) * c1:(3 - b) * c1]
            odd = got[c0:, (3 - b) * c1:(4 - b) * c1]
            low = 9 * c1 + (3 * a + b) * c0
            total[low:low + c0] = total[low:low + c0] + even + odd

    block = own[0].shape[0]
    mine = half_held()
    for targets, half_of in ((own, mine), (other, 1 - mine)):
        for far in range(lats):
            start = (half_of * lats + (band ^ far)) * block
            targets[far][...] = total[pl.ds(pl.multiple_of(start, block), block), :]


def last_kernel(lats, part, ends, taps, out, spread, values, total, turned):
    rows, c0, cols = out.shape
    half = cols // 2
    c2 = 2 * c0
    depth = spread.shape[2]
    first = position(lats)[1]
    spread[...] = part[...]
    c1 = depth // 4
    for j in range(4):
        values[:, j * c1:(j + 1) * c1] = ends[j].astype(F32)
    at = lax.broadcasted_iota(jnp.int32, (16, 2 * c1), 0)
    for r in range(rows + 3):
        n = 0 if r == rows + 2 else r
        for side, (low, spot) in enumerate(((0, 0), (half - 16, 15))):
            lanes = slice(2 * side * c1, 2 * (side + 1) * c1)
            new = values[n:n + 1, lanes]
            if n == 0:
                new = jnp.where(first == (r != 0), new, 0.0)
            tile = spread[r, low:low + 16, lanes].astype(F32)
            spread[r, low:low + 16, lanes] = jnp.where(at == spot, new, tile).astype(BF16)
    result = dot_nt(taps[:c2], spread[2:rows + 2].reshape(rows * half, depth))
    for a in (1, 2):
        result = result + dot_nt(taps[a * c2:(a + 1) * c2],
                                 spread[2 - a:2 - a + rows].reshape(rows * half, depth))
    total[...] = result
    total[:, :half] = total[:, :half] + dot_nt(taps[:c2], spread[rows + 2])
    for q in range(rows // 2):
        pair = total[:, q * cols:(q + 1) * cols].astype(BF16)
        turned[q, :, :cols] = pair[:c0]
        turned[q, :, cols:] = pair[c0:]
    k = lax.broadcasted_iota(jnp.int32, (2 * cols, 2 * cols), 0)
    n = lax.broadcasted_iota(jnp.int32, (2 * cols, 2 * cols), 1)
    order = one_at(n == ((k % cols) // half) * cols + 2 * (k % half) + k // cols)
    found = dot(turned[...].reshape(rows // 2 * c0, 2 * cols), order).astype(BF16)
    for q in range(rows // 2):
        for rp in range(2):
            out[2 * q + rp] = found[q * c0:(q + 1) * c0, rp * cols:(rp + 1) * cols]


def gather_kernel(mine, theirs, out_first, out_second):
    lats, rows, c1 = mine.shape
    band, held = lax.axis_index("lat"), half_held()
    size = out_second.shape[0]
    total = size + out_first.shape[0]
    for h in range(2):
        for i in range(lats):
            at = (h * lats + i) * rows
            for out, base, end in ((out_second, 0, size), (out_first, size, total)):
                low, high = max(at, base), min(at + rows, end)
                if low < high:
                    here, there = (x[i ^ band, low - at:high - at] for x in (mine, theirs))
                    out[low - base:high - base] = jnp.where(held == h, here, there).astype(F32)


def vmem(count):
    return [pl.BlockSpec(memory_space=pltpu.VMEM)] * count


def far(count):
    return [pl.BlockSpec(memory_space=pl.ANY)] * count


def params(mib):
    return pltpu.CompilerParams(vmem_limit_bytes=mib * 1024 * 1024)


def shape(dims, kind):
    return jax.ShapeDtypeStruct(dims, kind)


def body(inputs, pre_first, grad_out, w_first, w_second):
    rows, cols, c1 = pre_first.shape
    c0 = inputs.shape[2]
    half, pooled = cols // 2, rows // 2
    lats, lons = lax.axis_size("lat"), lax.axis_size("lon")
    depths = lons // 2
    band, place = lax.axis_index("lat"), lax.axis_index("lon")
    core = lax.rem(place, 2)
    even = lax.rem(band, 2) == 0

    edge = -(-(rows + pooled + 4) // 16) * 16
    row_a, row_b, col_a, col_b, held_pre = pl.pallas_call(
        functools.partial(pack_kernel, lats),
        out_shape=(
            pltpu.VMEM((cols + half, c1), BF16),
            pltpu.VMEM((cols + half, c1), BF16),
            pltpu.VMEM((edge, c1), BF16),
            pltpu.VMEM((edge, c1), BF16),
            pltpu.VMEM(pre_first.shape, BF16),
        ),
        in_specs=far(2),
        out_specs=tuple(vmem(5)),
        scratch_shapes=[
            pltpu.VMEM((2, edge, c1), F32),
            pltpu.VMEM(grad_out.shape, BF16),
            pltpu.SemaphoreType.DMA((2,)),
        ],
        compiler_params=params(58),
        cost_estimate=pl.CostEstimate(flops=1000, bytes_accessed=1 << 18, transcendentals=0),
    )(pre_first, grad_out)
    pairs = [(j, (j + lons // 2) % lons) for j in range(lons)]
    pairs += [((lats - 1) * lons + j, (lats - 1) * lons + (j ^ 1)) for j in range(lons)]
    for i in range(1, lats - 1, 2):
        for j in range(lons):
            pairs += [(i * lons + j, (i + 1) * lons + j), ((i + 1) * lons + j, i * lons + j)]
    every = [(i * lons + j, (i ^ 1) * lons + j) for i in range(lats) for j in range(lons)]
    row_b = lax.ppermute(row_b, AREA, pairs)
    row_a = lax.ppermute(row_a, AREA, every)

    slope, act_t, act_ends = pl.pallas_call(
        local_kernel,
        out_shape=(
            shape((rows, half, 2 * c1), F32),
            shape((2, 2 * c1, pooled * half), BF16),
            shape((2, rows, c1), F32),
        ),
        in_specs=vmem(1),
        out_specs=tuple(vmem(3)),
        scratch_shapes=[
            pltpu.VMEM((cols, c1), F32),
            pltpu.VMEM((2, pooled, half, 2 * c1), BF16),
        ],
        compiler_params=params(16),
        cost_estimate=pl.CostEstimate(flops=60 * rows * cols * c1, bytes_accessed=2 << 20,
                                      transcendentals=2 * rows * cols * c1),
    )(held_pre)

    fields_t, field_ends, taps_first, taps_second = pl.pallas_call(
        layout_kernel,
        out_shape=(
            shape((2 * c0, rows * half), BF16),
            shape((2 * c0, 2 * rows), BF16),
            shape((6 * c0, 4 * c1), BF16),
            shape((3, 2 * c1, 4 * c1), BF16),
        ),
        in_specs=vmem(3),
        out_specs=tuple(vmem(4)),
        scratch_shapes=[pltpu.VMEM((rows, c0, 2 * cols), BF16)],
        compiler_params=params(16),
        cost_estimate=pl.CostEstimate(flops=4 * rows * cols * c0 * cols, bytes_accessed=3 << 20, transcendentals=0),
    )(jnp.transpose(inputs, (0, 2, 1)), w_first, w_second)
    row_b, row_a, slope, fields_t = lax.optimization_barrier((row_b, row_a, slope, fields_t))

    def corners(at):
        places = (at * (cols - 1), cols + at * (half - 1))
        above, below = (jnp.where(even, one, two) for one, two in ((row_b, row_a), (row_a, row_b)))
        return jnp.concatenate([part[p:p + 1] for p in places for part in (above, below)], 0)

    low, high = corners(0), corners(1)
    pad = jnp.zeros((edge - rows - pooled - 4, c1), BF16)
    col_a = jnp.concatenate([col_a[:rows + pooled], jnp.where(core == 0, high, low), pad], 0)
    col_b = jnp.concatenate([col_b[:rows + pooled], jnp.where(core == 0, low, high), pad], 0)
    col_b = lax.ppermute(col_b, "lon", [(i, (i + 2 * (i % 2) - 1) % lons) for i in range(lons)])
    col_a = lax.ppermute(col_a, "lon", [(i, i ^ 1) for i in range(lons)])

    block = -(-9 * (c1 + c0) // (32 * lats)) * 16
    held = lats * block
    reach = -(-(rows + 2) // 16) * 16
    spread, keep, raw_ends, slope_ends, out_ends = pl.pallas_call(
        functools.partial(middle_kernel, lats),
        out_shape=(
            shape((rows + 3, half, 4 * c1), BF16),
            shape((2 * held, c1), F32),
            shape((2, reach, c1), F32),
            shape((2, reach, c1), F32),
            shape((2, -(-(pooled + 2) // 16) * 16, c1), F32),
        ),
        in_specs=vmem(7),
        out_specs=tuple(vmem(5)),
        scratch_shapes=[
            pltpu.VMEM((pooled + 2, half, c1), F32),
            pltpu.VMEM((pooled + 2, half, 4 * c1), BF16),
            pltpu.VMEM((3, pooled, half, 2 * c1), F32),
            pltpu.VMEM((4, half, 2 * c1), F32),
            pltpu.VMEM((cols, c1), F32),
            pltpu.VMEM((4, 2 * c1, 3 * c1), F32),
            pltpu.VMEM((2 * c1, 3 * c1), F32),
        ],
        compiler_params=params(16),
        cost_estimate=pl.CostEstimate(flops=2 * rows * cols * c1 * 9 * (2 * c1 + c0), bytes_accessed=8 << 20,
                                      transcendentals=0),
    )(grad_out, row_a, row_b, slope, act_t, fields_t, taps_second)
    col_a, col_b, keep = lax.optimization_barrier((col_a, col_b, keep))

    ends, *halves = pl.pallas_call(
        functools.partial(columns_kernel, lats),
        out_shape=(
            shape((4, reach, c1), BF16),
        ) + (shape((block, c1), F32),) * (2 * lats),
        in_specs=vmem(9),
        out_specs=tuple(vmem(2 * lats + 1)),
        scratch_shapes=[
            pltpu.VMEM((4, 4 * reach, 4 * c1), BF16),
            pltpu.VMEM((4, reach, c1), F32),
            pltpu.VMEM((4, 2 * rows, 4 * c1), BF16),
            pltpu.VMEM((2 * held, c1), F32),
        ],
        compiler_params=params(16),
        cost_estimate=pl.CostEstimate(flops=1 << 28, bytes_accessed=3 << 20, transcendentals=0),
    )(col_a, col_b, act_ends, field_ends, taps_second, keep, raw_ends, slope_ends, out_ends)

    swap = [(i, i ^ 1) for i in range(lons)]

    def between_chips(value, over_lat, over_lon):
        turn = odd(over_lat) ^ odd(over_lon)
        return lax.ppermute(value, AREA, [
            (i * lons + j, (i ^ over_lat) * lons + (j ^ (2 * over_lon) ^ turn)) for i in range(lats) for j in range(lons)])

    own, other = halves[:lats], halves[lats:]
    other = {far: lax.ppermute(other[far], "lon", swap) for far in reversed(range(lats))}
    parts = [own[far] + other[far] for far in range(lats)]
    got = [between_chips(parts[far].astype(BF16), far, 0) for far in reversed(range(1, lats))]
    grad_inputs = pl.pallas_call(
        functools.partial(last_kernel, lats),
        out_shape=shape((rows, c0, cols), BF16),
        in_specs=vmem(3),
        out_specs=vmem(1)[0],
        scratch_shapes=[
            pltpu.VMEM((rows + 3, half, 4 * c1), BF16),
            pltpu.VMEM((reach, 4 * c1), F32),
            pltpu.VMEM((2 * c0, rows * half), F32),
            pltpu.VMEM((pooled, c0, 2 * cols), BF16),
        ],
        compiler_params=params(12),
        cost_estimate=pl.CostEstimate(flops=2 * rows * cols * c1 * 9 * c0, bytes_accessed=3 << 20, transcendentals=0),
    )(spread, ends, taps_first)
    *got, grad_inputs = lax.optimization_barrier((*got, grad_inputs))
    total = parts[0]
    for value in got:
        total = total + value.astype(F32)
    part = total.astype(BF16)
    terms = [part] + [between_chips(part, 0, far) for far in range(1, depths)]
    terms = [term.astype(F32) for term in terms]
    while len(terms) > 1:
        terms = [terms[k + (k > 0)] + terms[k + (k == 0)] for k in range(0, len(terms), 2)]
    part = terms[0].astype(BF16)
    mine = jnp.stack([part] + [between_chips(part, far, 0) for far in range(1, lats)], 0)
    theirs = lax.ppermute(mine, "lon", swap)

    grad_w_first, grad_w_second = pl.pallas_call(
        gather_kernel,
        out_shape=(shape((9 * c0, c1), F32), shape((9 * c1, c1), F32)),
        in_specs=vmem(2),
        out_specs=tuple(vmem(2)),
        compiler_params=params(8),
        cost_estimate=pl.CostEstimate(flops=1000, bytes_accessed=3 << 19, transcendentals=0),
    )(mine, theirs)
    return (jnp.transpose(grad_inputs, (0, 2, 1)), grad_w_first.reshape(w_first.shape),
            grad_w_second.reshape(w_second.shape))


def solution(mesh):
    in_specs = (P("lat", "lon", None), P("lat", "lon", None), P("lat", "lon", None), P(), P())
    out_specs = (P("lat", "lon", None), P(), P())
    return jax.shard_map(body, mesh=mesh, in_specs=in_specs, out_specs=out_specs, check_vma=False)
```

```python
import functools

import jax
import jax.numpy as jnp
from jax import lax
from jax.experimental import pallas as pl
from jax.experimental.pallas import tpu as pltpu
from jax.sharding import PartitionSpec as P

inv_root = 0.7071067811865476
density = 0.3989422804014327

F32 = jnp.float32
BF16 = jnp.bfloat16
AREA = ("lat", "lon")


def cdf_of(value):
    return 0.5 * (1.0 + lax.erf(value * inv_root))


def slope_of(value, cdf):
    return 0.25 * (cdf + value * jnp.exp(-0.5 * value * value) * density)


def dot(left, right):
    return jnp.dot(left, right, preferred_element_type=F32)


def dot_nt(left, right):
    return lax.dot_general(left, right, (((1,), (1,)), ((), ())), preferred_element_type=F32)


def position(lats):
    band, place = lax.axis_index("lat"), lax.axis_index("lon")
    return band, band == 0, band == lats - 1, lax.rem(band, 2) == 0, lax.rem(place, 2)


def odd(value):
    for shift in (4, 2, 1):
        value = value ^ (value >> shift)
    return value & 1


def half_held():
    band, place = lax.axis_index("lat"), lax.axis_index("lon")
    return odd(band) ^ odd(place // 2) ^ (place % 2)


def pack_kernel(lats, pre_far, grad_far, row_a, row_b, col_a, col_b, pre, hold, grad_out, sems):
    copies = [pltpu.make_async_copy(pre_far, pre, sems.at[0]), pltpu.make_async_copy(grad_far, grad_out, sems.at[1])]
    for copy in copies:
        copy.start()
    for copy in copies:
        copy.wait()
    rows, cols, c1 = pre.shape
    pooled, half = grad_out.shape[:2]
    _, _, _, even, core = position(lats)
    for message, low in ((row_a, ~even), (row_b, even)):
        message[:cols] = pre[jnp.where(low, 0, rows - 1)]
        message[cols:] = grad_out[jnp.where(low, 0, pooled - 1)]
    hold[:, rows + pooled:] = jnp.zeros((2, hold.shape[1] - rows - pooled, c1), F32)
    for side, (p, g) in enumerate(((0, 0), (cols - 16, half - 16))):
        at = 15 * side
        for r in range(rows):
            hold[side, r:r + 1] = pre[r, p:p + 16].astype(F32)[at:at + 1]
        for i in range(pooled):
            hold[side, rows + i:rows + i + 1] = grad_out[i, g:g + 16].astype(F32)[at:at + 1]
    col_a[...] = hold[1 - core].astype(BF16)
    col_b[...] = hold[core].astype(BF16)


def one_at(where):
    return jnp.where(where, 1.0, 0.0).astype(BF16)


def local_kernel(pre, slope, act_t, act_ends, line, act_s):
    rows, cols, c1 = pre.shape
    half = cols // 2

    def one_row(r, carry):
        line[...] = pre[r].astype(F32)
        for pc in range(2):
            value = line[pl.ds(pc, half, stride=2), :]
            cdf = cdf_of(value)
            act = value * cdf
            act_s[r % 2, r // 2, :, pc * c1:(pc + 1) * c1] = act.astype(BF16)
            act_ends[pc, pl.ds(r, 1), :] = act[pc * (half - 1):pc * (half - 1) + 1]
            slope[r, :, pc * c1:(pc + 1) * c1] = slope_of(value, cdf)
        return carry

    lax.fori_loop(0, rows, one_row, 0)
    for pr in range(2):
        act_t[pr] = act_s[pr].reshape(rows // 2 * half, 2 * c1).T


def layout_kernel(fields, w_first, w_second, fields_t, field_ends, taps_first, taps_second, turned):
    rows, c0, cols = fields.shape
    c1 = w_first.shape[3]
    half = cols // 2
    col = lax.broadcasted_iota(jnp.int32, (cols, 2 * cols), 0)
    lane = lax.broadcasted_iota(jnp.int32, (cols, 2 * cols), 1)
    turn = lane // cols
    parity = (lane % cols) // half
    parity = parity + turn - 2 * parity * turn
    order = one_at(col == 2 * (lane % half) + parity)
    turned[...] = dot(fields[...].reshape(rows * c0, cols), order).astype(BF16).reshape(rows, c0, 2 * cols)
    low = lax.broadcasted_iota(jnp.int32, (c0, cols), 1) < half
    for q in range(rows // 2):
        fields_t[:c0, q * cols:(q + 1) * cols] = jnp.where(low, turned[2 * q, :, :cols], turned[2 * q + 1, :, cols:])
        fields_t[c0:, q * cols:(q + 1) * cols] = jnp.where(low, turned[2 * q, :, cols:], turned[2 * q + 1, :, :cols])
    cell = lax.broadcasted_iota(jnp.int32, (rows * half, 2 * rows), 0)
    n = lax.broadcasted_iota(jnp.int32, (rows * half, 2 * rows), 1)
    pick = one_at(cell == (n % rows) * half + (n // rows) * (half - 1))
    field_ends[...] = dot(fields_t[...], pick).astype(BF16)
    taps_second[...] = jnp.zeros_like(taps_second)
    taps_first[...] = jnp.zeros_like(taps_first)
    for a in range(3):
        for pc, blocks in ((0, (2, 1, None, 0)), (1, (None, 2, 0, 1))):
            for k, b in enumerate(blocks):
                if b is not None:
                    taps_second[a, pc * c1:(pc + 1) * c1, k * c1:(k + 1) * c1] = w_second[a, b]
        for pc, blocks in ((0, (2, 1, 0, None)), (1, (None, 2, 1, 0))):
            for k, b in enumerate(blocks):
                if b is not None:
                    start = (2 * a + pc) * c0
                    taps_first[start:start + c0, k * c1:(k + 1) * c1] = w_first[a, b]


def middle_kernel(lats, grad_out, row_a, row_b, slope, act_t, fields_t, taps,
                  spread, keep, raw_ends, slope_ends, out_ends,
                  grid, wide, prods, ends, line, sums, corner):
    _, first, last, even, _ = position(lats)
    top = jnp.where(even, row_b[...], row_a[...])
    bottom = jnp.where(even, row_a[...], row_b[...])
    rows, half, c2 = slope.shape
    c1 = c2 // 2
    pooled = rows // 2
    c0 = fields_t.shape[0] // 2
    cells = pooled * half
    raw_ends[...] = jnp.zeros_like(raw_ends)
    slope_ends[...] = jnp.zeros_like(slope_ends)
    out_ends[...] = jnp.zeros_like(out_ends)

    grid[1:pooled + 1] = grad_out[...].astype(F32)
    grid[0] = top[2 * half:, :].astype(F32)
    outside = jnp.where(last, 0.0, 1.0)
    grid[pooled + 1] = bottom[2 * half:, :].astype(F32) * outside
    at = lax.broadcasted_iota(jnp.int32, (half, c1), 0)
    for i in range(pooled + 2):
        here = grid[i]
        out_ends[0, i:i + 1] = here[:1]
        out_ends[1, i:i + 1] = here[half - 1:]
        wide[i, :, :c1] = jnp.where(at == 0, 0.0, pltpu.roll(here, 1, 0)).astype(BF16)
        wide[i, :, c1:2 * c1] = here.astype(BF16)
        wide[i, :, 2 * c1:3 * c1] = jnp.where(at == half - 1, 0.0, pltpu.roll(here, half - 1, 0)).astype(BF16)
        wide[i, :, 3 * c1:] = here.astype(BF16)

    flat = wide[1:pooled + 1].reshape(cells, 4 * c1)
    for a in range(3):
        prods[a] = dot_nt(flat, taps[a]).reshape(pooled, half, c2)
    fold = jnp.where(first, taps[0], taps[2])
    ends[0] = dot_nt(wide[0], fold)
    ends[1] = dot_nt(wide[0], taps[1])
    ends[2] = dot_nt(wide[pooled + 1], taps[0])
    ends[3] = dot_nt(wide[pooled + 1], taps[1])

    def place(r, total, incline):
        inner = total * incline
        raw_ends[0, pl.ds(r, 1), :] = total[:1, :c1]
        raw_ends[1, pl.ds(r, 1), :] = total[half - 1:, c1:]
        slope_ends[0, pl.ds(r, 1), :] = incline[:1, :c1]
        slope_ends[1, pl.ds(r, 1), :] = incline[half - 1:, c1:]
        even, odd = inner[:, :c1], inner[:, c1:]
        spread[r, :, :c1] = jnp.where(at == 0, 0.0, pltpu.roll(odd, 1, 0)).astype(BF16)
        spread[r, :, c1:2 * c1] = jnp.where(at == 0, 0.0, even).astype(BF16)
        spread[r, :, 2 * c1:3 * c1] = jnp.where(at == half - 1, 0.0, odd).astype(BF16)
        spread[r, :, 3 * c1:] = jnp.where(at == half - 1, 0.0, pltpu.roll(even, half - 1, 0)).astype(BF16)

    def halo_slope(message):
        line[...] = message[:2 * half, :].astype(F32)
        both = [line[pl.ds(pc, half, stride=2), :] for pc in range(2)]
        return jnp.concatenate([slope_of(v, cdf_of(v)) for v in both], axis=1)

    place(0, ends[0] + ends[1] + prods[0, 0], halo_slope(top))
    place(1, ends[0] + prods[1, 0] + prods[0, 0], slope[0])

    def pair(i, carry):
        middle = prods[2, i] + prods[1, i]
        place(2 * i + 2, middle + prods[0, i + 1], slope[2 * i + 1])
        place(2 * i + 3, prods[2, i] + prods[1, i + 1] + prods[0, i + 1], slope[2 * i + 2])
        return carry

    lax.fori_loop(0, pooled - 1, pair, 0)
    final = prods[2, pooled - 1]
    place(rows, final + prods[1, pooled - 1] + ends[2], slope[rows - 1])
    place(rows + 1, (final + ends[3] + ends[2]) * outside, halo_slope(bottom))

    is_first = jnp.where(first, 1.0, 0.0).astype(BF16)
    not_first = jnp.where(first, 0.0, 1.0).astype(BF16)
    above = wide[0, :, :3 * c1]
    wide[0, :, :3 * c1] = above * not_first
    for n, (pr, start) in enumerate(((0, 0), (0, 1), (1, 1), (1, 2))):
        around = wide[start:start + pooled, :, :3 * c1].reshape(cells, 3 * c1)
        sums[n] = dot(act_t[pr], around)
    corner[...] = dot(act_t[0, :, :half], above * is_first)

    unit = c0
    per_tap = c1 // unit
    count = 9 * per_tap + 9

    def put(k, value):
        keep[k * unit:(k + 1) * unit, :] = value

    pieces = {0: ((0, 1), (1, 3)), 1: ((0, 1), (1, 2)), 2: ((0, 0), (1, 2))}
    for a in range(3):
        for b in range(3):
            total = None
            for pr, n in pieces[a]:
                for pc in range(2):
                    k = (pc + 1 - b) // 2 + 1
                    term = sums[n, pc * c1:(pc + 1) * c1, k * c1:(k + 1) * c1]
                    total = term if total is None else total + term
            if a == 0:
                for pc in range(2):
                    k = (pc + 1 - b) // 2 + 1
                    total = total + corner[pc * c1:(pc + 1) * c1, k * c1:(k + 1) * c1]
            total = total * 0.25
            for part in range(per_tap):
                put((3 * a + b) * per_tap + part, total[part * unit:(part + 1) * unit])

    head = spread[0]
    spread[0] = head * not_first
    spread[rows + 2] = head * is_first
    folded = dot(fields_t[:, :half], spread[rows + 2])
    for a in range(3):
        around = spread[2 - a:2 - a + rows].reshape(rows * half, 4 * c1)
        got = dot(fields_t[...], around)
        if a == 0:
            got = got + folded
        for b in range(3):
            even = got[:c0, (2 - b) * c1:(3 - b) * c1]
            odd = got[c0:, (3 - b) * c1:(4 - b) * c1]
            put(9 * per_tap + 3 * a + b, even + odd)
    if keep.shape[0] > count * unit:
        keep[count * unit:] = jnp.zeros((keep.shape[0] - count * unit, c1), F32)


def columns_kernel(lats, col_a, col_b, act_ends, field_ends, taps, keep, raw_ends, slope_ends, out_ends,
                   ends, *rest):
    own, other, (lhs, values, right_hand, total) = rest[:lats], rest[lats:2 * lats], rest[2 * lats:]
    band, first, last, _, core = position(lats)
    c1 = act_ends.shape[2]
    rows = act_ends.shape[1]
    pooled = rows // 2
    c0 = field_ends.shape[0] // 2
    span, size = raw_ends.shape[1], col_a.shape[0]
    got_a, got_b = col_a[...].astype(F32), col_b[...].astype(F32)
    message = jnp.concatenate([jnp.where(core == 0, got_b, got_a), jnp.where(core == 0, got_a, got_b)], 1)
    at = lax.broadcasted_iota(jnp.int32, (size, 2 * c1), 0)
    message = jnp.where(jnp.logical_and(at == rows + pooled + 3, last), 0.0, message).astype(BF16)

    n = lax.broadcasted_iota(jnp.int32, (3 * span, size), 0)
    k = lax.broadcasted_iota(jnp.int32, (3 * span, size), 1)
    row = n % span
    want = (row - n // span + 2) // 2 - 1
    place = jnp.where(want < 0, rows + pooled + 2, jnp.where(want == pooled, rows + pooled + 3, rows + want))
    beside = dot(one_at(jnp.logical_and(k == place, row < rows + 2)), message)
    n = lax.broadcasted_iota(jnp.int32, (3 * span, out_ends.shape[1]), 0)
    k = lax.broadcasted_iota(jnp.int32, (3 * span, out_ends.shape[1]), 1)
    row = n % span
    want = (row - n // span + 2) // 2
    pick = one_at(jnp.logical_and(k == want, row < rows + 2))
    within = dot(pick, jnp.concatenate([out_ends[0], out_ends[1]], 1).astype(BF16))
    n = lax.broadcasted_iota(jnp.int32, (span, size), 0)
    k = lax.broadcasted_iota(jnp.int32, (span, size), 1)
    place = jnp.where(n == 0, rows + pooled, jnp.where(n == rows + 1, rows + pooled + 1, n - 1))
    saved = dot(one_at(jnp.logical_and(k == place, n < rows + 2)), message)
    incline = slope_of(saved, cdf_of(saved))

    head = lax.broadcasted_iota(jnp.int32, (span, 2 * c1), 0) < 2
    turned = jnp.logical_and(head, first)
    lhs[...] = jnp.zeros_like(lhs)
    rights = []
    for a in range(4):
        sides, inner = (x[min(a, 2) * span:(min(a, 2) + 1) * span] for x in (beside, within))
        if a == 2:
            sides, inner = jnp.where(turned, 0.0, sides), jnp.where(turned, 0.0, inner)
        if a == 3:
            sides, inner = jnp.where(turned, sides, 0.0), jnp.where(turned, inner, 0.0)
        rights.append(sides)
        sides, inner = sides.astype(BF16), inner.astype(BF16)
        left, right = sides[:, :c1], sides[:, c1:]
        lhs[a, :span, c1:2 * c1] = left
        lhs[a, :span, 2 * c1:3 * c1] = inner[:, :c1]
        lhs[a, :span, 3 * c1:] = left
        lhs[a, span:2 * span, :c1] = left
        lhs[a, 2 * span:3 * span, :c1] = inner[:, c1:]
        lhs[a, 2 * span:3 * span, c1:2 * c1] = right
        lhs[a, 2 * span:3 * span, 3 * c1:] = right
        lhs[a, 3 * span:, 2 * c1:3 * c1] = right
    found = dot_nt(lhs[0], taps[0]) + dot_nt(lhs[1], taps[1]) + dot_nt(lhs[2], taps[2]) + dot_nt(lhs[3], taps[0])
    row = lax.broadcasted_iota(jnp.int32, (span, c1), 0)
    inside = jnp.where(jnp.logical_or(row > rows + 1, jnp.logical_and(row == rows + 1, last)), 0.0, 1.0)
    values[0] = found[:span, c1:] * incline[:, :c1] * inside
    values[1] = (raw_ends[0] + found[span:2 * span, :c1]) * slope_ends[0] * inside
    values[2] = (raw_ends[1] + found[3 * span:, c1:]) * slope_ends[1] * inside
    values[3] = found[2 * span:3 * span, :c1] * incline[:, c1:] * inside
    ends[...] = values[...].astype(BF16)

    total[...] = keep[...]
    for side, b in ((0, 2), (1, 0)):
        around = jnp.concatenate([x[1:rows + 1, side * c1:(side + 1) * c1] for x in rights], 1).astype(BF16)
        terms = lax.dot_general(act_ends[side].astype(BF16), around, (((0,), (0,)), ((), ())),
                                preferred_element_type=F32) * 0.25
        for a in range(3):
            term = terms[:, a * c1:(a + 1) * c1]
            if a == 0:
                term = term + terms[:, 3 * c1:]
            low = (3 * a + b) * c1
            total[low:low + c1] = total[low:low + c1] + term
    right_hand[...] = jnp.zeros_like(right_hand)
    top = lax.broadcasted_iota(jnp.int32, (rows, c1), 0) == 0
    over = jnp.logical_and(top, first)
    for a in range(4):
        for j in range(4):
            value = values[j, 2 - min(a, 2):2 - min(a, 2) + rows]
            if a == 2:
                value = jnp.where(over, 0.0, value)
            if a == 3:
                value = jnp.where(over, value, 0.0)
            right_hand[a, j // 2 * rows:(j // 2 + 1) * rows, j * c1:(j + 1) * c1] = value.astype(BF16)
    for a in range(3):
        got = dot(field_ends[...], right_hand[a])
        if a == 0:
            got = got + dot(field_ends[...], right_hand[3])
        for b in range(3):
            even = got[:c0, (2 - b) * c1:(3 - b) * c1]
            odd = got[c0:, (3 - b) * c1:(4 - b) * c1]
            low = 9 * c1 + (3 * a + b) * c0
            total[low:low + c0] = total[low:low + c0] + even + odd

    block = own[0].shape[0]
    mine = half_held()
    for targets, half_of in ((own, mine), (other, 1 - mine)):
        for far in range(lats):
            start = (half_of * lats + (band ^ far)) * block
            targets[far][...] = total[pl.ds(pl.multiple_of(start, block), block), :]


def last_kernel(lats, part, ends, taps, out, spread, values, total, turned):
    rows, c0, cols = out.shape
    half = cols // 2
    c2 = 2 * c0
    depth = spread.shape[2]
    first = position(lats)[1]
    spread[...] = part[...]
    c1 = depth // 4
    for j in range(4):
        values[:, j * c1:(j + 1) * c1] = ends[j].astype(F32)
    at = lax.broadcasted_iota(jnp.int32, (16, 2 * c1), 0)
    for r in range(rows + 3):
        n = 0 if r == rows + 2 else r
        for side, (low, spot) in enumerate(((0, 0), (half - 16, 15))):
            lanes = slice(2 * side * c1, 2 * (side + 1) * c1)
            new = values[n:n + 1, lanes]
            if n == 0:
                new = jnp.where(first == (r != 0), new, 0.0)
            tile = spread[r, low:low + 16, lanes].astype(F32)
            spread[r, low:low + 16, lanes] = jnp.where(at == spot, new, tile).astype(BF16)
    result = dot_nt(taps[:c2], spread[2:rows + 2].reshape(rows * half, depth))
    for a in (1, 2):
        result = result + dot_nt(taps[a * c2:(a + 1) * c2],
                                 spread[2 - a:2 - a + rows].reshape(rows * half, depth))
    total[...] = result
    total[:, :half] = total[:, :half] + dot_nt(taps[:c2], spread[rows + 2])
    for q in range(rows // 2):
        pair = total[:, q * cols:(q + 1) * cols].astype(BF16)
        turned[q, :, :cols] = pair[:c0]
        turned[q, :, cols:] = pair[c0:]
    k = lax.broadcasted_iota(jnp.int32, (2 * cols, 2 * cols), 0)
    n = lax.broadcasted_iota(jnp.int32, (2 * cols, 2 * cols), 1)
    order = one_at(n == ((k % cols) // half) * cols + 2 * (k % half) + k // cols)
    found = dot(turned[...].reshape(rows // 2 * c0, 2 * cols), order).astype(BF16)
    for q in range(rows // 2):
        for rp in range(2):
            out[2 * q + rp] = found[q * c0:(q + 1) * c0, rp * cols:(rp + 1) * cols]


def gather_kernel(mine, theirs, out_first, out_second):
    lats, rows, c1 = mine.shape
    band, held = lax.axis_index("lat"), half_held()
    size = out_second.shape[0]
    total = size + out_first.shape[0]
    for h in range(2):
        for i in range(lats):
            at = (h * lats + i) * rows
            here, there = (x[i ^ band].astype(F32) for x in (mine, theirs))
            value = jnp.where(held == h, here, there)
            for out, base, end in ((out_second, 0, size), (out_first, size, total)):
                low, high = max(at, base), min(at + rows, end)
                if low < high:
                    out[low - base:high - base] = value[low - at:high - at]


def vmem(count):
    return [pl.BlockSpec(memory_space=pltpu.VMEM)] * count


def far(count):
    return [pl.BlockSpec(memory_space=pl.ANY)] * count


def params(mib):
    return pltpu.CompilerParams(vmem_limit_bytes=mib * 1024 * 1024)


def shape(dims, kind):
    return jax.ShapeDtypeStruct(dims, kind)


def body(inputs, pre_first, grad_out, w_first, w_second):
    rows, cols, c1 = pre_first.shape
    c0 = inputs.shape[2]
    half, pooled = cols // 2, rows // 2
    lats, lons = lax.axis_size("lat"), lax.axis_size("lon")
    depths = lons // 2
    band, place = lax.axis_index("lat"), lax.axis_index("lon")
    core = lax.rem(place, 2)
    even = lax.rem(band, 2) == 0

    edge = -(-(rows + pooled + 4) // 16) * 16
    row_a, row_b, col_a, col_b, held_pre = pl.pallas_call(
        functools.partial(pack_kernel, lats),
        out_shape=(
            pltpu.VMEM((cols + half, c1), BF16),
            pltpu.VMEM((cols + half, c1), BF16),
            pltpu.VMEM((edge, c1), BF16),
            pltpu.VMEM((edge, c1), BF16),
            pltpu.VMEM(pre_first.shape, BF16),
        ),
        in_specs=far(2),
        out_specs=tuple(vmem(5)),
        scratch_shapes=[
            pltpu.VMEM((2, edge, c1), F32),
            pltpu.VMEM(grad_out.shape, BF16),
            pltpu.SemaphoreType.DMA((2,)),
        ],
        compiler_params=params(58),
        cost_estimate=pl.CostEstimate(flops=1000, bytes_accessed=1 << 18, transcendentals=0),
    )(pre_first, grad_out)
    pairs = [(j, (j + lons // 2) % lons) for j in range(lons)]
    pairs += [((lats - 1) * lons + j, (lats - 1) * lons + (j ^ 1)) for j in range(lons)]
    for i in range(1, lats - 1, 2):
        for j in range(lons):
            pairs += [(i * lons + j, (i + 1) * lons + j), ((i + 1) * lons + j, i * lons + j)]
    every = [(i * lons + j, (i ^ 1) * lons + j) for i in range(lats) for j in range(lons)]
    row_b = lax.ppermute(row_b, AREA, pairs)
    row_a = lax.ppermute(row_a, AREA, every)

    slope, act_t, act_ends = pl.pallas_call(
        local_kernel,
        out_shape=(
            shape((rows, half, 2 * c1), F32),
            shape((2, 2 * c1, pooled * half), BF16),
            shape((2, rows, c1), F32),
        ),
        in_specs=vmem(1),
        out_specs=tuple(vmem(3)),
        scratch_shapes=[
            pltpu.VMEM((cols, c1), F32),
            pltpu.VMEM((2, pooled, half, 2 * c1), BF16),
        ],
        compiler_params=params(16),
        cost_estimate=pl.CostEstimate(flops=60 * rows * cols * c1, bytes_accessed=2 << 20,
                                      transcendentals=2 * rows * cols * c1),
    )(held_pre)

    fields_t, field_ends, taps_first, taps_second = pl.pallas_call(
        layout_kernel,
        out_shape=(
            shape((2 * c0, rows * half), BF16),
            shape((2 * c0, 2 * rows), BF16),
            shape((6 * c0, 4 * c1), BF16),
            shape((3, 2 * c1, 4 * c1), BF16),
        ),
        in_specs=vmem(3),
        out_specs=tuple(vmem(4)),
        scratch_shapes=[pltpu.VMEM((rows, c0, 2 * cols), BF16)],
        compiler_params=params(16),
        cost_estimate=pl.CostEstimate(flops=4 * rows * cols * c0 * cols, bytes_accessed=3 << 20, transcendentals=0),
    )(jnp.transpose(inputs, (0, 2, 1)), w_first, w_second)
    row_b, row_a, slope, fields_t = lax.optimization_barrier((row_b, row_a, slope, fields_t))

    def corners(at):
        places = (at * (cols - 1), cols + at * (half - 1))
        above, below = (jnp.where(even, one, two) for one, two in ((row_b, row_a), (row_a, row_b)))
        return jnp.concatenate([part[p:p + 1] for p in places for part in (above, below)], 0)

    low, high = corners(0), corners(1)
    pad = jnp.zeros((edge - rows - pooled - 4, c1), BF16)
    col_a = jnp.concatenate([col_a[:rows + pooled], jnp.where(core == 0, high, low), pad], 0)
    col_b = jnp.concatenate([col_b[:rows + pooled], jnp.where(core == 0, low, high), pad], 0)
    col_b = lax.ppermute(col_b, "lon", [(i, (i + 2 * (i % 2) - 1) % lons) for i in range(lons)])
    col_a = lax.ppermute(col_a, "lon", [(i, i ^ 1) for i in range(lons)])

    block = -(-9 * (c1 + c0) // (16 * lats)) * 8
    held = lats * block
    reach = -(-(rows + 2) // 16) * 16
    spread, keep, raw_ends, slope_ends, out_ends = pl.pallas_call(
        functools.partial(middle_kernel, lats),
        out_shape=(
            shape((rows + 3, half, 4 * c1), BF16),
            shape((2 * held, c1), F32),
            shape((2, reach, c1), F32),
            shape((2, reach, c1), F32),
            shape((2, -(-(pooled + 2) // 16) * 16, c1), F32),
        ),
        in_specs=vmem(7),
        out_specs=tuple(vmem(5)),
        scratch_shapes=[
            pltpu.VMEM((pooled + 2, half, c1), F32),
            pltpu.VMEM((pooled + 2, half, 4 * c1), BF16),
            pltpu.VMEM((3, pooled, half, 2 * c1), F32),
            pltpu.VMEM((4, half, 2 * c1), F32),
            pltpu.VMEM((cols, c1), F32),
            pltpu.VMEM((4, 2 * c1, 3 * c1), F32),
            pltpu.VMEM((2 * c1, 3 * c1), F32),
        ],
        compiler_params=params(16),
        cost_estimate=pl.CostEstimate(flops=2 * rows * cols * c1 * 9 * (2 * c1 + c0), bytes_accessed=8 << 20,
                                      transcendentals=0),
    )(grad_out, row_a, row_b, slope, act_t, fields_t, taps_second)
    col_a, col_b, keep = lax.optimization_barrier((col_a, col_b, keep))

    ends, *halves = pl.pallas_call(
        functools.partial(columns_kernel, lats),
        out_shape=(
            shape((4, reach, c1), BF16),
        ) + (shape((block, c1), F32),) * (2 * lats),
        in_specs=vmem(9),
        out_specs=tuple(vmem(2 * lats + 1)),
        scratch_shapes=[
            pltpu.VMEM((4, 4 * reach, 4 * c1), BF16),
            pltpu.VMEM((4, reach, c1), F32),
            pltpu.VMEM((4, 2 * rows, 4 * c1), BF16),
            pltpu.VMEM((2 * held, c1), F32),
        ],
        compiler_params=params(16),
        cost_estimate=pl.CostEstimate(flops=1 << 28, bytes_accessed=3 << 20, transcendentals=0),
    )(col_a, col_b, act_ends, field_ends, taps_second, keep, raw_ends, slope_ends, out_ends)

    swap = [(i, i ^ 1) for i in range(lons)]

    def between_chips(value, over_lat, over_lon):
        turn = odd(over_lat) ^ odd(over_lon)
        return lax.ppermute(value, AREA, [
            (i * lons + j, (i ^ over_lat) * lons + (j ^ (2 * over_lon) ^ turn)) for i in range(lats) for j in range(lons)])

    own, other = halves[:lats], halves[lats:]
    other = {far: lax.ppermute(other[far], "lon", swap) for far in reversed(range(lats))}
    parts = [own[far] + other[far] for far in range(lats)]
    got = [between_chips(parts[far].astype(BF16), far, 0) for far in reversed(range(1, lats))]
    grad_inputs = pl.pallas_call(
        functools.partial(last_kernel, lats),
        out_shape=shape((rows, c0, cols), BF16),
        in_specs=vmem(3),
        out_specs=vmem(1)[0],
        scratch_shapes=[
            pltpu.VMEM((rows + 3, half, 4 * c1), BF16),
            pltpu.VMEM((reach, 4 * c1), F32),
            pltpu.VMEM((2 * c0, rows * half), F32),
            pltpu.VMEM((pooled, c0, 2 * cols), BF16),
        ],
        compiler_params=params(12),
        cost_estimate=pl.CostEstimate(flops=2 * rows * cols * c1 * 9 * c0, bytes_accessed=3 << 20, transcendentals=0),
    )(spread, ends, taps_first)
    *got, grad_inputs = lax.optimization_barrier((*got, grad_inputs))
    total = parts[0]
    for value in got:
        total = total + value.astype(F32)
    part = total.astype(BF16)
    terms = [part] + [between_chips(part, 0, far) for far in range(1, depths)]
    terms = [term.astype(F32) for term in terms]
    while len(terms) > 1:
        terms = [terms[k + (k > 0)] + terms[k + (k == 0)] for k in range(0, len(terms), 2)]
    part = terms[0].astype(BF16)
    mine = jnp.stack([part] + [between_chips(part, far, 0) for far in range(1, lats)], 0)
    theirs = lax.ppermute(mine, "lon", swap)

    grad_w_first, grad_w_second = pl.pallas_call(
        gather_kernel,
        out_shape=(shape((9 * c0, c1), F32), shape((9 * c1, c1), F32)),
        in_specs=vmem(2),
        out_specs=tuple(vmem(2)),
        compiler_params=params(8),
        cost_estimate=pl.CostEstimate(flops=1000, bytes_accessed=3 << 19, transcendentals=0),
    )(mine, theirs)
    return (jnp.transpose(grad_inputs, (0, 2, 1)), grad_w_first.reshape(w_first.shape),
            grad_w_second.reshape(w_second.shape))


def solution(mesh):
    in_specs = (P("lat", "lon", None), P("lat", "lon", None), P("lat", "lon", None), P(), P())
    out_specs = (P("lat", "lon", None), P(), P())
    return jax.shard_map(body, mesh=mesh, in_specs=in_specs, out_specs=out_specs, check_vma=False)
```

```python
import functools

import jax
import jax.numpy as jnp
from jax import lax
from jax.experimental import pallas as pl
from jax.experimental.pallas import tpu as pltpu
from jax.sharding import PartitionSpec as P

inv_root = 0.7071067811865476
density = 0.3989422804014327

F32 = jnp.float32
BF16 = jnp.bfloat16
AREA = ("lat", "lon")


def cdf_of(value):
    return 0.5 * (1.0 + lax.erf(value * inv_root))


def slope_of(value, cdf):
    return 0.25 * (cdf + value * jnp.exp(-0.5 * value * value) * density)


def dot(left, right):
    return jnp.dot(left, right, preferred_element_type=F32)


def dot_nt(left, right):
    return lax.dot_general(left, right, (((1,), (1,)), ((), ())), preferred_element_type=F32)


def position(lats):
    band, place = lax.axis_index("lat"), lax.axis_index("lon")
    return band, band == 0, band == lats - 1, lax.rem(band, 2) == 0, lax.rem(place, 2)


def odd(value):
    for shift in (4, 2, 1):
        value = value ^ (value >> shift)
    return value & 1


def half_held():
    band, place = lax.axis_index("lat"), lax.axis_index("lon")
    return odd(band) ^ odd(place // 2) ^ (place % 2)


def pack_kernel(lats, pre_far, grad_far, row_a, row_b, col_a, col_b, pre, hold, grad_out, sems):
    copies = [pltpu.make_async_copy(pre_far, pre, sems.at[0]), pltpu.make_async_copy(grad_far, grad_out, sems.at[1])]
    for copy in copies:
        copy.start()
    for copy in copies:
        copy.wait()
    rows, cols, c1 = pre.shape
    pooled, half = grad_out.shape[:2]
    _, _, _, even, core = position(lats)
    up = jnp.logical_xor(even, core == 1)
    for message, low in ((row_a, up), (row_b, ~up)):
        message[:cols] = pre[jnp.where(low, 0, rows - 1)]
        message[cols:] = grad_out[jnp.where(low, 0, pooled - 1)]
    hold[:, rows + pooled:] = jnp.zeros((2, hold.shape[1] - rows - pooled, c1), F32)
    for side, (p, g) in enumerate(((0, 0), (cols - 16, half - 16))):
        at = 15 * side
        for r in range(rows):
            hold[side, r:r + 1] = pre[r, p:p + 16].astype(F32)[at:at + 1]
        for i in range(pooled):
            hold[side, rows + i:rows + i + 1] = grad_out[i, g:g + 16].astype(F32)[at:at + 1]
    col_a[...] = hold[1 - core].astype(BF16)
    col_b[...] = hold[core].astype(BF16)


def one_at(where):
    return jnp.where(where, 1.0, 0.0).astype(BF16)


def local_kernel(pre, slope, act_t, act_ends, line, act_s):
    rows, cols, c1 = pre.shape
    half = cols // 2

    def one_row(r, carry):
        line[...] = pre[r].astype(F32)
        for pc in range(2):
            value = line[pl.ds(pc, half, stride=2), :]
            cdf = cdf_of(value)
            act = value * cdf
            act_s[r % 2, r // 2, :, pc * c1:(pc + 1) * c1] = act.astype(BF16)
            act_ends[pc, pl.ds(r, 1), :] = act[pc * (half - 1):pc * (half - 1) + 1]
            slope[r, :, pc * c1:(pc + 1) * c1] = slope_of(value, cdf)
        return carry

    lax.fori_loop(0, rows, one_row, 0)
    for pr in range(2):
        act_t[pr] = act_s[pr].reshape(rows // 2 * half, 2 * c1).T


def layout_kernel(fields, w_first, w_second, fields_t, field_ends, taps_first, taps_second, turned):
    rows, c0, cols = fields.shape
    c1 = w_first.shape[3]
    half = cols // 2
    col = lax.broadcasted_iota(jnp.int32, (cols, 2 * cols), 0)
    lane = lax.broadcasted_iota(jnp.int32, (cols, 2 * cols), 1)
    turn = lane // cols
    parity = (lane % cols) // half
    parity = parity + turn - 2 * parity * turn
    order = one_at(col == 2 * (lane % half) + parity)
    turned[...] = dot(fields[...].reshape(rows * c0, cols), order).astype(BF16).reshape(rows, c0, 2 * cols)
    low = lax.broadcasted_iota(jnp.int32, (c0, cols), 1) < half
    for q in range(rows // 2):
        fields_t[:c0, q * cols:(q + 1) * cols] = jnp.where(low, turned[2 * q, :, :cols], turned[2 * q + 1, :, cols:])
        fields_t[c0:, q * cols:(q + 1) * cols] = jnp.where(low, turned[2 * q, :, cols:], turned[2 * q + 1, :, :cols])
    cell = lax.broadcasted_iota(jnp.int32, (rows * half, 2 * rows), 0)
    n = lax.broadcasted_iota(jnp.int32, (rows * half, 2 * rows), 1)
    pick = one_at(cell == (n % rows) * half + (n // rows) * (half - 1))
    field_ends[...] = dot(fields_t[...], pick).astype(BF16)
    taps_second[...] = jnp.zeros_like(taps_second)
    taps_first[...] = jnp.zeros_like(taps_first)
    for a in range(3):
        for pc, blocks in ((0, (2, 1, None, 0)), (1, (None, 2, 0, 1))):
            for k, b in enumerate(blocks):
                if b is not None:
                    taps_second[a, pc * c1:(pc + 1) * c1, k * c1:(k + 1) * c1] = w_second[a, b]
        for pc, blocks in ((0, (2, 1, 0, None)), (1, (None, 2, 1, 0))):
            for k, b in enumerate(blocks):
                if b is not None:
                    start = (2 * a + pc) * c0
                    taps_first[start:start + c0, k * c1:(k + 1) * c1] = w_first[a, b]


def middle_kernel(lats, grad_out, row_a, row_b, slope, act_t, fields_t, taps,
                  spread, keep, raw_ends, slope_ends, out_ends,
                  grid, wide, prods, ends, line, sums, corner):
    _, first, last, even, core = position(lats)
    up = jnp.logical_xor(even, core == 1)
    top = jnp.where(up, row_a[...], row_b[...])
    bottom = jnp.where(up, row_b[...], row_a[...])
    rows, half, c2 = slope.shape
    c1 = c2 // 2
    pooled = rows // 2
    c0 = fields_t.shape[0] // 2
    cells = pooled * half
    raw_ends[...] = jnp.zeros_like(raw_ends)
    slope_ends[...] = jnp.zeros_like(slope_ends)
    out_ends[...] = jnp.zeros_like(out_ends)

    grid[1:pooled + 1] = grad_out[...].astype(F32)
    grid[0] = top[2 * half:, :].astype(F32)
    outside = jnp.where(last, 0.0, 1.0)
    grid[pooled + 1] = bottom[2 * half:, :].astype(F32) * outside
    at = lax.broadcasted_iota(jnp.int32, (half, c1), 0)
    for i in range(pooled + 2):
        here = grid[i]
        out_ends[0, i:i + 1] = here[:1]
        out_ends[1, i:i + 1] = here[half - 1:]
        wide[i, :, :c1] = jnp.where(at == 0, 0.0, pltpu.roll(here, 1, 0)).astype(BF16)
        wide[i, :, c1:2 * c1] = here.astype(BF16)
        wide[i, :, 2 * c1:3 * c1] = jnp.where(at == half - 1, 0.0, pltpu.roll(here, half - 1, 0)).astype(BF16)
        wide[i, :, 3 * c1:] = here.astype(BF16)

    flat = wide[1:pooled + 1].reshape(cells, 4 * c1)
    for a in range(3):
        prods[a] = dot_nt(flat, taps[a]).reshape(pooled, half, c2)
    fold = jnp.where(first, taps[0], taps[2])
    ends[0] = dot_nt(wide[0], fold)
    ends[1] = dot_nt(wide[0], taps[1])
    ends[2] = dot_nt(wide[pooled + 1], taps[0])
    ends[3] = dot_nt(wide[pooled + 1], taps[1])

    def place(r, total, incline):
        inner = total * incline
        raw_ends[0, pl.ds(r, 1), :] = total[:1, :c1]
        raw_ends[1, pl.ds(r, 1), :] = total[half - 1:, c1:]
        slope_ends[0, pl.ds(r, 1), :] = incline[:1, :c1]
        slope_ends[1, pl.ds(r, 1), :] = incline[half - 1:, c1:]
        even, odd = inner[:, :c1], inner[:, c1:]
        spread[r, :, :c1] = jnp.where(at == 0, 0.0, pltpu.roll(odd, 1, 0)).astype(BF16)
        spread[r, :, c1:2 * c1] = jnp.where(at == 0, 0.0, even).astype(BF16)
        spread[r, :, 2 * c1:3 * c1] = jnp.where(at == half - 1, 0.0, odd).astype(BF16)
        spread[r, :, 3 * c1:] = jnp.where(at == half - 1, 0.0, pltpu.roll(even, half - 1, 0)).astype(BF16)

    def halo_slope(message):
        line[...] = message[:2 * half, :].astype(F32)
        both = [line[pl.ds(pc, half, stride=2), :] for pc in range(2)]
        return jnp.concatenate([slope_of(v, cdf_of(v)) for v in both], axis=1)

    place(0, ends[0] + ends[1] + prods[0, 0], halo_slope(top))
    place(1, ends[0] + prods[1, 0] + prods[0, 0], slope[0])

    def pair(i, carry):
        middle = prods[2, i] + prods[1, i]
        place(2 * i + 2, middle + prods[0, i + 1], slope[2 * i + 1])
        place(2 * i + 3, prods[2, i] + prods[1, i + 1] + prods[0, i + 1], slope[2 * i + 2])
        return carry

    lax.fori_loop(0, pooled - 1, pair, 0)
    final = prods[2, pooled - 1]
    place(rows, final + prods[1, pooled - 1] + ends[2], slope[rows - 1])
    place(rows + 1, (final + ends[3] + ends[2]) * outside, halo_slope(bottom))

    is_first = jnp.where(first, 1.0, 0.0).astype(BF16)
    not_first = jnp.where(first, 0.0, 1.0).astype(BF16)
    above = wide[0, :, :3 * c1]
    wide[0, :, :3 * c1] = above * not_first
    for n, (pr, start) in enumerate(((0, 0), (0, 1), (1, 1), (1, 2))):
        around = wide[start:start + pooled, :, :3 * c1].reshape(cells, 3 * c1)
        sums[n] = dot(act_t[pr], around)
    corner[...] = dot(act_t[0, :, :half], above * is_first)

    unit = c0
    per_tap = c1 // unit
    count = 9 * per_tap + 9

    def put(k, value):
        keep[k * unit:(k + 1) * unit, :] = value

    pieces = {0: ((0, 1), (1, 3)), 1: ((0, 1), (1, 2)), 2: ((0, 0), (1, 2))}
    for a in range(3):
        for b in range(3):
            total = None
            for pr, n in pieces[a]:
                for pc in range(2):
                    k = (pc + 1 - b) // 2 + 1
                    term = sums[n, pc * c1:(pc + 1) * c1, k * c1:(k + 1) * c1]
                    total = term if total is None else total + term
            if a == 0:
                for pc in range(2):
                    k = (pc + 1 - b) // 2 + 1
                    total = total + corner[pc * c1:(pc + 1) * c1, k * c1:(k + 1) * c1]
            total = total * 0.25
            for part in range(per_tap):
                put((3 * a + b) * per_tap + part, total[part * unit:(part + 1) * unit])

    head = spread[0]
    spread[0] = head * not_first
    spread[rows + 2] = head * is_first
    folded = dot(fields_t[:, :half], spread[rows + 2])
    for a in range(3):
        around = spread[2 - a:2 - a + rows].reshape(rows * half, 4 * c1)
        got = dot(fields_t[...], around)
        if a == 0:
            got = got + folded
        for b in range(3):
            even = got[:c0, (2 - b) * c1:(3 - b) * c1]
            odd = got[c0:, (3 - b) * c1:(4 - b) * c1]
            put(9 * per_tap + 3 * a + b, even + odd)
    if keep.shape[0] > count * unit:
        keep[count * unit:] = jnp.zeros((keep.shape[0] - count * unit, c1), F32)


def columns_kernel(lats, col_a, col_b, act_ends, field_ends, taps, keep, raw_ends, slope_ends, out_ends,
                   ends, *rest):
    own, other, (lhs, values, right_hand, total) = rest[:lats], rest[lats:2 * lats], rest[2 * lats:]
    band, first, last, _, core = position(lats)
    c1 = act_ends.shape[2]
    rows = act_ends.shape[1]
    pooled = rows // 2
    c0 = field_ends.shape[0] // 2
    span, size = raw_ends.shape[1], col_a.shape[0]
    got_a, got_b = col_a[...].astype(F32), col_b[...].astype(F32)
    message = jnp.concatenate([jnp.where(core == 0, got_b, got_a), jnp.where(core == 0, got_a, got_b)], 1)
    at = lax.broadcasted_iota(jnp.int32, (size, 2 * c1), 0)
    message = jnp.where(jnp.logical_and(at == rows + pooled + 3, last), 0.0, message).astype(BF16)

    n = lax.broadcasted_iota(jnp.int32, (3 * span, size), 0)
    k = lax.broadcasted_iota(jnp.int32, (3 * span, size), 1)
    row = n % span
    want = (row - n // span + 2) // 2 - 1
    place = jnp.where(want < 0, rows + pooled + 2, jnp.where(want == pooled, rows + pooled + 3, rows + want))
    beside = dot(one_at(jnp.logical_and(k == place, row < rows + 2)), message)
    n = lax.broadcasted_iota(jnp.int32, (3 * span, out_ends.shape[1]), 0)
    k = lax.broadcasted_iota(jnp.int32, (3 * span, out_ends.shape[1]), 1)
    row = n % span
    want = (row - n // span + 2) // 2
    pick = one_at(jnp.logical_and(k == want, row < rows + 2))
    within = dot(pick, jnp.concatenate([out_ends[0], out_ends[1]], 1).astype(BF16))
    n = lax.broadcasted_iota(jnp.int32, (span, size), 0)
    k = lax.broadcasted_iota(jnp.int32, (span, size), 1)
    place = jnp.where(n == 0, rows + pooled, jnp.where(n == rows + 1, rows + pooled + 1, n - 1))
    saved = dot(one_at(jnp.logical_and(k == place, n < rows + 2)), message)
    incline = slope_of(saved, cdf_of(saved))

    head = lax.broadcasted_iota(jnp.int32, (span, 2 * c1), 0) < 2
    turned = jnp.logical_and(head, first)
    lhs[...] = jnp.zeros_like(lhs)
    rights = []
    for a in range(4):
        sides, inner = (x[min(a, 2) * span:(min(a, 2) + 1) * span] for x in (beside, within))
        if a == 2:
            sides, inner = jnp.where(turned, 0.0, sides), jnp.where(turned, 0.0, inner)
        if a == 3:
            sides, inner = jnp.where(turned, sides, 0.0), jnp.where(turned, inner, 0.0)
        rights.append(sides)
        sides, inner = sides.astype(BF16), inner.astype(BF16)
        left, right = sides[:, :c1], sides[:, c1:]
        lhs[a, :span, c1:2 * c1] = left
        lhs[a, :span, 2 * c1:3 * c1] = inner[:, :c1]
        lhs[a, :span, 3 * c1:] = left
        lhs[a, span:2 * span, :c1] = left
        lhs[a, 2 * span:3 * span, :c1] = inner[:, c1:]
        lhs[a, 2 * span:3 * span, c1:2 * c1] = right
        lhs[a, 2 * span:3 * span, 3 * c1:] = right
        lhs[a, 3 * span:, 2 * c1:3 * c1] = right
    found = dot_nt(lhs[0], taps[0]) + dot_nt(lhs[1], taps[1]) + dot_nt(lhs[2], taps[2]) + dot_nt(lhs[3], taps[0])
    row = lax.broadcasted_iota(jnp.int32, (span, c1), 0)
    inside = jnp.where(jnp.logical_or(row > rows + 1, jnp.logical_and(row == rows + 1, last)), 0.0, 1.0)
    values[0] = found[:span, c1:] * incline[:, :c1] * inside
    values[1] = (raw_ends[0] + found[span:2 * span, :c1]) * slope_ends[0] * inside
    values[2] = (raw_ends[1] + found[3 * span:, c1:]) * slope_ends[1] * inside
    values[3] = found[2 * span:3 * span, :c1] * incline[:, c1:] * inside
    ends[...] = values[...].astype(BF16)

    total[...] = keep[...]
    for side, b in ((0, 2), (1, 0)):
        around = jnp.concatenate([x[1:rows + 1, side * c1:(side + 1) * c1] for x in rights], 1).astype(BF16)
        terms = lax.dot_general(act_ends[side].astype(BF16), around, (((0,), (0,)), ((), ())),
                                preferred_element_type=F32) * 0.25
        for a in range(3):
            term = terms[:, a * c1:(a + 1) * c1]
            if a == 0:
                term = term + terms[:, 3 * c1:]
            low = (3 * a + b) * c1
            total[low:low + c1] = total[low:low + c1] + term
    right_hand[...] = jnp.zeros_like(right_hand)
    top = lax.broadcasted_iota(jnp.int32, (rows, c1), 0) == 0
    over = jnp.logical_and(top, first)
    for a in range(4):
        for j in range(4):
            value = values[j, 2 - min(a, 2):2 - min(a, 2) + rows]
            if a == 2:
                value = jnp.where(over, 0.0, value)
            if a == 3:
                value = jnp.where(over, value, 0.0)
            right_hand[a, j // 2 * rows:(j // 2 + 1) * rows, j * c1:(j + 1) * c1] = value.astype(BF16)
    for a in range(3):
        got = dot(field_ends[...], right_hand[a])
        if a == 0:
            got = got + dot(field_ends[...], right_hand[3])
        for b in range(3):
            even = got[:c0, (2 - b) * c1:(3 - b) * c1]
            odd = got[c0:, (3 - b) * c1:(4 - b) * c1]
            low = 9 * c1 + (3 * a + b) * c0
            total[low:low + c0] = total[low:low + c0] + even + odd

    block = own[0].shape[0]
    mine = half_held()
    for targets, half_of in ((own, mine), (other, 1 - mine)):
        for far in range(lats):
            start = (half_of * lats + (band ^ far)) * block
            targets[far][...] = total[pl.ds(pl.multiple_of(start, block), block), :]


def last_kernel(lats, part, ends, taps, out, spread, values, total, turned):
    rows, c0, cols = out.shape
    half = cols // 2
    c2 = 2 * c0
    depth = spread.shape[2]
    first = position(lats)[1]
    spread[...] = part[...]
    c1 = depth // 4
    for j in range(4):
        values[:, j * c1:(j + 1) * c1] = ends[j].astype(F32)
    at = lax.broadcasted_iota(jnp.int32, (16, 2 * c1), 0)
    for r in range(rows + 3):
        n = 0 if r == rows + 2 else r
        for side, (low, spot) in enumerate(((0, 0), (half - 16, 15))):
            lanes = slice(2 * side * c1, 2 * (side + 1) * c1)
            new = values[n:n + 1, lanes]
            if n == 0:
                new = jnp.where(first == (r != 0), new, 0.0)
            tile = spread[r, low:low + 16, lanes].astype(F32)
            spread[r, low:low + 16, lanes] = jnp.where(at == spot, new, tile).astype(BF16)
    result = dot_nt(taps[:c2], spread[2:rows + 2].reshape(rows * half, depth))
    for a in (1, 2):
        result = result + dot_nt(taps[a * c2:(a + 1) * c2],
                                 spread[2 - a:2 - a + rows].reshape(rows * half, depth))
    total[...] = result
    total[:, :half] = total[:, :half] + dot_nt(taps[:c2], spread[rows + 2])
    for q in range(rows // 2):
        pair = total[:, q * cols:(q + 1) * cols].astype(BF16)
        turned[q, :, :cols] = pair[:c0]
        turned[q, :, cols:] = pair[c0:]
    k = lax.broadcasted_iota(jnp.int32, (2 * cols, 2 * cols), 0)
    n = lax.broadcasted_iota(jnp.int32, (2 * cols, 2 * cols), 1)
    order = one_at(n == ((k % cols) // half) * cols + 2 * (k % half) + k // cols)
    found = dot(turned[...].reshape(rows // 2 * c0, 2 * cols), order).astype(BF16)
    for q in range(rows // 2):
        for rp in range(2):
            out[2 * q + rp] = found[q * c0:(q + 1) * c0, rp * cols:(rp + 1) * cols]


def gather_kernel(mine, theirs, out_first, out_second):
    lats, rows, c1 = mine.shape
    band, held = lax.axis_index("lat"), half_held()
    size = out_second.shape[0]
    total = size + out_first.shape[0]
    for h in range(2):
        for i in range(lats):
            at = (h * lats + i) * rows
            here, there = (x[i ^ band].astype(F32) for x in (mine, theirs))
            value = jnp.where(held == h, here, there)
            for out, base, end in ((out_second, 0, size), (out_first, size, total)):
                low, high = max(at, base), min(at + rows, end)
                if low < high:
                    out[low - base:high - base] = value[low - at:high - at]


def vmem(count):
    return [pl.BlockSpec(memory_space=pltpu.VMEM)] * count


def far(count):
    return [pl.BlockSpec(memory_space=pl.ANY)] * count


def params(mib):
    return pltpu.CompilerParams(vmem_limit_bytes=mib * 1024 * 1024)


def shape(dims, kind):
    return jax.ShapeDtypeStruct(dims, kind)


def body(inputs, pre_first, grad_out, w_first, w_second):
    rows, cols, c1 = pre_first.shape
    c0 = inputs.shape[2]
    half, pooled = cols // 2, rows // 2
    lats, lons = lax.axis_size("lat"), lax.axis_size("lon")
    depths = lons // 2
    band, place = lax.axis_index("lat"), lax.axis_index("lon")
    core = lax.rem(place, 2)
    even = lax.rem(band, 2) == 0

    edge = -(-(rows + pooled + 4) // 16) * 16
    row_a, row_b, col_a, col_b, held_pre = pl.pallas_call(
        functools.partial(pack_kernel, lats),
        out_shape=(
            pltpu.VMEM((cols + half, c1), BF16),
            pltpu.VMEM((cols + half, c1), BF16),
            pltpu.VMEM((edge, c1), BF16),
            pltpu.VMEM((edge, c1), BF16),
            pltpu.VMEM(pre_first.shape, BF16),
        ),
        in_specs=far(2),
        out_specs=tuple(vmem(5)),
        scratch_shapes=[
            pltpu.VMEM((2, edge, c1), F32),
            pltpu.VMEM(grad_out.shape, BF16),
            pltpu.SemaphoreType.DMA((2,)),
        ],
        compiler_params=params(58),
        cost_estimate=pl.CostEstimate(flops=1000, bytes_accessed=1 << 18, transcendentals=0),
    )(pre_first, grad_out)
    def partner(i, j, near):
        if near:
            return (i ^ 1) * lons + j
        if i == 0:
            return (j + lons // 2) % lons
        if i == lats - 1:
            return i * lons + (j ^ 2)
        return (i + 1 if i % 2 else i - 1) * lons + j

    def rows_round(value, near):
        return lax.ppermute(value, AREA, [
            (i * lons + j, partner(i, j, near[j % 2])) for i in range(lats) for j in range(lons)])

    up = jnp.logical_xor(even, core == 1)
    row_a = rows_round(row_a, (False, True))
    row_b = rows_round(row_b, (True, False))

    slope, act_t, act_ends = pl.pallas_call(
        local_kernel,
        out_shape=(
            shape((rows, half, 2 * c1), F32),
            shape((2, 2 * c1, pooled * half), BF16),
            shape((2, rows, c1), F32),
        ),
        in_specs=vmem(1),
        out_specs=tuple(vmem(3)),
        scratch_shapes=[
            pltpu.VMEM((cols, c1), F32),
            pltpu.VMEM((2, pooled, half, 2 * c1), BF16),
        ],
        compiler_params=params(16),
        cost_estimate=pl.CostEstimate(flops=60 * rows * cols * c1, bytes_accessed=2 << 20,
                                      transcendentals=2 * rows * cols * c1),
    )(held_pre)

    fields_t, field_ends, taps_first, taps_second = pl.pallas_call(
        layout_kernel,
        out_shape=(
            shape((2 * c0, rows * half), BF16),
            shape((2 * c0, 2 * rows), BF16),
            shape((6 * c0, 4 * c1), BF16),
            shape((3, 2 * c1, 4 * c1), BF16),
        ),
        in_specs=vmem(3),
        out_specs=tuple(vmem(4)),
        scratch_shapes=[pltpu.VMEM((rows, c0, 2 * cols), BF16)],
        compiler_params=params(16),
        cost_estimate=pl.CostEstimate(flops=4 * rows * cols * c0 * cols, bytes_accessed=3 << 20, transcendentals=0),
    )(jnp.transpose(inputs, (0, 2, 1)), w_first, w_second)
    row_a, row_b, slope, fields_t = lax.optimization_barrier((row_a, row_b, slope, fields_t))

    def corners(at):
        places = (at * (cols - 1), cols + at * (half - 1))
        above, below = (jnp.where(up, one, two) for one, two in ((row_a, row_b), (row_b, row_a)))
        return jnp.concatenate([part[p:p + 1] for p in places for part in (above, below)], 0)

    low, high = corners(0), corners(1)
    pad = jnp.zeros((edge - rows - pooled - 4, c1), BF16)
    col_a = jnp.concatenate([col_a[:rows + pooled], jnp.where(core == 0, high, low), pad], 0)
    col_b = jnp.concatenate([col_b[:rows + pooled], jnp.where(core == 0, low, high), pad], 0)
    col_b = lax.ppermute(col_b, "lon", [(i, (i + 2 * (i % 2) - 1) % lons) for i in range(lons)])
    col_a = lax.ppermute(col_a, "lon", [(i, i ^ 1) for i in range(lons)])

    block = -(-9 * (c1 + c0) // (16 * lats)) * 8
    held = lats * block
    reach = -(-(rows + 2) // 16) * 16
    spread, keep, raw_ends, slope_ends, out_ends = pl.pallas_call(
        functools.partial(middle_kernel, lats),
        out_shape=(
            shape((rows + 3, half, 4 * c1), BF16),
            shape((2 * held, c1), F32),
            shape((2, reach, c1), F32),
            shape((2, reach, c1), F32),
            shape((2, -(-(pooled + 2) // 16) * 16, c1), F32),
        ),
        in_specs=vmem(7),
        out_specs=tuple(vmem(5)),
        scratch_shapes=[
            pltpu.VMEM((pooled + 2, half, c1), F32),
            pltpu.VMEM((pooled + 2, half, 4 * c1), BF16),
            pltpu.VMEM((3, pooled, half, 2 * c1), F32),
            pltpu.VMEM((4, half, 2 * c1), F32),
            pltpu.VMEM((cols, c1), F32),
            pltpu.VMEM((4, 2 * c1, 3 * c1), F32),
            pltpu.VMEM((2 * c1, 3 * c1), F32),
        ],
        compiler_params=params(16),
        cost_estimate=pl.CostEstimate(flops=2 * rows * cols * c1 * 9 * (2 * c1 + c0), bytes_accessed=8 << 20,
                                      transcendentals=0),
    )(grad_out, row_a, row_b, slope, act_t, fields_t, taps_second)
    col_a, col_b, keep = lax.optimization_barrier((col_a, col_b, keep))

    ends, *halves = pl.pallas_call(
        functools.partial(columns_kernel, lats),
        out_shape=(
            shape((4, reach, c1), BF16),
        ) + (shape((block, c1), F32),) * (2 * lats),
        in_specs=vmem(9),
        out_specs=tuple(vmem(2 * lats + 1)),
        scratch_shapes=[
            pltpu.VMEM((4, 4 * reach, 4 * c1), BF16),
            pltpu.VMEM((4, reach, c1), F32),
            pltpu.VMEM((4, 2 * rows, 4 * c1), BF16),
            pltpu.VMEM((2 * held, c1), F32),
        ],
        compiler_params=params(16),
        cost_estimate=pl.CostEstimate(flops=1 << 28, bytes_accessed=3 << 20, transcendentals=0),
    )(col_a, col_b, act_ends, field_ends, taps_second, keep, raw_ends, slope_ends, out_ends)

    swap = [(i, i ^ 1) for i in range(lons)]

    def between_chips(value, over_lat, over_lon):
        turn = odd(over_lat) ^ odd(over_lon)
        return lax.ppermute(value, AREA, [
            (i * lons + j, (i ^ over_lat) * lons + (j ^ (2 * over_lon) ^ turn)) for i in range(lats) for j in range(lons)])

    own, other = halves[:lats], halves[lats:]
    other = {far: lax.ppermute(other[far], "lon", swap) for far in reversed(range(lats))}
    parts = [own[far] + other[far] for far in range(lats)]
    got = [between_chips(parts[far].astype(BF16), far, 0) for far in reversed(range(1, lats))]
    grad_inputs = pl.pallas_call(
        functools.partial(last_kernel, lats),
        out_shape=shape((rows, c0, cols), BF16),
        in_specs=vmem(3),
        out_specs=vmem(1)[0],
        scratch_shapes=[
            pltpu.VMEM((rows + 3, half, 4 * c1), BF16),
            pltpu.VMEM((reach, 4 * c1), F32),
            pltpu.VMEM((2 * c0, rows * half), F32),
            pltpu.VMEM((pooled, c0, 2 * cols), BF16),
        ],
        compiler_params=params(12),
        cost_estimate=pl.CostEstimate(flops=2 * rows * cols * c1 * 9 * c0, bytes_accessed=3 << 20, transcendentals=0),
    )(spread, ends, taps_first)
    *got, grad_inputs = lax.optimization_barrier((*got, grad_inputs))
    total = parts[0]
    for value in got:
        total = total + value.astype(F32)
    part = total.astype(BF16)
    terms = [part] + [between_chips(part, 0, far) for far in range(1, depths)]
    terms = [term.astype(F32) for term in terms]
    while len(terms) > 1:
        terms = [terms[k + (k > 0)] + terms[k + (k == 0)] for k in range(0, len(terms), 2)]
    part = terms[0].astype(BF16)
    mine = jnp.stack([part] + [between_chips(part, far, 0) for far in range(1, lats)], 0)
    theirs = lax.ppermute(mine, "lon", swap)

    grad_w_first, grad_w_second = pl.pallas_call(
        gather_kernel,
        out_shape=(shape((9 * c0, c1), F32), shape((9 * c1, c1), F32)),
        in_specs=vmem(2),
        out_specs=tuple(vmem(2)),
        compiler_params=params(8),
        cost_estimate=pl.CostEstimate(flops=1000, bytes_accessed=3 << 19, transcendentals=0),
    )(mine, theirs)
    return (jnp.transpose(grad_inputs, (0, 2, 1)), grad_w_first.reshape(w_first.shape),
            grad_w_second.reshape(w_second.shape))


def solution(mesh):
    in_specs = (P("lat", "lon", None), P("lat", "lon", None), P("lat", "lon", None), P(), P())
    out_specs = (P("lat", "lon", None), P(), P())
    return jax.shard_map(body, mesh=mesh, in_specs=in_specs, out_specs=out_specs, check_vma=False)
```

```python
import functools

import jax
import jax.numpy as jnp
from jax import lax
from jax.experimental import pallas as pl
from jax.experimental.pallas import tpu as pltpu
from jax.sharding import PartitionSpec as P

inv_root = 0.7071067811865476
density = 0.3989422804014327

F32 = jnp.float32
BF16 = jnp.bfloat16
AREA = ("lat", "lon")


def cdf_of(value):
    return 0.5 * (1.0 + lax.erf(value * inv_root))


def slope_of(value, cdf):
    return 0.25 * (cdf + value * jnp.exp(-0.5 * value * value) * density)


def dot(left, right):
    return jnp.dot(left, right, preferred_element_type=F32)


def dot_nt(left, right):
    return lax.dot_general(left, right, (((1,), (1,)), ((), ())), preferred_element_type=F32)


def position(lats):
    band, place = lax.axis_index("lat"), lax.axis_index("lon")
    return band, band == 0, band == lats - 1, lax.rem(band, 2) == 0, lax.rem(place, 2)


def odd(value):
    for shift in (4, 2, 1):
        value = value ^ (value >> shift)
    return value & 1


def half_held():
    band, place = lax.axis_index("lat"), lax.axis_index("lon")
    return odd(band) ^ odd(place // 2) ^ (place % 2)


def pack_kernel(lats, pre_far, grad_far, row_a, row_b, col_a, col_b, pre, hold, grad_out, sems):
    copies = [pltpu.make_async_copy(pre_far, pre, sems.at[0]), pltpu.make_async_copy(grad_far, grad_out, sems.at[1])]
    for copy in copies:
        copy.start()
    for copy in copies:
        copy.wait()
    rows, cols, c1 = pre.shape
    pooled, half = grad_out.shape[:2]
    _, _, _, even, core = position(lats)
    for message, low in ((row_a, ~even), (row_b, even)):
        message[:cols] = pre[jnp.where(low, 0, rows - 1)]
        message[cols:] = grad_out[jnp.where(low, 0, pooled - 1)]
    hold[:, rows + pooled:] = jnp.zeros((2, hold.shape[1] - rows - pooled, c1), F32)
    for side, (p, g) in enumerate(((0, 0), (cols - 16, half - 16))):
        at = 15 * side
        for r in range(rows):
            hold[side, r:r + 1] = pre[r, p:p + 16].astype(F32)[at:at + 1]
        for i in range(pooled):
            hold[side, rows + i:rows + i + 1] = grad_out[i, g:g + 16].astype(F32)[at:at + 1]
    col_a[...] = hold[1 - core].astype(BF16)
    col_b[...] = hold[core].astype(BF16)


def one_at(where):
    return jnp.where(where, 1.0, 0.0).astype(BF16)


def local_kernel(pre, slope, act_t, act_ends, line, act_s):
    rows, cols, c1 = pre.shape
    half = cols // 2

    def one_row(r, carry):
        line[...] = pre[r].astype(F32)
        for pc in range(2):
            value = line[pl.ds(pc, half, stride=2), :]
            cdf = cdf_of(value)
            act = value * cdf
            act_s[r % 2, r // 2, :, pc * c1:(pc + 1) * c1] = act.astype(BF16)
            act_ends[pc, pl.ds(r, 1), :] = act[pc * (half - 1):pc * (half - 1) + 1]
            slope[r, :, pc * c1:(pc + 1) * c1] = slope_of(value, cdf)
        return carry

    lax.fori_loop(0, rows, one_row, 0)
    for pr in range(2):
        act_t[pr] = act_s[pr].reshape(rows // 2 * half, 2 * c1).T


def layout_kernel(fields, w_first, w_second, fields_t, field_ends, taps_first, taps_second, turned):
    rows, c0, cols = fields.shape
    c1 = w_first.shape[3]
    half = cols // 2
    col = lax.broadcasted_iota(jnp.int32, (cols, 2 * cols), 0)
    lane = lax.broadcasted_iota(jnp.int32, (cols, 2 * cols), 1)
    turn = lane // cols
    parity = (lane % cols) // half
    parity = parity + turn - 2 * parity * turn
    order = one_at(col == 2 * (lane % half) + parity)
    turned[...] = dot(fields[...].reshape(rows * c0, cols), order).astype(BF16).reshape(rows, c0, 2 * cols)
    low = lax.broadcasted_iota(jnp.int32, (c0, cols), 1) < half
    for q in range(rows // 2):
        fields_t[:c0, q * cols:(q + 1) * cols] = jnp.where(low, turned[2 * q, :, :cols], turned[2 * q + 1, :, cols:])
        fields_t[c0:, q * cols:(q + 1) * cols] = jnp.where(low, turned[2 * q, :, cols:], turned[2 * q + 1, :, :cols])
    cell = lax.broadcasted_iota(jnp.int32, (rows * half, 2 * rows), 0)
    n = lax.broadcasted_iota(jnp.int32, (rows * half, 2 * rows), 1)
    pick = one_at(cell == (n % rows) * half + (n // rows) * (half - 1))
    field_ends[...] = dot(fields_t[...], pick).astype(BF16)
    taps_second[...] = jnp.zeros_like(taps_second)
    taps_first[...] = jnp.zeros_like(taps_first)
    for a in range(3):
        for pc, blocks in ((0, (2, 1, None, 0)), (1, (None, 2, 0, 1))):
            for k, b in enumerate(blocks):
                if b is not None:
                    taps_second[a, pc * c1:(pc + 1) * c1, k * c1:(k + 1) * c1] = w_second[a, b]
        for pc, blocks in ((0, (2, 1, 0, None)), (1, (None, 2, 1, 0))):
            for k, b in enumerate(blocks):
                if b is not None:
                    start = (2 * a + pc) * c0
                    taps_first[start:start + c0, k * c1:(k + 1) * c1] = w_first[a, b]


def middle_kernel(lats, grad_out, row_a, row_b, slope, act_t, fields_t, taps,
                  spread, keep, raw_ends, slope_ends, out_ends,
                  grid, wide, prods, line, sums, corner):
    _, first, last, even, _ = position(lats)
    top = jnp.where(even, row_b[...], row_a[...])
    bottom = jnp.where(even, row_a[...], row_b[...])
    rows, half, c2 = slope.shape
    c1 = c2 // 2
    pooled = rows // 2
    c0 = fields_t.shape[0] // 2
    cells = pooled * half
    raw_ends[...] = jnp.zeros_like(raw_ends)
    slope_ends[...] = jnp.zeros_like(slope_ends)
    out_ends[...] = jnp.zeros_like(out_ends)

    grid[1:pooled + 1] = grad_out[...].astype(F32)
    grid[0] = top[2 * half:, :].astype(F32)
    outside = jnp.where(last, 0.0, 1.0)
    grid[pooled + 1] = bottom[2 * half:, :].astype(F32) * outside
    at = lax.broadcasted_iota(jnp.int32, (half, c1), 0)
    for i in range(pooled + 2):
        here = grid[i]
        out_ends[0, i:i + 1] = here[:1]
        out_ends[1, i:i + 1] = here[half - 1:]
        wide[i, :, :c1] = jnp.where(at == 0, 0.0, pltpu.roll(here, 1, 0)).astype(BF16)
        wide[i, :, c1:2 * c1] = here.astype(BF16)
        wide[i, :, 2 * c1:3 * c1] = jnp.where(at == half - 1, 0.0, pltpu.roll(here, half - 1, 0)).astype(BF16)
        wide[i, :, 3 * c1:] = here.astype(BF16)

    flat = wide[...].reshape((pooled + 2) * half, 4 * c1)
    for a in range(3):
        prods[a] = dot_nt(flat, taps[a]).reshape(pooled + 2, half, c2)
    fold = jnp.where(first, prods[0, 0], prods[2, 0])

    def place(r, total, incline):
        inner = total * incline
        raw_ends[0, pl.ds(r, 1), :] = total[:1, :c1]
        raw_ends[1, pl.ds(r, 1), :] = total[half - 1:, c1:]
        slope_ends[0, pl.ds(r, 1), :] = incline[:1, :c1]
        slope_ends[1, pl.ds(r, 1), :] = incline[half - 1:, c1:]
        even, odd = inner[:, :c1], inner[:, c1:]
        spread[r, :, :c1] = jnp.where(at == 0, 0.0, pltpu.roll(odd, 1, 0)).astype(BF16)
        spread[r, :, c1:2 * c1] = jnp.where(at == 0, 0.0, even).astype(BF16)
        spread[r, :, 2 * c1:3 * c1] = jnp.where(at == half - 1, 0.0, odd).astype(BF16)
        spread[r, :, 3 * c1:] = jnp.where(at == half - 1, 0.0, pltpu.roll(even, half - 1, 0)).astype(BF16)

    def halo_slope(message):
        line[...] = message[:2 * half, :].astype(F32)
        both = [line[pl.ds(pc, half, stride=2), :] for pc in range(2)]
        return jnp.concatenate([slope_of(v, cdf_of(v)) for v in both], axis=1)

    place(0, fold + prods[1, 0] + prods[0, 1], halo_slope(top))
    place(1, fold + prods[1, 1] + prods[0, 1], slope[0])

    def pair(i, carry):
        place(2 * i, prods[2, i] + prods[1, i] + prods[0, i + 1], slope[2 * i - 1])
        place(2 * i + 1, prods[2, i] + prods[1, i + 1] + prods[0, i + 1], slope[2 * i])
        return carry

    lax.fori_loop(1, pooled, pair, 0)
    final, below = prods[2, pooled], prods[0, pooled + 1]
    place(rows, final + prods[1, pooled] + below, slope[rows - 1])
    place(rows + 1, (final + prods[1, pooled + 1] + below) * outside, halo_slope(bottom))

    is_first = jnp.where(first, 1.0, 0.0).astype(BF16)
    not_first = jnp.where(first, 0.0, 1.0).astype(BF16)
    above = wide[0, :, :3 * c1]
    wide[0, :, :3 * c1] = above * not_first
    for n, (pr, start) in enumerate(((0, 0), (0, 1), (1, 1), (1, 2))):
        around = wide[start:start + pooled, :, :3 * c1].reshape(cells, 3 * c1)
        sums[n] = dot(act_t[pr], around)
    corner[...] = dot(act_t[0, :, :half], above * is_first)

    unit = c0
    per_tap = c1 // unit
    count = 9 * per_tap + 9

    def put(k, value):
        keep[k * unit:(k + 1) * unit, :] = value

    pieces = {0: ((0, 1), (1, 3)), 1: ((0, 1), (1, 2)), 2: ((0, 0), (1, 2))}
    for a in range(3):
        for b in range(3):
            total = None
            for pr, n in pieces[a]:
                for pc in range(2):
                    k = (pc + 1 - b) // 2 + 1
                    term = sums[n, pc * c1:(pc + 1) * c1, k * c1:(k + 1) * c1]
                    total = term if total is None else total + term
            if a == 0:
                for pc in range(2):
                    k = (pc + 1 - b) // 2 + 1
                    total = total + corner[pc * c1:(pc + 1) * c1, k * c1:(k + 1) * c1]
            total = total * 0.25
            for part in range(per_tap):
                put((3 * a + b) * per_tap + part, total[part * unit:(part + 1) * unit])

    head = spread[0]
    spread[0] = head * not_first
    spread[rows + 2] = head * is_first
    folded = dot(fields_t[:, :half], spread[rows + 2])
    for a in range(3):
        around = spread[2 - a:2 - a + rows].reshape(rows * half, 4 * c1)
        got = dot(fields_t[...], around)
        if a == 0:
            got = got + folded
        for b in range(3):
            even = got[:c0, (2 - b) * c1:(3 - b) * c1]
            odd = got[c0:, (3 - b) * c1:(4 - b) * c1]
            put(9 * per_tap + 3 * a + b, even + odd)
    if keep.shape[0] > count * unit:
        keep[count * unit:] = jnp.zeros((keep.shape[0] - count * unit, c1), F32)


def columns_kernel(lats, col_a, col_b, act_ends, field_ends, taps, keep, raw_ends, slope_ends, out_ends,
                   ends, *rest):
    own, other, (lhs, values, right_hand, total) = rest[:lats], rest[lats:2 * lats], rest[2 * lats:]
    band, first, last, _, core = position(lats)
    c1 = act_ends.shape[2]
    rows = act_ends.shape[1]
    pooled = rows // 2
    c0 = field_ends.shape[0] // 2
    span, size = raw_ends.shape[1], col_a.shape[0]
    got_a, got_b = col_a[...].astype(F32), col_b[...].astype(F32)
    message = jnp.concatenate([jnp.where(core == 0, got_b, got_a), jnp.where(core == 0, got_a, got_b)], 1)
    at = lax.broadcasted_iota(jnp.int32, (size, 2 * c1), 0)
    message = jnp.where(jnp.logical_and(at == rows + pooled + 3, last), 0.0, message).astype(BF16)

    n = lax.broadcasted_iota(jnp.int32, (3 * span, size), 0)
    k = lax.broadcasted_iota(jnp.int32, (3 * span, size), 1)
    row = n % span
    want = (row - n // span + 2) // 2 - 1
    place = jnp.where(want < 0, rows + pooled + 2, jnp.where(want == pooled, rows + pooled + 3, rows + want))
    beside = dot(one_at(jnp.logical_and(k == place, row < rows + 2)), message)
    n = lax.broadcasted_iota(jnp.int32, (3 * span, out_ends.shape[1]), 0)
    k = lax.broadcasted_iota(jnp.int32, (3 * span, out_ends.shape[1]), 1)
    row = n % span
    want = (row - n // span + 2) // 2
    pick = one_at(jnp.logical_and(k == want, row < rows + 2))
    within = dot(pick, jnp.concatenate([out_ends[0], out_ends[1]], 1).astype(BF16))
    n = lax.broadcasted_iota(jnp.int32, (span, size), 0)
    k = lax.broadcasted_iota(jnp.int32, (span, size), 1)
    place = jnp.where(n == 0, rows + pooled, jnp.where(n == rows + 1, rows + pooled + 1, n - 1))
    saved = dot(one_at(jnp.logical_and(k == place, n < rows + 2)), message)
    incline = slope_of(saved, cdf_of(saved))

    head = lax.broadcasted_iota(jnp.int32, (span, 2 * c1), 0) < 2
    turned = jnp.logical_and(head, first)
    lhs[...] = jnp.zeros_like(lhs)
    rights = []
    for a in range(4):
        sides, inner = (x[min(a, 2) * span:(min(a, 2) + 1) * span] for x in (beside, within))
        if a == 2:
            sides, inner = jnp.where(turned, 0.0, sides), jnp.where(turned, 0.0, inner)
        if a == 3:
            sides, inner = jnp.where(turned, sides, 0.0), jnp.where(turned, inner, 0.0)
        rights.append(sides)
        sides, inner = sides.astype(BF16), inner.astype(BF16)
        left, right = sides[:, :c1], sides[:, c1:]
        lhs[a, :span, c1:2 * c1] = left
        lhs[a, :span, 2 * c1:3 * c1] = inner[:, :c1]
        lhs[a, :span, 3 * c1:] = left
        lhs[a, span:2 * span, :c1] = left
        lhs[a, 2 * span:3 * span, :c1] = inner[:, c1:]
        lhs[a, 2 * span:3 * span, c1:2 * c1] = right
        lhs[a, 2 * span:3 * span, 3 * c1:] = right
        lhs[a, 3 * span:, 2 * c1:3 * c1] = right
    found = dot_nt(lhs[0], taps[0]) + dot_nt(lhs[1], taps[1]) + dot_nt(lhs[2], taps[2]) + dot_nt(lhs[3], taps[0])
    row = lax.broadcasted_iota(jnp.int32, (span, c1), 0)
    inside = jnp.where(jnp.logical_or(row > rows + 1, jnp.logical_and(row == rows + 1, last)), 0.0, 1.0)
    values[0] = found[:span, c1:] * incline[:, :c1] * inside
    values[1] = (raw_ends[0] + found[span:2 * span, :c1]) * slope_ends[0] * inside
    values[2] = (raw_ends[1] + found[3 * span:, c1:]) * slope_ends[1] * inside
    values[3] = found[2 * span:3 * span, :c1] * incline[:, c1:] * inside
    ends[...] = values[...].astype(BF16)

    total[...] = keep[...]
    for side, b in ((0, 2), (1, 0)):
        around = jnp.concatenate([x[1:rows + 1, side * c1:(side + 1) * c1] for x in rights], 1).astype(BF16)
        terms = lax.dot_general(act_ends[side].astype(BF16), around, (((0,), (0,)), ((), ())),
                                preferred_element_type=F32) * 0.25
        for a in range(3):
            term = terms[:, a * c1:(a + 1) * c1]
            if a == 0:
                term = term + terms[:, 3 * c1:]
            low = (3 * a + b) * c1
            total[low:low + c1] = total[low:low + c1] + term
    right_hand[...] = jnp.zeros_like(right_hand)
    top = lax.broadcasted_iota(jnp.int32, (rows, c1), 0) == 0
    over = jnp.logical_and(top, first)
    for a in range(4):
        for j in range(4):
            value = values[j, 2 - min(a, 2):2 - min(a, 2) + rows]
            if a == 2:
                value = jnp.where(over, 0.0, value)
            if a == 3:
                value = jnp.where(over, value, 0.0)
            right_hand[a, j // 2 * rows:(j // 2 + 1) * rows, j * c1:(j + 1) * c1] = value.astype(BF16)
    for a in range(3):
        got = dot(field_ends[...], right_hand[a])
        if a == 0:
            got = got + dot(field_ends[...], right_hand[3])
        for b in range(3):
            even = got[:c0, (2 - b) * c1:(3 - b) * c1]
            odd = got[c0:, (3 - b) * c1:(4 - b) * c1]
            low = 9 * c1 + (3 * a + b) * c0
            total[low:low + c0] = total[low:low + c0] + even + odd

    block = own[0].shape[0]
    mine = half_held()
    for targets, half_of in ((own, mine), (other, 1 - mine)):
        for far in range(lats):
            start = (half_of * lats + (band ^ far)) * block
            targets[far][...] = total[pl.ds(pl.multiple_of(start, block), block), :]


def last_kernel(lats, part, ends, taps, out, spread, values, total, turned):
    rows, c0, cols = out.shape
    half = cols // 2
    c2 = 2 * c0
    depth = spread.shape[2]
    first = position(lats)[1]
    spread[...] = part[...]
    c1 = depth // 4
    for j in range(4):
        values[:, j * c1:(j + 1) * c1] = ends[j].astype(F32)
    at = lax.broadcasted_iota(jnp.int32, (16, 2 * c1), 0)
    for r in range(rows + 3):
        n = 0 if r == rows + 2 else r
        for side, (low, spot) in enumerate(((0, 0), (half - 16, 15))):
            lanes = slice(2 * side * c1, 2 * (side + 1) * c1)
            new = values[n:n + 1, lanes]
            if n == 0:
                new = jnp.where(first == (r != 0), new, 0.0)
            tile = spread[r, low:low + 16, lanes].astype(F32)
            spread[r, low:low + 16, lanes] = jnp.where(at == spot, new, tile).astype(BF16)
    result = dot_nt(taps[:c2], spread[2:rows + 2].reshape(rows * half, depth))
    for a in (1, 2):
        result = result + dot_nt(taps[a * c2:(a + 1) * c2],
                                 spread[2 - a:2 - a + rows].reshape(rows * half, depth))
    total[...] = result
    total[:, :half] = total[:, :half] + dot_nt(taps[:c2], spread[rows + 2])
    for q in range(rows // 2):
        pair = total[:, q * cols:(q + 1) * cols].astype(BF16)
        turned[q, :, :cols] = pair[:c0]
        turned[q, :, cols:] = pair[c0:]
    k = lax.broadcasted_iota(jnp.int32, (2 * cols, 2 * cols), 0)
    n = lax.broadcasted_iota(jnp.int32, (2 * cols, 2 * cols), 1)
    order = one_at(n == ((k % cols) // half) * cols + 2 * (k % half) + k // cols)
    found = dot(turned[...].reshape(rows // 2 * c0, 2 * cols), order).astype(BF16)
    for q in range(rows // 2):
        for rp in range(2):
            out[2 * q + rp] = found[q * c0:(q + 1) * c0, rp * cols:(rp + 1) * cols]


def gather_kernel(mine, theirs, out_first, out_second):
    lats, rows, c1 = mine.shape
    band, held = lax.axis_index("lat"), half_held()
    size = out_second.shape[0]
    total = size + out_first.shape[0]
    for h in range(2):
        for i in range(lats):
            at = (h * lats + i) * rows
            here, there = (x[i ^ band].astype(F32) for x in (mine, theirs))
            value = jnp.where(held == h, here, there)
            for out, base, end in ((out_second, 0, size), (out_first, size, total)):
                low, high = max(at, base), min(at + rows, end)
                if low < high:
                    out[low - base:high - base] = value[low - at:high - at]


def vmem(count):
    return [pl.BlockSpec(memory_space=pltpu.VMEM)] * count


def far(count):
    return [pl.BlockSpec(memory_space=pl.ANY)] * count


def params(mib):
    return pltpu.CompilerParams(vmem_limit_bytes=mib * 1024 * 1024)


def shape(dims, kind):
    return jax.ShapeDtypeStruct(dims, kind)


def body(inputs, pre_first, grad_out, w_first, w_second):
    rows, cols, c1 = pre_first.shape
    c0 = inputs.shape[2]
    half, pooled = cols // 2, rows // 2
    lats, lons = lax.axis_size("lat"), lax.axis_size("lon")
    depths = lons // 2
    band, place = lax.axis_index("lat"), lax.axis_index("lon")
    core = lax.rem(place, 2)
    even = lax.rem(band, 2) == 0

    edge = -(-(rows + pooled + 4) // 16) * 16
    row_a, row_b, col_a, col_b, held_pre = pl.pallas_call(
        functools.partial(pack_kernel, lats),
        out_shape=(
            pltpu.VMEM((cols + half, c1), BF16),
            pltpu.VMEM((cols + half, c1), BF16),
            pltpu.VMEM((edge, c1), BF16),
            pltpu.VMEM((edge, c1), BF16),
            pltpu.VMEM(pre_first.shape, BF16),
        ),
        in_specs=far(2),
        out_specs=tuple(vmem(5)),
        scratch_shapes=[
            pltpu.VMEM((2, edge, c1), F32),
            pltpu.VMEM(grad_out.shape, BF16),
            pltpu.SemaphoreType.DMA((2,)),
        ],
        compiler_params=params(58),
        cost_estimate=pl.CostEstimate(flops=1000, bytes_accessed=1 << 18, transcendentals=0),
    )(pre_first, grad_out)
    pairs = [(j, (j + lons // 2) % lons) for j in range(lons)]
    pairs += [((lats - 1) * lons + j, (lats - 1) * lons + (j ^ 1)) for j in range(lons)]
    for i in range(1, lats - 1, 2):
        for j in range(lons):
            pairs += [(i * lons + j, (i + 1) * lons + j), ((i + 1) * lons + j, i * lons + j)]
    every = [(i * lons + j, (i ^ 1) * lons + j) for i in range(lats) for j in range(lons)]
    row_b = lax.ppermute(row_b, AREA, pairs)
    row_a = lax.ppermute(row_a, AREA, every)

    slope, act_t, act_ends = pl.pallas_call(
        local_kernel,
        out_shape=(
            shape((rows, half, 2 * c1), F32),
            shape((2, 2 * c1, pooled * half), BF16),
            shape((2, rows, c1), F32),
        ),
        in_specs=vmem(1),
        out_specs=tuple(vmem(3)),
        scratch_shapes=[
            pltpu.VMEM((cols, c1), F32),
            pltpu.VMEM((2, pooled, half, 2 * c1), BF16),
        ],
        compiler_params=params(16),
        cost_estimate=pl.CostEstimate(flops=60 * rows * cols * c1, bytes_accessed=2 << 20,
                                      transcendentals=2 * rows * cols * c1),
    )(held_pre)

    fields_t, field_ends, taps_first, taps_second = pl.pallas_call(
        layout_kernel,
        out_shape=(
            shape((2 * c0, rows * half), BF16),
            shape((2 * c0, 2 * rows), BF16),
            shape((6 * c0, 4 * c1), BF16),
            shape((3, 2 * c1, 4 * c1), BF16),
        ),
        in_specs=vmem(3),
        out_specs=tuple(vmem(4)),
        scratch_shapes=[pltpu.VMEM((rows, c0, 2 * cols), BF16)],
        compiler_params=params(16),
        cost_estimate=pl.CostEstimate(flops=4 * rows * cols * c0 * cols, bytes_accessed=3 << 20, transcendentals=0),
    )(jnp.transpose(inputs, (0, 2, 1)), w_first, w_second)
    row_b, row_a, slope, fields_t = lax.optimization_barrier((row_b, row_a, slope, fields_t))

    def corners(at):
        places = (at * (cols - 1), cols + at * (half - 1))
        above, below = (jnp.where(even, one, two) for one, two in ((row_b, row_a), (row_a, row_b)))
        return jnp.concatenate([part[p:p + 1] for p in places for part in (above, below)], 0)

    low, high = corners(0), corners(1)
    pad = jnp.zeros((edge - rows - pooled - 4, c1), BF16)
    col_a = jnp.concatenate([col_a[:rows + pooled], jnp.where(core == 0, high, low), pad], 0)
    col_b = jnp.concatenate([col_b[:rows + pooled], jnp.where(core == 0, low, high), pad], 0)
    col_b = lax.ppermute(col_b, "lon", [(i, (i + 2 * (i % 2) - 1) % lons) for i in range(lons)])
    col_a = lax.ppermute(col_a, "lon", [(i, i ^ 1) for i in range(lons)])

    block = -(-9 * (c1 + c0) // (16 * lats)) * 8
    held = lats * block
    reach = -(-(rows + 2) // 16) * 16
    spread, keep, raw_ends, slope_ends, out_ends = pl.pallas_call(
        functools.partial(middle_kernel, lats),
        out_shape=(
            shape((rows + 3, half, 4 * c1), BF16),
            shape((2 * held, c1), F32),
            shape((2, reach, c1), F32),
            shape((2, reach, c1), F32),
            shape((2, -(-(pooled + 2) // 16) * 16, c1), F32),
        ),
        in_specs=vmem(7),
        out_specs=tuple(vmem(5)),
        scratch_shapes=[
            pltpu.VMEM((pooled + 2, half, c1), F32),
            pltpu.VMEM((pooled + 2, half, 4 * c1), BF16),
            pltpu.VMEM((3, pooled + 2, half, 2 * c1), F32),
            pltpu.VMEM((cols, c1), F32),
            pltpu.VMEM((4, 2 * c1, 3 * c1), F32),
            pltpu.VMEM((2 * c1, 3 * c1), F32),
        ],
        compiler_params=params(16),
        cost_estimate=pl.CostEstimate(flops=2 * rows * cols * c1 * 9 * (2 * c1 + c0), bytes_accessed=8 << 20,
                                      transcendentals=0),
    )(grad_out, row_a, row_b, slope, act_t, fields_t, taps_second)
    col_a, col_b, keep = lax.optimization_barrier((col_a, col_b, keep))

    ends, *halves = pl.pallas_call(
        functools.partial(columns_kernel, lats),
        out_shape=(
            shape((4, reach, c1), BF16),
        ) + (shape((block, c1), F32),) * (2 * lats),
        in_specs=vmem(9),
        out_specs=tuple(vmem(2 * lats + 1)),
        scratch_shapes=[
            pltpu.VMEM((4, 4 * reach, 4 * c1), BF16),
            pltpu.VMEM((4, reach, c1), F32),
            pltpu.VMEM((4, 2 * rows, 4 * c1), BF16),
            pltpu.VMEM((2 * held, c1), F32),
        ],
        compiler_params=params(16),
        cost_estimate=pl.CostEstimate(flops=1 << 28, bytes_accessed=3 << 20, transcendentals=0),
    )(col_a, col_b, act_ends, field_ends, taps_second, keep, raw_ends, slope_ends, out_ends)

    swap = [(i, i ^ 1) for i in range(lons)]

    def between_chips(value, over_lat, over_lon):
        turn = odd(over_lat) ^ odd(over_lon)
        return lax.ppermute(value, AREA, [
            (i * lons + j, (i ^ over_lat) * lons + (j ^ (2 * over_lon) ^ turn)) for i in range(lats) for j in range(lons)])

    own, other = halves[:lats], halves[lats:]
    other = {far: lax.ppermute(other[far], "lon", swap) for far in reversed(range(lats))}
    parts = [own[far] + other[far] for far in range(lats)]
    got = [between_chips(parts[far].astype(BF16), far, 0) for far in reversed(range(1, lats))]
    grad_inputs = pl.pallas_call(
        functools.partial(last_kernel, lats),
        out_shape=shape((rows, c0, cols), BF16),
        in_specs=vmem(3),
        out_specs=vmem(1)[0],
        scratch_shapes=[
            pltpu.VMEM((rows + 3, half, 4 * c1), BF16),
            pltpu.VMEM((reach, 4 * c1), F32),
            pltpu.VMEM((2 * c0, rows * half), F32),
            pltpu.VMEM((pooled, c0, 2 * cols), BF16),
        ],
        compiler_params=params(12),
        cost_estimate=pl.CostEstimate(flops=2 * rows * cols * c1 * 9 * c0, bytes_accessed=3 << 20, transcendentals=0),
    )(spread, ends, taps_first)
    *got, grad_inputs = lax.optimization_barrier((*got, grad_inputs))
    total = parts[0]
    for value in got:
        total = total + value.astype(F32)
    part = total.astype(BF16)
    terms = [part] + [between_chips(part, 0, far) for far in range(1, depths)]
    terms = [term.astype(F32) for term in terms]
    while len(terms) > 1:
        terms = [terms[k + (k > 0)] + terms[k + (k == 0)] for k in range(0, len(terms), 2)]
    part = terms[0].astype(BF16)
    mine = jnp.stack([part] + [between_chips(part, far, 0) for far in range(1, lats)], 0)
    theirs = lax.ppermute(mine, "lon", swap)

    grad_w_first, grad_w_second = pl.pallas_call(
        gather_kernel,
        out_shape=(shape((9 * c0, c1), F32), shape((9 * c1, c1), F32)),
        in_specs=vmem(2),
        out_specs=tuple(vmem(2)),
        compiler_params=params(8),
        cost_estimate=pl.CostEstimate(flops=1000, bytes_accessed=3 << 19, transcendentals=0),
    )(mine, theirs)
    return (jnp.transpose(grad_inputs, (0, 2, 1)), grad_w_first.reshape(w_first.shape),
            grad_w_second.reshape(w_second.shape))


def solution(mesh):
    in_specs = (P("lat", "lon", None), P("lat", "lon", None), P("lat", "lon", None), P(), P())
    out_specs = (P("lat", "lon", None), P(), P())
    return jax.shard_map(body, mesh=mesh, in_specs=in_specs, out_specs=out_specs, check_vma=False)
```

```python
import functools

import jax
import jax.numpy as jnp
from jax import lax
from jax.experimental import pallas as pl
from jax.experimental.pallas import tpu as pltpu
from jax.sharding import PartitionSpec as P

inv_root = 0.7071067811865476
density = 0.3989422804014327

F32 = jnp.float32
BF16 = jnp.bfloat16
AREA = ("lat", "lon")


def cdf_of(value):
    return 0.5 * (1.0 + lax.erf(value * inv_root))


def slope_of(value, cdf):
    return 0.25 * (cdf + value * jnp.exp(-0.5 * value * value) * density)


def dot(left, right):
    return jnp.dot(left, right, preferred_element_type=F32)


def dot_nt(left, right):
    return lax.dot_general(left, right, (((1,), (1,)), ((), ())), preferred_element_type=F32)


def position(lats):
    band, place = lax.axis_index("lat"), lax.axis_index("lon")
    return band, band == 0, band == lats - 1, lax.rem(band, 2) == 0, lax.rem(place, 2)


def odd(value):
    for shift in (4, 2, 1):
        value = value ^ (value >> shift)
    return value & 1


def half_held():
    band, place = lax.axis_index("lat"), lax.axis_index("lon")
    return odd(band) ^ odd(place // 2) ^ (place % 2)


def pack_kernel(lats, pre_far, grad_far, row_a, row_b, col_a, col_b, pre, hold, grad_out, sems):
    copies = [pltpu.make_async_copy(pre_far, pre, sems.at[0]), pltpu.make_async_copy(grad_far, grad_out, sems.at[1])]
    for copy in copies:
        copy.start()
    for copy in copies:
        copy.wait()
    rows, cols, c1 = pre.shape
    pooled, half = grad_out.shape[:2]
    _, _, _, even, core = position(lats)
    for message, low in ((row_a, ~even), (row_b, even)):
        message[:cols] = pre[jnp.where(low, 0, rows - 1)]
        message[cols:] = grad_out[jnp.where(low, 0, pooled - 1)]
    hold[:, rows + pooled:] = jnp.zeros((2, hold.shape[1] - rows - pooled, c1), F32)
    for side, (p, g) in enumerate(((0, 0), (cols - 16, half - 16))):
        at = 15 * side
        for r in range(rows):
            hold[side, r:r + 1] = pre[r, p:p + 16].astype(F32)[at:at + 1]
        for i in range(pooled):
            hold[side, rows + i:rows + i + 1] = grad_out[i, g:g + 16].astype(F32)[at:at + 1]
    col_a[...] = hold[1 - core].astype(BF16)
    col_b[...] = hold[core].astype(BF16)


def one_at(where):
    return jnp.where(where, 1.0, 0.0).astype(BF16)


def local_kernel(pre, slope, act_t, act_ends, line, act_s):
    rows, cols, c1 = pre.shape
    half = cols // 2

    def one_row(r, carry):
        line[...] = pre[r].astype(F32)
        for pc in range(2):
            value = line[pl.ds(pc, half, stride=2), :]
            cdf = cdf_of(value)
            act = value * cdf
            act_s[r % 2, r // 2, :, pc * c1:(pc + 1) * c1] = act.astype(BF16)
            act_ends[pc, pl.ds(r, 1), :] = act[pc * (half - 1):pc * (half - 1) + 1]
            slope[r, :, pc * c1:(pc + 1) * c1] = slope_of(value, cdf)
        return carry

    lax.fori_loop(0, rows, one_row, 0)
    for pr in range(2):
        act_t[pr] = act_s[pr].reshape(rows // 2 * half, 2 * c1).T


def layout_kernel(fields, w_first, w_second, fields_t, field_ends, taps_first, taps_second, turned):
    rows, c0, cols = fields.shape
    c1 = w_first.shape[3]
    half = cols // 2
    col = lax.broadcasted_iota(jnp.int32, (cols, 2 * cols), 0)
    lane = lax.broadcasted_iota(jnp.int32, (cols, 2 * cols), 1)
    turn = lane // cols
    parity = (lane % cols) // half
    parity = parity + turn - 2 * parity * turn
    order = one_at(col == 2 * (lane % half) + parity)
    turned[...] = dot(fields[...].reshape(rows * c0, cols), order).astype(BF16).reshape(rows, c0, 2 * cols)
    low = lax.broadcasted_iota(jnp.int32, (c0, cols), 1) < half
    for q in range(rows // 2):
        fields_t[:c0, q * cols:(q + 1) * cols] = jnp.where(low, turned[2 * q, :, :cols], turned[2 * q + 1, :, cols:])
        fields_t[c0:, q * cols:(q + 1) * cols] = jnp.where(low, turned[2 * q, :, cols:], turned[2 * q + 1, :, :cols])
    cell = lax.broadcasted_iota(jnp.int32, (rows * half, 2 * rows), 0)
    n = lax.broadcasted_iota(jnp.int32, (rows * half, 2 * rows), 1)
    pick = one_at(cell == (n % rows) * half + (n // rows) * (half - 1))
    field_ends[...] = dot(fields_t[...], pick).astype(BF16)
    taps_second[...] = jnp.zeros_like(taps_second)
    taps_first[...] = jnp.zeros_like(taps_first)
    for a in range(3):
        for pc, blocks in ((0, (2, 1, None, 0)), (1, (None, 2, 0, 1))):
            for k, b in enumerate(blocks):
                if b is not None:
                    taps_second[a, pc * c1:(pc + 1) * c1, k * c1:(k + 1) * c1] = w_second[a, b]
        for pc, blocks in ((0, (2, 1, 0, None)), (1, (None, 2, 1, 0))):
            for k, b in enumerate(blocks):
                if b is not None:
                    start = (2 * a + pc) * c0
                    taps_first[start:start + c0, k * c1:(k + 1) * c1] = w_first[a, b]


def middle_kernel(lats, grad_out, row_a, row_b, slope, act_t, fields_t, taps,
                  spread, keep, raw_ends, slope_ends, out_ends,
                  grid, wide, prods, ends, line, sums, corner):
    _, first, last, even, _ = position(lats)
    top = jnp.where(even, row_b[...], row_a[...])
    bottom = jnp.where(even, row_a[...], row_b[...])
    rows, half, c2 = slope.shape
    c1 = c2 // 2
    pooled = rows // 2
    c0 = fields_t.shape[0] // 2
    cells = pooled * half
    raw_ends[...] = jnp.zeros_like(raw_ends)
    slope_ends[...] = jnp.zeros_like(slope_ends)
    out_ends[...] = jnp.zeros_like(out_ends)

    grid[1:pooled + 1] = grad_out[...].astype(F32)
    grid[0] = top[2 * half:, :].astype(F32)
    outside = jnp.where(last, 0.0, 1.0)
    grid[pooled + 1] = bottom[2 * half:, :].astype(F32) * outside
    at = lax.broadcasted_iota(jnp.int32, (half, c1), 0)
    for i in range(pooled + 2):
        here = grid[i]
        out_ends[0, i:i + 1] = here[:1]
        out_ends[1, i:i + 1] = here[half - 1:]
        wide[i, :, :c1] = jnp.where(at == 0, 0.0, pltpu.roll(here, 1, 0)).astype(BF16)
        wide[i, :, c1:2 * c1] = here.astype(BF16)
        wide[i, :, 2 * c1:3 * c1] = jnp.where(at == half - 1, 0.0, pltpu.roll(here, half - 1, 0)).astype(BF16)
        wide[i, :, 3 * c1:] = here.astype(BF16)

    flat = wide[1:pooled + 1].reshape(cells, 4 * c1)
    for a in range(3):
        prods[a] = dot_nt(flat, taps[a]).reshape(pooled, half, c2)
    fold = jnp.where(first, taps[0], taps[2])
    ends[0] = dot_nt(wide[0], fold)
    ends[1] = dot_nt(wide[0], taps[1])
    ends[2] = dot_nt(wide[pooled + 1], taps[0])
    ends[3] = dot_nt(wide[pooled + 1], taps[1])

    def place(r, total, incline):
        inner = total * incline
        raw_ends[0, pl.ds(r, 1), :] = total[:1, :c1]
        raw_ends[1, pl.ds(r, 1), :] = total[half - 1:, c1:]
        slope_ends[0, pl.ds(r, 1), :] = incline[:1, :c1]
        slope_ends[1, pl.ds(r, 1), :] = incline[half - 1:, c1:]
        even, odd = inner[:, :c1], inner[:, c1:]
        spread[r, :, :c1] = jnp.where(at == 0, 0.0, pltpu.roll(odd, 1, 0)).astype(BF16)
        spread[r, :, c1:2 * c1] = jnp.where(at == 0, 0.0, even).astype(BF16)
        spread[r, :, 2 * c1:3 * c1] = jnp.where(at == half - 1, 0.0, odd).astype(BF16)
        spread[r, :, 3 * c1:] = jnp.where(at == half - 1, 0.0, pltpu.roll(even, half - 1, 0)).astype(BF16)

    def halo_slope(message):
        line[...] = message[:2 * half, :].astype(F32)
        both = [line[pl.ds(pc, half, stride=2), :] for pc in range(2)]
        return jnp.concatenate([slope_of(v, cdf_of(v)) for v in both], axis=1)

    place(0, ends[0] + ends[1] + prods[0, 0], halo_slope(top))
    place(1, ends[0] + prods[1, 0] + prods[0, 0], slope[0])

    def pair(i, carry):
        middle = prods[2, i] + prods[1, i]
        place(2 * i + 2, middle + prods[0, i + 1], slope[2 * i + 1])
        place(2 * i + 3, prods[2, i] + prods[1, i + 1] + prods[0, i + 1], slope[2 * i + 2])
        return carry

    lax.fori_loop(0, pooled - 1, pair, 0)
    final = prods[2, pooled - 1]
    place(rows, final + prods[1, pooled - 1] + ends[2], slope[rows - 1])
    place(rows + 1, (final + ends[3] + ends[2]) * outside, halo_slope(bottom))

    is_first = jnp.where(first, 1.0, 0.0).astype(BF16)
    not_first = jnp.where(first, 0.0, 1.0).astype(BF16)
    above = wide[0, :, :3 * c1]
    wide[0, :, :3 * c1] = above * not_first
    for n, (pr, start) in enumerate(((0, 0), (0, 1), (1, 1), (1, 2))):
        around = wide[start:start + pooled, :, :3 * c1].reshape(cells, 3 * c1)
        sums[n] = dot(act_t[pr], around)
    corner[...] = dot(act_t[0, :, :half], above * is_first)

    unit = c0
    per_tap = c1 // unit
    count = 9 * per_tap + 9

    def put(k, value):
        keep[k * unit:(k + 1) * unit, :] = value

    pieces = {0: ((0, 1), (1, 3)), 1: ((0, 1), (1, 2)), 2: ((0, 0), (1, 2))}
    for a in range(3):
        for b in range(3):
            total = None
            for pr, n in pieces[a]:
                for pc in range(2):
                    k = (pc + 1 - b) // 2 + 1
                    term = sums[n, pc * c1:(pc + 1) * c1, k * c1:(k + 1) * c1]
                    total = term if total is None else total + term
            if a == 0:
                for pc in range(2):
                    k = (pc + 1 - b) // 2 + 1
                    total = total + corner[pc * c1:(pc + 1) * c1, k * c1:(k + 1) * c1]
            total = total * 0.25
            for part in range(per_tap):
                put((3 * a + b) * per_tap + part, total[part * unit:(part + 1) * unit])

    head = spread[0]
    spread[0] = head * not_first
    spread[rows + 2] = head * is_first
    folded = dot(fields_t[:, :half], spread[rows + 2])
    for a in range(3):
        around = spread[2 - a:2 - a + rows].reshape(rows * half, 4 * c1)
        got = dot(fields_t[...], around)
        if a == 0:
            got = got + folded
        for b in range(3):
            even = got[:c0, (2 - b) * c1:(3 - b) * c1]
            odd = got[c0:, (3 - b) * c1:(4 - b) * c1]
            put(9 * per_tap + 3 * a + b, even + odd)
    if keep.shape[0] > count * unit:
        keep[count * unit:] = jnp.zeros((keep.shape[0] - count * unit, c1), F32)


def columns_kernel(lats, col_a, col_b, act_ends, field_ends, taps, keep, raw_ends, slope_ends, out_ends,
                   ends, *rest):
    own, other, (lhs, values, right_hand, total) = rest[:lats], rest[lats:2 * lats], rest[2 * lats:]
    band, first, last, _, core = position(lats)
    c1 = act_ends.shape[2]
    rows = act_ends.shape[1]
    pooled = rows // 2
    c0 = field_ends.shape[0] // 2
    span, size = raw_ends.shape[1], col_a.shape[0]
    got_a, got_b = col_a[...].astype(F32), col_b[...].astype(F32)
    message = jnp.concatenate([jnp.where(core == 0, got_b, got_a), jnp.where(core == 0, got_a, got_b)], 1)
    at = lax.broadcasted_iota(jnp.int32, (size, 2 * c1), 0)
    message = jnp.where(jnp.logical_and(at == rows + pooled + 3, last), 0.0, message).astype(BF16)

    n = lax.broadcasted_iota(jnp.int32, (3 * span, size), 0)
    k = lax.broadcasted_iota(jnp.int32, (3 * span, size), 1)
    row = n % span
    want = (row - n // span + 2) // 2 - 1
    place = jnp.where(want < 0, rows + pooled + 2, jnp.where(want == pooled, rows + pooled + 3, rows + want))
    beside = dot(one_at(jnp.logical_and(k == place, row < rows + 2)), message)
    n = lax.broadcasted_iota(jnp.int32, (3 * span, out_ends.shape[1]), 0)
    k = lax.broadcasted_iota(jnp.int32, (3 * span, out_ends.shape[1]), 1)
    row = n % span
    want = (row - n // span + 2) // 2
    pick = one_at(jnp.logical_and(k == want, row < rows + 2))
    within = dot(pick, jnp.concatenate([out_ends[0], out_ends[1]], 1).astype(BF16))
    n = lax.broadcasted_iota(jnp.int32, (span, size), 0)
    k = lax.broadcasted_iota(jnp.int32, (span, size), 1)
    place = jnp.where(n == 0, rows + pooled, jnp.where(n == rows + 1, rows + pooled + 1, n - 1))
    saved = dot(one_at(jnp.logical_and(k == place, n < rows + 2)), message)
    incline = slope_of(saved, cdf_of(saved))

    head = lax.broadcasted_iota(jnp.int32, (span, 2 * c1), 0) < 2
    turned = jnp.logical_and(head, first)
    lhs[...] = jnp.zeros_like(lhs)
    rights = []
    for a in range(4):
        sides, inner = (x[min(a, 2) * span:(min(a, 2) + 1) * span] for x in (beside, within))
        if a == 2:
            sides, inner = jnp.where(turned, 0.0, sides), jnp.where(turned, 0.0, inner)
        if a == 3:
            sides, inner = jnp.where(turned, sides, 0.0), jnp.where(turned, inner, 0.0)
        rights.append(sides)
        sides, inner = sides.astype(BF16), inner.astype(BF16)
        left, right = sides[:, :c1], sides[:, c1:]
        lhs[a, :span, c1:2 * c1] = left
        lhs[a, :span, 2 * c1:3 * c1] = inner[:, :c1]
        lhs[a, :span, 3 * c1:] = left
        lhs[a, span:2 * span, :c1] = left
        lhs[a, 2 * span:3 * span, :c1] = inner[:, c1:]
        lhs[a, 2 * span:3 * span, c1:2 * c1] = right
        lhs[a, 2 * span:3 * span, 3 * c1:] = right
        lhs[a, 3 * span:, 2 * c1:3 * c1] = right
    found = dot_nt(lhs[0], taps[0]) + dot_nt(lhs[1], taps[1]) + dot_nt(lhs[2], taps[2]) + dot_nt(lhs[3], taps[0])
    row = lax.broadcasted_iota(jnp.int32, (span, c1), 0)
    inside = jnp.where(jnp.logical_or(row > rows + 1, jnp.logical_and(row == rows + 1, last)), 0.0, 1.0)
    values[0] = found[:span, c1:] * incline[:, :c1] * inside
    values[1] = (raw_ends[0] + found[span:2 * span, :c1]) * slope_ends[0] * inside
    values[2] = (raw_ends[1] + found[3 * span:, c1:]) * slope_ends[1] * inside
    values[3] = found[2 * span:3 * span, :c1] * incline[:, c1:] * inside
    ends[...] = values[...].astype(BF16)

    total[...] = keep[...]
    for side, b in ((0, 2), (1, 0)):
        around = jnp.concatenate([x[1:rows + 1, side * c1:(side + 1) * c1] for x in rights], 1).astype(BF16)
        terms = lax.dot_general(act_ends[side].astype(BF16), around, (((0,), (0,)), ((), ())),
                                preferred_element_type=F32) * 0.25
        for a in range(3):
            term = terms[:, a * c1:(a + 1) * c1]
            if a == 0:
                term = term + terms[:, 3 * c1:]
            low = (3 * a + b) * c1
            total[low:low + c1] = total[low:low + c1] + term
    right_hand[...] = jnp.zeros_like(right_hand)
    top = lax.broadcasted_iota(jnp.int32, (rows, c1), 0) == 0
    over = jnp.logical_and(top, first)
    for a in range(4):
        for j in range(4):
            value = values[j, 2 - min(a, 2):2 - min(a, 2) + rows]
            if a == 2:
                value = jnp.where(over, 0.0, value)
            if a == 3:
                value = jnp.where(over, value, 0.0)
            right_hand[a, j // 2 * rows:(j // 2 + 1) * rows, j * c1:(j + 1) * c1] = value.astype(BF16)
    for a in range(3):
        got = dot(field_ends[...], right_hand[a])
        if a == 0:
            got = got + dot(field_ends[...], right_hand[3])
        for b in range(3):
            even = got[:c0, (2 - b) * c1:(3 - b) * c1]
            odd = got[c0:, (3 - b) * c1:(4 - b) * c1]
            low = 9 * c1 + (3 * a + b) * c0
            total[low:low + c0] = total[low:low + c0] + even + odd

    block = own[0].shape[0]
    mine = half_held()
    for targets, half_of in ((own, mine), (other, 1 - mine)):
        for far in range(lats):
            start = (half_of * lats + (band ^ far)) * block
            targets[far][...] = total[pl.ds(pl.multiple_of(start, block), block), :]


def last_kernel(lats, part, ends, taps, out, spread, values, total, turned):
    rows, c0, cols = out.shape
    half = cols // 2
    c2 = 2 * c0
    depth = spread.shape[2]
    first = position(lats)[1]
    spread[...] = part[...]
    c1 = depth // 4
    for j in range(4):
        values[:, j * c1:(j + 1) * c1] = ends[j].astype(F32)
    at = lax.broadcasted_iota(jnp.int32, (16, 2 * c1), 0)
    for r in range(rows + 3):
        n = 0 if r == rows + 2 else r
        for side, (low, spot) in enumerate(((0, 0), (half - 16, 15))):
            lanes = slice(2 * side * c1, 2 * (side + 1) * c1)
            new = values[n:n + 1, lanes]
            if n == 0:
                new = jnp.where(first == (r != 0), new, 0.0)
            tile = spread[r, low:low + 16, lanes].astype(F32)
            spread[r, low:low + 16, lanes] = jnp.where(at == spot, new, tile).astype(BF16)
    result = dot_nt(taps[:c2], spread[2:rows + 2].reshape(rows * half, depth))
    for a in (1, 2):
        result = result + dot_nt(taps[a * c2:(a + 1) * c2],
                                 spread[2 - a:2 - a + rows].reshape(rows * half, depth))
    total[...] = result
    total[:, :half] = total[:, :half] + dot_nt(taps[:c2], spread[rows + 2])
    for q in range(rows // 2):
        pair = total[:, q * cols:(q + 1) * cols].astype(BF16)
        turned[q, :, :cols] = pair[:c0]
        turned[q, :, cols:] = pair[c0:]
    k = lax.broadcasted_iota(jnp.int32, (2 * cols, 2 * cols), 0)
    n = lax.broadcasted_iota(jnp.int32, (2 * cols, 2 * cols), 1)
    order = one_at(n == ((k % cols) // half) * cols + 2 * (k % half) + k // cols)
    found = dot(turned[...].reshape(rows // 2 * c0, 2 * cols), order).astype(BF16)
    for q in range(rows // 2):
        for rp in range(2):
            out[2 * q + rp] = found[q * c0:(q + 1) * c0, rp * cols:(rp + 1) * cols]


def gather_kernel(mine, theirs, out_first, out_second):
    lats, rows, c1 = mine.shape
    band, held = lax.axis_index("lat"), half_held()
    size = out_second.shape[0]
    total = size + out_first.shape[0]
    for h in range(2):
        for i in range(lats):
            at = (h * lats + i) * rows
            here, there = (x[i ^ band].astype(F32) for x in (mine, theirs))
            value = jnp.where(held == h, here, there)
            for out, base, end in ((out_second, 0, size), (out_first, size, total)):
                low, high = max(at, base), min(at + rows, end)
                if low < high:
                    out[low - base:high - base] = value[low - at:high - at]


def vmem(count):
    return [pl.BlockSpec(memory_space=pltpu.VMEM)] * count


def far(count):
    return [pl.BlockSpec(memory_space=pl.ANY)] * count


def params(mib):
    return pltpu.CompilerParams(vmem_limit_bytes=mib * 1024 * 1024)


def shape(dims, kind):
    return jax.ShapeDtypeStruct(dims, kind)


def body(inputs, pre_first, grad_out, w_first, w_second):
    rows, cols, c1 = pre_first.shape
    c0 = inputs.shape[2]
    half, pooled = cols // 2, rows // 2
    lats, lons = lax.axis_size("lat"), lax.axis_size("lon")
    depths = lons // 2
    band, place = lax.axis_index("lat"), lax.axis_index("lon")
    core = lax.rem(place, 2)
    even = lax.rem(band, 2) == 0

    edge = -(-(rows + pooled + 4) // 16) * 16
    row_a, row_b, col_a, col_b, held_pre = pl.pallas_call(
        functools.partial(pack_kernel, lats),
        out_shape=(
            pltpu.VMEM((cols + half, c1), BF16),
            pltpu.VMEM((cols + half, c1), BF16),
            pltpu.VMEM((edge, c1), BF16),
            pltpu.VMEM((edge, c1), BF16),
            pltpu.VMEM(pre_first.shape, BF16),
        ),
        in_specs=far(2),
        out_specs=tuple(vmem(5)),
        scratch_shapes=[
            pltpu.VMEM((2, edge, c1), F32),
            pltpu.VMEM(grad_out.shape, BF16),
            pltpu.SemaphoreType.DMA((2,)),
        ],
        compiler_params=params(58),
        cost_estimate=pl.CostEstimate(flops=1000, bytes_accessed=1 << 18, transcendentals=0),
    )(pre_first, grad_out)
    pairs = [(j, (j + lons // 2) % lons) for j in range(lons)]
    pairs += [((lats - 1) * lons + j, (lats - 1) * lons + (j ^ 1)) for j in range(lons)]
    for i in range(1, lats - 1, 2):
        for j in range(lons):
            pairs += [(i * lons + j, (i + 1) * lons + j), ((i + 1) * lons + j, i * lons + j)]
    every = [(i * lons + j, (i ^ 1) * lons + j) for i in range(lats) for j in range(lons)]
    row_b = lax.ppermute(row_b, AREA, pairs)
    row_a = lax.ppermute(row_a, AREA, every)

    slope, act_t, act_ends = pl.pallas_call(
        local_kernel,
        out_shape=(
            shape((rows, half, 2 * c1), F32),
            shape((2, 2 * c1, pooled * half), BF16),
            shape((2, rows, c1), F32),
        ),
        in_specs=vmem(1),
        out_specs=tuple(vmem(3)),
        scratch_shapes=[
            pltpu.VMEM((cols, c1), F32),
            pltpu.VMEM((2, pooled, half, 2 * c1), BF16),
        ],
        compiler_params=params(16),
        cost_estimate=pl.CostEstimate(flops=60 * rows * cols * c1, bytes_accessed=2 << 20,
                                      transcendentals=2 * rows * cols * c1),
    )(held_pre)

    fields_t, field_ends, taps_first, taps_second = pl.pallas_call(
        layout_kernel,
        out_shape=(
            shape((2 * c0, rows * half), BF16),
            shape((2 * c0, 2 * rows), BF16),
            shape((6 * c0, 4 * c1), BF16),
            shape((3, 2 * c1, 4 * c1), BF16),
        ),
        in_specs=vmem(3),
        out_specs=tuple(vmem(4)),
        scratch_shapes=[pltpu.VMEM((rows, c0, 2 * cols), BF16)],
        compiler_params=params(16),
        cost_estimate=pl.CostEstimate(flops=4 * rows * cols * c0 * cols, bytes_accessed=3 << 20, transcendentals=0),
    )(jnp.transpose(inputs, (0, 2, 1)), w_first, w_second)
    row_b, row_a, slope, fields_t = lax.optimization_barrier((row_b, row_a, slope, fields_t))

    def corners(at):
        places = (at * (cols - 1), cols + at * (half - 1))
        above, below = (jnp.where(even, one, two) for one, two in ((row_b, row_a), (row_a, row_b)))
        return jnp.concatenate([part[p:p + 1] for p in places for part in (above, below)], 0)

    low, high = corners(0), corners(1)
    pad = jnp.zeros((edge - rows - pooled - 4, c1), BF16)
    col_a = jnp.concatenate([col_a[:rows + pooled], jnp.where(core == 0, high, low), pad], 0)
    col_b = jnp.concatenate([col_b[:rows + pooled], jnp.where(core == 0, low, high), pad], 0)
    col_b = lax.ppermute(col_b, "lon", [(i, (i + 2 * (i % 2) - 1) % lons) for i in range(lons)])
    col_a = lax.ppermute(col_a, "lon", [(i, i ^ 1) for i in range(lons)])

    block = -(-9 * (c1 + c0) // (16 * lats)) * 8
    held = lats * block
    reach = -(-(rows + 2) // 16) * 16
    spread, keep, raw_ends, slope_ends, out_ends = pl.pallas_call(
        functools.partial(middle_kernel, lats),
        out_shape=(
            shape((rows + 3, half, 4 * c1), BF16),
            shape((2 * held, c1), F32),
            shape((2, reach, c1), F32),
            shape((2, reach, c1), F32),
            shape((2, -(-(pooled + 2) // 16) * 16, c1), F32),
        ),
        in_specs=vmem(7),
        out_specs=tuple(vmem(5)),
        scratch_shapes=[
            pltpu.VMEM((pooled + 2, half, c1), F32),
            pltpu.VMEM((pooled + 2, half, 4 * c1), BF16),
            pltpu.VMEM((3, pooled, half, 2 * c1), F32),
            pltpu.VMEM((4, half, 2 * c1), F32),
            pltpu.VMEM((cols, c1), F32),
            pltpu.VMEM((4, 2 * c1, 3 * c1), F32),
            pltpu.VMEM((2 * c1, 3 * c1), F32),
        ],
        compiler_params=params(16),
        cost_estimate=pl.CostEstimate(flops=2 * rows * cols * c1 * 9 * (2 * c1 + c0), bytes_accessed=8 << 20,
                                      transcendentals=0),
    )(grad_out, row_a, row_b, slope, act_t, fields_t, taps_second)
    col_a, col_b, keep = lax.optimization_barrier((col_a, col_b, keep))

    ends, *halves = pl.pallas_call(
        functools.partial(columns_kernel, lats),
        out_shape=(
            shape((4, reach, c1), BF16),
        ) + (shape((block, c1), F32),) * (2 * lats),
        in_specs=vmem(9),
        out_specs=tuple(vmem(2 * lats + 1)),
        scratch_shapes=[
            pltpu.VMEM((4, 4 * reach, 4 * c1), BF16),
            pltpu.VMEM((4, reach, c1), F32),
            pltpu.VMEM((4, 2 * rows, 4 * c1), BF16),
            pltpu.VMEM((2 * held, c1), F32),
        ],
        compiler_params=params(16),
        cost_estimate=pl.CostEstimate(flops=1 << 28, bytes_accessed=3 << 20, transcendentals=0),
    )(col_a, col_b, act_ends, field_ends, taps_second, keep, raw_ends, slope_ends, out_ends)

    swap = [(i, i ^ 1) for i in range(lons)]

    def between_chips(value, over_lat, over_lon):
        turn = odd(over_lat) ^ odd(over_lon)
        return lax.ppermute(value, AREA, [
            (i * lons + j, (i ^ over_lat) * lons + (j ^ (2 * over_lon) ^ turn)) for i in range(lats) for j in range(lons)])

    own, other = halves[:lats], halves[lats:]
    swapped = {far: lax.ppermute(other[far], "lon", swap) for far in reversed(range(1, lats))}
    sent = {far: (own[far] + swapped[far]).astype(BF16) for far in reversed(range(1, lats))}
    sent[lats - 1], late = lax.optimization_barrier((sent[lats - 1], other[0]))
    got = [between_chips(sent[far], far, 0) for far in reversed(range(1, lats))]
    parts = [own[0] + lax.ppermute(late, "lon", swap)]
    grad_inputs = pl.pallas_call(
        functools.partial(last_kernel, lats),
        out_shape=shape((rows, c0, cols), BF16),
        in_specs=vmem(3),
        out_specs=vmem(1)[0],
        scratch_shapes=[
            pltpu.VMEM((rows + 3, half, 4 * c1), BF16),
            pltpu.VMEM((reach, 4 * c1), F32),
            pltpu.VMEM((2 * c0, rows * half), F32),
            pltpu.VMEM((pooled, c0, 2 * cols), BF16),
        ],
        compiler_params=params(12),
        cost_estimate=pl.CostEstimate(flops=2 * rows * cols * c1 * 9 * c0, bytes_accessed=3 << 20, transcendentals=0),
    )(spread, ends, taps_first)
    *got, grad_inputs = lax.optimization_barrier((*got, grad_inputs))
    total = parts[0]
    for value in got:
        total = total + value.astype(F32)
    part = total.astype(BF16)
    terms = [part] + [between_chips(part, 0, far) for far in range(1, depths)]
    terms = [term.astype(F32) for term in terms]
    while len(terms) > 1:
        terms = [terms[k + (k > 0)] + terms[k + (k == 0)] for k in range(0, len(terms), 2)]
    part = terms[0].astype(BF16)
    mine = jnp.stack([part] + [between_chips(part, far, 0) for far in range(1, lats)], 0)
    theirs = lax.ppermute(mine, "lon", swap)

    grad_w_first, grad_w_second = pl.pallas_call(
        gather_kernel,
        out_shape=(shape((9 * c0, c1), F32), shape((9 * c1, c1), F32)),
        in_specs=vmem(2),
        out_specs=tuple(vmem(2)),
        compiler_params=params(8),
        cost_estimate=pl.CostEstimate(flops=1000, bytes_accessed=3 << 19, transcendentals=0),
    )(mine, theirs)
    return (jnp.transpose(grad_inputs, (0, 2, 1)), grad_w_first.reshape(w_first.shape),
            grad_w_second.reshape(w_second.shape))


def solution(mesh):
    in_specs = (P("lat", "lon", None), P("lat", "lon", None), P("lat", "lon", None), P(), P())
    out_specs = (P("lat", "lon", None), P(), P())
    return jax.shard_map(body, mesh=mesh, in_specs=in_specs, out_specs=out_specs, check_vma=False)
```

```python
import functools

import jax
import jax.numpy as jnp
from jax import lax
from jax.experimental import pallas as pl
from jax.experimental.pallas import tpu as pltpu
from jax.sharding import PartitionSpec as P

inv_root = 0.7071067811865476
density = 0.3989422804014327

F32 = jnp.float32
BF16 = jnp.bfloat16
AREA = ("lat", "lon")


def cdf_of(value):
    return 0.5 * (1.0 + lax.erf(value * inv_root))


def slope_of(value, cdf):
    return 0.25 * (cdf + value * jnp.exp(-0.5 * value * value) * density)


def dot(left, right):
    return jnp.dot(left, right, preferred_element_type=F32)


def dot_nt(left, right):
    return lax.dot_general(left, right, (((1,), (1,)), ((), ())), preferred_element_type=F32)


def position(lats):
    band, place = lax.axis_index("lat"), lax.axis_index("lon")
    return band, band == 0, band == lats - 1, lax.rem(band, 2) == 0, lax.rem(place, 2)


def odd(value):
    for shift in (4, 2, 1):
        value = value ^ (value >> shift)
    return value & 1


def half_held():
    band, place = lax.axis_index("lat"), lax.axis_index("lon")
    return odd(band) ^ odd(place // 2) ^ (place % 2)


def pack_kernel(lats, pre_far, grad_far, row_a, row_b, col_a, col_b, pre, hold, grad_out, sems):
    copies = [pltpu.make_async_copy(pre_far, pre, sems.at[0]), pltpu.make_async_copy(grad_far, grad_out, sems.at[1])]
    for copy in copies:
        copy.start()
    for copy in copies:
        copy.wait()
    rows, cols, c1 = pre.shape
    pooled, half = grad_out.shape[:2]
    _, _, _, even, core = position(lats)
    for message, low in ((row_a, ~even), (row_b, even)):
        message[:cols] = pre[jnp.where(low, 0, rows - 1)]
        message[cols:] = grad_out[jnp.where(low, 0, pooled - 1)]
    hold[:, rows + pooled:] = jnp.zeros((2, hold.shape[1] - rows - pooled, c1), F32)
    for side, (p, g) in enumerate(((0, 0), (cols - 16, half - 16))):
        at = 15 * side
        for r in range(rows):
            hold[side, r:r + 1] = pre[r, p:p + 16].astype(F32)[at:at + 1]
        for i in range(pooled):
            hold[side, rows + i:rows + i + 1] = grad_out[i, g:g + 16].astype(F32)[at:at + 1]
    col_a[...] = hold[1 - core].astype(BF16)
    col_b[...] = hold[core].astype(BF16)


def one_at(where):
    return jnp.where(where, 1.0, 0.0).astype(BF16)


def local_kernel(pre, slope, act_t, act_ends, line, act_s):
    rows, cols, c1 = pre.shape
    half = cols // 2

    def one_row(r, carry):
        line[...] = pre[r].astype(F32)
        for pc in range(2):
            value = line[pl.ds(pc, half, stride=2), :]
            cdf = cdf_of(value)
            act = value * cdf
            act_s[r % 2, r // 2, :, pc * c1:(pc + 1) * c1] = act.astype(BF16)
            act_ends[pc, pl.ds(r, 1), :] = act[pc * (half - 1):pc * (half - 1) + 1]
            slope[r, :, pc * c1:(pc + 1) * c1] = slope_of(value, cdf)
        return carry

    lax.fori_loop(0, rows, one_row, 0)
    for pr in range(2):
        act_t[pr] = act_s[pr].reshape(rows // 2 * half, 2 * c1).T


def layout_kernel(fields, w_first, w_second, fields_t, field_ends, taps_first, taps_second, turned):
    rows, c0, cols = fields.shape
    c1 = w_first.shape[3]
    half = cols // 2
    col = lax.broadcasted_iota(jnp.int32, (cols, 2 * cols), 0)
    lane = lax.broadcasted_iota(jnp.int32, (cols, 2 * cols), 1)
    turn = lane // cols
    parity = (lane % cols) // half
    parity = parity + turn - 2 * parity * turn
    order = one_at(col == 2 * (lane % half) + parity)
    turned[...] = dot(fields[...].reshape(rows * c0, cols), order).astype(BF16).reshape(rows, c0, 2 * cols)
    low = lax.broadcasted_iota(jnp.int32, (c0, cols), 1) < half
    for q in range(rows // 2):
        fields_t[:c0, q * cols:(q + 1) * cols] = jnp.where(low, turned[2 * q, :, :cols], turned[2 * q + 1, :, cols:])
        fields_t[c0:, q * cols:(q + 1) * cols] = jnp.where(low, turned[2 * q, :, cols:], turned[2 * q + 1, :, :cols])
    cell = lax.broadcasted_iota(jnp.int32, (rows * half, 2 * rows), 0)
    n = lax.broadcasted_iota(jnp.int32, (rows * half, 2 * rows), 1)
    pick = one_at(cell == (n % rows) * half + (n // rows) * (half - 1))
    field_ends[...] = dot(fields_t[...], pick).astype(BF16)
    taps_second[...] = jnp.zeros_like(taps_second)
    taps_first[...] = jnp.zeros_like(taps_first)
    for a in range(3):
        for pc, blocks in ((0, (2, 1, None, 0)), (1, (None, 2, 0, 1))):
            for k, b in enumerate(blocks):
                if b is not None:
                    taps_second[a, pc * c1:(pc + 1) * c1, k * c1:(k + 1) * c1] = w_second[a, b]
        for pc, blocks in ((0, (2, 1, 0, None)), (1, (None, 2, 1, 0))):
            for k, b in enumerate(blocks):
                if b is not None:
                    start = (2 * a + pc) * c0
                    taps_first[start:start + c0, k * c1:(k + 1) * c1] = w_first[a, b]


def middle_kernel(lats, grad_out, row_a, row_b, slope, act_t, fields_t, taps,
                  spread, keep, raw_ends, slope_ends, out_ends,
                  grid, wide, prods, ends, line, sums, corner):
    _, first, last, even, _ = position(lats)
    top = jnp.where(even, row_b[...], row_a[...])
    bottom = jnp.where(even, row_a[...], row_b[...])
    rows, half, c2 = slope.shape
    c1 = c2 // 2
    pooled = rows // 2
    c0 = fields_t.shape[0] // 2
    cells = pooled * half
    raw_ends[...] = jnp.zeros_like(raw_ends)
    slope_ends[...] = jnp.zeros_like(slope_ends)
    out_ends[...] = jnp.zeros_like(out_ends)

    grid[1:pooled + 1] = grad_out[...].astype(F32)
    grid[0] = top[2 * half:, :].astype(F32)
    outside = jnp.where(last, 0.0, 1.0)
    grid[pooled + 1] = bottom[2 * half:, :].astype(F32) * outside
    at = lax.broadcasted_iota(jnp.int32, (half, c1), 0)
    for i in range(pooled + 2):
        here = grid[i]
        out_ends[0, i:i + 1] = here[:1]
        out_ends[1, i:i + 1] = here[half - 1:]
        wide[i, :, :c1] = jnp.where(at == 0, 0.0, pltpu.roll(here, 1, 0)).astype(BF16)
        wide[i, :, c1:2 * c1] = here.astype(BF16)
        wide[i, :, 2 * c1:3 * c1] = jnp.where(at == half - 1, 0.0, pltpu.roll(here, half - 1, 0)).astype(BF16)
        wide[i, :, 3 * c1:] = here.astype(BF16)

    flat = wide[1:pooled + 1].reshape(cells, 4 * c1)
    for a in range(3):
        prods[a] = dot_nt(flat, taps[a]).reshape(pooled, half, c2)
    fold = jnp.where(first, taps[0], taps[2])
    ends[0] = dot_nt(wide[0], fold)
    ends[1] = dot_nt(wide[0], taps[1])
    ends[2] = dot_nt(wide[pooled + 1], taps[0])
    ends[3] = dot_nt(wide[pooled + 1], taps[1])

    def place(r, total, incline):
        inner = total * incline
        raw_ends[0, pl.ds(r, 1), :] = total[:1, :c1]
        raw_ends[1, pl.ds(r, 1), :] = total[half - 1:, c1:]
        slope_ends[0, pl.ds(r, 1), :] = incline[:1, :c1]
        slope_ends[1, pl.ds(r, 1), :] = incline[half - 1:, c1:]
        even, odd = inner[:, :c1], inner[:, c1:]
        spread[r, :, :c1] = jnp.where(at == 0, 0.0, pltpu.roll(odd, 1, 0)).astype(BF16)
        spread[r, :, c1:2 * c1] = jnp.where(at == 0, 0.0, even).astype(BF16)
        spread[r, :, 2 * c1:3 * c1] = jnp.where(at == half - 1, 0.0, odd).astype(BF16)
        spread[r, :, 3 * c1:] = jnp.where(at == half - 1, 0.0, pltpu.roll(even, half - 1, 0)).astype(BF16)

    def halo_slope(message):
        line[...] = message[:2 * half, :].astype(F32)
        both = [line[pl.ds(pc, half, stride=2), :] for pc in range(2)]
        return jnp.concatenate([slope_of(v, cdf_of(v)) for v in both], axis=1)

    place(0, ends[0] + ends[1] + prods[0, 0], halo_slope(top))
    place(1, ends[0] + prods[1, 0] + prods[0, 0], slope[0])

    def pair(i, carry):
        middle = prods[2, i] + prods[1, i]
        place(2 * i + 2, middle + prods[0, i + 1], slope[2 * i + 1])
        place(2 * i + 3, prods[2, i] + prods[1, i + 1] + prods[0, i + 1], slope[2 * i + 2])
        return carry

    lax.fori_loop(0, pooled - 1, pair, 0)
    final = prods[2, pooled - 1]
    place(rows, final + prods[1, pooled - 1] + ends[2], slope[rows - 1])
    place(rows + 1, (final + ends[3] + ends[2]) * outside, halo_slope(bottom))

    is_first = jnp.where(first, 1.0, 0.0).astype(BF16)
    not_first = jnp.where(first, 0.0, 1.0).astype(BF16)
    above = wide[0, :, :3 * c1]
    wide[0, :, :3 * c1] = above * not_first
    for n, (pr, start) in enumerate(((0, 0), (0, 1), (1, 1), (1, 2))):
        around = wide[start:start + pooled, :, :3 * c1].reshape(cells, 3 * c1)
        sums[n] = dot(act_t[pr], around)
    corner[...] = dot(act_t[0, :, :half], above * is_first)

    unit = c0
    per_tap = c1 // unit
    count = 9 * per_tap + 9

    def put(k, value):
        keep[k * unit:(k + 1) * unit, :] = value

    pieces = {0: ((0, 1), (1, 3)), 1: ((0, 1), (1, 2)), 2: ((0, 0), (1, 2))}
    for a in range(3):
        for b in range(3):
            total = None
            for pr, n in pieces[a]:
                for pc in range(2):
                    k = (pc + 1 - b) // 2 + 1
                    term = sums[n, pc * c1:(pc + 1) * c1, k * c1:(k + 1) * c1]
                    total = term if total is None else total + term
            if a == 0:
                for pc in range(2):
                    k = (pc + 1 - b) // 2 + 1
                    total = total + corner[pc * c1:(pc + 1) * c1, k * c1:(k + 1) * c1]
            total = total * 0.25
            for part in range(per_tap):
                put((3 * a + b) * per_tap + part, total[part * unit:(part + 1) * unit])

    head = spread[0]
    spread[0] = head * not_first
    spread[rows + 2] = head * is_first
    folded = dot(fields_t[:, :half], spread[rows + 2])
    for a in range(3):
        around = spread[2 - a:2 - a + rows].reshape(rows * half, 4 * c1)
        got = dot(fields_t[...], around)
        if a == 0:
            got = got + folded
        for b in range(3):
            even = got[:c0, (2 - b) * c1:(3 - b) * c1]
            odd = got[c0:, (3 - b) * c1:(4 - b) * c1]
            put(9 * per_tap + 3 * a + b, even + odd)
    if keep.shape[0] > count * unit:
        keep[count * unit:] = jnp.zeros((keep.shape[0] - count * unit, c1), F32)


def columns_kernel(lats, col_a, col_b, act_ends, field_ends, taps, keep, raw_ends, slope_ends, out_ends,
                   ends, *rest):
    own, other, (lhs, values, right_hand, total) = rest[:lats], rest[lats:2 * lats], rest[2 * lats:]
    band, first, last, _, core = position(lats)
    c1 = act_ends.shape[2]
    rows = act_ends.shape[1]
    pooled = rows // 2
    c0 = field_ends.shape[0] // 2
    span, size = raw_ends.shape[1], col_a.shape[0]
    got_a, got_b = col_a[...].astype(F32), col_b[...].astype(F32)
    message = jnp.concatenate([jnp.where(core == 0, got_b, got_a), jnp.where(core == 0, got_a, got_b)], 1)
    at = lax.broadcasted_iota(jnp.int32, (size, 2 * c1), 0)
    message = jnp.where(jnp.logical_and(at == rows + pooled + 3, last), 0.0, message).astype(BF16)

    n = lax.broadcasted_iota(jnp.int32, (3 * span, size), 0)
    k = lax.broadcasted_iota(jnp.int32, (3 * span, size), 1)
    row = n % span
    want = (row - n // span + 2) // 2 - 1
    place = jnp.where(want < 0, rows + pooled + 2, jnp.where(want == pooled, rows + pooled + 3, rows + want))
    beside = dot(one_at(jnp.logical_and(k == place, row < rows + 2)), message)
    n = lax.broadcasted_iota(jnp.int32, (3 * span, out_ends.shape[1]), 0)
    k = lax.broadcasted_iota(jnp.int32, (3 * span, out_ends.shape[1]), 1)
    row = n % span
    want = (row - n // span + 2) // 2
    pick = one_at(jnp.logical_and(k == want, row < rows + 2))
    within = dot(pick, jnp.concatenate([out_ends[0], out_ends[1]], 1).astype(BF16))
    n = lax.broadcasted_iota(jnp.int32, (span, size), 0)
    k = lax.broadcasted_iota(jnp.int32, (span, size), 1)
    place = jnp.where(n == 0, rows + pooled, jnp.where(n == rows + 1, rows + pooled + 1, n - 1))
    saved = dot(one_at(jnp.logical_and(k == place, n < rows + 2)), message)
    incline = slope_of(saved, cdf_of(saved))

    head = lax.broadcasted_iota(jnp.int32, (span, 2 * c1), 0) < 2
    turned = jnp.logical_and(head, first)
    lhs[...] = jnp.zeros_like(lhs)
    rights = []
    for a in range(4):
        sides, inner = (x[min(a, 2) * span:(min(a, 2) + 1) * span] for x in (beside, within))
        if a == 2:
            sides, inner = jnp.where(turned, 0.0, sides), jnp.where(turned, 0.0, inner)
        if a == 3:
            sides, inner = jnp.where(turned, sides, 0.0), jnp.where(turned, inner, 0.0)
        rights.append(sides)
        sides, inner = sides.astype(BF16), inner.astype(BF16)
        left, right = sides[:, :c1], sides[:, c1:]
        lhs[a, :span, c1:2 * c1] = left
        lhs[a, :span, 2 * c1:3 * c1] = inner[:, :c1]
        lhs[a, :span, 3 * c1:] = left
        lhs[a, span:2 * span, :c1] = left
        lhs[a, 2 * span:3 * span, :c1] = inner[:, c1:]
        lhs[a, 2 * span:3 * span, c1:2 * c1] = right
        lhs[a, 2 * span:3 * span, 3 * c1:] = right
        lhs[a, 3 * span:, 2 * c1:3 * c1] = right
    found = dot_nt(lhs[0], taps[0]) + dot_nt(lhs[1], taps[1]) + dot_nt(lhs[2], taps[2]) + dot_nt(lhs[3], taps[0])
    row = lax.broadcasted_iota(jnp.int32, (span, c1), 0)
    inside = jnp.where(jnp.logical_or(row > rows + 1, jnp.logical_and(row == rows + 1, last)), 0.0, 1.0)
    values[0] = found[:span, c1:] * incline[:, :c1] * inside
    values[1] = (raw_ends[0] + found[span:2 * span, :c1]) * slope_ends[0] * inside
    values[2] = (raw_ends[1] + found[3 * span:, c1:]) * slope_ends[1] * inside
    values[3] = found[2 * span:3 * span, :c1] * incline[:, c1:] * inside
    ends[...] = values[...].astype(BF16)

    total[...] = keep[...]
    for side, b in ((0, 2), (1, 0)):
        around = jnp.concatenate([x[1:rows + 1, side * c1:(side + 1) * c1] for x in rights], 1).astype(BF16)
        terms = lax.dot_general(act_ends[side].astype(BF16), around, (((0,), (0,)), ((), ())),
                                preferred_element_type=F32) * 0.25
        for a in range(3):
            term = terms[:, a * c1:(a + 1) * c1]
            if a == 0:
                term = term + terms[:, 3 * c1:]
            low = (3 * a + b) * c1
            total[low:low + c1] = total[low:low + c1] + term
    right_hand[...] = jnp.zeros_like(right_hand)
    top = lax.broadcasted_iota(jnp.int32, (rows, c1), 0) == 0
    over = jnp.logical_and(top, first)
    for a in range(4):
        for j in range(4):
            value = values[j, 2 - min(a, 2):2 - min(a, 2) + rows]
            if a == 2:
                value = jnp.where(over, 0.0, value)
            if a == 3:
                value = jnp.where(over, value, 0.0)
            right_hand[a, j // 2 * rows:(j // 2 + 1) * rows, j * c1:(j + 1) * c1] = value.astype(BF16)
    for a in range(3):
        got = dot(field_ends[...], right_hand[a])
        if a == 0:
            got = got + dot(field_ends[...], right_hand[3])
        for b in range(3):
            even = got[:c0, (2 - b) * c1:(3 - b) * c1]
            odd = got[c0:, (3 - b) * c1:(4 - b) * c1]
            low = 9 * c1 + (3 * a + b) * c0
            total[low:low + c0] = total[low:low + c0] + even + odd

    block = own[0].shape[0]
    mine = half_held()
    for targets, half_of in ((own, mine), (other, 1 - mine)):
        for far in range(lats):
            start = (half_of * lats + (band ^ far)) * block
            targets[far][...] = total[pl.ds(pl.multiple_of(start, block), block), :]


def last_kernel(lats, part, ends, taps, out, spread, values, total, turned):
    rows, c0, cols = out.shape
    half = cols // 2
    c2 = 2 * c0
    depth = spread.shape[2]
    first = position(lats)[1]
    spread[...] = part[...]
    c1 = depth // 4
    for j in range(4):
        values[:, j * c1:(j + 1) * c1] = ends[j].astype(F32)
    at = lax.broadcasted_iota(jnp.int32, (16, 2 * c1), 0)
    for r in range(rows + 3):
        n = 0 if r == rows + 2 else r
        for side, (low, spot) in enumerate(((0, 0), (half - 16, 15))):
            lanes = slice(2 * side * c1, 2 * (side + 1) * c1)
            new = values[n:n + 1, lanes]
            if n == 0:
                new = jnp.where(first == (r != 0), new, 0.0)
            tile = spread[r, low:low + 16, lanes].astype(F32)
            spread[r, low:low + 16, lanes] = jnp.where(at == spot, new, tile).astype(BF16)
    result = dot_nt(taps[:c2], spread[2:rows + 2].reshape(rows * half, depth))
    for a in (1, 2):
        result = result + dot_nt(taps[a * c2:(a + 1) * c2],
                                 spread[2 - a:2 - a + rows].reshape(rows * half, depth))
    total[...] = result
    total[:, :half] = total[:, :half] + dot_nt(taps[:c2], spread[rows + 2])
    for q in range(rows // 2):
        pair = total[:, q * cols:(q + 1) * cols].astype(BF16)
        turned[q, :, :cols] = pair[:c0]
        turned[q, :, cols:] = pair[c0:]
    k = lax.broadcasted_iota(jnp.int32, (2 * cols, 2 * cols), 0)
    n = lax.broadcasted_iota(jnp.int32, (2 * cols, 2 * cols), 1)
    order = one_at(n == ((k % cols) // half) * cols + 2 * (k % half) + k // cols)
    found = dot(turned[...].reshape(rows // 2 * c0, 2 * cols), order).astype(BF16)
    for q in range(rows // 2):
        for rp in range(2):
            out[2 * q + rp] = found[q * c0:(q + 1) * c0, rp * cols:(rp + 1) * cols]


def gather_kernel(mine, theirs, out_first, out_second):
    lats, rows, c1 = mine.shape
    band, held = lax.axis_index("lat"), half_held()
    size = out_second.shape[0]
    total = size + out_first.shape[0]
    for h in range(2):
        for i in range(lats):
            at = (h * lats + i) * rows
            here, there = (x[i ^ band].astype(F32) for x in (mine, theirs))
            value = jnp.where(held == h, here, there)
            for out, base, end in ((out_second, 0, size), (out_first, size, total)):
                low, high = max(at, base), min(at + rows, end)
                if low < high:
                    out[low - base:high - base] = value[low - at:high - at]


def vmem(count):
    return [pl.BlockSpec(memory_space=pltpu.VMEM)] * count


def far(count):
    return [pl.BlockSpec(memory_space=pl.ANY)] * count


def params(mib):
    return pltpu.CompilerParams(vmem_limit_bytes=mib * 1024 * 1024)


def shape(dims, kind):
    return jax.ShapeDtypeStruct(dims, kind)


def body(inputs, pre_first, grad_out, w_first, w_second):
    rows, cols, c1 = pre_first.shape
    c0 = inputs.shape[2]
    half, pooled = cols // 2, rows // 2
    lats, lons = lax.axis_size("lat"), lax.axis_size("lon")
    depths = lons // 2
    band, place = lax.axis_index("lat"), lax.axis_index("lon")
    core = lax.rem(place, 2)
    even = lax.rem(band, 2) == 0

    edge = -(-(rows + pooled + 4) // 16) * 16
    row_a, row_b, col_a, col_b, held_pre = pl.pallas_call(
        functools.partial(pack_kernel, lats),
        out_shape=(
            pltpu.VMEM((cols + half, c1), BF16),
            pltpu.VMEM((cols + half, c1), BF16),
            pltpu.VMEM((edge, c1), BF16),
            pltpu.VMEM((edge, c1), BF16),
            pltpu.VMEM(pre_first.shape, BF16),
        ),
        in_specs=far(2),
        out_specs=tuple(vmem(5)),
        scratch_shapes=[
            pltpu.VMEM((2, edge, c1), F32),
            pltpu.VMEM(grad_out.shape, BF16),
            pltpu.SemaphoreType.DMA((2,)),
        ],
        compiler_params=params(58),
        cost_estimate=pl.CostEstimate(flops=1000, bytes_accessed=1 << 18, transcendentals=0),
    )(pre_first, grad_out)
    pairs = [(j, (j + lons // 2) % lons) for j in range(lons)]
    pairs += [((lats - 1) * lons + j, (lats - 1) * lons + (j ^ 1)) for j in range(lons)]
    for i in range(1, lats - 1, 2):
        for j in range(lons):
            pairs += [(i * lons + j, (i + 1) * lons + j), ((i + 1) * lons + j, i * lons + j)]
    every = [(i * lons + j, (i ^ 1) * lons + j) for i in range(lats) for j in range(lons)]
    row_b = lax.ppermute(row_b, AREA, pairs)
    row_a = lax.ppermute(row_a, AREA, every)

    slope, act_t, act_ends = pl.pallas_call(
        local_kernel,
        out_shape=(
            shape((rows, half, 2 * c1), F32),
            shape((2, 2 * c1, pooled * half), BF16),
            shape((2, rows, c1), F32),
        ),
        in_specs=vmem(1),
        out_specs=tuple(vmem(3)),
        scratch_shapes=[
            pltpu.VMEM((cols, c1), F32),
            pltpu.VMEM((2, pooled, half, 2 * c1), BF16),
        ],
        compiler_params=params(16),
        cost_estimate=pl.CostEstimate(flops=60 * rows * cols * c1, bytes_accessed=2 << 20,
                                      transcendentals=2 * rows * cols * c1),
    )(held_pre)

    fields_t, field_ends, taps_first, taps_second = pl.pallas_call(
        layout_kernel,
        out_shape=(
            shape((2 * c0, rows * half), BF16),
            shape((2 * c0, 2 * rows), BF16),
            shape((6 * c0, 4 * c1), BF16),
            shape((3, 2 * c1, 4 * c1), BF16),
        ),
        in_specs=vmem(3),
        out_specs=tuple(vmem(4)),
        scratch_shapes=[pltpu.VMEM((rows, c0, 2 * cols), BF16)],
        compiler_params=params(16),
        cost_estimate=pl.CostEstimate(flops=4 * rows * cols * c0 * cols, bytes_accessed=3 << 20, transcendentals=0),
    )(jnp.transpose(inputs, (0, 2, 1)), w_first, w_second)
    row_b, row_a, slope, fields_t = lax.optimization_barrier((row_b, row_a, slope, fields_t))

    def corners(at):
        places = (at * (cols - 1), cols + at * (half - 1))
        above, below = (jnp.where(even, one, two) for one, two in ((row_b, row_a), (row_a, row_b)))
        return jnp.concatenate([part[p:p + 1] for p in places for part in (above, below)], 0)

    low, high = corners(0), corners(1)
    pad = jnp.zeros((edge - rows - pooled - 4, c1), BF16)
    col_a = jnp.concatenate([col_a[:rows + pooled], jnp.where(core == 0, high, low), pad], 0)
    col_b = jnp.concatenate([col_b[:rows + pooled], jnp.where(core == 0, low, high), pad], 0)
    col_b = lax.ppermute(col_b, "lon", [(i, (i + 2 * (i % 2) - 1) % lons) for i in range(lons)])
    col_a = lax.ppermute(col_a, "lon", [(i, i ^ 1) for i in range(lons)])

    block = -(-9 * (c1 + c0) // (16 * lats)) * 8
    held = lats * block
    reach = -(-(rows + 2) // 16) * 16
    spread, keep, raw_ends, slope_ends, out_ends = pl.pallas_call(
        functools.partial(middle_kernel, lats),
        out_shape=(
            shape((rows + 3, half, 4 * c1), BF16),
            shape((2 * held, c1), F32),
            shape((2, reach, c1), F32),
            shape((2, reach, c1), F32),
            shape((2, -(-(pooled + 2) // 16) * 16, c1), F32),
        ),
        in_specs=vmem(7),
        out_specs=tuple(vmem(5)),
        scratch_shapes=[
            pltpu.VMEM((pooled + 2, half, c1), F32),
            pltpu.VMEM((pooled + 2, half, 4 * c1), BF16),
            pltpu.VMEM((3, pooled, half, 2 * c1), F32),
            pltpu.VMEM((4, half, 2 * c1), F32),
            pltpu.VMEM((cols, c1), F32),
            pltpu.VMEM((4, 2 * c1, 3 * c1), F32),
            pltpu.VMEM((2 * c1, 3 * c1), F32),
        ],
        compiler_params=params(16),
        cost_estimate=pl.CostEstimate(flops=2 * rows * cols * c1 * 9 * (2 * c1 + c0), bytes_accessed=8 << 20,
                                      transcendentals=0),
    )(grad_out, row_a, row_b, slope, act_t, fields_t, taps_second)
    col_a, col_b, keep = lax.optimization_barrier((col_a, col_b, keep))

    ends, *halves = pl.pallas_call(
        functools.partial(columns_kernel, lats),
        out_shape=(
            shape((4, reach, c1), BF16),
        ) + (shape((block, c1), F32),) * (2 * lats),
        in_specs=vmem(9),
        out_specs=tuple(vmem(2 * lats + 1)),
        scratch_shapes=[
            pltpu.VMEM((4, 4 * reach, 4 * c1), BF16),
            pltpu.VMEM((4, reach, c1), F32),
            pltpu.VMEM((4, 2 * rows, 4 * c1), BF16),
            pltpu.VMEM((2 * held, c1), F32),
        ],
        compiler_params=params(16),
        cost_estimate=pl.CostEstimate(flops=1 << 28, bytes_accessed=3 << 20, transcendentals=0),
    )(col_a, col_b, act_ends, field_ends, taps_second, keep, raw_ends, slope_ends, out_ends)

    swap = [(i, i ^ 1) for i in range(lons)]

    def between_chips(value, over_lat, over_lon):
        turn = odd(over_lat) ^ odd(over_lon)
        return lax.ppermute(value, AREA, [
            (i * lons + j, (i ^ over_lat) * lons + (j ^ (2 * over_lon) ^ turn)) for i in range(lats) for j in range(lons)])

    own, other = halves[:lats], halves[lats:]
    other = {far: lax.ppermute(other[far], "lon", swap) for far in reversed(range(lats))}
    parts = [own[far] + other[far] for far in range(lats)]
    got = [between_chips(parts[far].astype(BF16), far, 0) for far in reversed(range(1, lats))]
    grad_inputs = pl.pallas_call(
        functools.partial(last_kernel, lats),
        out_shape=shape((rows, c0, cols), BF16),
        in_specs=vmem(3),
        out_specs=vmem(1)[0],
        scratch_shapes=[
            pltpu.VMEM((rows + 3, half, 4 * c1), BF16),
            pltpu.VMEM((reach, 4 * c1), F32),
            pltpu.VMEM((2 * c0, rows * half), F32),
            pltpu.VMEM((pooled, c0, 2 * cols), BF16),
        ],
        compiler_params=params(12),
        cost_estimate=pl.CostEstimate(flops=2 * rows * cols * c1 * 9 * c0, bytes_accessed=3 << 20, transcendentals=0),
    )(spread, ends, taps_first)
    *got, grad_inputs = lax.optimization_barrier((*got, grad_inputs))
    total = parts[0]
    for value in got:
        total = total + value.astype(F32)
    part = total.astype(BF16)
    terms = [part] + [between_chips(part, 0, far) for far in range(1, depths)]
    terms = [term.astype(F32) for term in terms]
    while len(terms) > 1:
        terms = [terms[k] + terms[k + 1] for k in range(0, len(terms), 2)]
    part = terms[0].astype(BF16)
    mine = jnp.stack([part] + [between_chips(part, far, 0) for far in range(1, lats)], 0)
    theirs = lax.ppermute(mine, "lon", swap)

    grad_w_first, grad_w_second = pl.pallas_call(
        gather_kernel,
        out_shape=(shape((9 * c0, c1), F32), shape((9 * c1, c1), F32)),
        in_specs=vmem(2),
        out_specs=tuple(vmem(2)),
        compiler_params=params(8),
        cost_estimate=pl.CostEstimate(flops=1000, bytes_accessed=3 << 19, transcendentals=0),
    )(mine, theirs)
    return (jnp.transpose(grad_inputs, (0, 2, 1)), grad_w_first.reshape(w_first.shape),
            grad_w_second.reshape(w_second.shape))


def solution(mesh):
    in_specs = (P("lat", "lon", None), P("lat", "lon", None), P("lat", "lon", None), P(), P())
    out_specs = (P("lat", "lon", None), P(), P())
    return jax.shard_map(body, mesh=mesh, in_specs=in_specs, out_specs=out_specs, check_vma=False)
```
